32 devices in a mesh: dp: 8 (over y, x, core), head: 4 (over z).
Axes of the slice: x: 2, y: 2, z: 4, core: 2. Of those that a mesh axis runs over, the one named last changes fastest.
Arguments:
- char_ids: int32 [16, 1024, 16], P('dp', 'head'), may hold values from 0 to 255
- char_counts: int32 [16, 1024], P('dp', 'head'), may hold values from 1 to 16
- language: int32 [16], P('dp'), may hold values from 0 to 3
- words_in: bfloat16 [16, 1024, 512], P('dp', 'head'), may hold values from -6 to 6
- out_cotangent: bfloat16 [16, 1024, 512], P('dp', 'head'), may hold values from -6 to 6
- char_table: float32 [1024, 256], P('dp', 'head'), may hold values from -0.6 to 0.6
- char_in: float32 [256, 2560], P('dp', 'head'), may hold values from -1.06066017 to 1.06066017
- char_down: float32 [1024, 256], P('dp', 'head'), may hold values from -0.1875 to 0.1875
- word_in: float32 [512, 4096], P('dp', 'head'), may hold values from -1.5 to 1.5
- word_down: float32 [2048, 512], P('dp', 'head'), may hold values from -0.125 to 0.125
- norm_gains: float32 [1536], replicated, may hold values from 0.4 to 3
- old_table_first: float32 [1024, 256], P('dp', 'head'), may hold values from -0.0029296875 to 0.0029296875
- old_table_second: float32 [1024, 256], P('dp', 'head'), may hold values from 2.311117e-07 to 9.244468e-07
- old_char_in_first: float32 [256, 2560], P('dp', 'head'), may hold values from -0.0029296875 to 0.0029296875
- old_char_in_second: float32 [256, 2560], P('dp', 'head'), may hold values from 2.311117e-07 to 9.244468e-07
- old_char_down_first: float32 [1024, 256], P('dp', 'head'), may hold values from -0.0029296875 to 0.0029296875
- old_char_down_second: float32 [1024, 256], P('dp', 'head'), may hold values from 2.311117e-07 to 9.244468e-07
- old_word_in_first: float32 [512, 4096], P('dp', 'head'), may hold values from -0.0029296875 to 0.0029296875
- old_word_in_second: float32 [512, 4096], P('dp', 'head'), may hold values from 2.311117e-07 to 9.244468e-07
- old_word_down_first: float32 [2048, 512], P('dp', 'head'), may hold values from -0.0029296875 to 0.0029296875
- old_word_down_second: float32 [2048, 512], P('dp', 'head'), may hold values from 2.311117e-07 to 9.244468e-07
- old_gains_first: float32 [1536], replicated, may hold values from -0.01171875 to 0.01171875
- old_gains_second: float32 [1536], replicated, may hold values from 3.6977872e-06 to 1.4791149e-05
Outputs:
- output: bfloat16 [16, 1024, 512], P('dp', 'head')
- input_grad: float32 [16, 1024, 512], P('dp', 'head')
- grad_norm: float32 [], replicated
- table_grad: float32 [1024, 256], P('dp', 'head')
- table_first: float32 [1024, 256], P('dp', 'head')
- table_second: float32 [1024, 256], P('dp', 'head')
- table_new: float32 [1024, 256], P('dp', 'head')
- table_copy: bfloat16 [1024, 256], P('dp', 'head')
- char_in_grad: float32 [256, 2560], P('dp', 'head')
- char_in_first: float32 [256, 2560], P('dp', 'head')
- char_in_second: float32 [256, 2560], P('dp', 'head')
- char_in_new: float32 [256, 2560], P('dp', 'head')
- char_in_copy: bfloat16 [256, 2560], P('dp', 'head')
- char_down_grad: float32 [1024, 256], P('dp', 'head')
- char_down_first: float32 [1024, 256], P('dp', 'head')
- char_down_second: float32 [1024, 256], P('dp', 'head')
- char_down_new: float32 [1024, 256], P('dp', 'head')
- char_down_copy: bfloat16 [1024, 256], P('dp', 'head')
- word_in_grad: float32 [512, 4096], P('dp', 'head')
- word_in_first: float32 [512, 4096], P('dp', 'head')
- word_in_second: float32 [512, 4096], P('dp', 'head')
- word_in_new: float32 [512, 4096], P('dp', 'head')
- word_in_copy: bfloat16 [512, 4096], P('dp', 'head')
- word_down_grad: float32 [2048, 512], P('dp', 'head')
- word_down_first: float32 [2048, 512], P('dp', 'head')
- word_down_second: float32 [2048, 512], P('dp', 'head')
- word_down_new: float32 [2048, 512], P('dp', 'head')
- word_down_copy: bfloat16 [2048, 512], P('dp', 'head')
- gains_grad: float32 [1536], replicated
- gains_first: float32 [1536], replicated
- gains_second: float32 [1536], replicated
- gains_new: float32 [1536], replicated
- gains_copy: bfloat16 [1536], replicated
The draws below stay inside these ranges and needn't reach their ends.
Inputs may be any that keep to these rules, and one draw needn't show every extreme that they name: `char_counts`: the number of real characters of each word; slots at and past it are padding.
All inputs are finite; a program needn't handle non-finite values.
Results may differ from the reference program's by a relative error of at most 0.015.
The reference program's roundings to bfloat16 on the way count: a program that leaves them out, or rounds other values in their place, can miss the bound.
Values may be sent and summed in bfloat16 or wider, within the bound.
A program may use at most 320 MiB of HBM per device.

```python
import math
import jax
import jax.numpy as jnp
import numpy as np
from jax import lax

D = 512
HEADS = 8
FF = 2048
CD = 256
CHEADS = 4
CFF = 1024
CV = 256
GROUPS = 4
CHARS = 16
LEN = 1024
STEP = 5
SEQS = 16
PARAMS = 4326912


def scaled_sample(key, shape, spread):
    sample = jax.random.truncated_normal(key, -6.0, 6.0, shape, jnp.float32)
    return sample * spread


def draw_char_in(key, part):
    key = jax.random.fold_in(key, 11)
    columns = 4 * CD + CFF + D
    index = lax.broadcasted_iota(jnp.int32, (CD, columns), 1)
    fan = jnp.where(index < 3 * CD, CD, jnp.where(index < 4 * CD, CD // 8, jnp.where(index < 4 * CD + CFF, CD, CD // 8)))
    spread = lax.rsqrt(fan.astype(jnp.float32))
    return scaled_sample(key, (CD, columns), spread)


def draw_word_in(key, part):
    key = jax.random.fold_in(key, 23)
    columns = 4 * D + FF
    index = lax.broadcasted_iota(jnp.int32, (D, columns), 1)
    fan = jnp.where(index < 3 * D, D, jnp.where(index < 4 * D, D // 32, D))
    spread = lax.rsqrt(fan.astype(jnp.float32))
    return scaled_sample(key, (D, columns), spread)


def draw_norm_gains(key, part):
    key = jax.random.fold_in(key, 37)
    total = 2 * CD + 2 * D
    index = lax.iota(jnp.int32, total)
    start = jnp.where(index < CD, 0, jnp.where(index < 2 * CD, CD, jnp.where(index < 2 * CD + D, 2 * CD, 2 * CD + D)))
    length = jnp.where(index < 2 * CD, CD, D)
    place = (index - start).astype(jnp.float32) / (length - 1).astype(jnp.float32)
    lowest = 0.6
    highest = 1.8
    rising = jnp.exp(jnp.log(lowest) + (jnp.log(highest) - jnp.log(lowest)) * place)
    jitter = jax.random.uniform(key, (total,), jnp.float32, 0.85, 1.15)
    return rising * jitter


def touch_ends(drawn, key, smallest, largest):
    longest = drawn.shape.index(max(drawn.shape))
    spots = []
    for shift in (0, 1):
        where = [jax.random.randint(jax.random.fold_in(key, axis), (), 0, length) for axis, length in enumerate(drawn.shape)]
        where[longest] = (where[longest] + shift) % drawn.shape[longest]
        spots.append(tuple(where))
    return drawn.at[spots[0]].set(smallest).at[spots[1]].set(largest)


def block_scale(own_key, shape, split, least, high):
    level = 1.0
    for dim, shards_of in split:
        draws = jax.random.uniform(jax.random.fold_in(jax.random.fold_in(own_key, 6), dim), (shards_of,), jnp.float32, least / len(split), high / len(split))
        level = level * jnp.repeat(jnp.exp(draws), shape[dim] // shards_of).reshape((-1,) + (1,) * (len(shape) - 1 - dim))
    return level


def rank_bounds(count, skew):
    portions = [(1 << 20) // math.isqrt(standing ** skew) + 1 for standing in range(1, count + 1)]
    scale = 1 + sum(portions) // (1 << 30)
    return np.cumsum(np.array([max(1, weight // scale) for weight in portions]))


def skewed_ids(stream_key, shape, number_of, slope):
    listing = rank_bounds(number_of, slope)
    ticket = jax.random.randint(jax.random.fold_in(stream_key, 1), shape, 0, int(listing[number_of - 1]))
    standing = jnp.searchsorted(jnp.asarray(listing, jnp.int32), ticket, side="right")
    return jax.random.permutation(jax.random.fold_in(stream_key, 2), number_of)[standing].astype(jnp.int32)


def scatter_about(key, extent, scale, reach, shards=(), dtype=jnp.bfloat16):
    values = scale * jax.random.normal(key, extent, jnp.float32)
    if shards:
        values = values * block_scale(key, extent, shards, -0.22, 0.18)
    return jnp.clip(values, -reach, reach).astype(dtype)


def setup_inputs(seed: int = 0) -> dict:
    key_of = jax.random.split(jax.random.key(seed), 24)
    return {
        "char_ids": touch_ends(skewed_ids(key_of[0], (SEQS, LEN, CHARS), CV, 2), jax.random.fold_in(key_of[0], 3), 0, CV - 1).astype(jnp.int32),
        "char_counts": touch_ends(jax.random.randint(key_of[1], (SEQS, LEN), 1, CHARS + 1), jax.random.fold_in(key_of[1], 1), 1, CHARS).astype(jnp.int32),
        "language": touch_ends(jax.random.randint(key_of[2], (SEQS,), 0, GROUPS), jax.random.fold_in(key_of[2], 1), 0, GROUPS - 1).astype(jnp.int32),
        "words_in": scatter_about(key_of[3], (SEQS, LEN, D), 1.0, 6.0, ((0, 8), (1, 4))),
        "out_cotangent": scatter_about(key_of[4], (SEQS, LEN, D), 1.0, 6.0, ((0, 8), (1, 4))),
        "char_table": scatter_about(key_of[5], (GROUPS * CV, CD), 0.1, 0.6, ((0, 8), (1, 4)), jnp.float32),
        "char_in": draw_char_in(jax.random.fold_in(key_of[23], 71), 0),
        "char_down": scatter_about(key_of[7], (CFF, CD), CFF ** -0.5, 0.1875, ((0, 8), (1, 4)), jnp.float32),
        "word_in": draw_word_in(jax.random.fold_in(key_of[23], 71), 0),
        "word_down": scatter_about(key_of[9], (FF, D), FF ** -0.5, 0.125, ((0, 8), (1, 4)), jnp.float32),
        "norm_gains": draw_norm_gains(jax.random.fold_in(key_of[23], 71), 0),
        "old_table_first": scatter_about(key_of[11], (GROUPS * CV, CD), (PARAMS ** -0.5), 0.0029296875, ((0, 8), (1, 4)), jnp.float32),
        "old_table_second": jnp.clip(jnp.exp(math.log(9.244467946700752e-07) - 1.3862944 * jax.random.uniform(key_of[12], (GROUPS * CV, CD), jnp.float32) ** block_scale(key_of[12], (GROUPS * CV, CD), ((0, 8), (1, 4)), -0.2, 0.2)), 2.311116986675188e-07, 9.244467946700752e-07),
        "old_char_in_first": scatter_about(key_of[13], (CD, 4 * CD + CFF + D), (PARAMS ** -0.5), 0.0029296875, ((0, 8), (1, 4)), jnp.float32),
        "old_char_in_second": jnp.clip(jnp.exp(math.log(9.244467946700752e-07) - 1.3862944 * jax.random.uniform(key_of[14], (CD, 4 * CD + CFF + D), jnp.float32) ** block_scale(key_of[14], (CD, 4 * CD + CFF + D), ((0, 8), (1, 4)), -0.2, 0.2)), 2.311116986675188e-07, 9.244467946700752e-07),
        "old_char_down_first": scatter_about(key_of[15], (CFF, CD), (PARAMS ** -0.5), 0.0029296875, ((0, 8), (1, 4)), jnp.float32),
        "old_char_down_second": jnp.clip(jnp.exp(math.log(9.244467946700752e-07) - 1.3862944 * jax.random.uniform(key_of[16], (CFF, CD), jnp.float32) ** block_scale(key_of[16], (CFF, CD), ((0, 8), (1, 4)), -0.2, 0.2)), 2.311116986675188e-07, 9.244467946700752e-07),
        "old_word_in_first": scatter_about(key_of[17], (D, 4 * D + FF), (PARAMS ** -0.5), 0.0029296875, ((0, 8), (1, 4)), jnp.float32),
        "old_word_in_second": jnp.clip(jnp.exp(math.log(9.244467946700752e-07) - 1.3862944 * jax.random.uniform(key_of[18], (D, 4 * D + FF), jnp.float32) ** block_scale(key_of[18], (D, 4 * D + FF), ((0, 8), (1, 4)), -0.2, 0.2)), 2.311116986675188e-07, 9.244467946700752e-07),
        "old_word_down_first": scatter_about(key_of[19], (FF, D), (PARAMS ** -0.5), 0.0029296875, ((0, 8), (1, 4)), jnp.float32),
        "old_word_down_second": jnp.clip(jnp.exp(math.log(9.244467946700752e-07) - 1.3862944 * jax.random.uniform(key_of[20], (FF, D), jnp.float32) ** block_scale(key_of[20], (FF, D), ((0, 8), (1, 4)), -0.2, 0.2)), 2.311116986675188e-07, 9.244467946700752e-07),
        "old_gains_first": scatter_about(key_of[21], (2 * CD + 2 * D,), (4 * PARAMS ** -0.5), 0.01171875, (), jnp.float32),
        "old_gains_second": jnp.clip(jnp.exp(jax.random.uniform(key_of[22], (2 * CD + 2 * D,), jnp.float32, math.log(3.6977871786803007e-06), math.log(1.4791148714721203e-05))), 3.6977871786803007e-06, 1.4791148714721203e-05),
    }


EPS = 1e-05
CLIP = 1.0
MATRIX_RATE = 0.03
GAIN_RATE = 0.25
MATRIX_DECAY = 0.1
BETA_ONE = 0.5
BETA_TWO = 0.5
ADAM_EPS = 1e-08
NEG_FILL = -1e+30

@jax.custom_vjp
def low(v):
    return lax.optimization_barrier(v.astype(jnp.bfloat16)).astype(jnp.float32)

@jax.custom_vjp
def low_back(v):
    return v

def low_keep(v):
    return (low(v), None)

def low_pass(kept, grad):
    return (grad,)

def back_keep(v):
    return (v, None)

def back_low(kept, grad):
    return (low(grad),)
low.defvjp(low_keep, low_pass)
low_back.defvjp(back_keep, back_low)

def dense(left_side, right_side):
    return jnp.matmul(left_side, right_side, precision=lax.Precision.HIGHEST)

def rms_gain(values, gain_vec):
    return values * lax.rsqrt(lax.optimization_barrier(jnp.mean(values * values, axis=-1, keepdims=True)) + EPS) * gain_vec

def attend(queries, key_rows, value_rows, allowed):
    factor = queries.shape[-1] ** (-0.5)
    raw_scores = jnp.einsum('bqhd,bkhd->bhqk', queries, key_rows, precision=lax.Precision.HIGHEST)
    scores = jnp.where(allowed, low_back(raw_scores) * factor, NEG_FILL)
    weights_low = low(jax.nn.softmax(scores, axis=-1))
    mixed = jnp.einsum('bhqk,bkhd->bqhd', weights_low, value_rows, precision=lax.Precision.HIGHEST)
    return low(low_back(mixed))

def forward(params, words, char_ids, char_counts, lang):
    char_table, char_in, char_down, word_in, word_down, norm_gains = params
    table_low = low(char_table)
    char_in_low = low(char_in)
    char_down_low = low(char_down)
    word_in_low = low(word_in)
    word_down_low = low(word_down)
    gain_one = norm_gains[:CD]
    gain_two = norm_gains[CD:2 * CD]
    gain_three = norm_gains[2 * CD:2 * CD + D]
    gain_four = norm_gains[2 * CD + D:]
    index = char_ids + CV * lang
    embedded = low_back(table_low[index])
    key_mask = jnp.arange(CHARS)[None, :] < char_counts[:, None]
    act_one = low(rms_gain(embedded, gain_one))
    char_qkv = low(low_back(dense(act_one, char_in_low[:, :3 * CD])))
    char_qkv = char_qkv.reshape(LEN, CHARS, 3, CHEADS, CD // CHEADS)
    char_mixed = attend(char_qkv[:, :, 0], char_qkv[:, :, 1], char_qkv[:, :, 2], key_mask[:, None, None, :])
    char_mixed = char_mixed.reshape(LEN, CHARS, CD)
    char_first = embedded + low_back(dense(char_mixed, char_in_low[:, 3 * CD:4 * CD]))
    act_two = low(rms_gain(char_first, gain_two))
    char_upper = low_back(dense(act_two, char_in_low[:, 4 * CD:4 * CD + CFF]))
    char_hidden = low(jax.nn.gelu(char_upper, approximate=False))
    char_second = char_first + low_back(dense(char_hidden, char_down_low))
    pooled = lax.optimization_barrier(jnp.sum(jnp.where(key_mask[:, :, None], char_second, 0.0), axis=1)) / char_counts[:, None].astype(jnp.float32)
    word_vector = low_back(dense(low(pooled), char_in_low[:, 4 * CD + CFF:]))
    word_start = words + word_vector
    act_three = low(rms_gain(word_start, gain_three))
    word_qkv = low(low_back(dense(act_three, word_in_low[:, :3 * D])))
    word_qkv = word_qkv.reshape(1, LEN, 3, HEADS, D // HEADS)
    positions = jnp.arange(LEN)
    causal = (positions[:, None] >= positions[None, :])[None, None]
    word_mixed = attend(word_qkv[:, :, 0], word_qkv[:, :, 1], word_qkv[:, :, 2], causal).reshape(LEN, D)
    word_after = word_start + low_back(dense(word_mixed, word_in_low[:, 3 * D:4 * D]))
    act_four = low(rms_gain(word_after, gain_four))
    word_upper = low_back(dense(act_four, word_in_low[:, 4 * D:]))
    word_hidden = low(jax.nn.gelu(word_upper, approximate=False))
    return word_after + low_back(dense(word_hidden, word_down_low))

def adam_step(weight, grad, first_old, second_old, clip_factor, rate, decay):
    clipped = grad * clip_factor
    first_new = BETA_ONE * first_old + (1.0 - BETA_ONE) * clipped
    second_new = BETA_TWO * second_old + (1.0 - BETA_TWO) * clipped * clipped
    first_hat = first_new / (1.0 - BETA_ONE ** STEP)
    second_hat = second_new / (1.0 - BETA_TWO ** STEP)
    weight_new = weight - rate * (first_hat / (jnp.sqrt(second_hat) + ADAM_EPS) + decay * weight)
    return (grad, first_new, second_new, weight_new, weight_new.astype(jnp.bfloat16))

def reference(char_ids, char_counts, language, words_in, out_cotangent, char_table, char_in, char_down, word_in, word_down, norm_gains, old_table_first, old_table_second, old_char_in_first, old_char_in_second, old_char_down_first, old_char_down_second, old_word_in_first, old_word_in_second, old_word_down_first, old_word_down_second, old_gains_first, old_gains_second):
    params = (char_table, char_in, char_down, word_in, word_down, norm_gains)

    def one_sequence(totals, inputs):
        seq_ids, seq_counts, seq_lang, seq_words, seq_cot = inputs
        result, pullback = jax.vjp(lambda weights, words: forward(weights, words, seq_ids, seq_counts, seq_lang), params, seq_words.astype(jnp.float32))
        grads, grad_words = pullback(seq_cot.astype(jnp.float32))
        totals = jax.tree.map(lambda total_part, grad_part: total_part + grad_part, totals, grads)
        return (totals, (result.astype(jnp.bfloat16), grad_words))
    zeros = jax.tree.map(jnp.zeros_like, params)
    totals, stacked = lax.scan(one_sequence, zeros, (char_ids, char_counts, language, words_in, out_cotangent))
    output, input_grad = stacked
    square = jnp.sum(totals[0] * totals[0])
    for grad_part in totals[1:]:
        square = square + jnp.sum(grad_part * grad_part)
    grad_norm = jnp.sqrt(square)
    clip_factor = jnp.minimum(1.0, CLIP / grad_norm)
    table_out = adam_step(char_table, totals[0], old_table_first, old_table_second, clip_factor, MATRIX_RATE, MATRIX_DECAY)
    cin_out = adam_step(char_in, totals[1], old_char_in_first, old_char_in_second, clip_factor, MATRIX_RATE, MATRIX_DECAY)
    cdown_out = adam_step(char_down, totals[2], old_char_down_first, old_char_down_second, clip_factor, MATRIX_RATE, MATRIX_DECAY)
    win_out = adam_step(word_in, totals[3], old_word_in_first, old_word_in_second, clip_factor, MATRIX_RATE, MATRIX_DECAY)
    wdown_out = adam_step(word_down, totals[4], old_word_down_first, old_word_down_second, clip_factor, MATRIX_RATE, MATRIX_DECAY)
    gains_out = adam_step(norm_gains, totals[5], old_gains_first, old_gains_second, clip_factor, GAIN_RATE, 0.0)
    return (output, input_grad, grad_norm, table_out[0], table_out[1], table_out[2], table_out[3], table_out[4], cin_out[0], cin_out[1], cin_out[2], cin_out[3], cin_out[4], cdown_out[0], cdown_out[1], cdown_out[2], cdown_out[3], cdown_out[4], win_out[0], win_out[1], win_out[2], win_out[3], win_out[4], wdown_out[0], wdown_out[1], wdown_out[2], wdown_out[3], wdown_out[4], gains_out[0], gains_out[1], gains_out[2], gains_out[3], gains_out[4])
```

```python
import jax
import jax.numpy as jnp
from jax import lax
from jax.experimental import pallas as pl
from jax.experimental.pallas import tpu as pltpu
from jax.sharding import PartitionSpec as P

D = 512
HEADS = 8
CD = 256
CHEADS = 4
CFF = 1024
CV = 256
STEP = 5


EPS = 1e-05
CLIP = 1.0
MATRIX_RATE = 0.03
GAIN_RATE = 0.25
MATRIX_DECAY = 0.1
BETA_ONE = 0.5
BETA_TWO = 0.5
ADAM_EPS = 1e-08
NEG_FILL = -1e30
SQRT_HALF = 0.7071067811865476
INV_ROOT_TWO_PI = 0.3989422804014327


def matmul(left_side, right_side):
    return jnp.dot(left_side, right_side, preferred_element_type=jnp.float32)


def matmul_tn(left_side, right_side):
    return lax.dot_general(
        left_side, right_side, (((0,), (0,)), ((), ())), preferred_element_type=jnp.float32
    )


def matmul_nt(left_side, right_side):
    return lax.dot_general(
        left_side, right_side, (((1,), (1,)), ((), ())), preferred_element_type=jnp.float32
    )


def gelu_value(upper_in):
    return upper_in * 0.5 * (1.0 + lax.erf(upper_in * SQRT_HALF))


def gelu_slope(upper_in):
    return (
        0.5 * (1.0 + lax.erf(upper_in * SQRT_HALF))
        + upper_in * jnp.exp(-0.5 * upper_in * upper_in) * INV_ROOT_TWO_PI
    )


def rms_forward(values, gain_vec):
    inverse = lax.rsqrt(jnp.mean(values * values, axis=-1, keepdims=True) + EPS)
    normed = values * inverse
    return (normed * gain_vec, normed, inverse)


def rms_backward(grad_in, gain_vec, normed, inverse):
    grad_gain = jnp.sum(grad_in * normed, axis=0)
    scaled = grad_in * gain_vec
    grad_values = inverse * (scaled - normed * jnp.mean(scaled * normed, axis=-1, keepdims=True))
    return (grad_values, grad_gain)


def causal_mask(length):
    row_pos = lax.broadcasted_iota(jnp.int32, (length, length), 0)
    col_pos = lax.broadcasted_iota(jnp.int32, (length, length), 1)
    return (row_pos >= col_pos)[None, None]


def score_block(queries, key_rows, allowed):
    factor = queries.shape[-1] ** (-0.5)
    scores = (
        jnp.einsum("bqhd,bkhd->bhqk", queries, key_rows, preferred_element_type=jnp.float32)
        * factor
    )
    return (jnp.where(allowed, scores, NEG_FILL), factor)


def attend_forward(queries, key_rows, value_rows, allowed):
    scores, factor = score_block(queries, key_rows, allowed)
    highest = jnp.max(scores, axis=-1, keepdims=True)
    powers = jnp.exp(scores - highest)
    totals = jnp.sum(powers, axis=-1, keepdims=True)
    weights_low = (powers / totals).astype(jnp.bfloat16)
    mixed = jnp.einsum(
        "bhqk,bkhd->bqhd", weights_low, value_rows, preferred_element_type=jnp.float32
    )
    return (mixed.astype(jnp.bfloat16), highest + jnp.log(totals))


def attend_backward(queries, key_rows, value_rows, allowed, log_total, grad_mixed):
    scores, factor = score_block(queries, key_rows, allowed)
    weights_soft = jnp.exp(scores - log_total)
    grad_weights = jnp.einsum(
        "bqhd,bkhd->bhqk", grad_mixed, value_rows, preferred_element_type=jnp.float32
    )
    grad_values = jnp.einsum(
        "bhqk,bqhd->bkhd",
        weights_soft.astype(jnp.bfloat16),
        grad_mixed,
        preferred_element_type=jnp.float32,
    )
    grad_scores = weights_soft * (
        grad_weights - jnp.sum(grad_weights * weights_soft, axis=-1, keepdims=True)
    )
    grad_raw = (grad_scores * factor).astype(jnp.bfloat16)
    grad_queries = jnp.einsum(
        "bhqk,bkhd->bqhd", grad_raw, key_rows, preferred_element_type=jnp.float32
    )
    grad_keys = jnp.einsum("bhqk,bqhd->bkhd", grad_raw, queries, preferred_element_type=jnp.float32)
    return jnp.stack([grad_queries, grad_keys, grad_values], axis=2)


ROWS = 256
SLOTS = 16
GROUP = 128
VMEM_BYTES = 56 * 1024 * 1024
ERFC_P = 0.39
ERFC = (0.235325887, 0.091384224, 0.649569841, -0.635413203, 0.886672317, -0.227539068)


def dot_nn(left_side, right_side):
    return lax.dot_general(
        left_side, right_side, (((1,), (0,)), ((), ())), preferred_element_type=jnp.float32
    )


def dot_tn(left_side, right_side):
    return lax.dot_general(
        left_side, right_side, (((0,), (0,)), ((), ())), preferred_element_type=jnp.float32
    )


def dot_nt(left_side, right_side):
    return lax.dot_general(
        left_side, right_side, (((1,), (1,)), ((), ())), preferred_element_type=jnp.float32
    )


def gelu_pair(upper):
    size = jnp.abs(upper)
    t = 1.0 / (1.0 + (ERFC_P * SQRT_HALF) * size)
    poly = ERFC[5]
    for c in ERFC[4::-1]:
        poly = poly * t + c
    bell = jnp.exp(upper * upper * -0.5)
    half = 0.5 * (poly * t * bell)
    phi = jnp.where(upper > 0, 1.0 - half, half)
    return upper * phi, phi + upper * (bell * INV_ROOT_TWO_PI)


def iota(shape, dim):
    return lax.broadcasted_iota(jnp.int32, shape, dim)


def split_two(values):
    high = values.astype(jnp.bfloat16)
    return high, (values - high.astype(jnp.float32)).astype(jnp.bfloat16)


def pack_kernel(count_row_ref, count_col_ref, ids_ref, ids_back_ref, out_ref, tiles_ref):
    row = count_row_ref[0]
    col = count_col_ref[0]
    n = row.shape[1]
    sub, lane = iota((n, n), 0), iota((n, n), 1)
    ahead = (row > col) | ((row == col) & (lane < sub))
    rank_col = jnp.sum(ahead.astype(jnp.float32), axis=1, keepdims=True).astype(jnp.int32)
    ahead = (col > row) | ((col == row) & (sub < lane))
    rank_row = jnp.sum(ahead.astype(jnp.float32), axis=0, keepdims=True).astype(jnp.int32)
    clash = (rank_col < rank_row) & (col + row > SLOTS)
    alone = jnp.max(jnp.where(clash, rank_col + rank_row, 0).astype(jnp.float32))
    alone = jnp.maximum(alone.astype(jnp.int32) - n + 2, 0)
    partner = n - 1 + alone - rank_row
    second = (rank_row >= alone) & (rank_row > partner)
    bins = jnp.where(second, partner, rank_row)
    here = sub == bins
    first_map = (here & jnp.logical_not(second)).astype(jnp.float32).astype(jnp.bfloat16)
    second_map = (here & second).astype(jnp.float32).astype(jnp.bfloat16)
    pos = lax.rem(iota((n, GROUP), 1), SLOTS)
    word = iota((n, GROUP), 0) + 1
    wide = jnp.broadcast_to(col, (n, GROUP))
    in_first, in_second = pos < wide, pos >= SLOTS - wide

    def kept(mask, values):
        return jnp.where(mask, values, 0).astype(jnp.float32).astype(jnp.bfloat16)

    groups = n * SLOTS // GROUP
    per = GROUP // SLOTS
    own = iota((groups, per, GROUP), 1) == lax.div(iota((groups, per, GROUP), 2), SLOTS)
    ids, back = ids_ref[0], ids_back_ref[0]
    zero = jnp.zeros_like(wide)
    for k, (one, two) in enumerate(
        ((ids + 1, back + 1), (word, word), (zero, SLOTS - wide), (wide, zero + SLOTS))
    ):
        full = dot_nn(first_map, kept(in_first, one)) + dot_nn(second_map, kept(in_second, two))
        full = jnp.where(own, full.reshape(groups, per, GROUP), 0.0)
        out_ref[0, k] = jnp.sum(full, axis=1).astype(jnp.int32)
    used = alone + lax.div(n - alone + 1, 2)
    tiles_ref[pl.program_id(0)] = lax.div(used * SLOTS + ROWS - 1, ROWS)


def pack_rows(char_ids, char_counts):
    seqs, words, slots = char_ids.shape
    ids = jnp.tile(char_ids, (1, 1, GROUP // slots))
    back = jnp.tile(char_ids[:, :, ::-1], (1, 1, GROUP // slots))
    groups = words * slots // GROUP
    return pl.pallas_call(
        pack_kernel,
        grid=(seqs,),
        in_specs=[
            pl.BlockSpec((1, 1, words), lambda s: (s, 0, 0)),
            pl.BlockSpec((1, words, 1), lambda s: (s, 0, 0)),
            pl.BlockSpec((1, words, GROUP), lambda s: (s, 0, 0)),
            pl.BlockSpec((1, words, GROUP), lambda s: (s, 0, 0)),
        ],
        out_specs=[
            pl.BlockSpec((1, 4, groups, GROUP), lambda s: (s, 0, 0, 0)),
            pl.BlockSpec(memory_space=pltpu.SMEM),
        ],
        out_shape=[
            jax.ShapeDtypeStruct((seqs, 4, groups, GROUP), jnp.int32),
            jax.ShapeDtypeStruct((seqs,), jnp.int32),
        ],
        name="pack",
    )(char_counts[:, None, :], char_counts[:, :, None], ids, back)


def tile_maps(pack_ref, step, words):
    per = ROWS // GROUP
    id_rows = pack_ref[0, pl.ds(step * per, per), :]
    word_rows = pack_ref[1, pl.ds(step * per, per), :]
    letters = iota((CV, GROUP), 0) + 1
    spots = iota((words, GROUP), 0) + 1
    one_hot = [
        (letters == id_rows[g : g + 1]).astype(jnp.float32).astype(jnp.bfloat16) for g in range(per)
    ]
    word_map = [
        (spots == word_rows[g : g + 1]).astype(jnp.float32).astype(jnp.bfloat16) for g in range(per)
    ]
    return jnp.concatenate(one_hot, axis=1), jnp.concatenate(word_map, axis=1)


def column_rms(values):
    inverse = lax.rsqrt(jnp.mean(values * values, axis=0, keepdims=True) + EPS)
    return values * inverse, inverse


def own_block():
    per = GROUP // SLOTS
    shape = (per, SLOTS, GROUP)
    return iota(shape, 0) == lax.div(iota(shape, 2), SLOTS)


def to_compact(block, own):
    per = GROUP // SLOTS
    return jnp.sum(jnp.where(own, block.reshape(per, SLOTS, GROUP), 0.0), axis=0)


def from_compact(compact, own):
    per = GROUP // SLOTS
    wide = jnp.broadcast_to(compact[None], (per, SLOTS, GROUP))
    return jnp.where(own, wide, 0.0).astype(jnp.bfloat16).reshape(GROUP, GROUP)


def char_fwd_kernel(tiles_ref, *refs):
    @pl.when(pl.program_id(0) < tiles_ref[0])
    def _():
        char_fwd_tile(*refs)


def char_fwd_tile(
    pack_ref, table_ref, qkv_ref, out_ref, up_ref, down_ref, g1_ref, g2_ref,
    pooled_ref, keep_qkv, keep_probs, keep_mixed, keep_first, keep_hidden, keep_slope,
):
    step = pl.program_id(0)
    words = pooled_ref.shape[0]
    per = ROWS // GROUP
    head = CD // CHEADS

    @pl.when(step == 0)
    def _():
        pooled_ref[...] = jnp.zeros_like(pooled_ref)

    one_hot, word_map = tile_maps(pack_ref, step, words)
    embedded = dot_nn(table_ref[...], one_hot)
    act_one = (column_rms(embedded)[0] * g1_ref[...]).astype(jnp.bfloat16)
    triple = dot_nn(qkv_ref[...], act_one).astype(jnp.bfloat16)
    keep_qkv[...] = triple
    low_rows = pack_ref[2, pl.ds(step * per, per), :]
    high_rows = pack_ref[3, pl.ds(step * per, per), :]
    own = own_block()
    key_pos = iota((SLOTS, GROUP), 0)
    mixed = []
    for g in range(per):
        valid = (key_pos >= low_rows[g : g + 1]) & (key_pos < high_rows[g : g + 1])
        lanes = slice(g * GROUP, (g + 1) * GROUP)
        parts = []
        for h in range(CHEADS):
            q = triple[h * head : (h + 1) * head, lanes]
            k = triple[CD + h * head : CD + (h + 1) * head, lanes]
            v = triple[2 * CD + h * head : 2 * CD + (h + 1) * head, lanes]
            scores = jnp.where(valid, to_compact(dot_tn(k, q), own) * head**-0.5, NEG_FILL)
            powers = jnp.exp(scores - jnp.max(scores, axis=0, keepdims=True))
            powers = jnp.where(valid, powers, 0.0)
            total = jnp.sum(powers, axis=0, keepdims=True)
            probs = powers / jnp.where(total > 0, total, 1.0)
            keep_probs[h * SLOTS : (h + 1) * SLOTS, lanes] = probs
            parts.append(dot_nn(v, from_compact(probs, own)).astype(jnp.bfloat16))
        mixed.append(jnp.concatenate(parts, axis=0))
    mixed = jnp.concatenate(mixed, axis=1)
    keep_mixed[...] = mixed
    first = embedded + dot_nn(out_ref[...], mixed)
    keep_first[...] = first
    act_two = (column_rms(first)[0] * g2_ref[...]).astype(jnp.bfloat16)
    branch = None
    for c in range(CFF // CD):
        rows = slice(c * CD, (c + 1) * CD)
        hidden, slope = gelu_pair(dot_nn(up_ref[rows, :], act_two))
        hidden = hidden.astype(jnp.bfloat16)
        keep_hidden[rows, :] = hidden
        keep_slope[rows, :] = slope.astype(jnp.bfloat16)
        part = dot_nn(down_ref[:, rows], hidden)
        branch = part if branch is None else branch + part
    high, low = split_two(first + branch)
    pooled_ref[...] += dot_nt(word_map, high) + dot_nt(word_map, low)


KEPT = (
    (3 * CD, jnp.bfloat16),
    (CHEADS * SLOTS, jnp.float32),
    (CD, jnp.bfloat16),
    (CD, jnp.float32),
    (CFF, jnp.bfloat16),
    (CFF, jnp.bfloat16),
)


def whole(array):
    zeros = (0,) * array.ndim
    return pl.BlockSpec(array.shape, lambda *_: zeros)


def kept_place(step, tiles):
    return 0, jnp.minimum(step, tiles[0] - 1)


def char_fwd(tiles, pack, weights, words):
    rows = words * SLOTS
    operands = (pack,) + weights
    return pl.pallas_call(
        char_fwd_kernel,
        grid_spec=pltpu.PrefetchScalarGridSpec(
            num_scalar_prefetch=1,
            grid=(rows // ROWS,),
            in_specs=[whole(a) for a in operands],
            out_specs=[pl.BlockSpec((words, CD), lambda t, n: (0, 0))]
            + [pl.BlockSpec((depth, ROWS), kept_place) for depth, _ in KEPT],
        ),
        out_shape=[jax.ShapeDtypeStruct((words, CD), jnp.float32)]
        + [jax.ShapeDtypeStruct((depth, rows), dtype) for depth, dtype in KEPT],
        compiler_params=pltpu.CompilerParams(vmem_limit_bytes=VMEM_BYTES),
        name="char_fwd",
    )(tiles, *operands)


def fold_lanes(values):
    total = values[:, :GROUP]
    for g in range(1, values.shape[1] // GROUP):
        total = total + values[:, g * GROUP : (g + 1) * GROUP]
    return total


def column_rms_back(grad_in, gain, normed, inverse):
    scaled = grad_in * gain
    return inverse * (scaled - normed * jnp.mean(scaled * normed, axis=0, keepdims=True))


def char_bwd_kernel(tiles_ref, *refs):
    @pl.when(pl.program_id(0) < tiles_ref[0])
    def _():
        char_bwd_tile(*refs)


def char_bwd_tile(
    pack_ref, spread_ref, table_ref, qkv_ref, out_ref, up_ref, down_ref, g1_ref, g2_ref,
    keep_qkv, keep_probs, keep_mixed, keep_first, keep_hidden, keep_slope,
    d_table, d_qkv, d_out, d_up, d_down, d_g1, d_g2,
):
    step = pl.program_id(0)
    words = spread_ref.shape[1]
    per = ROWS // GROUP
    head = CD // CHEADS

    @pl.when(step == 0)
    def _():
        for ref in (d_table, d_qkv, d_out, d_up, d_down, d_g1, d_g2):
            ref[...] = jnp.zeros_like(ref)

    one_hot, word_map = tile_maps(pack_ref, step, words)
    halves = dot_nn(spread_ref[...], word_map)
    grad_second = halves[:CD] + halves[CD:]
    grad_branch = grad_second.astype(jnp.bfloat16)
    first = keep_first[...]
    normed_two, inverse_two = column_rms(first)
    act_two = (normed_two * g2_ref[...]).astype(jnp.bfloat16)
    grad_act_two = None
    for c in range(CFF // CD):
        rows = slice(c * CD, (c + 1) * CD)
        d_down[rows, :] += dot_nt(keep_hidden[rows, :], grad_branch)
        grad_upper = dot_nn(down_ref[rows, :], grad_branch) * keep_slope[rows, :].astype(
            jnp.float32
        )
        grad_upper = grad_upper.astype(jnp.bfloat16)
        d_up[:, rows] += dot_nt(act_two, grad_upper)
        part = dot_nn(up_ref[:, rows], grad_upper)
        grad_act_two = part if grad_act_two is None else grad_act_two + part
    d_g2[...] += fold_lanes(grad_act_two * normed_two)
    grad_first = grad_second + column_rms_back(
        grad_act_two, g2_ref[...], normed_two, inverse_two
    )
    grad_attn = grad_first.astype(jnp.bfloat16)
    d_out[...] += dot_nt(keep_mixed[...], grad_attn)
    grad_mixed = dot_nn(out_ref[...], grad_attn).astype(jnp.bfloat16)
    own = own_block()
    triple = keep_qkv[...]
    columns = []
    for g in range(per):
        lanes = slice(g * GROUP, (g + 1) * GROUP)
        gq, gk, gv = [], [], []
        for h in range(CHEADS):
            q = triple[h * head : (h + 1) * head, lanes]
            k = triple[CD + h * head : CD + (h + 1) * head, lanes]
            v = triple[2 * CD + h * head : 2 * CD + (h + 1) * head, lanes]
            grad_o = grad_mixed[h * head : (h + 1) * head, lanes]
            probs = keep_probs[h * SLOTS : (h + 1) * SLOTS, lanes]
            grad_probs = to_compact(dot_tn(v, grad_o), own)
            grad_scores = probs * (
                grad_probs - jnp.sum(probs * grad_probs, axis=0, keepdims=True)
            )
            grad_raw = from_compact(grad_scores * head**-0.5, own)
            gq.append(dot_nn(k, grad_raw).astype(jnp.bfloat16))
            gk.append(dot_nt(q, grad_raw).astype(jnp.bfloat16))
            gv.append(dot_nt(grad_o, from_compact(probs, own)).astype(jnp.bfloat16))
        columns.append(jnp.concatenate(gq + gk + gv, axis=0))
    grad_triple = jnp.concatenate(columns, axis=1)
    embedded = dot_nn(table_ref[...], one_hot)
    normed_one, inverse_one = column_rms(embedded)
    act_one = (normed_one * g1_ref[...]).astype(jnp.bfloat16)
    d_qkv[...] += dot_nt(act_one, grad_triple)
    grad_act_one = dot_nn(qkv_ref[...], grad_triple)
    d_g1[...] += fold_lanes(grad_act_one * normed_one)
    back_one = column_rms_back(grad_act_one, g1_ref[...], normed_one, inverse_one)
    grad_embedded = (grad_first + back_one).astype(jnp.bfloat16)
    d_table[...] += dot_nt(one_hot, grad_embedded)


def char_bwd(tiles, pack, spread, weights, kept):
    operands = (pack, spread) + weights
    shapes = ((CV, CD), (CD, 3 * CD), (CD, CD), (CD, CFF), (CFF, CD), (CD, GROUP), (CD, GROUP))
    return pl.pallas_call(
        char_bwd_kernel,
        grid_spec=pltpu.PrefetchScalarGridSpec(
            num_scalar_prefetch=1,
            grid=(kept[0].shape[1] // ROWS,),
            in_specs=[whole(a) for a in operands]
            + [pl.BlockSpec((depth, ROWS), kept_place) for depth, _ in KEPT],
            out_specs=[pl.BlockSpec(s, lambda t, n: (0, 0)) for s in shapes],
        ),
        out_shape=[jax.ShapeDtypeStruct(s, jnp.float32) for s in shapes],
        compiler_params=pltpu.CompilerParams(vmem_limit_bytes=VMEM_BYTES),
        name="char_bwd",
    )(tiles, *operands, *kept)


def adam_step(weight, grad, first_old, second_old, clip_factor, rate, decay):
    clipped = grad * clip_factor
    first_new = BETA_ONE * first_old + (1.0 - BETA_ONE) * clipped
    second_new = BETA_TWO * second_old + (1.0 - BETA_TWO) * clipped * clipped
    first_hat = first_new / (1.0 - BETA_ONE**STEP)
    second_hat = second_new / (1.0 - BETA_TWO**STEP)
    weight_new = weight - rate * (first_hat / (jnp.sqrt(second_hat) + ADAM_EPS) + decay * weight)
    return (grad, first_new, second_new, weight_new, weight_new.astype(jnp.bfloat16))


def body(
    char_ids,
    char_counts,
    language,
    words_in,
    out_cotangent,
    char_table,
    char_in,
    char_down,
    word_in,
    word_down,
    norm_gains,
    old_table_first,
    old_table_second,
    old_char_in_first,
    old_char_in_second,
    old_char_down_first,
    old_char_down_second,
    old_word_in_first,
    old_word_in_second,
    old_word_down_first,
    old_word_down_second,
    old_gains_first,
    old_gains_second,
):
    by_cols = (
        lax.all_gather(char_table.astype(jnp.bfloat16), "head", axis=1, tiled=True),
        lax.all_gather(char_in.astype(jnp.bfloat16), "head", axis=1, tiled=True),
        lax.all_gather(char_down.astype(jnp.bfloat16), "head", axis=1, tiled=True),
        lax.all_gather(word_in.astype(jnp.bfloat16), "head", axis=1, tiled=True),
        lax.all_gather(word_down.astype(jnp.bfloat16), "head", axis=1, tiled=True),
    )
    table_low, char_in_low, char_down_low, word_in_low, word_down_low = (
        lax.all_gather(by_cols[0], "dp", axis=0, tiled=True),
        lax.all_gather(by_cols[1], "dp", axis=0, tiled=True),
        lax.all_gather(by_cols[2], "dp", axis=0, tiled=True),
        lax.all_gather(by_cols[3], "dp", axis=0, tiled=True),
        lax.all_gather(by_cols[4], "dp", axis=0, tiled=True),
    )
    gain_one = norm_gains[:CD]
    gain_two = norm_gains[CD : 2 * CD]
    gain_three = norm_gains[2 * CD : 2 * CD + D]
    gain_four = norm_gains[2 * CD + D :]
    seq_count, local_words = (words_in.shape[0], words_in.shape[1])
    word_total = seq_count * local_words
    head_size = D // HEADS
    packed, tiles = pack_rows(char_ids, char_counts)
    tables = table_low.reshape(-1, CV, CD)
    lanes = lambda g: jnp.broadcast_to(g[:, None], (g.shape[0], ROWS))
    gains = (lanes(gain_one), lanes(gain_two))
    table_t = [
        lax.dynamic_index_in_dim(tables, language[i], 0, keepdims=False).T
        for i in range(seq_count)
    ]
    char_parts = (
        char_in_low[:, : 3 * CD],
        char_in_low[:, 3 * CD : 4 * CD],
        char_in_low[:, 4 * CD : 4 * CD + CFF],
        char_down_low,
    )
    flipped = tuple(part.T for part in char_parts)
    kept, pooled = [], []
    for i in range(seq_count):
        first_out, *saved = char_fwd(
            tiles[i : i + 1], packed[i], (table_t[i],) + flipped + gains, local_words
        )
        pooled.append(first_out)
        kept.append(saved)
    counts = char_counts.reshape(word_total, 1).astype(jnp.float32)
    pooled = (jnp.concatenate(pooled, axis=0) / counts).astype(jnp.bfloat16)
    word_vector = matmul(pooled, char_in_low[:, 4 * CD + CFF :])
    word_start = words_in.reshape(word_total, D).astype(jnp.float32) + word_vector
    scaled_three, normed_three, inverse_three = rms_forward(word_start, gain_three)
    act_three = scaled_three.astype(jnp.bfloat16)
    word_triple = matmul(act_three, word_in_low[:, : 3 * D]).astype(jnp.bfloat16)
    word_triple = word_triple.reshape(seq_count, local_words, 3, HEADS, head_size)
    block = lax.all_to_all(word_triple, "head", split_axis=3, concat_axis=1, tiled=True)
    mixed, log_total = attend_forward(
        block[:, :, 0], block[:, :, 1], block[:, :, 2], causal_mask(block.shape[1])
    )
    returned = lax.all_to_all(mixed, "head", split_axis=1, concat_axis=2, tiled=True)
    mixed_flat = returned.reshape(word_total, D)
    word_after = word_start + matmul(mixed_flat, word_in_low[:, 3 * D : 4 * D])
    scaled_four, normed_four, inverse_four = rms_forward(word_after, gain_four)
    act_four = scaled_four.astype(jnp.bfloat16)
    word_upper = matmul(act_four, word_in_low[:, 4 * D :])
    word_hidden = gelu_value(word_upper).astype(jnp.bfloat16)
    result = word_after + matmul(word_hidden, word_down_low)
    output = result.astype(jnp.bfloat16).reshape(seq_count, local_words, D)
    grad_result = out_cotangent.reshape(word_total, D).astype(jnp.float32)
    grad_down_in = grad_result.astype(jnp.bfloat16)
    grad_wdown = matmul_tn(word_hidden, grad_down_in)
    grad_hidden = matmul_nt(grad_down_in, word_down_low)
    grad_upper = (grad_hidden * gelu_slope(word_upper)).astype(jnp.bfloat16)
    grad_wup = matmul_tn(act_four, grad_upper)
    grad_act_four = matmul_nt(grad_upper, word_in_low[:, 4 * D :])
    back_four, grad_gain_four = rms_backward(grad_act_four, gain_four, normed_four, inverse_four)
    grad_after = grad_result + back_four
    grad_out_in = grad_after.astype(jnp.bfloat16)
    grad_wout = matmul_tn(mixed_flat, grad_out_in)
    grad_mixed = matmul_nt(grad_out_in, word_in_low[:, 3 * D : 4 * D]).astype(jnp.bfloat16)
    grad_mixed = grad_mixed.reshape(seq_count, local_words, HEADS, head_size)
    head_grads = lax.all_to_all(grad_mixed, "head", split_axis=2, concat_axis=1, tiled=True)
    triple_heads = attend_backward(
        block[:, :, 0],
        block[:, :, 1],
        block[:, :, 2],
        causal_mask(block.shape[1]),
        log_total,
        head_grads,
    )
    triple_grads = lax.all_to_all(
        triple_heads.astype(jnp.bfloat16), "head", split_axis=1, concat_axis=3, tiled=True
    )
    triple_grads = triple_grads.reshape(word_total, 3 * D)
    grad_wtriple = matmul_tn(act_three, triple_grads)
    grad_act_three = matmul_nt(triple_grads, word_in_low[:, : 3 * D])
    back_three, grad_gain_three = rms_backward(
        grad_act_three, gain_three, normed_three, inverse_three
    )
    grad_start = grad_after + back_three
    input_grad = grad_start.reshape(seq_count, local_words, D)
    grad_vector = grad_start.astype(jnp.bfloat16)
    grad_pool = matmul_tn(pooled, grad_vector)
    grad_pooled = matmul_nt(grad_vector, char_in_low[:, 4 * CD + CFF :])
    scaled_pooled = (grad_pooled / counts).reshape(seq_count, local_words, CD)
    char_grads = []
    grad_table = jnp.zeros((tables.shape[0], CV, CD), jnp.float32)
    for i in range(seq_count):
        high, low = split_two(scaled_pooled[i].T)
        one_table, *rest = char_bwd(
            tiles[i : i + 1],
            packed[i],
            jnp.concatenate([high, low], axis=0),
            (table_t[i],) + char_parts + gains,
            kept[i],
        )
        char_grads.append(rest)
        grad_table = grad_table + jnp.where(
            (jnp.arange(tables.shape[0]) == language[i])[:, None, None], one_table[None], 0.0
        )
    grad_table = grad_table.reshape(-1, CD)
    grad_ctriple, grad_cout, grad_cup, grad_cdown, grad_gain_one, grad_gain_two = (
        sum(parts[1:], parts[0]) for parts in zip(*char_grads)
    )
    grad_gain_one = jnp.sum(grad_gain_one, axis=1)
    grad_gain_two = jnp.sum(grad_gain_two, axis=1)
    grad_cin = jnp.concatenate([grad_ctriple, grad_cout, grad_cup, grad_pool], axis=1)
    grad_win = jnp.concatenate([grad_wtriple, grad_wout, grad_wup], axis=1)
    gain_grads = jnp.concatenate([grad_gain_one, grad_gain_two, grad_gain_three, grad_gain_four])
    owned_parts = (char_table, char_in, char_down, word_in, word_down)
    summed = lax.psum(
        (grad_table, grad_cin, grad_cdown, grad_win, grad_wdown, gain_grads), ("dp", "head")
    )
    square = jnp.sum(summed[0] * summed[0])
    for grad_part in summed[1:]:
        square = square + jnp.sum(grad_part * grad_part)
    row_index = lax.axis_index("dp")
    col_index = lax.axis_index("head")
    reduced = [
        lax.dynamic_slice(
            full_grad,
            (row_index * shard_part.shape[0], col_index * shard_part.shape[1]),
            shard_part.shape,
        )
        for full_grad, shard_part in zip(summed[:5], owned_parts)
    ]
    gains_sum = summed[5]
    grad_norm = jnp.sqrt(square)
    clip_factor = jnp.minimum(1.0, CLIP / grad_norm)
    table_out = adam_step(
        char_table,
        reduced[0],
        old_table_first,
        old_table_second,
        clip_factor,
        MATRIX_RATE,
        MATRIX_DECAY,
    )
    cin_out = adam_step(
        char_in,
        reduced[1],
        old_char_in_first,
        old_char_in_second,
        clip_factor,
        MATRIX_RATE,
        MATRIX_DECAY,
    )
    cdown_out = adam_step(
        char_down,
        reduced[2],
        old_char_down_first,
        old_char_down_second,
        clip_factor,
        MATRIX_RATE,
        MATRIX_DECAY,
    )
    win_out = adam_step(
        word_in,
        reduced[3],
        old_word_in_first,
        old_word_in_second,
        clip_factor,
        MATRIX_RATE,
        MATRIX_DECAY,
    )
    wdown_out = adam_step(
        word_down,
        reduced[4],
        old_word_down_first,
        old_word_down_second,
        clip_factor,
        MATRIX_RATE,
        MATRIX_DECAY,
    )
    gains_out = adam_step(
        norm_gains, gains_sum, old_gains_first, old_gains_second, clip_factor, GAIN_RATE, 0.0
    )
    return (
        (output, input_grad, grad_norm)
        + table_out
        + cin_out
        + cdown_out
        + win_out
        + wdown_out
        + gains_out
    )


def solution(mesh):
    return jax.shard_map(
        body,
        mesh=mesh,
        in_specs=(
            P("dp", "head", None),
            P("dp", "head"),
            P("dp"),
            P("dp", "head", None),
            P("dp", "head", None),
            P("dp", "head"),
            P("dp", "head"),
            P("dp", "head"),
            P("dp", "head"),
            P("dp", "head"),
            P(),
            P("dp", "head"),
            P("dp", "head"),
            P("dp", "head"),
            P("dp", "head"),
            P("dp", "head"),
            P("dp", "head"),
            P("dp", "head"),
            P("dp", "head"),
            P("dp", "head"),
            P("dp", "head"),
            P(),
            P(),
        ),
        out_specs=(
            P("dp", "head", None),
            P("dp", "head", None),
            P(),
            P("dp", "head"),
            P("dp", "head"),
            P("dp", "head"),
            P("dp", "head"),
            P("dp", "head"),
            P("dp", "head"),
            P("dp", "head"),
            P("dp", "head"),
            P("dp", "head"),
            P("dp", "head"),
            P("dp", "head"),
            P("dp", "head"),
            P("dp", "head"),
            P("dp", "head"),
            P("dp", "head"),
            P("dp", "head"),
            P("dp", "head"),
            P("dp", "head"),
            P("dp", "head"),
            P("dp", "head"),
            P("dp", "head"),
            P("dp", "head"),
            P("dp", "head"),
            P("dp", "head"),
            P("dp", "head"),
            P(),
            P(),
            P(),
            P(),
            P(),
        ),
        check_vma=False,
    )
```

```python
import functools

import jax
import jax.numpy as jnp
from jax import lax
from jax.experimental import pallas as pl
from jax.experimental.pallas import tpu as pltpu
from jax.sharding import PartitionSpec as P

D = 512
HEADS = 8
CD = 256
CHEADS = 4
CFF = 1024
CV = 256
STEP = 5


EPS = 1e-05
CLIP = 1.0
MATRIX_RATE = 0.03
GAIN_RATE = 0.25
MATRIX_DECAY = 0.1
BETA_ONE = 0.5
BETA_TWO = 0.5
ADAM_EPS = 1e-08
NEG_FILL = -1e30
SQRT_HALF = 0.7071067811865476
INV_ROOT_TWO_PI = 0.3989422804014327


ROWS = 512
SLOTS = 16
GROUP = 128
VMEM_BYTES = 56 * 1024 * 1024
ERFC_P = 0.39
ERFC = (0.235325887, 0.091384224, 0.649569841, -0.635413203, 0.886672317, -0.227539068)


def dot_nn(left_side, right_side):
    return lax.dot_general(
        left_side, right_side, (((1,), (0,)), ((), ())), preferred_element_type=jnp.float32
    )


def dot_tn(left_side, right_side):
    return lax.dot_general(
        left_side, right_side, (((0,), (0,)), ((), ())), preferred_element_type=jnp.float32
    )


def dot_nt(left_side, right_side):
    return lax.dot_general(
        left_side, right_side, (((1,), (1,)), ((), ())), preferred_element_type=jnp.float32
    )


def gelu_pair(upper):
    size = jnp.abs(upper)
    t = 1.0 / (1.0 + (ERFC_P * SQRT_HALF) * size)
    poly = ERFC[5]
    for c in ERFC[4::-1]:
        poly = poly * t + c
    bell = jnp.exp(upper * upper * -0.5)
    half = 0.5 * (poly * t * bell)
    phi = jnp.where(upper > 0, 1.0 - half, half)
    return upper * phi, phi + upper * (bell * INV_ROOT_TWO_PI)


def iota(shape, dim):
    return lax.broadcasted_iota(jnp.int32, shape, dim)


def split_two(values):
    high = values.astype(jnp.bfloat16)
    return high, (values - high.astype(jnp.float32)).astype(jnp.bfloat16)


def pack_kernel(count_row_ref, count_col_ref, ids_ref, ids_back_ref, out_ref, tiles_ref):
    row = count_row_ref[0]
    col = count_col_ref[0]
    n = row.shape[1]
    sub, lane = iota((n, n), 0), iota((n, n), 1)
    ahead = (row > col) | ((row == col) & (lane < sub))
    rank_col = jnp.sum(ahead.astype(jnp.float32), axis=1, keepdims=True).astype(jnp.int32)
    ahead = (col > row) | ((col == row) & (sub < lane))
    rank_row = jnp.sum(ahead.astype(jnp.float32), axis=0, keepdims=True).astype(jnp.int32)
    clash = (rank_col < rank_row) & (col + row > SLOTS)
    alone = jnp.max(jnp.where(clash, rank_col + rank_row, 0).astype(jnp.float32))
    alone = jnp.maximum(alone.astype(jnp.int32) - n + 2, 0)
    partner = n - 1 + alone - rank_row
    second = (rank_row >= alone) & (rank_row > partner)
    bins = jnp.where(second, partner, rank_row)
    here = sub == bins
    first_map = (here & jnp.logical_not(second)).astype(jnp.float32).astype(jnp.bfloat16)
    second_map = (here & second).astype(jnp.float32).astype(jnp.bfloat16)
    pos = lax.rem(iota((n, GROUP), 1), SLOTS)
    word = iota((n, GROUP), 0) + 1
    wide = jnp.broadcast_to(col, (n, GROUP))
    in_first, in_second = pos < wide, pos >= SLOTS - wide

    def kept(mask, values):
        return jnp.where(mask, values, 0).astype(jnp.float32).astype(jnp.bfloat16)

    groups = n * SLOTS // GROUP
    per = GROUP // SLOTS
    own = iota((groups, per, GROUP), 1) == lax.div(iota((groups, per, GROUP), 2), SLOTS)
    ids, back = ids_ref[0], ids_back_ref[0]
    zero = jnp.zeros_like(wide)
    for k, (one, two) in enumerate(
        ((ids + 1, back + 1), (word, word), (zero, SLOTS - wide), (wide, zero + SLOTS))
    ):
        full = dot_nn(first_map, kept(in_first, one)) + dot_nn(second_map, kept(in_second, two))
        full = jnp.where(own, full.reshape(groups, per, GROUP), 0.0)
        out_ref[0, k] = jnp.sum(full, axis=1).astype(jnp.int32)
    used = alone + lax.div(n - alone + 1, 2)
    tiles_ref[pl.program_id(0)] = lax.div(used * SLOTS + ROWS - 1, ROWS)


def pack_rows(char_ids, char_counts):
    seqs, words, slots = char_ids.shape
    ids = jnp.tile(char_ids, (1, 1, GROUP // slots))
    back = jnp.tile(char_ids[:, :, ::-1], (1, 1, GROUP // slots))
    groups = words * slots // GROUP
    return pl.pallas_call(
        pack_kernel,
        grid=(seqs,),
        in_specs=[
            pl.BlockSpec((1, 1, words), lambda s: (s, 0, 0)),
            pl.BlockSpec((1, words, 1), lambda s: (s, 0, 0)),
            pl.BlockSpec((1, words, GROUP), lambda s: (s, 0, 0)),
            pl.BlockSpec((1, words, GROUP), lambda s: (s, 0, 0)),
        ],
        out_specs=[
            pl.BlockSpec((1, 4, groups, GROUP), lambda s: (s, 0, 0, 0)),
            pl.BlockSpec(memory_space=pltpu.SMEM),
        ],
        out_shape=[
            jax.ShapeDtypeStruct((seqs, 4, groups, GROUP), jnp.int32),
            jax.ShapeDtypeStruct((seqs,), jnp.int32),
        ],
        name="pack",
    )(char_counts[:, None, :], char_counts[:, :, None], ids, back)


def tile_maps(pack_ref, step, words):
    per = ROWS // GROUP
    id_rows = pack_ref[0, pl.ds(step * per, per), :]
    word_rows = pack_ref[1, pl.ds(step * per, per), :]
    letters = iota((CV, GROUP), 0) + 1
    spots = iota((words, GROUP), 0) + 1
    one_hot = [
        (letters == id_rows[g : g + 1]).astype(jnp.float32).astype(jnp.bfloat16) for g in range(per)
    ]
    word_map = [
        (spots == word_rows[g : g + 1]).astype(jnp.float32).astype(jnp.bfloat16) for g in range(per)
    ]
    return jnp.concatenate(one_hot, axis=1), jnp.concatenate(word_map, axis=1)


def column_rms(values):
    inverse = lax.rsqrt(jnp.mean(values * values, axis=0, keepdims=True) + EPS)
    return values * inverse, inverse


def own_block():
    shape = (GROUP // SLOTS, SLOTS, CHEADS * GROUP)
    return iota(shape, 0) == lax.div(lax.rem(iota(shape, 2), GROUP), SLOTS)


def to_compact(block, own):
    return jnp.sum(jnp.where(own, block.reshape(own.shape), 0.0), axis=0)


def from_compact(compact, own):
    wide = jnp.broadcast_to(compact[None], own.shape)
    return jnp.where(own, wide, 0.0).astype(jnp.bfloat16).reshape(GROUP, -1)


def spread_heads(values):
    head = values.shape[0] // CHEADS
    zero = jnp.zeros((head, GROUP), values.dtype)
    rows = []
    for h in range(CHEADS):
        parts = [zero] * CHEADS
        parts[h] = values[h * head : (h + 1) * head]
        rows.append(jnp.concatenate(parts, axis=1))
    return jnp.concatenate(rows, axis=0)


def char_fwd_kernel(tiles_ref, *refs):
    @pl.when(pl.program_id(0) < tiles_ref[0])
    def _():
        char_fwd_tile(*refs)


def char_fwd_tile(
    pack_ref, table_ref, qkv_ref, out_ref, up_ref, down_ref, g1_ref, g2_ref,
    pooled_ref, keep_values, keep_probs, keep_qkv, keep_mixed, keep_first, keep_hidden, keep_slope,
):
    step = pl.program_id(0)
    words = pooled_ref.shape[0]
    per = ROWS // GROUP
    head = CD // CHEADS

    @pl.when(step == 0)
    def _():
        pooled_ref[...] = jnp.zeros_like(pooled_ref)

    one_hot, word_map = tile_maps(pack_ref, step, words)
    embedded = dot_nn(table_ref[...], one_hot)
    act_one = (column_rms(embedded)[0] * g1_ref[...]).astype(jnp.bfloat16)
    triple = dot_nn(qkv_ref[...], act_one).astype(jnp.bfloat16)
    keep_qkv[...] = triple
    low_rows = pack_ref[2, pl.ds(step * per, per), :]
    high_rows = pack_ref[3, pl.ds(step * per, per), :]
    own = own_block()
    key_pos = iota((SLOTS, GROUP), 0)
    key_rows = triple[CD : 2 * CD].T
    keep_values[...] = triple[2 * CD :].T
    mixed = []
    for g in range(per):
        valid = (key_pos >= low_rows[g : g + 1]) & (key_pos < high_rows[g : g + 1])
        valid = jnp.concatenate([valid.astype(jnp.float32)] * CHEADS, axis=1) > 0
        lanes = slice(g * GROUP, (g + 1) * GROUP)
        scores = to_compact(dot_nn(key_rows[lanes], spread_heads(triple[:CD, lanes])), own)
        scores = jnp.where(valid, scores * head**-0.5, NEG_FILL)
        powers = jnp.exp(scores - jnp.max(scores, axis=0, keepdims=True))
        powers = jnp.where(valid, powers, 0.0)
        total = jnp.sum(powers, axis=0, keepdims=True)
        probs = powers / jnp.where(total > 0, total, 1.0)
        keep_probs[:, g * CHEADS * GROUP : (g + 1) * CHEADS * GROUP] = probs
        probs = from_compact(probs, own)
        parts = []
        for h in range(CHEADS):
            v = triple[2 * CD + h * head : 2 * CD + (h + 1) * head, lanes]
            parts.append(dot_nn(v, probs[:, h * GROUP : (h + 1) * GROUP]).astype(jnp.bfloat16))
        mixed.append(jnp.concatenate(parts, axis=0))
    mixed = jnp.concatenate(mixed, axis=1)
    keep_mixed[...] = mixed
    first = embedded + dot_nn(out_ref[...], mixed)
    keep_first[...] = first
    act_two = (column_rms(first)[0] * g2_ref[...]).astype(jnp.bfloat16)
    branch = None
    for c in range(CFF // CD):
        rows = slice(c * CD, (c + 1) * CD)
        hidden, slope = gelu_pair(dot_nn(up_ref[rows, :], act_two))
        hidden = hidden.astype(jnp.bfloat16)
        keep_hidden[rows, :] = hidden
        keep_slope[rows, :] = slope.astype(jnp.bfloat16)
        part = dot_nn(down_ref[:, rows], hidden)
        branch = part if branch is None else branch + part
    high, low = split_two(first + branch)
    pooled_ref[...] += dot_nt(word_map, high) + dot_nt(word_map, low)


KEPT = (
    (3 * CD, jnp.bfloat16),
    (CD, jnp.bfloat16),
    (CD, jnp.float32),
    (CFF, jnp.bfloat16),
    (CFF, jnp.bfloat16),
)


def kept_specs():
    return [
        pl.BlockSpec((ROWS, CD), lambda t, n: (kept_place(t, n)[1], 0)),
        pl.BlockSpec((SLOTS, CHEADS * ROWS), kept_place),
    ] + [pl.BlockSpec((depth, ROWS), kept_place) for depth, _ in KEPT]


def kept_shapes(rows):
    return [
        jax.ShapeDtypeStruct((rows, CD), jnp.bfloat16),
        jax.ShapeDtypeStruct((SLOTS, CHEADS * rows), jnp.float32),
    ] + [jax.ShapeDtypeStruct((depth, rows), dtype) for depth, dtype in KEPT]


def whole(array):
    zeros = (0,) * array.ndim
    return pl.BlockSpec(array.shape, lambda *_: zeros)


def kept_place(step, tiles):
    return 0, jnp.minimum(step, tiles[0] - 1)


def char_fwd(tiles, pack, weights, words):
    rows = words * SLOTS
    operands = (pack,) + weights
    return pl.pallas_call(
        char_fwd_kernel,
        grid_spec=pltpu.PrefetchScalarGridSpec(
            num_scalar_prefetch=1,
            grid=(rows // ROWS,),
            in_specs=[whole(a) for a in operands],
            out_specs=[pl.BlockSpec((words, CD), lambda t, n: (0, 0))]
            + kept_specs(),
        ),
        out_shape=[jax.ShapeDtypeStruct((words, CD), jnp.float32)] + kept_shapes(rows),
        compiler_params=pltpu.CompilerParams(vmem_limit_bytes=VMEM_BYTES),
        name="char_fwd",
    )(tiles, *operands)


def fold_lanes(values):
    total = values[:, :GROUP]
    for g in range(1, values.shape[1] // GROUP):
        total = total + values[:, g * GROUP : (g + 1) * GROUP]
    return total


def column_rms_back(grad_in, gain, normed, inverse):
    scaled = grad_in * gain
    return inverse * (scaled - normed * jnp.mean(scaled * normed, axis=0, keepdims=True))


def char_bwd_kernel(tiles_ref, *refs):
    @pl.when(pl.program_id(0) < tiles_ref[0])
    def _():
        char_bwd_tile(*refs)


def char_bwd_tile(
    pack_ref, spread_ref, table_ref, qkv_ref, out_ref, up_ref, down_ref, g1_ref, g2_ref,
    keep_values, keep_probs, keep_qkv, keep_mixed, keep_first, keep_hidden, keep_slope,
    d_table, d_qkv, d_out, d_up, d_down, d_g1, d_g2,
):
    step = pl.program_id(0)
    words = spread_ref.shape[1]
    per = ROWS // GROUP
    head = CD // CHEADS

    @pl.when(step == 0)
    def _():
        for ref in (d_table, d_qkv, d_out, d_up, d_down, d_g1, d_g2):
            ref[...] = jnp.zeros_like(ref)

    one_hot, word_map = tile_maps(pack_ref, step, words)
    halves = dot_nn(spread_ref[...], word_map)
    grad_second = halves[:CD] + halves[CD:]
    grad_branch = grad_second.astype(jnp.bfloat16)
    first = keep_first[...]
    normed_two, inverse_two = column_rms(first)
    act_two = (normed_two * g2_ref[...]).astype(jnp.bfloat16)
    grad_act_two = None
    for c in range(CFF // CD):
        rows = slice(c * CD, (c + 1) * CD)
        d_down[rows, :] += dot_nt(keep_hidden[rows, :], grad_branch)
        grad_upper = dot_nn(down_ref[rows, :], grad_branch) * keep_slope[rows, :].astype(
            jnp.float32
        )
        grad_upper = grad_upper.astype(jnp.bfloat16)
        d_up[:, rows] += dot_nt(act_two, grad_upper)
        part = dot_nn(up_ref[:, rows], grad_upper)
        grad_act_two = part if grad_act_two is None else grad_act_two + part
    d_g2[...] += fold_lanes(grad_act_two * normed_two)
    grad_first = grad_second + column_rms_back(
        grad_act_two, g2_ref[...], normed_two, inverse_two
    )
    grad_attn = grad_first.astype(jnp.bfloat16)
    d_out[...] += dot_nt(keep_mixed[...], grad_attn)
    grad_mixed = dot_nn(out_ref[...], grad_attn).astype(jnp.bfloat16)
    own = own_block()
    triple = keep_qkv[...]
    columns = []
    for g in range(per):
        lanes = slice(g * GROUP, (g + 1) * GROUP)
        wide = slice(g * CHEADS * GROUP, (g + 1) * CHEADS * GROUP)
        probs = keep_probs[:, wide]
        grad_probs = to_compact(
            dot_nn(keep_values[lanes, :], spread_heads(grad_mixed[:, lanes])), own
        )
        grad_scores = probs * (
            grad_probs - jnp.sum(probs * grad_probs, axis=0, keepdims=True)
        )
        grad_raw = from_compact(grad_scores * head**-0.5, own)
        probs = from_compact(probs, own)
        gq, gk, gv = [], [], []
        for h in range(CHEADS):
            q = triple[h * head : (h + 1) * head, lanes]
            k = triple[CD + h * head : CD + (h + 1) * head, lanes]
            grad_o = grad_mixed[h * head : (h + 1) * head, lanes]
            part = slice(h * GROUP, (h + 1) * GROUP)
            gq.append(dot_nn(k, grad_raw[:, part]).astype(jnp.bfloat16))
            gk.append(dot_nt(q, grad_raw[:, part]).astype(jnp.bfloat16))
            gv.append(dot_nt(grad_o, probs[:, part]).astype(jnp.bfloat16))
        columns.append(jnp.concatenate(gq + gk + gv, axis=0))
    grad_triple = jnp.concatenate(columns, axis=1)
    embedded = dot_nn(table_ref[...], one_hot)
    normed_one, inverse_one = column_rms(embedded)
    act_one = (normed_one * g1_ref[...]).astype(jnp.bfloat16)
    d_qkv[...] += dot_nt(act_one, grad_triple)
    grad_act_one = dot_nn(qkv_ref[...], grad_triple)
    d_g1[...] += fold_lanes(grad_act_one * normed_one)
    back_one = column_rms_back(grad_act_one, g1_ref[...], normed_one, inverse_one)
    grad_embedded = (grad_first + back_one).astype(jnp.bfloat16)
    d_table[...] += dot_nt(one_hot, grad_embedded)


def char_bwd(tiles, pack, spread, weights, kept):
    operands = (pack, spread) + weights
    shapes = ((CV, CD), (CD, 3 * CD), (CD, CD), (CD, CFF), (CFF, CD), (CD, GROUP), (CD, GROUP))
    return pl.pallas_call(
        char_bwd_kernel,
        grid_spec=pltpu.PrefetchScalarGridSpec(
            num_scalar_prefetch=1,
            grid=(kept[0].shape[0] // ROWS,),
            in_specs=[whole(a) for a in operands]
            + kept_specs(),
            out_specs=[pl.BlockSpec(s, lambda t, n: (0, 0)) for s in shapes],
        ),
        out_shape=[jax.ShapeDtypeStruct(s, jnp.float32) for s in shapes],
        compiler_params=pltpu.CompilerParams(vmem_limit_bytes=VMEM_BYTES),
        name="char_bwd",
    )(tiles, *operands, *kept)


def cost(flops, moved, powers):
    return pl.CostEstimate(flops=int(flops), bytes_accessed=int(moved), transcendentals=int(powers))


def single(kernel, outs, name, flops):
    return pl.pallas_call(
        kernel,
        out_shape=[jax.ShapeDtypeStruct(shape, dtype) for shape, dtype in outs],
        compiler_params=pltpu.CompilerParams(vmem_limit_bytes=VMEM_BYTES),
        cost_estimate=cost(flops, 8e6, 1e5),
        name=name,
    )


def word_in_kernel(sum_ref, count_ref, words_ref, pool_ref, qkv_ref, g3_ref, start_ref, triple_ref):
    pooled = (sum_ref[...] / count_ref[...]).astype(jnp.bfloat16)
    words = words_ref[...].astype(jnp.float32).T
    start = words + dot_nt(pool_ref[...], pooled)
    start_ref[...] = start
    act = (column_rms(start)[0] * g3_ref[...]).astype(jnp.bfloat16)
    parts, depth, _ = triple_ref.shape
    for p in range(parts):
        rows = slice(p * depth, (p + 1) * depth)
        triple_ref[p] = dot_nn(qkv_ref[rows, :], act).astype(jnp.bfloat16)


def chunk_scores(ref, h, i, j, width):
    head = D // HEADS
    own = ref.shape[1] // 3
    lo = h * head
    q = ref[i, lo : lo + head, :]
    k = ref[j, own + lo : own + lo + head, :]
    scores = dot_tn(k, q) * head**-0.5
    if i == j:
        scores = jnp.where(
            iota((width, width), 0) <= iota((width, width), 1), scores, NEG_FILL
        )
    return scores


def word_attn_kernel(triple_ref, mixed_ref, lse_ref):
    parts, depth, width = triple_ref.shape
    head = D // HEADS
    own = depth // 3
    for h in range(own // head):
        lo = h * head
        for i in range(parts):
            scores = [chunk_scores(triple_ref, h, i, j, width) for j in range(i + 1)]
            highest = jnp.max(scores[0], axis=0, keepdims=True)
            for block in scores[1:]:
                highest = jnp.maximum(highest, jnp.max(block, axis=0, keepdims=True))
            powers = [jnp.exp(block - highest) for block in scores]
            total = jnp.sum(powers[0], axis=0, keepdims=True)
            for block in powers[1:]:
                total = total + jnp.sum(block, axis=0, keepdims=True)
            inverse = 1.0 / total
            mixed = None
            for j, block in enumerate(powers):
                v = triple_ref[j, 2 * own + lo : 2 * own + lo + head, :]
                part = dot_nn(v, (block * inverse).astype(jnp.bfloat16))
                mixed = part if mixed is None else mixed + part
            mixed_ref[i, lo : lo + head, :] = mixed.astype(jnp.bfloat16)
            lse_ref[h * parts + i : h * parts + i + 1, :] = highest + jnp.log(total)


def word_attn_back_kernel(triple_ref, lse_ref, grad_ref, out_ref, dk, dv):
    parts, depth, width = triple_ref.shape
    head = D // HEADS
    own = depth // 3
    for h in range(own // head):
        lo = h * head
        for i in range(parts):
            grad_o = grad_ref[i, lo : lo + head, :]
            lse = lse_ref[h * parts + i : h * parts + i + 1, :]
            probs, grads = [], []
            dot_sum = None
            for j in range(i + 1):
                probs.append(jnp.exp(chunk_scores(triple_ref, h, i, j, width) - lse))
                v = triple_ref[j, 2 * own + lo : 2 * own + lo + head, :]
                grads.append(dot_tn(v, grad_o))
                part = jnp.sum(probs[-1] * grads[-1], axis=0, keepdims=True)
                dot_sum = part if dot_sum is None else dot_sum + part
            q = triple_ref[i, lo : lo + head, :]
            grad_q = None
            for j in range(i + 1):
                k = triple_ref[j, own + lo : own + lo + head, :]
                raw = (probs[j] * (grads[j] - dot_sum) * head**-0.5).astype(jnp.bfloat16)
                part = dot_nn(k, raw)
                grad_q = part if grad_q is None else grad_q + part
                part_k = dot_nt(q, raw)
                part_v = dot_nt(grad_o, probs[j].astype(jnp.bfloat16))
                if i == j:
                    dk[j] = part_k
                    dv[j] = part_v
                else:
                    dk[j] += part_k
                    dv[j] += part_v
            out_ref[i, lo : lo + head, :] = grad_q.astype(jnp.bfloat16)
        for j in range(parts):
            out_ref[j, own + lo : own + lo + head, :] = dk[j].astype(jnp.bfloat16)
            out_ref[j, 2 * own + lo : 2 * own + lo + head, :] = dv[j].astype(jnp.bfloat16)


def word_mid_kernel(has_prev, *refs):
    (mixed_ref, start_ref, cot_ref, g4_ref, outt_ref, out_ref) = refs[:6]
    (upt_ref, up_ref, downt_ref, down_ref) = refs[6:10]
    place = 10
    prev = (None, None, None, None)
    if has_prev:
        prev = refs[10:14]
        place = 14
    (output_ref, after_grad_ref, mixed_grad_ref, d_up, d_down, d_out, d_g4) = refs[place : place + 7]
    (after, act, result, act_grad, cot_t) = refs[place + 7 :]
    step = pl.program_id(0)
    prev_up, prev_down, prev_out, prev_g4 = prev

    def put(ref, value, old):
        if old is not None:
            value = value + old[...]
        ref[...] = value.astype(ref.dtype)

    mixed = mixed_ref[...].reshape(D, -1)

    @pl.when(step == 0)
    def _():
        value = start_ref[...] + dot_nn(outt_ref[...], mixed)
        after[...] = value
        act[...] = (column_rms(value)[0] * g4_ref[...]).astype(jnp.bfloat16)
        result[...] = value
        act_grad[...] = jnp.zeros_like(act_grad)
        cot_t[...] = cot_ref[...].astype(jnp.float32).T.astype(jnp.bfloat16)

    hidden, slope = gelu_pair(dot_nn(upt_ref[...], act[...]))
    hidden = hidden.astype(jnp.bfloat16)
    result[...] += dot_nn(downt_ref[...], hidden)
    put(d_down, dot_nt(hidden, cot_t[...]), prev_down)
    grad_upper = (dot_nn(down_ref[...], cot_t[...]) * slope).astype(jnp.bfloat16)
    put(d_up, dot_nt(act[...], grad_upper), prev_up)
    act_grad[...] += dot_nn(up_ref[...], grad_upper)

    @pl.when(step == pl.num_programs(0) - 1)
    def _():
        output_ref[...] = result[...].T.astype(jnp.bfloat16)
        normed, inverse = column_rms(after[...])
        grad = act_grad[...]
        put(d_g4, fold_lanes(grad * normed), prev_g4)
        total = cot_t[...].astype(jnp.float32) + column_rms_back(
            grad, g4_ref[...], normed, inverse
        )
        after_grad_ref[...] = total
        low = total.astype(jnp.bfloat16)
        put(d_out, dot_nt(mixed, low), prev_out)
        mixed_grad_ref[...] = dot_nn(out_ref[...], low).astype(jnp.bfloat16).reshape(
            mixed_grad_ref.shape
        )


def word_mid(mixed, start, cot, g4, parts, prev):
    outt, out, upt, up, downt, down = parts
    width = start.shape[1]
    hidden = up.shape[1]
    block = D
    fixed = (mixed, start, cot, g4, outt, out)
    rows = pl.BlockSpec((block, D), lambda c: (c, 0))
    cols = pl.BlockSpec((D, block), lambda c: (0, c))

    def still(shape):
        return pl.BlockSpec(shape, lambda c: (0,) * len(shape))

    kind = jnp.float32 if prev is None else jnp.bfloat16
    earlier = () if prev is None else tuple(prev)
    return pl.pallas_call(
        functools.partial(word_mid_kernel, prev is not None),
        grid=(hidden // block,),
        in_specs=[still(a.shape) for a in fixed]
        + [rows, cols, cols, rows]
        + ([] if prev is None else [cols, rows, still((D, D)), still((D, GROUP))]),
        out_specs=[
            still((width, D)),
            still((D, width)),
            still(mixed.shape),
            cols,
            rows,
            still((D, D)),
            still((D, GROUP)),
        ],
        out_shape=[
            jax.ShapeDtypeStruct((width, D), jnp.bfloat16),
            jax.ShapeDtypeStruct((D, width), jnp.float32),
            jax.ShapeDtypeStruct(mixed.shape, jnp.bfloat16),
            jax.ShapeDtypeStruct((D, hidden), kind),
            jax.ShapeDtypeStruct((hidden, D), kind),
            jax.ShapeDtypeStruct((D, D), kind),
            jax.ShapeDtypeStruct((D, GROUP), jnp.float32),
        ],
        scratch_shapes=[
            pltpu.VMEM((D, width), jnp.float32),
            pltpu.VMEM((D, width), jnp.bfloat16),
            pltpu.VMEM((D, width), jnp.float32),
            pltpu.VMEM((D, width), jnp.float32),
            pltpu.VMEM((D, width), jnp.bfloat16),
        ],
        compiler_params=pltpu.CompilerParams(vmem_limit_bytes=VMEM_BYTES),
        cost_estimate=cost(6 * width * D * (2 * hidden + D), 2e7, 2 * width * hidden),
        name="word_mid",
    )(*fixed, upt, up, downt, down, *earlier)


def word_out_kernel(has_prev, *refs):
    (triple_ref, start_ref, after_grad_ref, qkv_ref, pool_ref, g3_ref) = refs[:6]
    (sum_ref, count_ref, count_row_ref) = refs[6:9]
    place = 9
    prev = (None, None, None)
    if has_prev:
        prev = refs[9:12]
        place = 12
    (input_grad_ref, spread_ref, d_qkv, d_pool, d_g3) = refs[place:]
    normed, inverse = column_rms(start_ref[...])
    act = (normed * g3_ref[...]).astype(jnp.bfloat16)
    parts, depth, _ = triple_ref.shape
    own = depth // 3
    grad = None
    for p in range(parts):
        triple = triple_ref[p]
        part = dot_nn(qkv_ref[:, p * depth : (p + 1) * depth], triple)
        grad = part if grad is None else grad + part
        weight = dot_nt(act, triple)
        for t in range(3):
            cols = slice(t * D + p * own, t * D + (p + 1) * own)
            value = weight[:, t * own : (t + 1) * own]
            if has_prev:
                value = value + prev[0][:, cols]
            d_qkv[:, cols] = value.astype(d_qkv.dtype)
    gain = fold_lanes(grad * normed)
    if has_prev:
        gain = gain + prev[2][...]
    d_g3[...] = gain
    total = after_grad_ref[...] + column_rms_back(grad, g3_ref[...], normed, inverse)
    input_grad_ref[...] = total.T
    low = total.astype(jnp.bfloat16)
    pooled = (sum_ref[...] / count_ref[...]).T.astype(jnp.bfloat16)
    value = dot_nt(pooled, low)
    if has_prev:
        value = value + prev[1][...]
    d_pool[...] = value.astype(d_pool.dtype)
    high, low = split_two(dot_nn(pool_ref[...], low) / count_row_ref[...])
    spread_ref[:CD, :] = high
    spread_ref[CD:, :] = low


def adam_step(weight, grad, first_old, second_old, clip_factor, rate, decay):
    clipped = grad * clip_factor
    first_new = BETA_ONE * first_old + (1.0 - BETA_ONE) * clipped
    second_new = BETA_TWO * second_old + (1.0 - BETA_TWO) * clipped * clipped
    first_hat = first_new / (1.0 - BETA_ONE**STEP)
    second_hat = second_new / (1.0 - BETA_TWO**STEP)
    weight_new = weight - rate * (first_hat / (jnp.sqrt(second_hat) + ADAM_EPS) + decay * weight)
    return (grad, first_new, second_new, weight_new, weight_new.astype(jnp.bfloat16))


class Ring:
    def __init__(self, dp, ranks):
        self.chips, self.ranks = dp // 2, ranks
        self.d, self.h = lax.axis_index("dp"), lax.axis_index("head")
        self.chip, self.core = lax.div(self.d, 2), lax.rem(self.d, 2)

    def sibling(self):
        return (self.d + 1 - 2 * self.core, self.h)

    def chip_at(self, k):
        return lax.rem(self.chip + k, self.chips)

    def plane(self, k):
        return (2 * self.chip_at(k) + self.core, self.h)

    def rank_at(self, k):
        return lax.rem(self.h + k, self.ranks)

    def line(self, k):
        return (self.d, self.rank_at(k))

    def meet(self):
        barrier = pltpu.get_barrier_semaphore()
        peers = [self.sibling()]
        peers += [self.plane(k) for k in range(1, self.chips)]
        peers += [self.line(k) for k in range(1, self.ranks)]
        for peer in peers:
            pl.semaphore_signal(barrier, inc=1, device_id=peer, device_id_type=pl.DeviceIdType.MESH)
        pl.semaphore_wait(barrier, len(peers))


def send(src, dst, sems, place, peer):
    copy = pltpu.make_async_remote_copy(
        src_ref=src,
        dst_ref=dst,
        send_sem=sems.at[(0,) + place],
        recv_sem=sems.at[(1,) + place],
        device_id=peer,
        device_id_type=pl.DeviceIdType.MESH,
    )
    copy.start()
    return copy


def gather_kernel(dp, ranks, count, *refs):
    shards, outs = refs[:count], refs[count : 2 * count]
    own_sem, line_sem, plane_sem, pair_sem = refs[2 * count :]
    ring = Ring(dp, ranks)
    ring.meet()
    sent, first, own = [], [], []
    for m in range(count):
        place = outs[m].at[ring.d, ring.h]
        own.append(pltpu.make_async_copy(shards[m], place, own_sem.at[m]))
        own[-1].start()
        first.append(
            [send(shards[m], place, line_sem, (m, k), ring.line(k)) for k in range(1, ranks)]
        )
    second = []
    for m in range(count):
        own[m].wait()
        for copy in first[m]:
            copy.wait_recv()
        block = outs[m].at[ring.d]
        second.append(
            [send(block, block, plane_sem, (m, k), ring.plane(k)) for k in range(1, ring.chips)]
        )
        sent.append(send(block, block, pair_sem, (m, 0), ring.sibling()))
    for m in range(count):
        for k in range(1, ring.chips):
            second[m][k - 1].wait_recv()
            block = outs[m].at[2 * ring.chip_at(ring.chips - k) + ring.core]
            sent.append(send(block, block, pair_sem, (m, k), ring.sibling()))
    for copy in sent:
        copy.wait()
    for m in range(count):
        for copy in first[m] + second[m]:
            copy.wait_send()


def gather(shards, collective):
    dp, ranks = lax.axis_size("dp"), lax.axis_size("head")
    count = len(shards)
    return pl.pallas_call(
        functools.partial(gather_kernel, dp, ranks, count),
        in_specs=[pl.BlockSpec(memory_space=pl.ANY)] * count,
        out_specs=[pl.BlockSpec(memory_space=pl.ANY)] * count,
        out_shape=[jax.ShapeDtypeStruct((dp, ranks) + s.shape, s.dtype) for s in shards],
        scratch_shapes=[
            pltpu.SemaphoreType.DMA((count,)),
            pltpu.SemaphoreType.DMA((2, count, ranks)),
            pltpu.SemaphoreType.DMA((2, count, dp // 2)),
            pltpu.SemaphoreType.DMA((2, count, dp // 2)),
        ],
        compiler_params=pltpu.CompilerParams(collective_id=collective, has_side_effects=True),
        name="gather",
    )(*shards)


def column_cuts(widths, ranks):
    block = sum(widths) // ranks
    cuts, start = [], 0
    for width in widths:
        mine, at = [], 0
        while at < width:
            rank, inside = divmod(start + at, block)
            take = min(width - at, block - inside)
            mine.append((rank, at, at + take, inside))
            at += take
        cuts.append(mine)
        start += width
    return cuts


def reduce_kernel(dp, ranks, groups, extra, *refs):
    pieces = sum(len(g) for g in groups)
    mats = len(groups)
    parts = refs[:pieces]
    gain_ref = refs[pieces]
    ready = refs[pieces + 1 : pieces + 1 + extra]
    place = pieces + 1 + extra
    outs = refs[place : place + mats]
    gain_out, square_out = refs[place + mats : place + mats + 2]
    place += mats + 2
    pair_in = refs[place : place + pieces]
    pair_sum = refs[place + pieces : place + 2 * pieces]
    plane_in = refs[place + 2 * pieces : place + 3 * pieces]
    place += 3 * pieces
    line_sum, line_in = refs[place : place + mats], refs[place + mats : place + 2 * mats]
    place += 2 * mats
    small, pair_sem, plane_sem, line_sem, small_sem = refs[place:]
    ring = Ring(dp, ranks)
    chips = ring.chips
    f32, bf16 = jnp.float32, jnp.bfloat16
    ring.meet()
    sent = []

    def share(slot, value, stage):
        others, here, count = (
            (lambda k: ring.sibling(), ring.core, 2),
            (ring.plane, ring.chip, chips),
            (ring.line, ring.h, ranks),
        )[stage]
        small[slot, stage, here] = value
        copies = []
        for k in range(1, count):
            spot = small.at[slot, stage, here]
            copies.append(send(spot, spot, small_sem, (slot, stage, k), others(k)))
        return copies

    def shared(slot, copies, stage):
        for copy in copies:
            copy.wait()
        count = (2, chips, ranks)[stage]
        total = small[slot, stage, 0]
        for k in range(1, count):
            total = total + small[slot, stage, k]
        return total

    def total_of(slot, value):
        for stage in range(3):
            value = shared(slot, share(slot, value, stage), stage)
        return value

    pairs = [
        send(parts[i].at[:, 1 - ring.core], pair_in[i], pair_sem, (i,), ring.sibling())
        for i in range(pieces)
    ]
    gain = shared(0, share(0, gain_ref[...], 0), 0)
    planes = []
    for i in range(pieces):
        pairs[i].wait()

        def add_pair(p, carry, i=i):
            both = parts[i][p, ring.core].astype(f32) + pair_in[i][p].astype(f32)
            pair_sum[i][p] = both.astype(bf16)
            return carry

        lax.fori_loop(0, chips, add_pair, 0)
        planes.append(
            [
                send(
                    pair_sum[i].at[ring.chip_at(k)],
                    plane_in[i].at[k],
                    plane_sem,
                    (i, k),
                    ring.plane(k),
                )
                for k in range(1, chips)
            ]
        )
    gain = shared(0, share(0, gain, 1), 1)
    gain_out[...] = shared(0, share(0, gain, 2), 2)
    lines, i = [], 0
    for m, widths in enumerate(groups):
        for cuts in column_cuts(widths, ranks):
            total = pair_sum[i][ring.chip].astype(f32)
            for k in range(1, chips):
                planes[i][k - 1].wait()
                total = total + plane_in[i][k].astype(f32)
            total = total.astype(bf16)
            for rank, first, last, inside in cuts:
                line_sum[m][rank, :, inside : inside + last - first] = total[:, first:last]
            i += 1
        lines.append(
            [
                send(
                    line_sum[m].at[ring.rank_at(k)], line_in[m].at[k], line_sem, (m, k), ring.line(k)
                )
                for k in range(1, ranks)
            ]
        )
    square = jnp.zeros(square_out.shape, f32)

    def squares(value):
        value = value * value
        rows, cols = value.shape
        if cols % GROUP:
            value = jnp.concatenate([value, jnp.zeros((rows, GROUP - cols % GROUP), f32)], axis=1)
        return jnp.sum(fold_lanes(value).reshape(rows // 8, 8, GROUP), axis=0)

    for ref in ready:
        square = square + squares(ref[...])
    for m in range(mats):
        total = line_sum[m][ring.h].astype(f32)
        for k in range(1, ranks):
            lines[m][k - 1].wait()
            total = total + line_in[m][k].astype(f32)
        outs[m][...] = total
        square = square + squares(total)
    small_square = jnp.concatenate([square, jnp.zeros_like(square)], axis=0)
    square_out[...] = total_of(1, small_square)[:8]


def reduce_grads(groups, gains, ready, collective):
    dp, ranks = lax.axis_size("dp"), lax.axis_size("head")
    chips = dp // 2
    bf16, f32 = jnp.bfloat16, jnp.float32
    pieces, widths, shards = [], [], []
    for group in groups:
        rows = group[0].shape[0] // dp
        pieces += [p.reshape(chips, 2, rows, p.shape[1]) for p in group]
        widths.append(tuple(p.shape[1] for p in group))
        shards.append((rows, sum(widths[-1]) // ranks))
    blocks = [p.shape[2:] for p in pieces]
    vmem = pl.BlockSpec(memory_space=pltpu.VMEM)
    n, mats = len(pieces), len(groups)
    return pl.pallas_call(
        functools.partial(reduce_kernel, dp, ranks, widths, len(ready)),
        in_specs=[vmem] * (n + 1 + len(ready)),
        out_specs=[vmem] * (mats + 2),
        out_shape=[jax.ShapeDtypeStruct(s, f32) for s in shards]
        + [jax.ShapeDtypeStruct(gains.shape, f32), jax.ShapeDtypeStruct((8, GROUP), f32)],
        scratch_shapes=[pltpu.VMEM((chips,) + b, bf16) for b in blocks] * 3
        + [pltpu.VMEM((ranks,) + s, bf16) for s in shards] * 2
        + [
            pltpu.VMEM((2, 3, max(2, chips, ranks)) + gains.shape, f32),
            pltpu.SemaphoreType.DMA((2, n)),
            pltpu.SemaphoreType.DMA((2, n, chips)),
            pltpu.SemaphoreType.DMA((2, mats, ranks)),
            pltpu.SemaphoreType.DMA((2, 2, 3, max(2, chips, ranks))),
        ],
        compiler_params=pltpu.CompilerParams(
            collective_id=collective, has_side_effects=True, vmem_limit_bytes=VMEM_BYTES
        ),
        name="reduce_grads",
    )(*pieces, gains, *ready)


def update_kernel(count, *refs):
    weights, grads = refs[:count], refs[count : 2 * count]
    firsts, seconds = refs[2 * count : 3 * count], refs[3 * count : 4 * count]
    square_ref = refs[4 * count]
    norm_ref, outs = refs[4 * count + 1], refs[4 * count + 2 :]
    gain_grad = grads[-1][...]
    square = jnp.sum(square_ref[...]) + jnp.sum(gain_grad * gain_grad)
    norm = jnp.sqrt(jnp.full((1, GROUP), square, jnp.float32))
    norm_ref[...] = norm
    clip_factor = jnp.minimum(1.0, CLIP / norm)[:, :1]
    for i in range(count):
        gains = i == count - 1
        result = adam_step(
            weights[i][...],
            grads[i][...],
            firsts[i][...],
            seconds[i][...],
            clip_factor,
            GAIN_RATE if gains else MATRIX_RATE,
            0.0 if gains else MATRIX_DECAY,
        )
        for ref, value in zip(outs[5 * i : 5 * i + 5], result):
            ref[...] = value


def update(weights, grads, firsts, seconds, square):
    count = len(weights)
    shapes = [jax.ShapeDtypeStruct((1, GROUP), jnp.float32)]
    for w in weights:
        shapes += [jax.ShapeDtypeStruct(w.shape, jnp.float32)] * 4
        shapes.append(jax.ShapeDtypeStruct(w.shape, jnp.bfloat16))
    return pl.pallas_call(
        functools.partial(update_kernel, count),
        out_shape=shapes,
        compiler_params=pltpu.CompilerParams(vmem_limit_bytes=VMEM_BYTES),
        name="update",
    )(*weights, *grads, *firsts, *seconds, square)


def body(
    char_ids,
    char_counts,
    language,
    words_in,
    out_cotangent,
    char_table,
    char_in,
    char_down,
    word_in,
    word_down,
    norm_gains,
    old_table_first,
    old_table_second,
    old_char_in_first,
    old_char_in_second,
    old_char_down_first,
    old_char_down_second,
    old_word_in_first,
    old_word_in_second,
    old_word_down_first,
    old_word_down_second,
    old_gains_first,
    old_gains_second,
):
    bf16, f32 = jnp.bfloat16, jnp.float32
    blocks = gather(
        (
            char_table.T.astype(bf16),
            char_in.astype(bf16),
            char_down.T.astype(bf16),
            word_in.astype(bf16),
            word_down.astype(bf16),
        ),
        0,
    )

    def joined(block):
        dp, ranks, rows, cols = block.shape
        return block.transpose(0, 2, 1, 3).reshape(dp * rows, ranks * cols)

    def joined_flat(block):
        dp, ranks, cols, rows = block.shape
        return block.transpose(1, 2, 0, 3).reshape(ranks * cols, dp * rows)

    table_t_low, char_in_low = joined_flat(blocks[0]), joined(blocks[1])
    char_down_t = joined_flat(blocks[2])
    word_in_low, word_down_low = joined(blocks[3]), joined(blocks[4])
    seq_count, local_words = (words_in.shape[0], words_in.shape[1])
    ranks = lax.axis_size("head")
    width = 3 * D // ranks
    own = width // 3
    packed, tiles = pack_rows(char_ids, char_counts)
    languages = table_t_low.shape[1] // CV

    def lanes(gain, width):
        return jnp.broadcast_to(gain[:, None], (gain.shape[0], width))

    gains = (lanes(norm_gains[:CD], ROWS), lanes(norm_gains[CD : 2 * CD], ROWS))
    g3 = lanes(norm_gains[2 * CD : 2 * CD + D], local_words)
    g4 = lanes(norm_gains[2 * CD + D :], local_words)
    table_t = [
        lax.dynamic_slice_in_dim(table_t_low, language[i] * CV, CV, axis=1)
        for i in range(seq_count)
    ]
    char_parts = (
        char_in_low[:, : 3 * CD],
        char_in_low[:, 3 * CD : 4 * CD],
        char_in_low[:, 4 * CD : 4 * CD + CFF],
        char_down_t.T,
    )
    flipped = tuple(part.T for part in char_parts[:3]) + (char_down_t,)
    pool = char_in_low[:, 4 * CD + CFF :]
    pool_t = pool.T
    qkv = word_in_low[:, : 3 * D].reshape(D, 3, ranks, own).transpose(0, 2, 1, 3).reshape(D, 3 * D)
    qkv_t = qkv.T
    out = word_in_low[:, 3 * D : 4 * D]
    up = word_in_low[:, 4 * D :]
    mid_parts = (out.T, out, up.T, up, word_down_low.T, word_down_low)
    count_row = char_counts.astype(jnp.float32)[:, None, :]
    count_col = char_counts.astype(jnp.float32)[:, :, None]
    triple_shape = (ranks, width, local_words)
    mixed_shape = (ranks, own, local_words)

    def swap(values):
        return lax.all_to_all(values, "head", 0, 0, tiled=True)

    seqs = range(seq_count)
    kept, sums, starts, triples = [], [], [], []
    for i in seqs:
        total, *saved = char_fwd(
            tiles[i : i + 1], packed[i], (table_t[i],) + flipped + gains, local_words
        )
        kept.append(saved)
        sums.append(total)
        start, triple = single(
            word_in_kernel,
            [((D, local_words), f32), (triple_shape, bf16)],
            "word_in",
            2 * local_words * D * 3 * D,
        )(total, count_col[i], words_in[i], pool_t, qkv_t, g3)
        starts.append(start)
        triples.append(swap(triple))
    mixes, lses = [], []
    for i in seqs:
        mixed, lse = single(
            word_attn_kernel,
            [(mixed_shape, bf16), ((own // (D // HEADS) * ranks, local_words), f32)],
            "word_attn",
            4e9,
        )(triples[i])
        lses.append(lse)
        mixes.append(swap(mixed))
    outputs, after_grads, mixed_grads = [], [], []
    mid = None
    for i in seqs:
        output, after_grad, mixed_grad, *mid = word_mid(
            mixes[i], starts[i], out_cotangent[i], g4, mid_parts, mid
        )
        outputs.append(output)
        after_grads.append(after_grad)
        mixed_grads.append(swap(mixed_grad))
    triple_grads = []
    for i in seqs:
        grads = pl.pallas_call(
            word_attn_back_kernel,
            out_shape=jax.ShapeDtypeStruct(triple_shape, bf16),
            scratch_shapes=[pltpu.VMEM((ranks, D // HEADS, local_words), f32)] * 2,
            compiler_params=pltpu.CompilerParams(vmem_limit_bytes=VMEM_BYTES),
            cost_estimate=cost(1e10, 2e6, 1e6),
            name="word_attn_back",
        )(triples[i], lses[i], mixed_grads[i])
        triple_grads.append(swap(grads))
    input_grads, last = [], None
    char_last = None
    tables_out = []
    for i in seqs:
        kind = f32 if last is None else bf16
        earlier = () if last is None else tuple(last)
        input_grad, spread, *last = single(
            functools.partial(word_out_kernel, last is not None),
            [
                ((local_words, D), f32),
                ((2 * CD, local_words), bf16),
                ((D, 3 * D), kind),
                ((CD, D), kind),
                ((D, GROUP), f32),
            ],
            "word_out",
            4 * local_words * D * 3 * D,
        )(
            triple_grads[i],
            starts[i],
            after_grads[i],
            qkv,
            pool,
            g3,
            sums[i],
            count_col[i],
            count_row[i],
            *earlier,
        )
        input_grads.append(input_grad)
        one_table, *rest = char_bwd(
            tiles[i : i + 1], packed[i], spread, (table_t[i],) + char_parts + gains, kept[i]
        )
        tables_out.append(one_table)
        char_last = rest if char_last is None else [a + b for a, b in zip(char_last, rest)]
    output = jnp.stack(outputs)
    input_grad = jnp.stack(input_grads)
    grad_table = sum(
        jnp.where(
            (jnp.arange(languages) == language[i])[:, None, None], tables_out[i][None], 0.0
        )
        for i in seqs
    ).reshape(-1, CD)
    grad_up, grad_down, grad_out, gain_four = mid
    grad_qkv, grad_pool, gain_three = last
    c_qkv, c_out, c_up, c_down, gain_one, gain_two = char_last

    gain_grads = jnp.concatenate(
        [jnp.sum(g, axis=1) for g in (gain_one, gain_two, gain_three, gain_four)]
    )
    flat = (gain_grads.shape[0] // GROUP, GROUP)
    rest = 16 - flat[0]
    *shards, gains_sum, square = reduce_grads(
        [
            [grad_table.astype(bf16)],
            [g.astype(bf16) for g in (c_qkv, c_out, c_up, grad_pool)],
            [c_down.astype(bf16)],
            [grad_qkv, grad_out, grad_up],
            [grad_down],
        ],
        jnp.pad(gain_grads.reshape(flat), ((0, rest), (0, 0))),
        [],
        1,
    )
    norm, *updated = update(
        (char_table, char_in, char_down, word_in, word_down, norm_gains.reshape(flat)),
        (*shards, gains_sum[: flat[0]]),
        (
            old_table_first,
            old_char_in_first,
            old_char_down_first,
            old_word_in_first,
            old_word_down_first,
            old_gains_first.reshape(flat),
        ),
        (
            old_table_second,
            old_char_in_second,
            old_char_down_second,
            old_word_in_second,
            old_word_down_second,
            old_gains_second.reshape(flat),
        ),
        square,
    )
    updated[-5:] = [part.reshape(norm_gains.shape) for part in updated[-5:]]
    return (output, input_grad, norm[0, 0], *updated)


def solution(mesh):
    return jax.shard_map(
        body,
        mesh=mesh,
        in_specs=(
            P("dp", "head", None),
            P("dp", "head"),
            P("dp"),
            P("dp", "head", None),
            P("dp", "head", None),
            P("dp", "head"),
            P("dp", "head"),
            P("dp", "head"),
            P("dp", "head"),
            P("dp", "head"),
            P(),
            P("dp", "head"),
            P("dp", "head"),
            P("dp", "head"),
            P("dp", "head"),
            P("dp", "head"),
            P("dp", "head"),
            P("dp", "head"),
            P("dp", "head"),
            P("dp", "head"),
            P("dp", "head"),
            P(),
            P(),
        ),
        out_specs=(
            P("dp", "head", None),
            P("dp", "head", None),
            P(),
            P("dp", "head"),
            P("dp", "head"),
            P("dp", "head"),
            P("dp", "head"),
            P("dp", "head"),
            P("dp", "head"),
            P("dp", "head"),
            P("dp", "head"),
            P("dp", "head"),
            P("dp", "head"),
            P("dp", "head"),
            P("dp", "head"),
            P("dp", "head"),
            P("dp", "head"),
            P("dp", "head"),
            P("dp", "head"),
            P("dp", "head"),
            P("dp", "head"),
            P("dp", "head"),
            P("dp", "head"),
            P("dp", "head"),
            P("dp", "head"),
            P("dp", "head"),
            P("dp", "head"),
            P("dp", "head"),
            P(),
            P(),
            P(),
            P(),
            P(),
        ),
        check_vma=False,
    )
```

```python
import functools

import jax
import jax.numpy as jnp
from jax import lax
from jax.experimental import pallas as pl
from jax.experimental.pallas import tpu as pltpu
from jax.sharding import PartitionSpec as P

D = 512
HEADS = 8
CD = 256
CHEADS = 4
CFF = 1024
CV = 256
STEP = 5


EPS = 1e-05
CLIP = 1.0
MATRIX_RATE = 0.03
GAIN_RATE = 0.25
MATRIX_DECAY = 0.1
BETA_ONE = 0.5
BETA_TWO = 0.5
ADAM_EPS = 1e-08
NEG_FILL = -1e30
SQRT_HALF = 0.7071067811865476
INV_ROOT_TWO_PI = 0.3989422804014327


ROWS = 512
SLOTS = 16
GROUP = 128
VMEM_BYTES = 56 * 1024 * 1024
ERFC_P = 0.39
ERFC = (0.235325887, 0.091384224, 0.649569841, -0.635413203, 0.886672317, -0.227539068)


def dot_nn(left_side, right_side):
    return lax.dot_general(
        left_side, right_side, (((1,), (0,)), ((), ())), preferred_element_type=jnp.float32
    )


def dot_tn(left_side, right_side):
    return lax.dot_general(
        left_side, right_side, (((0,), (0,)), ((), ())), preferred_element_type=jnp.float32
    )


def dot_nt(left_side, right_side):
    return lax.dot_general(
        left_side, right_side, (((1,), (1,)), ((), ())), preferred_element_type=jnp.float32
    )


def gelu_pair(upper):
    size = jnp.abs(upper)
    t = 1.0 / (1.0 + (ERFC_P * SQRT_HALF) * size)
    poly = ERFC[5]
    for c in ERFC[4::-1]:
        poly = poly * t + c
    bell = jnp.exp(upper * upper * -0.5)
    half = 0.5 * (poly * t * bell)
    phi = jnp.where(upper > 0, 1.0 - half, half)
    return upper * phi, phi + upper * (bell * INV_ROOT_TWO_PI)


def iota(shape, dim):
    return lax.broadcasted_iota(jnp.int32, shape, dim)


def split_two(values):
    high = values.astype(jnp.bfloat16)
    return high, (values - high.astype(jnp.float32)).astype(jnp.bfloat16)


def pack_words(row, ids, out_ref, tiles_ref, seq):
    n = row.shape[1]
    col = jnp.broadcast_to(row.astype(jnp.float32), (8, n)).T[:, :1].astype(jnp.int32)
    sub, lane = iota((n, n), 0), iota((n, n), 1)
    ahead = (row > col) | ((row == col) & (lane < sub))
    rank_col = jnp.sum(ahead.astype(jnp.float32), axis=1, keepdims=True).astype(jnp.int32)
    ahead = (col > row) | ((col == row) & (sub < lane))
    rank_row = jnp.sum(ahead.astype(jnp.float32), axis=0, keepdims=True).astype(jnp.int32)
    clash = (rank_col < rank_row) & (col + row > SLOTS)
    alone = jnp.max(jnp.where(clash, rank_col + rank_row, 0).astype(jnp.float32))
    alone = jnp.maximum(alone.astype(jnp.int32) - n + 2, 0)
    partner = n - 1 + alone - rank_row
    second = (rank_row >= alone) & (rank_row > partner)
    bins = jnp.where(second, partner, rank_row)
    here = sub == bins
    first_map = (here & jnp.logical_not(second)).astype(jnp.float32).astype(jnp.bfloat16)
    second_map = (here & second).astype(jnp.float32).astype(jnp.bfloat16)
    pos = lax.rem(iota((GROUP, n), 0), SLOTS)
    word = iota((GROUP, n), 1) + 1
    wide = jnp.broadcast_to(row, (GROUP, n))
    in_first, in_second = pos < wide, pos >= SLOTS - wide

    def kept(mask, values):
        return jnp.where(mask, values, 0).astype(jnp.float32).astype(jnp.bfloat16)

    groups = n * SLOTS // GROUP
    per = GROUP // SLOTS
    own = iota((groups, per, GROUP), 1) == lax.div(iota((groups, per, GROUP), 2), SLOTS)
    back = jnp.concatenate([ids[SLOTS - 1 - j : SLOTS - j] for j in range(SLOTS)] * per, axis=0)
    ids = jnp.concatenate([ids] * per, axis=0)
    zero = jnp.zeros_like(wide)
    for k, (one, two) in enumerate(
        ((ids + 1, back + 1), (word, word), (zero, SLOTS - wide), (wide, zero + SLOTS))
    ):
        full = dot_nt(first_map, kept(in_first, one)) + dot_nt(second_map, kept(in_second, two))
        full = jnp.where(own, full.reshape(groups, per, GROUP), 0.0)
        out_ref[seq, k] = jnp.sum(full, axis=1).astype(jnp.int32)
    used = alone + lax.div(n - alone + 1, 2)
    tiles_ref[seq] = lax.div(used * SLOTS + ROWS - 1, ROWS)


def pack_kernel(counts_ref, ids_ref, out_ref, tiles_ref):
    for seq in range(ids_ref.shape[0]):
        pack_words(counts_ref[seq : seq + 1, :], ids_ref[seq], out_ref, tiles_ref, seq)


def pack_rows(char_ids, char_counts):
    seqs, words, slots = char_ids.shape
    vmem = pl.BlockSpec(memory_space=pltpu.VMEM)
    return pl.pallas_call(
        pack_kernel,
        in_specs=[vmem, vmem],
        out_specs=[vmem, pl.BlockSpec(memory_space=pltpu.SMEM)],
        out_shape=[
            jax.ShapeDtypeStruct((seqs, 4, words * slots // GROUP, GROUP), jnp.int32),
            jax.ShapeDtypeStruct((seqs,), jnp.int32),
        ],
        name="pack",
    )(char_counts, char_ids.transpose(0, 2, 1))


def tile_maps(pack_ref, step, words):
    per = ROWS // GROUP
    id_rows = pack_ref[0, pl.ds(step * per, per), :]
    word_rows = pack_ref[1, pl.ds(step * per, per), :]
    letters = iota((CV, GROUP), 0) + 1
    spots = iota((words, GROUP), 0) + 1
    one_hot = [
        (letters == id_rows[g : g + 1]).astype(jnp.float32).astype(jnp.bfloat16) for g in range(per)
    ]
    word_map = [
        (spots == word_rows[g : g + 1]).astype(jnp.float32).astype(jnp.bfloat16) for g in range(per)
    ]
    return jnp.concatenate(one_hot, axis=1), jnp.concatenate(word_map, axis=1)


def column_rms(values):
    inverse = lax.rsqrt(jnp.mean(values * values, axis=0, keepdims=True) + EPS)
    return values * inverse, inverse


def own_block():
    shape = (GROUP // SLOTS, SLOTS, CHEADS * GROUP)
    return iota(shape, 0) == lax.div(lax.rem(iota(shape, 2), GROUP), SLOTS)


def to_compact(block, own):
    return jnp.sum(jnp.where(own, block.reshape(own.shape), 0.0), axis=0)


def from_compact(compact, own):
    wide = jnp.broadcast_to(compact[None], own.shape)
    return jnp.where(own, wide, 0.0).astype(jnp.bfloat16).reshape(GROUP, -1)


def spread_heads(values):
    head = values.shape[0] // CHEADS
    zero = jnp.zeros((head, GROUP), values.dtype)
    rows = []
    for h in range(CHEADS):
        parts = [zero] * CHEADS
        parts[h] = values[h * head : (h + 1) * head]
        rows.append(jnp.concatenate(parts, axis=1))
    return jnp.concatenate(rows, axis=0)


def char_fwd_kernel(tiles_ref, *refs):
    @pl.when(pl.program_id(0) < tiles_ref[0])
    def _():
        char_fwd_tile(*refs)


def char_fwd_tile(
    pack_ref, table_ref, qkv_ref, out_ref, up_ref, down_ref, g1_ref, g2_ref,
    pooled_ref, keep_values, keep_probs, keep_qkv, keep_mixed, keep_first, keep_hidden, keep_slope,
):
    step = pl.program_id(0)
    words = pooled_ref.shape[0]
    per = ROWS // GROUP
    head = CD // CHEADS

    @pl.when(step == 0)
    def _():
        pooled_ref[...] = jnp.zeros_like(pooled_ref)

    one_hot, word_map = tile_maps(pack_ref, step, words)
    embedded = dot_nn(table_ref[...], one_hot)
    act_one = (column_rms(embedded)[0] * g1_ref[...]).astype(jnp.bfloat16)
    triple = dot_nn(qkv_ref[...], act_one).astype(jnp.bfloat16)
    keep_qkv[...] = triple
    low_rows = pack_ref[2, pl.ds(step * per, per), :]
    high_rows = pack_ref[3, pl.ds(step * per, per), :]
    own = own_block()
    key_pos = iota((SLOTS, GROUP), 0)
    key_rows = triple[CD : 2 * CD].T
    keep_values[...] = triple[2 * CD :].T
    mixed = []
    for g in range(per):
        valid = (key_pos >= low_rows[g : g + 1]) & (key_pos < high_rows[g : g + 1])
        valid = jnp.concatenate([valid.astype(jnp.float32)] * CHEADS, axis=1) > 0
        lanes = slice(g * GROUP, (g + 1) * GROUP)
        scores = to_compact(dot_nn(key_rows[lanes], spread_heads(triple[:CD, lanes])), own)
        scores = jnp.where(valid, scores * head**-0.5, NEG_FILL)
        powers = jnp.exp(scores - jnp.max(scores, axis=0, keepdims=True))
        powers = jnp.where(valid, powers, 0.0)
        total = jnp.sum(powers, axis=0, keepdims=True)
        probs = powers / jnp.where(total > 0, total, 1.0)
        keep_probs[:, g * CHEADS * GROUP : (g + 1) * CHEADS * GROUP] = probs
        probs = from_compact(probs, own)
        parts = []
        for h in range(CHEADS):
            v = triple[2 * CD + h * head : 2 * CD + (h + 1) * head, lanes]
            parts.append(dot_nn(v, probs[:, h * GROUP : (h + 1) * GROUP]).astype(jnp.bfloat16))
        mixed.append(jnp.concatenate(parts, axis=0))
    mixed = jnp.concatenate(mixed, axis=1)
    keep_mixed[...] = mixed
    first = embedded + dot_nn(out_ref[...], mixed)
    keep_first[...] = first
    act_two = (column_rms(first)[0] * g2_ref[...]).astype(jnp.bfloat16)
    branch = None
    for c in range(CFF // CD):
        rows = slice(c * CD, (c + 1) * CD)
        hidden, slope = gelu_pair(dot_nn(up_ref[rows, :], act_two))
        hidden = hidden.astype(jnp.bfloat16)
        keep_hidden[rows, :] = hidden
        keep_slope[rows, :] = slope.astype(jnp.bfloat16)
        part = dot_nn(down_ref[:, rows], hidden)
        branch = part if branch is None else branch + part
    high, low = split_two(first + branch)
    pooled_ref[...] += dot_nt(word_map, high) + dot_nt(word_map, low)


KEPT = (
    (3 * CD, jnp.bfloat16),
    (CD, jnp.bfloat16),
    (CD, jnp.float32),
    (CFF, jnp.bfloat16),
    (CFF, jnp.bfloat16),
)


def kept_specs():
    return [
        pl.BlockSpec((ROWS, CD), lambda t, n: (kept_place(t, n)[1], 0)),
        pl.BlockSpec((SLOTS, CHEADS * ROWS), kept_place),
    ] + [pl.BlockSpec((depth, ROWS), kept_place) for depth, _ in KEPT]


def kept_shapes(rows):
    return [
        jax.ShapeDtypeStruct((rows, CD), jnp.bfloat16),
        jax.ShapeDtypeStruct((SLOTS, CHEADS * rows), jnp.float32),
    ] + [jax.ShapeDtypeStruct((depth, rows), dtype) for depth, dtype in KEPT]


def whole(array):
    zeros = (0,) * array.ndim
    return pl.BlockSpec(array.shape, lambda *_: zeros)


def kept_place(step, tiles):
    return 0, jnp.minimum(step, tiles[0] - 1)


def char_fwd(tiles, pack, weights, words):
    rows = words * SLOTS
    operands = (pack,) + weights
    return pl.pallas_call(
        char_fwd_kernel,
        grid_spec=pltpu.PrefetchScalarGridSpec(
            num_scalar_prefetch=1,
            grid=(rows // ROWS,),
            in_specs=[whole(a) for a in operands],
            out_specs=[pl.BlockSpec((words, CD), lambda t, n: (0, 0))]
            + kept_specs(),
        ),
        out_shape=[jax.ShapeDtypeStruct((words, CD), jnp.float32)] + kept_shapes(rows),
        compiler_params=pltpu.CompilerParams(vmem_limit_bytes=VMEM_BYTES),
        name="char_fwd",
    )(tiles, *operands)


def fold_lanes(values):
    total = values[:, :GROUP]
    for g in range(1, values.shape[1] // GROUP):
        total = total + values[:, g * GROUP : (g + 1) * GROUP]
    return total


def column_rms_back(grad_in, gain, normed, inverse):
    scaled = grad_in * gain
    return inverse * (scaled - normed * jnp.mean(scaled * normed, axis=0, keepdims=True))


def char_bwd_kernel(tiles_ref, *refs):
    @pl.when(pl.program_id(0) < tiles_ref[0])
    def _():
        char_bwd_tile(tiles_ref[0] - 1, *refs)


def char_bwd_tile(
    last, pack_ref, spread_ref, table_ref, qkv_ref, out_ref, up_ref, down_ref, g1_ref, g2_ref,
    keep_values, keep_probs, keep_qkv, keep_mixed, keep_first, keep_hidden, keep_slope,
    *refs,
):
    sums = 7
    earlier, results, totals = (), refs[-2 * sums : -sums], refs[-sums:]
    if len(refs) == 3 * sums - 1:
        earlier = refs[: sums - 1]
    d_table, d_qkv, d_out, d_up, d_down, d_g1, d_g2 = totals
    step = pl.program_id(0)
    words = spread_ref.shape[1]
    per = ROWS // GROUP
    head = CD // CHEADS

    @pl.when(step == 0)
    def _():
        d_table[...] = jnp.zeros_like(d_table)
        for i, ref in enumerate(totals[1:]):
            ref[...] = earlier[i][...] if earlier else jnp.zeros_like(ref)

    one_hot, word_map = tile_maps(pack_ref, step, words)
    halves = dot_nn(spread_ref[...], word_map)
    grad_second = halves[:CD] + halves[CD:]
    grad_branch = grad_second.astype(jnp.bfloat16)
    first = keep_first[...]
    normed_two, inverse_two = column_rms(first)
    act_two = (normed_two * g2_ref[...]).astype(jnp.bfloat16)
    grad_act_two = None
    for c in range(CFF // CD):
        rows = slice(c * CD, (c + 1) * CD)
        d_down[rows, :] += dot_nt(keep_hidden[rows, :], grad_branch)
        grad_upper = dot_nn(down_ref[rows, :], grad_branch) * keep_slope[rows, :].astype(
            jnp.float32
        )
        grad_upper = grad_upper.astype(jnp.bfloat16)
        d_up[:, rows] += dot_nt(act_two, grad_upper)
        part = dot_nn(up_ref[:, rows], grad_upper)
        grad_act_two = part if grad_act_two is None else grad_act_two + part
    d_g2[...] += fold_lanes(grad_act_two * normed_two)
    grad_first = grad_second + column_rms_back(
        grad_act_two, g2_ref[...], normed_two, inverse_two
    )
    grad_attn = grad_first.astype(jnp.bfloat16)
    d_out[...] += dot_nt(keep_mixed[...], grad_attn)
    grad_mixed = dot_nn(out_ref[...], grad_attn).astype(jnp.bfloat16)
    own = own_block()
    triple = keep_qkv[...]
    columns = []
    for g in range(per):
        lanes = slice(g * GROUP, (g + 1) * GROUP)
        wide = slice(g * CHEADS * GROUP, (g + 1) * CHEADS * GROUP)
        probs = keep_probs[:, wide]
        grad_probs = to_compact(
            dot_nn(keep_values[lanes, :], spread_heads(grad_mixed[:, lanes])), own
        )
        grad_scores = probs * (
            grad_probs - jnp.sum(probs * grad_probs, axis=0, keepdims=True)
        )
        grad_raw = from_compact(grad_scores * head**-0.5, own)
        probs = from_compact(probs, own)
        gq, gk, gv = [], [], []
        for h in range(CHEADS):
            q = triple[h * head : (h + 1) * head, lanes]
            k = triple[CD + h * head : CD + (h + 1) * head, lanes]
            grad_o = grad_mixed[h * head : (h + 1) * head, lanes]
            part = slice(h * GROUP, (h + 1) * GROUP)
            gq.append(dot_nn(k, grad_raw[:, part]).astype(jnp.bfloat16))
            gk.append(dot_nt(q, grad_raw[:, part]).astype(jnp.bfloat16))
            gv.append(dot_nt(grad_o, probs[:, part]).astype(jnp.bfloat16))
        columns.append(jnp.concatenate(gq + gk + gv, axis=0))
    grad_triple = jnp.concatenate(columns, axis=1)
    embedded = dot_nn(table_ref[...], one_hot)
    normed_one, inverse_one = column_rms(embedded)
    act_one = (normed_one * g1_ref[...]).astype(jnp.bfloat16)
    d_qkv[...] += dot_nt(act_one, grad_triple)
    grad_act_one = dot_nn(qkv_ref[...], grad_triple)
    d_g1[...] += fold_lanes(grad_act_one * normed_one)
    back_one = column_rms_back(grad_act_one, g1_ref[...], normed_one, inverse_one)
    grad_embedded = (grad_first + back_one).astype(jnp.bfloat16)
    d_table[...] += dot_nt(one_hot, grad_embedded)

    @pl.when(step == last)
    def _():
        for ref, total in zip(results, totals):
            ref[...] = total[...].astype(ref.dtype)


def char_bwd(tiles, pack, spread, weights, kept, earlier):
    operands = (pack, spread) + weights
    shapes = ((CV, CD), (CD, 3 * CD), (CD, CD), (CD, CFF), (CFF, CD), (CD, GROUP), (CD, GROUP))
    f32, bf16 = jnp.float32, jnp.bfloat16
    kinds = [f32] * 7 if earlier is None else [f32] + [bf16] * 4 + [f32] * 2
    earlier = () if earlier is None else tuple(earlier)
    return pl.pallas_call(
        char_bwd_kernel,
        grid_spec=pltpu.PrefetchScalarGridSpec(
            num_scalar_prefetch=1,
            grid=(kept[0].shape[0] // ROWS,),
            in_specs=[whole(a) for a in operands] + kept_specs() + [whole(a) for a in earlier],
            out_specs=[pl.BlockSpec(s, lambda t, n: (0, 0)) for s in shapes],
            scratch_shapes=[pltpu.VMEM(s, f32) for s in shapes],
        ),
        out_shape=[jax.ShapeDtypeStruct(s, kind) for s, kind in zip(shapes, kinds)],
        compiler_params=pltpu.CompilerParams(vmem_limit_bytes=VMEM_BYTES),
        name="char_bwd",
    )(tiles, *operands, *kept, *earlier)


def adam_step(weight, grad, first_old, second_old, clip_factor, rate, decay):
    clipped = grad * clip_factor
    first_new = BETA_ONE * first_old + (1.0 - BETA_ONE) * clipped
    second_new = BETA_TWO * second_old + (1.0 - BETA_TWO) * clipped * clipped
    first_hat = first_new / (1.0 - BETA_ONE**STEP)
    second_hat = second_new / (1.0 - BETA_TWO**STEP)
    weight_new = weight - rate * (first_hat / (jnp.sqrt(second_hat) + ADAM_EPS) + decay * weight)
    return (grad, first_new, second_new, weight_new, weight_new.astype(jnp.bfloat16))


class Ring:
    def __init__(self, dp, ranks):
        self.chips, self.ranks = dp // 2, ranks
        self.d, self.h = lax.axis_index("dp"), lax.axis_index("head")
        self.chip, self.core = lax.div(self.d, 2), lax.rem(self.d, 2)

    def sibling(self):
        return (self.d + 1 - 2 * self.core, self.h)

    def chip_at(self, k):
        return lax.rem(self.chip + k, self.chips)

    def plane(self, k):
        return (2 * self.chip_at(k) + self.core, self.h)

    def rank_at(self, k):
        return lax.rem(self.h + k, self.ranks)

    def line(self, k):
        return (self.d, self.rank_at(k))

    def meet(self):
        barrier = pltpu.get_barrier_semaphore()
        peers = [self.sibling()]
        peers += [self.plane(k) for k in range(1, self.chips)]
        peers += [self.line(k) for k in range(1, self.ranks)]
        for peer in peers:
            pl.semaphore_signal(barrier, inc=1, device_id=peer, device_id_type=pl.DeviceIdType.MESH)
        pl.semaphore_wait(barrier, len(peers))


def send(src, dst, sems, place, peer):
    copy = pltpu.make_async_remote_copy(
        src_ref=src,
        dst_ref=dst,
        send_sem=sems.at[(0,) + place],
        recv_sem=sems.at[(1,) + place],
        device_id=peer,
        device_id_type=pl.DeviceIdType.MESH,
    )
    copy.start()
    return copy


def word_scores(q, k, diagonal):
    scores = dot_tn(k, q) * (D // HEADS) ** -0.5
    if diagonal:
        scores = jnp.where(iota(scores.shape, 0) <= iota(scores.shape, 1), scores, NEG_FILL)
    return scores


def head_rows(ref, seq, part, kind, h):
    head = D // HEADS
    start = pl.multiple_of(kind * (ref.shape[2] // 3) + h * head, head)
    return ref[seq, part, pl.ds(start, head), :]


def word_attention(seq, triple_ref, mixed_ref, lse_ref):
    parts, depth, _ = triple_ref.shape[1:]
    head = D // HEADS

    def one_head(h, carry):
        start = pl.multiple_of(h * head, head)
        for i in range(parts):
            q = head_rows(triple_ref, seq, i, 0, h)
            scores = [
                word_scores(q, head_rows(triple_ref, seq, j, 1, h), i == j) for j in range(i + 1)
            ]
            highest = jnp.max(scores[0], axis=0, keepdims=True)
            for block in scores[1:]:
                highest = jnp.maximum(highest, jnp.max(block, axis=0, keepdims=True))
            powers = [jnp.exp(block - highest) for block in scores]
            total = jnp.sum(powers[0], axis=0, keepdims=True)
            for block in powers[1:]:
                total = total + jnp.sum(block, axis=0, keepdims=True)
            inverse = 1.0 / total
            mixed = None
            for j, block in enumerate(powers):
                v = head_rows(triple_ref, seq, j, 2, h)
                part = dot_nn(v, (block * inverse).astype(jnp.bfloat16))
                mixed = part if mixed is None else mixed + part
            mixed_ref[seq, i, pl.ds(start, head), :] = mixed.astype(jnp.bfloat16)
            lse_ref[seq, h, i] = jnp.broadcast_to(highest + jnp.log(total), lse_ref.shape[3:])
        return carry

    lax.fori_loop(0, depth // 3 // head, one_head, 0)


def word_attention_back(seq, triple_ref, lse_ref, grad_ref, out_ref, dk, dv):
    parts, depth, _ = triple_ref.shape[1:]
    head = D // HEADS
    own = depth // 3

    def one_head(h, carry):
        start = pl.multiple_of(h * head, head)
        for i in range(parts):
            q = head_rows(triple_ref, seq, i, 0, h)
            grad_o = grad_ref[seq, i, pl.ds(start, head), :]
            lse = lse_ref[seq, h, i][:1]
            probs, grads = [], []
            dot_sum = None
            for j in range(i + 1):
                scores = word_scores(q, head_rows(triple_ref, seq, j, 1, h), i == j)
                probs.append(jnp.exp(scores - lse))
                grads.append(dot_tn(head_rows(triple_ref, seq, j, 2, h), grad_o))
                part = jnp.sum(probs[-1] * grads[-1], axis=0, keepdims=True)
                dot_sum = part if dot_sum is None else dot_sum + part
            grad_q = None
            for j in range(i + 1):
                k = head_rows(triple_ref, seq, j, 1, h)
                raw = (probs[j] * (grads[j] - dot_sum) * head**-0.5).astype(jnp.bfloat16)
                part = dot_nn(k, raw)
                grad_q = part if grad_q is None else grad_q + part
                part_k = dot_nt(q, raw)
                part_v = dot_nt(grad_o, probs[j].astype(jnp.bfloat16))
                if i == j:
                    dk[j] = part_k
                    dv[j] = part_v
                else:
                    dk[j] += part_k
                    dv[j] += part_v
            out_ref[seq, i, pl.ds(start, head), :] = grad_q.astype(jnp.bfloat16)
        for j in range(parts):
            k_start = pl.multiple_of(own + h * head, head)
            v_start = pl.multiple_of(2 * own + h * head, head)
            out_ref[seq, j, pl.ds(k_start, head), :] = dk[j].astype(jnp.bfloat16)
            out_ref[seq, j, pl.ds(v_start, head), :] = dv[j].astype(jnp.bfloat16)
        return carry

    lax.fori_loop(0, own // head, one_head, 0)


def swap_start(ring, src, dst, seq, sems):
    copies = [
        send(src.at[seq, ring.rank_at(k)], dst.at[seq, ring.h], sems, (seq, k), ring.line(k))
        for k in range(1, ring.ranks)
    ]
    dst[seq, ring.h] = src[seq, ring.h]
    return copies


def wait_all(copies):
    for copy in copies:
        copy.wait()


def word_fwd_kernel(dp, ranks, *refs):
    (sum_ref, count_ref, words_ref, pool_ref, early_ref, g3_ref, up_rows, down_rows) = refs[:8]
    (start_ref, pooled_ref, triple_in, lse_ref, mixed_in, up_ref, down_ref) = refs[8:15]
    triple_ref, mixed_ref, own_sem, late_sem, pair_sem, triple_sem, mixed_sem = refs[15:]
    ring = Ring(dp, ranks)
    ring.meet()
    wide = early_ref.shape[1]
    late = ((up_rows.at[:, wide:], up_ref), (down_rows, down_ref))
    own, planes, pairs = [], [], []
    for m, (rows, out) in enumerate(late):
        own.append(pltpu.make_async_copy(rows, out.at[ring.d], own_sem.at[m]))
        own[-1].start()
        planes.append(
            [
                send(rows, out.at[ring.d], late_sem, (m, k), ring.plane(k))
                for k in range(1, ring.chips)
            ]
        )
        pairs.append(send(rows, out.at[ring.d], pair_sem, (m, 0), ring.sibling()))
    seqs = words_ref.shape[0]
    part = D // ranks
    moving = []
    for s in range(seqs):
        pooled = (sum_ref[s] / count_ref[s]).T.astype(jnp.bfloat16)
        pooled_ref[s] = pooled
        start = words_ref[s].astype(jnp.float32).T + dot_tn(pool_ref[...], pooled)
        start_ref[s] = start
        act = (column_rms(start)[0] * g3_ref[...]).astype(jnp.bfloat16)
        for t in range(3):
            triple = dot_tn(early_ref[:, t * D : (t + 1) * D], act).astype(jnp.bfloat16)
            for r in range(ranks):
                triple_ref[s, r, t * part : (t + 1) * part, :] = triple[r * part : (r + 1) * part]
        moving.append(swap_start(ring, triple_ref, triple_in, s, triple_sem))
    for m, (_, out) in enumerate(late):
        for k in range(1, ring.chips):
            planes[m][k - 1].wait_recv()
            block = out.at[2 * ring.chip_at(ring.chips - k) + ring.core]
            pairs.append(send(block, block, pair_sem, (m, k), ring.sibling()))
    back = []
    for s in range(seqs):
        wait_all(moving[s])
        word_attention(s, triple_in, mixed_ref, lse_ref)
        back.append(swap_start(ring, mixed_ref, mixed_in, s, mixed_sem))
    for m in range(2):
        own[m].wait()
        for copy in planes[m]:
            copy.wait_send()
    wait_all(pairs)
    for copies in back:
        wait_all(copies)


def word_fwd(sums, counts, words, pool, early, g3, up_rows, down_rows, collective):
    dp, ranks = lax.axis_size("dp"), lax.axis_size("head")
    seqs, width, _ = words.shape
    part = D // ranks
    bf16, f32 = jnp.bfloat16, jnp.float32
    vmem = pl.BlockSpec(memory_space=pltpu.VMEM)
    anywhere = pl.BlockSpec(memory_space=pl.ANY)
    triple = (seqs, ranks, 3 * part, width)
    mixed = (seqs, ranks, part, width)
    late = up_rows.shape[1] - early.shape[1]
    dma = pltpu.SemaphoreType.DMA
    return pl.pallas_call(
        functools.partial(word_fwd_kernel, dp, ranks),
        in_specs=[vmem] * 6 + [anywhere] * 2,
        out_specs=[vmem] * 5 + [anywhere] * 2,
        out_shape=[
            jax.ShapeDtypeStruct((seqs, D, width), f32),
            jax.ShapeDtypeStruct((seqs, CD, width), bf16),
            jax.ShapeDtypeStruct(triple, bf16),
            jax.ShapeDtypeStruct((seqs, HEADS // ranks, ranks, 8, width), f32),
            jax.ShapeDtypeStruct(mixed, bf16),
            jax.ShapeDtypeStruct((dp, up_rows.shape[0], late), bf16),
            jax.ShapeDtypeStruct((dp,) + down_rows.shape, bf16),
        ],
        scratch_shapes=[
            pltpu.VMEM(triple, bf16),
            pltpu.VMEM(mixed, bf16),
            dma((2,)),
            dma((2, 2, dp // 2)),
            dma((2, 2, dp // 2)),
            dma((2, seqs, ranks)),
            dma((2, seqs, ranks)),
        ],
        compiler_params=pltpu.CompilerParams(
            collective_id=collective, has_side_effects=True, vmem_limit_bytes=VMEM_BYTES
        ),
        name="word_fwd",
    )(sums, counts, words, pool, early, g3, up_rows, down_rows)


def word_bwd_kernel(dp, ranks, *refs):
    (start_ref, pooled_ref, triple_in, lse_ref, mixed_in, cot_ref, count_ref) = refs[:7]
    (pool_ref, early_ref, up_ref, down_ref, g3_ref, g4_ref) = refs[7:13]
    (output_ref, input_grad_ref, spread_ref, d_qkv, d_pool, d_g3, d_g4) = refs[13:20]
    sums = refs[20:23]
    (acts, hiddens, grad_ups, cots, lows, mixes, triples) = refs[23:30]
    (afters, mixed_ref, mixed_back, triple_ref, triple_back, dk, dv) = refs[30:37]
    grads, pair_in, plane_in = refs[37:40], refs[40:43], refs[43:46]
    mixed_sem, triple_sem, pair_sem, plane_sem = refs[46:]
    ring = Ring(dp, ranks)
    chips = ring.chips
    f32, bf16 = jnp.float32, jnp.bfloat16
    ring.meet()
    seqs, _, width = start_ref.shape
    hidden_size = up_ref.shape[1]
    part = D // ranks
    pairs, planes = {}, {}

    def put_grad(i, value):
        grads[i][...] = value.astype(bf16).reshape(grads[i].shape)
        pairs[i] = send(
            grads[i].at[:, 1 - ring.core], pair_in[i], pair_sem, (i,), ring.sibling()
        )

    def pass_on(i):
        pairs[i].wait()

        def add_pair(p, carry):
            both = grads[i][p, ring.core].astype(f32) + pair_in[i][p].astype(f32)
            pair_in[i][p] = both.astype(bf16)
            return carry

        lax.fori_loop(0, chips, add_pair, 0)
        planes[i] = [
            send(
                pair_in[i].at[ring.chip_at(k)], plane_in[i].at[k], plane_sem, (i, k), ring.plane(k)
            )
            for k in range(1, chips)
        ]

    moving = []
    gain = None
    for s in range(seqs):
        lanes = slice(s * width, (s + 1) * width)
        mixed = mixed_in[s].reshape(D, width)
        mixes[:, lanes] = mixed
        after = start_ref[s] + dot_tn(early_ref[:, 3 * D :], mixed)
        normed, inverse = column_rms(after)
        act = (normed * g4_ref[...]).astype(bf16)
        acts[:, lanes] = act
        cot = cot_ref[s].astype(f32).T
        cot_low = cot.astype(bf16)
        cots[:, lanes] = cot_low
        result, grad = after, None
        for c in range(hidden_size // D):
            rows = slice(c * D, (c + 1) * D)
            hidden, slope = gelu_pair(dot_tn(up_ref[:, rows], act))
            hidden = hidden.astype(bf16)
            hiddens[rows, lanes] = hidden
            result = result + dot_tn(down_ref[rows, :], hidden)
            grad_upper = (dot_nn(down_ref[rows, :], cot_low) * slope).astype(bf16)
            grad_ups[rows, lanes] = grad_upper
            piece = dot_nn(up_ref[:, rows], grad_upper)
            grad = piece if grad is None else grad + piece
        output_ref[s] = result.T.astype(bf16)
        piece = fold_lanes(grad * normed)
        gain = piece if gain is None else gain + piece
        total = cot + column_rms_back(grad, g4_ref[...], normed, inverse)
        afters[s] = total
        low = total.astype(bf16)
        lows[:, lanes] = low
        mixed_ref[s] = dot_nn(early_ref[:, 3 * D :], low).astype(bf16).reshape(ranks, part, width)
        moving.append(swap_start(ring, mixed_ref, mixed_back, s, mixed_sem))
    d_g4[...] = gain
    put_grad(0, dot_nt(hiddens[...], cots[...]))
    moved = []
    for s in range(seqs):
        wait_all(moving[s])
        word_attention_back(s, triple_in, lse_ref, mixed_back, triple_ref, dk, dv)
        moved.append(swap_start(ring, triple_ref, triple_back, s, triple_sem))
        if s == 0:
            pass_on(0)
    put_grad(1, dot_nt(acts[...], grad_ups[...]))
    put_grad(2, dot_nt(mixes[...], lows[...]))
    pass_on(1)
    pass_on(2)
    gain = None
    for s in range(seqs):
        lanes = slice(s * width, (s + 1) * width)
        wait_all(moved[s])
        for t in range(3):
            for r in range(ranks):
                triples[t * D + r * part : t * D + (r + 1) * part, lanes] = triple_back[
                    s, r, t * part : (t + 1) * part, :
                ]
        normed, inverse = column_rms(start_ref[s])
        acts[:, lanes] = (normed * g3_ref[...]).astype(bf16)
        grad = dot_nn(early_ref[:, : 3 * D], triples[:, lanes])
        piece = fold_lanes(grad * normed)
        gain = piece if gain is None else gain + piece
        total = afters[s] + column_rms_back(grad, g3_ref[...], normed, inverse)
        input_grad_ref[s] = total.T
        low = total.astype(bf16)
        lows[:, lanes] = low
        high, rest = split_two(dot_nn(pool_ref[...], low) / count_ref[s])
        spread_ref[s, :CD, :] = high
        spread_ref[s, CD:, :] = rest
    d_g3[...] = gain
    d_qkv[...] = dot_nt(acts[...], triples[...]).astype(bf16)
    d_pool[...] = sum(
        dot_nt(pooled_ref[s], lows[:, s * width : (s + 1) * width]) for s in range(seqs)
    ).astype(bf16)
    for i in range(3):
        total = pair_in[i][ring.chip].astype(f32)
        for k in range(1, chips):
            planes[i][k - 1].wait()
            total = total + plane_in[i][k].astype(f32)
        sums[i][...] = total.astype(bf16)


def word_bwd(saved, cot, counts, weights, gains, collective):
    dp, ranks = lax.axis_size("dp"), lax.axis_size("head")
    start, pooled, triple, lse, mixed = saved
    pool, early, up, down = weights
    seqs, _, width = start.shape
    hidden = up.shape[1]
    chips = dp // 2
    bf16, f32 = jnp.bfloat16, jnp.float32
    vmem = pl.BlockSpec(memory_space=pltpu.VMEM)
    rows = ((hidden // dp, D), (D // dp, hidden), (D // dp, D))
    columns = seqs * width
    dma = pltpu.SemaphoreType.DMA
    operands = (*saved, cot, counts, pool, early, up, down, *gains)
    shapes = [
        ((seqs, width, D), bf16),
        ((seqs, width, D), f32),
        ((seqs, 2 * CD, width), bf16),
        ((D, 3 * D), bf16),
        ((CD, D), bf16),
        ((D, GROUP), f32),
        ((D, GROUP), f32),
    ] + [(r, bf16) for r in rows]
    return pl.pallas_call(
        functools.partial(word_bwd_kernel, dp, ranks),
        in_specs=[vmem] * len(operands),
        out_specs=[vmem] * len(shapes),
        out_shape=[jax.ShapeDtypeStruct(shape, kind) for shape, kind in shapes],
        scratch_shapes=[
            pltpu.VMEM((D, columns), bf16),
            pltpu.VMEM((hidden, columns), bf16),
            pltpu.VMEM((hidden, columns), bf16),
            pltpu.VMEM((D, columns), bf16),
            pltpu.VMEM((D, columns), bf16),
            pltpu.VMEM((D, columns), bf16),
            pltpu.VMEM((3 * D, columns), bf16),
            pltpu.VMEM((seqs, D, width), f32),
            pltpu.VMEM(mixed.shape, bf16),
            pltpu.VMEM(mixed.shape, bf16),
            pltpu.VMEM(triple.shape, bf16),
            pltpu.VMEM(triple.shape, bf16),
            pltpu.VMEM((ranks, D // HEADS, width), f32),
            pltpu.VMEM((ranks, D // HEADS, width), f32),
        ]
        + [pltpu.VMEM((chips, 2) + r, bf16) for r in rows]
        + [pltpu.VMEM((chips,) + r, bf16) for r in rows] * 2
        + [
            dma((2, seqs, ranks)),
            dma((2, seqs, ranks)),
            dma((2, 3)),
            dma((2, 3, chips)),
        ],
        compiler_params=pltpu.CompilerParams(
            collective_id=collective, has_side_effects=True, vmem_limit_bytes=VMEM_BYTES
        ),
        name="word_bwd",
    )(*operands)


def gather_kernel(dp, ranks, *refs):
    shards, outs, low = refs[:5], refs[5:11], refs[11:16]
    own_sem, line_sem, plane_sem, pair_sem, copy_sem = refs[16:]
    table, char_in, down, early, word_rows, down_rows = outs
    ring = Ring(dp, ranks)
    for shard, ref in zip(shards, low):
        ref[...] = shard[...].astype(jnp.bfloat16)
    ring.meet()

    def column(ref, like):
        wide = like.shape[1]
        return ref.at[:, pl.ds(pl.multiple_of(ring.h * wide, GROUP), wide)]

    places = (
        table.at[ring.d, ring.h],
        column(char_in.at[ring.d], low[1]),
        down.at[ring.d, ring.h],
        column(word_rows, low[3]),
        column(down_rows, low[4]),
    )
    own, first = [], []

    def along_line(m):
        own.append(pltpu.make_async_copy(low[m], places[m], own_sem.at[m]))
        own[m].start()
        first.append(
            [send(low[m], places[m], line_sem, (m, k), ring.line(k)) for k in range(1, ranks)]
        )

    def arrived(m):
        own[m].wait()
        for copy in first[m]:
            copy.wait_recv()

    blocks = (table, char_in, down, early)
    second, sent = [], []

    def onward(m, block):
        place = blocks[m].at[ring.d]
        second.append(
            [send(block, place, plane_sem, (m, k), ring.plane(k)) for k in range(1, ring.chips)]
        )
        sent.append(send(block, place, pair_sem, (m, 0), ring.sibling()))

    for m in range(3):
        along_line(m)
    for m in range(3):
        arrived(m)
        onward(m, blocks[m].at[ring.d])
    along_line(3)
    along_line(4)
    arrived(3)
    block = word_rows.at[:, : early.shape[2]]
    copy = pltpu.make_async_copy(block, early.at[ring.d], copy_sem)
    copy.start()
    onward(3, block)
    for m in range(4):
        for k in range(1, ring.chips):
            second[m][k - 1].wait_recv()
            block = blocks[m].at[2 * ring.chip_at(ring.chips - k) + ring.core]
            sent.append(send(block, block, pair_sem, (m, k), ring.sibling()))
    arrived(4)
    copy.wait()
    wait_all(sent)
    for m in range(5):
        for copy in first[m]:
            copy.wait_send()
    for m in range(4):
        for copy in second[m]:
            copy.wait_send()


def gather(shards, collective):
    dp, ranks = lax.axis_size("dp"), lax.axis_size("head")
    bf16 = jnp.bfloat16
    vmem = pl.BlockSpec(memory_space=pltpu.VMEM)
    anywhere = pl.BlockSpec(memory_space=pl.ANY)
    table, char_in, down, word_in, word_down = (s.shape for s in shards)
    dma = pltpu.SemaphoreType.DMA
    outs = [
        (dp, ranks) + table,
        (dp, char_in[0], ranks * char_in[1]),
        (dp, ranks) + down,
        (dp, word_in[0], 4 * D),
        (word_in[0], ranks * word_in[1]),
        (word_down[0], ranks * word_down[1]),
    ]
    return pl.pallas_call(
        functools.partial(gather_kernel, dp, ranks),
        in_specs=[vmem] * 5,
        out_specs=[anywhere] * 6,
        out_shape=[jax.ShapeDtypeStruct(s, bf16) for s in outs],
        scratch_shapes=[pltpu.VMEM(s.shape, bf16) for s in shards]
        + [
            dma((5,)),
            dma((2, 5, ranks)),
            dma((2, 4, dp // 2)),
            dma((2, 4, dp // 2)),
            dma(()),
        ],
        compiler_params=pltpu.CompilerParams(
            collective_id=collective, has_side_effects=True, vmem_limit_bytes=VMEM_BYTES
        ),
        name="gather",
    )(*shards)


def column_cuts(widths, ranks):
    block = sum(widths) // ranks
    cuts, start = [], 0
    for width in widths:
        mine, at = [], 0
        while at < width:
            rank, inside = divmod(start + at, block)
            take = min(width - at, block - inside)
            mine.append((rank, at, at + take, inside))
            at += take
        cuts.append(mine)
        start += width
    return cuts


def reduce_kernel(dp, ranks, groups, extra, *refs):
    pieces = sum(len(g) - done for g, done in groups)
    mats = len(groups)
    parts = refs[:pieces]
    gain_ref = refs[pieces]
    ready = refs[pieces + 1 : pieces + 1 + extra]
    place = pieces + 1 + extra
    outs = refs[place : place + mats]
    gain_out, square_out = refs[place + mats : place + mats + 2]
    place += mats + 2
    pair_in = refs[place : place + pieces]
    pair_sum = refs[place + pieces : place + 2 * pieces]
    plane_in = refs[place + 2 * pieces : place + 3 * pieces]
    place += 3 * pieces
    line_sum, line_in = refs[place : place + mats], refs[place + mats : place + 2 * mats]
    place += 2 * mats
    small, pair_sem, plane_sem, line_sem, small_sem = refs[place:]
    ring = Ring(dp, ranks)
    chips = ring.chips
    f32, bf16 = jnp.float32, jnp.bfloat16
    ring.meet()
    sent = []

    def share(slot, value, stage):
        others, here, count = (
            (lambda k: ring.sibling(), ring.core, 2),
            (ring.plane, ring.chip, chips),
            (ring.line, ring.h, ranks),
        )[stage]
        small[slot, stage, here] = value
        copies = []
        for k in range(1, count):
            spot = small.at[slot, stage, here]
            copies.append(send(spot, spot, small_sem, (slot, stage, k), others(k)))
        return copies

    def shared(slot, copies, stage):
        for copy in copies:
            copy.wait()
        count = (2, chips, ranks)[stage]
        total = small[slot, stage, 0]
        for k in range(1, count):
            total = total + small[slot, stage, k]
        return total

    def total_of(slot, value):
        for stage in range(3):
            value = shared(slot, share(slot, value, stage), stage)
        return value

    pairs = [
        send(parts[i].at[:, 1 - ring.core], pair_in[i], pair_sem, (i,), ring.sibling())
        for i in range(pieces)
    ]
    gain = shared(0, share(0, gain_ref[...], 0), 0)
    planes = []
    for i in range(pieces):
        pairs[i].wait()

        def add_pair(p, carry, i=i):
            both = parts[i][p, ring.core].astype(f32) + pair_in[i][p].astype(f32)
            pair_sum[i][p] = both.astype(bf16)
            return carry

        lax.fori_loop(0, chips, add_pair, 0)
        planes.append(
            [
                send(
                    pair_sum[i].at[ring.chip_at(k)],
                    plane_in[i].at[k],
                    plane_sem,
                    (i, k),
                    ring.plane(k),
                )
                for k in range(1, chips)
            ]
        )
    gain = shared(0, share(0, gain, 1), 1)
    gain_out[...] = shared(0, share(0, gain, 2), 2)
    lines, i, j = [], 0, 0
    for m, (widths, done) in enumerate(groups):
        for at, cuts in enumerate(column_cuts(widths, ranks)):
            if at < len(widths) - done:
                total = pair_sum[i][ring.chip].astype(f32)
                for k in range(1, chips):
                    planes[i][k - 1].wait()
                    total = total + plane_in[i][k].astype(f32)
                total = total.astype(bf16)
                i += 1
            else:
                total = ready[j][...]
                j += 1
            for rank, first, last, inside in cuts:
                line_sum[m][rank, :, inside : inside + last - first] = total[:, first:last]
        lines.append(
            [
                send(
                    line_sum[m].at[ring.rank_at(k)], line_in[m].at[k], line_sem, (m, k), ring.line(k)
                )
                for k in range(1, ranks)
            ]
        )
    square = jnp.zeros(square_out.shape, f32)

    def squares(value):
        value = value * value
        rows, cols = value.shape
        if cols % GROUP:
            value = jnp.concatenate([value, jnp.zeros((rows, GROUP - cols % GROUP), f32)], axis=1)
        return jnp.sum(fold_lanes(value).reshape(rows // 8, 8, GROUP), axis=0)

    for m in range(mats):
        total = line_sum[m][ring.h].astype(f32)
        for k in range(1, ranks):
            lines[m][k - 1].wait()
            total = total + line_in[m][k].astype(f32)
        outs[m][...] = total
        square = square + squares(total)
    small_square = jnp.concatenate([square, jnp.zeros_like(square)], axis=0)
    square_out[...] = total_of(1, small_square)[:8]


def reduce_grads(groups, gains, collective):
    dp, ranks = lax.axis_size("dp"), lax.axis_size("head")
    chips = dp // 2
    bf16, f32 = jnp.bfloat16, jnp.float32
    pieces, ready, widths, shards = [], [], [], []
    for group, done in groups:
        rows = done[0].shape[0] if done else group[0].shape[0] // dp
        pieces += [p.reshape(chips, 2, rows, p.shape[1]) for p in group]
        ready += done
        widths.append((tuple(p.shape[1] for p in group + done), len(done)))
        shards.append((rows, sum(widths[-1][0]) // ranks))
    blocks = [p.shape[2:] for p in pieces]
    vmem = pl.BlockSpec(memory_space=pltpu.VMEM)
    n, mats = len(pieces), len(groups)
    return pl.pallas_call(
        functools.partial(reduce_kernel, dp, ranks, widths, len(ready)),
        in_specs=[vmem] * (n + 1 + len(ready)),
        out_specs=[vmem] * (mats + 2),
        out_shape=[jax.ShapeDtypeStruct(s, f32) for s in shards]
        + [jax.ShapeDtypeStruct(gains.shape, f32), jax.ShapeDtypeStruct((8, GROUP), f32)],
        scratch_shapes=[pltpu.VMEM((chips,) + b, bf16) for b in blocks] * 3
        + [pltpu.VMEM((ranks,) + s, bf16) for s in shards] * 2
        + [
            pltpu.VMEM((2, 3, max(2, chips, ranks)) + gains.shape, f32),
            pltpu.SemaphoreType.DMA((2, n)),
            pltpu.SemaphoreType.DMA((2, n, chips)),
            pltpu.SemaphoreType.DMA((2, mats, ranks)),
            pltpu.SemaphoreType.DMA((2, 2, 3, max(2, chips, ranks))),
        ],
        compiler_params=pltpu.CompilerParams(
            collective_id=collective, has_side_effects=True, vmem_limit_bytes=VMEM_BYTES
        ),
        name="reduce_grads",
    )(*pieces, gains, *ready)


def update_kernel(count, *refs):
    weights, grads = refs[:count], refs[count : 2 * count]
    firsts, seconds = refs[2 * count : 3 * count], refs[3 * count : 4 * count]
    square_ref = refs[4 * count]
    norm_ref, outs = refs[4 * count + 1], refs[4 * count + 2 :]
    gain_grad = grads[-1][...]
    square = jnp.sum(square_ref[...]) + jnp.sum(gain_grad * gain_grad)
    norm = jnp.sqrt(jnp.full((1, GROUP), square, jnp.float32))
    norm_ref[...] = norm
    clip_factor = jnp.minimum(1.0, CLIP / norm)[:, :1]
    for i in range(count):
        gains = i == count - 1
        result = adam_step(
            weights[i][...],
            grads[i][...],
            firsts[i][...],
            seconds[i][...],
            clip_factor,
            GAIN_RATE if gains else MATRIX_RATE,
            0.0 if gains else MATRIX_DECAY,
        )
        for ref, value in zip(outs[5 * i : 5 * i + 5], result):
            ref[...] = value


def update(weights, grads, firsts, seconds, square):
    count = len(weights)
    shapes = [jax.ShapeDtypeStruct((1, GROUP), jnp.float32)]
    for w in weights:
        shapes += [jax.ShapeDtypeStruct(w.shape, jnp.float32)] * 4
        shapes.append(jax.ShapeDtypeStruct(w.shape, jnp.bfloat16))
    return pl.pallas_call(
        functools.partial(update_kernel, count),
        out_shape=shapes,
        compiler_params=pltpu.CompilerParams(vmem_limit_bytes=VMEM_BYTES),
        name="update",
    )(*weights, *grads, *firsts, *seconds, square)


def body(
    char_ids,
    char_counts,
    language,
    words_in,
    out_cotangent,
    char_table,
    char_in,
    char_down,
    word_in,
    word_down,
    norm_gains,
    old_table_first,
    old_table_second,
    old_char_in_first,
    old_char_in_second,
    old_char_down_first,
    old_char_down_second,
    old_word_in_first,
    old_word_in_second,
    old_word_down_first,
    old_word_down_second,
    old_gains_first,
    old_gains_second,
):
    bf16, f32 = jnp.bfloat16, jnp.float32
    packed, tiles = pack_rows(char_ids, char_counts)
    table_t_low, char_in_low, char_down_t, early, up_rows, down_rows = gather(
        (char_table.T, char_in, char_down.T, word_in, word_down), 0
    )

    def joined(block):
        dp, ranks, cols, rows = block.shape
        return block.transpose(1, 2, 0, 3).reshape(ranks * cols, dp * rows)

    def stacked(block):
        return block.reshape(-1, block.shape[2])

    table_t_low, char_down_t = joined(table_t_low), joined(char_down_t)
    char_in_low, early = stacked(char_in_low), stacked(early)
    seq_count, local_words = (words_in.shape[0], words_in.shape[1])
    languages = table_t_low.shape[1] // CV

    def lanes(gain, width):
        return jnp.broadcast_to(gain[:, None], (gain.shape[0], width))

    gains = (lanes(norm_gains[:CD], ROWS), lanes(norm_gains[CD : 2 * CD], ROWS))
    g3 = lanes(norm_gains[2 * CD : 2 * CD + D], local_words)
    g4 = lanes(norm_gains[2 * CD + D :], local_words)
    table_t = [
        lax.dynamic_slice_in_dim(table_t_low, language[i] * CV, CV, axis=1)
        for i in range(seq_count)
    ]
    char_parts = (
        char_in_low[:, : 3 * CD],
        char_in_low[:, 3 * CD : 4 * CD],
        char_in_low[:, 4 * CD : 4 * CD + CFF],
        char_down_t.T,
    )
    flipped = tuple(part.T for part in char_parts[:3]) + (char_down_t,)
    pool = char_in_low[:, 4 * CD + CFF :]
    count_row = char_counts.astype(f32)[:, None, :]
    count_col = char_counts.astype(f32)[:, :, None]
    seqs = range(seq_count)
    kept, sums = [], []
    for i in seqs:
        total, *saved = char_fwd(
            tiles[i : i + 1], packed[i], (table_t[i],) + flipped + gains, local_words
        )
        kept.append(saved)
        sums.append(total)
    *saved, up, down = word_fwd(
        jnp.stack(sums), count_col, words_in, pool, early, g3, up_rows, down_rows, 1
    )
    (
        output,
        input_grad,
        spread,
        grad_qkv,
        grad_pool,
        gain_three,
        gain_four,
        down_sum,
        up_sum,
        out_sum,
    ) = word_bwd(
        tuple(saved),
        out_cotangent,
        count_row,
        (pool, early, stacked(up), stacked(down)),
        (g3, g4),
        2,
    )
    last, tables_out = None, []
    for i in seqs:
        one_table, *last = char_bwd(
            tiles[i : i + 1],
            packed[i],
            spread[i],
            (table_t[i],) + char_parts + gains,
            kept[i],
            last,
        )
        tables_out.append(one_table)
    grad_table = sum(
        jnp.where(
            (jnp.arange(languages) == language[i])[:, None, None], tables_out[i][None], 0.0
        )
        for i in seqs
    ).reshape(-1, CD)
    c_qkv, c_out, c_up, c_down, gain_one, gain_two = last
    gain_grads = jnp.concatenate(
        [jnp.sum(g, axis=1) for g in (gain_one, gain_two, gain_three, gain_four)]
    )
    flat = (gain_grads.shape[0] // GROUP, GROUP)
    rest = 16 - flat[0]
    *shards, gains_sum, square = reduce_grads(
        [
            ([grad_table.astype(bf16)], []),
            ([c_qkv.astype(bf16), c_out.astype(bf16), c_up.astype(bf16), grad_pool], []),
            ([c_down.astype(bf16)], []),
            ([grad_qkv], [out_sum, up_sum]),
            ([], [down_sum]),
        ],
        jnp.pad(gain_grads.reshape(flat), ((0, rest), (0, 0))),
        3,
    )

    def turned(parts):
        parts = list(parts)
        parts[0], parts[2] = parts[0].T, parts[2].T
        parts[5] = parts[5].reshape(flat)
        return parts

    norm, *updated = update(
        turned((char_table, char_in, char_down, word_in, word_down, norm_gains)),
        turned((*shards, gains_sum[: flat[0]])),
        turned(
            (
                old_table_first,
                old_char_in_first,
                old_char_down_first,
                old_word_in_first,
                old_word_down_first,
                old_gains_first,
            )
        ),
        turned(
            (
                old_table_second,
                old_char_in_second,
                old_char_down_second,
                old_word_in_second,
                old_word_down_second,
                old_gains_second,
            )
        ),
        square,
    )
    for place in (*range(5), *range(10, 15)):
        updated[place] = updated[place].T
    updated[-5:] = [part.reshape(norm_gains.shape) for part in updated[-5:]]
    return (output, input_grad, norm[0, 0], *updated)


def solution(mesh):
    return jax.shard_map(
        body,
        mesh=mesh,
        in_specs=(
            P("dp", "head", None),
            P("dp", "head"),
            P("dp"),
            P("dp", "head", None),
            P("dp", "head", None),
            P("dp", "head"),
            P("dp", "head"),
            P("dp", "head"),
            P("dp", "head"),
            P("dp", "head"),
            P(),
            P("dp", "head"),
            P("dp", "head"),
            P("dp", "head"),
            P("dp", "head"),
            P("dp", "head"),
            P("dp", "head"),
            P("dp", "head"),
            P("dp", "head"),
            P("dp", "head"),
            P("dp", "head"),
            P(),
            P(),
        ),
        out_specs=(
            P("dp", "head", None),
            P("dp", "head", None),
            P(),
            P("dp", "head"),
            P("dp", "head"),
            P("dp", "head"),
            P("dp", "head"),
            P("dp", "head"),
            P("dp", "head"),
            P("dp", "head"),
            P("dp", "head"),
            P("dp", "head"),
            P("dp", "head"),
            P("dp", "head"),
            P("dp", "head"),
            P("dp", "head"),
            P("dp", "head"),
            P("dp", "head"),
            P("dp", "head"),
            P("dp", "head"),
            P("dp", "head"),
            P("dp", "head"),
            P("dp", "head"),
            P("dp", "head"),
            P("dp", "head"),
            P("dp", "head"),
            P("dp", "head"),
            P("dp", "head"),
            P(),
            P(),
            P(),
            P(),
            P(),
        ),
        check_vma=False,
    )
```

```python
import functools

import jax
import jax.numpy as jnp
from jax import lax
from jax.experimental import pallas as pl
from jax.experimental.pallas import tpu as pltpu
from jax.sharding import PartitionSpec as P

D = 512
HEADS = 8
CD = 256
CHEADS = 4
CFF = 1024
CV = 256
STEP = 5


EPS = 1e-05
CLIP = 1.0
MATRIX_RATE = 0.03
GAIN_RATE = 0.25
MATRIX_DECAY = 0.1
BETA_ONE = 0.5
BETA_TWO = 0.5
ADAM_EPS = 1e-08
NEG_FILL = -1e30
SQRT_HALF = 0.7071067811865476
INV_ROOT_TWO_PI = 0.3989422804014327


ROWS = 512
SLOTS = 16
CHAINS = 1
GROUP = 128
VMEM_BYTES = 56 * 1024 * 1024


def dot_nn(left_side, right_side):
    return lax.dot_general(
        left_side, right_side, (((1,), (0,)), ((), ())), preferred_element_type=jnp.float32
    )


def dot_tn(left_side, right_side):
    return lax.dot_general(
        left_side, right_side, (((0,), (0,)), ((), ())), preferred_element_type=jnp.float32
    )


def dot_nt(left_side, right_side):
    return lax.dot_general(
        left_side, right_side, (((1,), (1,)), ((), ())), preferred_element_type=jnp.float32
    )


def gelu_pair(upper):
    phi = 0.5 + 0.5 * lax.erf(upper * SQRT_HALF)
    bell = jnp.exp(upper * upper * -0.5)
    return upper * phi, phi + upper * (bell * INV_ROOT_TWO_PI)


def iota(shape, dim):
    return lax.broadcasted_iota(jnp.int32, shape, dim)


def split_two(values):
    high = values.astype(jnp.bfloat16)
    return high, (values - high.astype(jnp.float32)).astype(jnp.bfloat16)


def pack_words(row, ids, out_ref, tiles_ref, seq):
    n = row.shape[1]
    col = jnp.broadcast_to(row.astype(jnp.float32), (8, n)).T[:, :1].astype(jnp.int32)
    sub, lane = iota((n, n), 0), iota((n, n), 1)
    ahead = (row > col) | ((row == col) & (lane < sub))
    rank_col = jnp.sum(ahead.astype(jnp.float32), axis=1, keepdims=True).astype(jnp.int32)
    ahead = (col > row) | ((col == row) & (sub < lane))
    rank_row = jnp.sum(ahead.astype(jnp.float32), axis=0, keepdims=True).astype(jnp.int32)
    clash = (rank_col < rank_row) & (col + row > SLOTS)
    alone = jnp.max(jnp.where(clash, rank_col + rank_row, 0).astype(jnp.float32))
    alone = jnp.maximum(alone.astype(jnp.int32) - n + 2, 0)
    partner = n - 1 + alone - rank_row
    second = (rank_row >= alone) & (rank_row > partner)
    bins = jnp.where(second, partner, rank_row)
    here = sub == bins
    first_map = (here & jnp.logical_not(second)).astype(jnp.float32).astype(jnp.bfloat16)
    second_map = (here & second).astype(jnp.float32).astype(jnp.bfloat16)
    pos = lax.rem(iota((GROUP, n), 0), SLOTS)
    word = iota((GROUP, n), 1) + 1
    wide = jnp.broadcast_to(row, (GROUP, n))
    in_first, in_second = pos < wide, pos >= SLOTS - wide

    def kept(mask, values):
        return jnp.where(mask, values, 0).astype(jnp.float32).astype(jnp.bfloat16)

    groups = n * SLOTS // GROUP
    spare = out_ref.shape[2] - groups
    per = GROUP // SLOTS
    own = iota((groups, per, GROUP), 1) == lax.div(iota((groups, per, GROUP), 2), SLOTS)
    back = jnp.concatenate([ids[SLOTS - 1 - j : SLOTS - j] for j in range(SLOTS)] * per, axis=0)
    ids = jnp.concatenate([ids] * per, axis=0)
    zero = jnp.zeros_like(wide)
    for k, (one, two) in enumerate(
        ((ids + 1, back + 1), (word, word), (zero, SLOTS - wide), (wide, zero + SLOTS))
    ):
        full = dot_nt(first_map, kept(in_first, one)) + dot_nt(second_map, kept(in_second, two))
        full = jnp.where(own, full.reshape(groups, per, GROUP), 0.0)
        full = jnp.sum(full, axis=1).astype(jnp.int32)
        if spare:
            full = jnp.concatenate([full, jnp.zeros((spare, GROUP), jnp.int32)], axis=0)
        out_ref[seq, k] = full
    used = alone + lax.div(n - alone + 1, 2)
    tiles_ref[seq] = lax.div(used * SLOTS + ROWS - 1, ROWS)


def lane_map(rows, size):
    spots = iota((size, GROUP), 0) + 1
    maps = [
        (spots == rows[g : g + 1]).astype(jnp.float32).astype(jnp.bfloat16)
        for g in range(rows.shape[0])
    ]
    return jnp.concatenate(maps, axis=1)


def in_step(chains):
    results = [None] * len(chains)
    waiting = list(enumerate(chains))
    running = []
    while waiting or running:
        if waiting:
            running.append(waiting.pop(0))
        for item in list(running):
            try:
                next(item[1])
            except StopIteration as stop:
                results[item[0]] = stop.value
                running.remove(item)
    return results


def lane_copies(ref, width):
    return jnp.concatenate([ref[...]] * (width // GROUP), axis=1)


def column_rms(values):
    inverse = lax.rsqrt(jnp.mean(values * values, axis=0, keepdims=True) + EPS)
    return values * inverse, inverse


def tile_count(words):
    return -(-words * SLOTS // ROWS)


def tile_at(step, tiles_ref, seqs):
    seq, start, total = 0, 0, tiles_ref[0]
    for s in range(1, seqs):
        past = step >= total
        seq, start = jnp.where(past, s, seq), jnp.where(past, total, start)
        total = total + tiles_ref[s]
    return seq, step - start, total


def placed(seqs, index):
    def place(step, tiles_ref, language_ref):
        total = tile_at(step, tiles_ref, seqs)[2]
        seq, tile, _ = tile_at(jnp.minimum(step, total - 1), tiles_ref, seqs)
        return index(seq, tile, language_ref)

    return place


def own_block():
    shape = (GROUP // SLOTS, SLOTS, CHEADS * GROUP)
    return iota(shape, 0) == lax.div(lax.rem(iota(shape, 2), GROUP), SLOTS)


def to_compact(block, own):
    return jnp.sum(jnp.where(own, block.reshape(own.shape), 0.0), axis=0)


def from_compact(compact, own):
    wide = jnp.broadcast_to(compact[None], own.shape)
    return jnp.where(own, wide, 0.0).astype(jnp.bfloat16).reshape(GROUP, -1)


def spread_heads(values):
    head = values.shape[0] // CHEADS
    zero = jnp.zeros((head, GROUP), values.dtype)
    rows = []
    for h in range(CHEADS):
        parts = [zero] * CHEADS
        parts[h] = values[h * head : (h + 1) * head]
        rows.append(jnp.concatenate(parts, axis=1))
    return jnp.concatenate(rows, axis=0)


def char_fwd_kernel(seqs, tiles_ref, language_ref, *refs):
    step = pl.program_id(0)
    _, tile, total = tile_at(step, tiles_ref, seqs)

    @pl.when(step < total)
    def _():
        char_fwd_tile(tile, *refs)


def char_fwd_tile(
    step, pack_ref, table_ref, in_ref, down_ref, g1_ref, g2_ref, pooled_ref,
    keep_values, keep_probs, keep_qkv, keep_mixed, keep_first, keep_hidden, keep_slope,
):
    words = pooled_ref.shape[1]
    per = ROWS // GROUP
    head = CD // CHEADS

    @pl.when(step == 0)
    def _():
        pooled_ref[...] = jnp.zeros_like(pooled_ref)

    own = own_block()
    key_pos = iota((SLOTS, GROUP), 0)
    packs = [pack_ref[0, k, pl.ds(step * per, per), :] for k in range(4)]

    def chain(part):
        groups = per // CHAINS
        cols = slice(part * groups * GROUP, (part + 1) * groups * GROUP)
        size = groups * GROUP
        ids, spots, low_rows, high_rows = (p[part * groups : (part + 1) * groups] for p in packs)
        embedded = dot_nn(table_ref[...], lane_map(ids, CV))
        yield
        act_one = (column_rms(embedded)[0] * lane_copies(g1_ref, size)).astype(jnp.bfloat16)
        triple = dot_tn(in_ref[:, : 3 * CD], act_one).astype(jnp.bfloat16)
        keep_qkv[:, cols] = triple
        yield
        key_rows = triple[CD : 2 * CD].T
        keep_values[cols, :] = triple[2 * CD :].T
        all_probs = []
        for g in range(groups):
            valid = (key_pos >= low_rows[g : g + 1]) & (key_pos < high_rows[g : g + 1])
            valid = jnp.concatenate([valid.astype(jnp.float32)] * CHEADS, axis=1) > 0
            lanes = slice(g * GROUP, (g + 1) * GROUP)
            scores = to_compact(dot_nn(key_rows[lanes], spread_heads(triple[:CD, lanes])), own)
            scores = jnp.where(valid, scores * head**-0.5, NEG_FILL)
            powers = jnp.exp(scores - jnp.max(scores, axis=0, keepdims=True))
            powers = jnp.where(valid, powers, 0.0)
            total = jnp.sum(powers, axis=0, keepdims=True)
            probs = powers / jnp.where(total > 0, total, 1.0)
            wide = (part * groups + g) * CHEADS * GROUP
            keep_probs[:, wide : wide + CHEADS * GROUP] = probs
            all_probs.append(from_compact(probs, own))
        yield
        mixed = []
        for g in range(groups):
            lanes = slice(g * GROUP, (g + 1) * GROUP)
            heads = []
            for h in range(CHEADS):
                v = triple[2 * CD + h * head : 2 * CD + (h + 1) * head, lanes]
                probs = all_probs[g][:, h * GROUP : (h + 1) * GROUP]
                heads.append(dot_nn(v, probs).astype(jnp.bfloat16))
            mixed.append(jnp.concatenate(heads, axis=0))
        mixed = jnp.concatenate(mixed, axis=1)
        keep_mixed[:, cols] = mixed
        yield
        first = embedded + dot_tn(in_ref[:, 3 * CD : 4 * CD], mixed)
        keep_first[:, cols] = first
        act_two = (column_rms(first)[0] * lane_copies(g2_ref, size)).astype(jnp.bfloat16)
        second = first
        for c in range(CFF // CD):
            yield
            rows = slice(c * CD, (c + 1) * CD)
            up = in_ref[:, 4 * CD + c * CD : 4 * CD + (c + 1) * CD]
            hidden, slope = gelu_pair(dot_tn(up, act_two))
            hidden = hidden.astype(jnp.bfloat16)
            keep_hidden[rows, cols] = hidden
            keep_slope[rows, cols] = slope.astype(jnp.bfloat16)
            second = second + dot_nn(down_ref[:, rows], hidden)
        yield
        return lane_map(spots, words), split_two(second)

    ends = in_step([chain(part) for part in range(CHAINS)])
    word_map = jnp.concatenate([end[0] for end in ends], axis=1)
    high = jnp.concatenate([end[1][0] for end in ends], axis=1)
    low = jnp.concatenate([end[1][1] for end in ends], axis=1)
    pooled_ref[0] += dot_nt(word_map, high) + dot_nt(word_map, low)


KEPT = (
    (3 * CD, jnp.bfloat16),
    (CD, jnp.bfloat16),
    (CD, jnp.float32),
    (CFF, jnp.bfloat16),
    (CFF, jnp.bfloat16),
)


def kept_specs(seqs, count):
    place = placed(seqs, lambda seq, tile, _: (0, seq * count + tile))
    return [
        pl.BlockSpec((ROWS, CD), lambda *at: place(*at)[::-1]),
        pl.BlockSpec((SLOTS, CHEADS * ROWS), place),
    ] + [pl.BlockSpec((depth, ROWS), place) for depth, _ in KEPT]


def kept_shapes(rows):
    return [
        jax.ShapeDtypeStruct((rows, CD), jnp.bfloat16),
        jax.ShapeDtypeStruct((SLOTS, CHEADS * rows), jnp.float32),
    ] + [jax.ShapeDtypeStruct((depth, rows), dtype) for depth, dtype in KEPT]


def whole(array):
    zeros = (0,) * array.ndim
    return pl.BlockSpec(array.shape, lambda *_: zeros)


def char_specs(seqs, pack, others):
    one = (1,) + pack.shape[1:]
    return [
        pl.BlockSpec(one, placed(seqs, lambda seq, tile, _: (seq, 0, 0, 0))),
        pl.BlockSpec((CD, CV), placed(seqs, lambda seq, tile, language: (0, language[seq]))),
    ] + [whole(a) for a in others]


def char_fwd(tiles, language, pack, table, others, words):
    seqs = pack.shape[0]
    count = tile_count(words)
    one = placed(seqs, lambda seq, tile, _: (seq, 0, 0))
    return pl.pallas_call(
        functools.partial(char_fwd_kernel, seqs),
        grid_spec=pltpu.PrefetchScalarGridSpec(
            num_scalar_prefetch=2,
            grid=(seqs * count,),
            in_specs=char_specs(seqs, pack, others),
            out_specs=[pl.BlockSpec((1, words, CD), one)] + kept_specs(seqs, count),
        ),
        out_shape=[jax.ShapeDtypeStruct((seqs, words, CD), jnp.float32)]
        + kept_shapes(seqs * count * ROWS),
        compiler_params=pltpu.CompilerParams(vmem_limit_bytes=VMEM_BYTES),
        name="char_fwd",
    )(tiles, language, pack, table, *others)


def fold_lanes(values):
    total = values[:, :GROUP]
    for g in range(1, values.shape[1] // GROUP):
        total = total + values[:, g * GROUP : (g + 1) * GROUP]
    return total


def column_rms_back(grad_in, gain, normed, inverse):
    scaled = grad_in * gain
    return inverse * (scaled - normed * jnp.mean(scaled * normed, axis=0, keepdims=True))


def char_bwd_kernel(seqs, tiles_ref, language_ref, *refs):
    step = pl.program_id(0)
    seq, tile, total = tile_at(step, tiles_ref, seqs)

    @pl.when(step < total)
    def _():
        char_bwd_tile(tile, step == 0, step == total - 1, language_ref[seq] * CV, *refs)


def char_bwd_tile(
    step, at_start, at_end, letter, pack_ref, table_ref, in_ref, down_ref, g1_ref, g2_ref, spread_ref,
    keep_values, keep_probs, keep_qkv, keep_mixed, keep_first, keep_hidden, keep_slope,
    *refs,
):
    results, totals = refs[:7], refs[7:]
    d_table, d_qkv, d_out, d_up, d_down, d_g1, d_g2 = totals
    words = spread_ref.shape[2]
    per = ROWS // GROUP
    head = CD // CHEADS

    @pl.when(at_start)
    def _():
        for ref in totals:
            ref[...] = jnp.zeros_like(ref)

    own = own_block()
    packs = [pack_ref[0, k, pl.ds(step * per, per), :] for k in range(2)]

    def chain(part):
        groups = per // CHAINS
        cols = slice(part * groups * GROUP, (part + 1) * groups * GROUP)
        size = groups * GROUP
        ids, spots = (p[part * groups : (part + 1) * groups] for p in packs)
        halves = dot_nn(spread_ref[0], lane_map(spots, words))
        grad_second = halves[:CD] + halves[CD:]
        grad_branch = grad_second.astype(jnp.bfloat16)
        normed_two, inverse_two = column_rms(keep_first[:, cols])
        gain_two = lane_copies(g2_ref, size)
        act_two = (normed_two * gain_two).astype(jnp.bfloat16)
        grad_uppers = []
        grad_act_two = None
        for c in range(CFF // CD):
            yield
            rows = slice(c * CD, (c + 1) * CD)
            slope = keep_slope[rows, cols].astype(jnp.float32)
            grad_upper = dot_tn(down_ref[:, rows], grad_branch) * slope
            grad_upper = grad_upper.astype(jnp.bfloat16)
            grad_uppers.append(grad_upper)
            piece = dot_nn(in_ref[:, 4 * CD + c * CD : 4 * CD + (c + 1) * CD], grad_upper)
            grad_act_two = piece if grad_act_two is None else grad_act_two + piece
        yield
        gain_sum_two = fold_lanes(grad_act_two * normed_two)
        grad_first = grad_second + column_rms_back(
            grad_act_two, gain_two, normed_two, inverse_two
        )
        grad_attn = grad_first.astype(jnp.bfloat16)
        grad_mixed = dot_nn(in_ref[:, 3 * CD : 4 * CD], grad_attn).astype(jnp.bfloat16)
        yield
        triple = keep_qkv[:, cols]
        raws, lows = [], []
        for g in range(groups):
            lanes = slice(g * GROUP, (g + 1) * GROUP)
            at = part * groups + g
            wide = slice(at * CHEADS * GROUP, (at + 1) * CHEADS * GROUP)
            probs = keep_probs[:, wide]
            values = keep_values[at * GROUP : (at + 1) * GROUP, :]
            grad_probs = to_compact(dot_nn(values, spread_heads(grad_mixed[:, lanes])), own)
            grad_scores = probs * (
                grad_probs - jnp.sum(probs * grad_probs, axis=0, keepdims=True)
            )
            raws.append(from_compact(grad_scores * head**-0.5, own))
            lows.append(from_compact(probs, own))
        yield
        columns = []
        for g in range(groups):
            lanes = slice(g * GROUP, (g + 1) * GROUP)
            gq, gk, gv = [], [], []
            for h in range(CHEADS):
                q = triple[h * head : (h + 1) * head, lanes]
                k = triple[CD + h * head : CD + (h + 1) * head, lanes]
                grad_o = grad_mixed[h * head : (h + 1) * head, lanes]
                piece = slice(h * GROUP, (h + 1) * GROUP)
                gq.append(dot_nn(k, raws[g][:, piece]).astype(jnp.bfloat16))
                gk.append(dot_nt(q, raws[g][:, piece]).astype(jnp.bfloat16))
                gv.append(dot_nt(grad_o, lows[g][:, piece]).astype(jnp.bfloat16))
            columns.append(jnp.concatenate(gq + gk + gv, axis=0))
        grad_triple = jnp.concatenate(columns, axis=1)
        yield
        one_hot = lane_map(ids, CV)
        embedded = dot_nn(table_ref[...], one_hot)
        normed_one, inverse_one = column_rms(embedded)
        gain_one = lane_copies(g1_ref, size)
        act_one = (normed_one * gain_one).astype(jnp.bfloat16)
        grad_act_one = dot_nn(in_ref[:, : 3 * CD], grad_triple)
        yield
        gain_sum_one = fold_lanes(grad_act_one * normed_one)
        back_one = column_rms_back(grad_act_one, gain_one, normed_one, inverse_one)
        grad_embedded = (grad_first + back_one).astype(jnp.bfloat16)
        grad_upper = jnp.concatenate(grad_uppers, axis=0)
        return (
            gain_sum_one, gain_sum_two, grad_branch, act_two, grad_upper, grad_attn,
            act_one, grad_triple, one_hot, grad_embedded,
        )

    ends = in_step([chain(part) for part in range(CHAINS)])
    for end in ends:
        d_g1[...] += end[0]
        d_g2[...] += end[1]
    grad_branch, act_two, grad_upper, grad_attn, act_one, grad_triple, one_hot, grad_embedded = (
        jnp.concatenate(parts, axis=1) for parts in list(zip(*ends))[2:]
    )
    d_down[...] += dot_nt(keep_hidden[...], grad_branch)
    d_up[...] += dot_nt(act_two, grad_upper)
    d_out[...] += dot_nt(keep_mixed[...], grad_attn)
    d_qkv[...] += dot_nt(act_one, grad_triple)
    d_table[pl.ds(pl.multiple_of(letter, CV), CV), :] += dot_nt(one_hot, grad_embedded)

    @pl.when(at_end)
    def _():
        for ref, total in zip(results, totals):
            ref[...] = total[...].astype(ref.dtype)


def char_bwd(tiles, language, pack, table, others, spread, kept):
    shapes = (
        table.shape[::-1],
        (CD, 3 * CD),
        (CD, CD),
        (CD, CFF),
        (CFF, CD),
        (CD, GROUP),
        (CD, GROUP),
    )
    f32, bf16 = jnp.float32, jnp.bfloat16
    kinds = [bf16] * 5 + [f32] * 2
    seqs = pack.shape[0]
    count = tile_count(spread.shape[2])
    one = (1,) + spread.shape[1:]
    return pl.pallas_call(
        functools.partial(char_bwd_kernel, seqs),
        grid_spec=pltpu.PrefetchScalarGridSpec(
            num_scalar_prefetch=2,
            grid=(seqs * count,),
            in_specs=char_specs(seqs, pack, others)
            + [pl.BlockSpec(one, placed(seqs, lambda seq, tile, _: (seq, 0, 0)))]
            + kept_specs(seqs, count),
            out_specs=[pl.BlockSpec(s, lambda *_: (0, 0)) for s in shapes],
            scratch_shapes=[pltpu.VMEM(s, f32) for s in shapes],
        ),
        out_shape=[jax.ShapeDtypeStruct(s, kind) for s, kind in zip(shapes, kinds)],
        compiler_params=pltpu.CompilerParams(vmem_limit_bytes=VMEM_BYTES),
        name="char_bwd",
    )(tiles, language, pack, table, *others, spread, *kept)


def adam_step(weight, grad, first_old, second_old, clip_factor, rate, decay):
    clipped = grad * clip_factor
    first_new = BETA_ONE * first_old + (1.0 - BETA_ONE) * clipped
    second_new = BETA_TWO * second_old + (1.0 - BETA_TWO) * clipped * clipped
    first_hat = first_new / (1.0 - BETA_ONE**STEP)
    second_hat = second_new / (1.0 - BETA_TWO**STEP)
    weight_new = weight - rate * (first_hat / (jnp.sqrt(second_hat) + ADAM_EPS) + decay * weight)
    return (grad, first_new, second_new, weight_new, weight_new.astype(jnp.bfloat16))


class Ring:
    def __init__(self, dp, ranks):
        self.chips, self.ranks = dp // 2, ranks
        self.d, self.h = lax.axis_index("dp"), lax.axis_index("head")
        self.chip, self.core = lax.div(self.d, 2), lax.rem(self.d, 2)

    def sibling(self):
        return (self.d + 1 - 2 * self.core, self.h)

    def chip_at(self, k):
        return lax.rem(self.chip + k, self.chips)

    def plane(self, k):
        return (2 * self.chip_at(k) + self.core, self.h)

    def rank_at(self, k):
        return lax.rem(self.h + k, self.ranks)

    def line(self, k):
        return (self.d, self.rank_at(k))

    def meet(self):
        barrier = pltpu.get_barrier_semaphore()
        peers = [self.sibling()]
        peers += [self.plane(k) for k in range(1, self.chips)]
        peers += [self.line(k) for k in range(1, self.ranks)]
        for peer in peers:
            pl.semaphore_signal(barrier, inc=1, device_id=peer, device_id_type=pl.DeviceIdType.MESH)
        pl.semaphore_wait(barrier, len(peers))


def send(src, dst, sems, place, peer):
    copy = pltpu.make_async_remote_copy(
        src_ref=src,
        dst_ref=dst,
        send_sem=sems.at[(0,) + place],
        recv_sem=sems.at[(1,) + place],
        device_id=peer,
        device_id_type=pl.DeviceIdType.MESH,
    )
    copy.start()
    return copy


def word_scores(q, k, diagonal):
    scores = dot_tn(k, q) * (D // HEADS) ** -0.5
    if diagonal:
        scores = jnp.where(iota(scores.shape, 0) <= iota(scores.shape, 1), scores, NEG_FILL)
    return scores


def head_rows(ref, seq, part, kind, h):
    head = D // HEADS
    start = pl.multiple_of(kind * (ref.shape[2] // 3) + h * head, head)
    return ref[seq, part, pl.ds(start, head), :]


def word_attention(seq, triple_ref, mixed_ref, lse_ref):
    parts, depth, _ = triple_ref.shape[1:]
    head = D // HEADS

    def one_head(h, carry):
        start = pl.multiple_of(h * head, head)
        for i in range(parts):
            q = head_rows(triple_ref, seq, i, 0, h)
            scores = [
                word_scores(q, head_rows(triple_ref, seq, j, 1, h), i == j) for j in range(i + 1)
            ]
            highest = jnp.max(scores[0], axis=0, keepdims=True)
            for block in scores[1:]:
                highest = jnp.maximum(highest, jnp.max(block, axis=0, keepdims=True))
            powers = [jnp.exp(block - highest) for block in scores]
            total = jnp.sum(powers[0], axis=0, keepdims=True)
            for block in powers[1:]:
                total = total + jnp.sum(block, axis=0, keepdims=True)
            inverse = 1.0 / total
            mixed = None
            for j, block in enumerate(powers):
                v = head_rows(triple_ref, seq, j, 2, h)
                part = dot_nn(v, (block * inverse).astype(jnp.bfloat16))
                mixed = part if mixed is None else mixed + part
            mixed_ref[seq, i, pl.ds(start, head), :] = mixed.astype(jnp.bfloat16)
            lse_ref[seq, h, i] = jnp.broadcast_to(highest + jnp.log(total), lse_ref.shape[3:])
        return carry

    lax.fori_loop(0, depth // 3 // head, one_head, 0)


def word_attention_back(seq, triple_ref, lse_ref, grad_ref, out_ref, dk, dv):
    parts, depth, _ = triple_ref.shape[1:]
    head = D // HEADS
    own = depth // 3

    def one_head(h, carry):
        start = pl.multiple_of(h * head, head)
        for i in range(parts):
            q = head_rows(triple_ref, seq, i, 0, h)
            grad_o = grad_ref[seq, i, pl.ds(start, head), :]
            lse = lse_ref[seq, h, i][:1]
            probs, grads = [], []
            dot_sum = None
            for j in range(i + 1):
                scores = word_scores(q, head_rows(triple_ref, seq, j, 1, h), i == j)
                probs.append(jnp.exp(scores - lse))
                grads.append(dot_tn(head_rows(triple_ref, seq, j, 2, h), grad_o))
                part = jnp.sum(probs[-1] * grads[-1], axis=0, keepdims=True)
                dot_sum = part if dot_sum is None else dot_sum + part
            grad_q = None
            for j in range(i + 1):
                k = head_rows(triple_ref, seq, j, 1, h)
                raw = (probs[j] * (grads[j] - dot_sum) * head**-0.5).astype(jnp.bfloat16)
                part = dot_nn(k, raw)
                grad_q = part if grad_q is None else grad_q + part
                part_k = dot_nt(q, raw)
                part_v = dot_nt(grad_o, probs[j].astype(jnp.bfloat16))
                if i == j:
                    dk[j] = part_k
                    dv[j] = part_v
                else:
                    dk[j] += part_k
                    dv[j] += part_v
            out_ref[seq, i, pl.ds(start, head), :] = grad_q.astype(jnp.bfloat16)
        for j in range(parts):
            k_start = pl.multiple_of(own + h * head, head)
            v_start = pl.multiple_of(2 * own + h * head, head)
            out_ref[seq, j, pl.ds(k_start, head), :] = dk[j].astype(jnp.bfloat16)
            out_ref[seq, j, pl.ds(v_start, head), :] = dv[j].astype(jnp.bfloat16)
        return carry

    lax.fori_loop(0, own // head, one_head, 0)


def swap_start(ring, src, dst, seq, sems):
    copies = [
        send(src.at[seq, ring.rank_at(k)], dst.at[seq, ring.h], sems, (seq, k), ring.line(k))
        for k in range(1, ring.ranks)
    ]
    dst[seq, ring.h] = src[seq, ring.h]
    return copies


def wait_all(copies):
    for copy in copies:
        copy.wait()


def word_fwd_kernel(dp, ranks, *refs):
    (sum_ref, count_ref, words_ref, in_ref, early_ref, g3_ref, up_rows, down_rows) = refs[:8]
    (start_ref, pooled_ref, triple_in, lse_ref, mixed_in, up_ref, down_ref) = refs[8:15]
    triple_ref, mixed_ref, own_sem, late_sem, pair_sem, triple_sem, mixed_sem = refs[15:]
    ring = Ring(dp, ranks)
    ring.meet()
    wide = early_ref.shape[1]
    late = ((up_rows.at[:, wide:], up_ref), (down_rows, down_ref))
    own, planes, pairs = [], [], []
    for m, (rows, out) in enumerate(late):
        own.append(pltpu.make_async_copy(rows, out.at[ring.d], own_sem.at[m]))
        own[-1].start()
        planes.append(
            [
                send(rows, out.at[ring.d], late_sem, (m, k), ring.plane(k))
                for k in range(1, ring.chips)
            ]
        )
        pairs.append(send(rows, out.at[ring.d], pair_sem, (m, 0), ring.sibling()))
    seqs = words_ref.shape[0]
    part = D // ranks
    moving = []
    for s in range(seqs):
        count = count_ref[s : s + 1, :].astype(jnp.float32)
        pooled = (sum_ref[s].T / count).astype(jnp.bfloat16)
        pooled_ref[s] = pooled
        start = words_ref[s].astype(jnp.float32).T + dot_tn(in_ref[:, 4 * CD + CFF :], pooled)
        start_ref[s] = start
        act = (column_rms(start)[0] * lane_copies(g3_ref, start.shape[1])).astype(jnp.bfloat16)
        for t in range(3):
            triple = dot_tn(early_ref[:, t * D : (t + 1) * D], act).astype(jnp.bfloat16)
            for r in range(ranks):
                triple_ref[s, r, t * part : (t + 1) * part, :] = triple[r * part : (r + 1) * part]
        moving.append(swap_start(ring, triple_ref, triple_in, s, triple_sem))
    for m, (_, out) in enumerate(late):
        for k in range(1, ring.chips):
            planes[m][k - 1].wait_recv()
            block = out.at[2 * ring.chip_at(ring.chips - k) + ring.core]
            pairs.append(send(block, block, pair_sem, (m, k), ring.sibling()))
    back = []
    for s in range(seqs):
        wait_all(moving[s])
        word_attention(s, triple_in, mixed_ref, lse_ref)
        back.append(swap_start(ring, mixed_ref, mixed_in, s, mixed_sem))
    for m in range(2):
        own[m].wait()
        for copy in planes[m]:
            copy.wait_send()
    wait_all(pairs)
    for copies in back:
        wait_all(copies)


def word_fwd(sums, counts, words, char_in, early, g3, up_rows, down_rows, collective):
    dp, ranks = lax.axis_size("dp"), lax.axis_size("head")
    seqs, width, _ = words.shape
    part = D // ranks
    bf16, f32 = jnp.bfloat16, jnp.float32
    vmem = pl.BlockSpec(memory_space=pltpu.VMEM)
    anywhere = pl.BlockSpec(memory_space=pl.ANY)
    triple = (seqs, ranks, 3 * part, width)
    mixed = (seqs, ranks, part, width)
    late = up_rows.shape[1] - early.shape[1]
    dma = pltpu.SemaphoreType.DMA
    return pl.pallas_call(
        functools.partial(word_fwd_kernel, dp, ranks),
        in_specs=[vmem] * 6 + [anywhere] * 2,
        out_specs=[vmem] * 5 + [anywhere] * 2,
        out_shape=[
            jax.ShapeDtypeStruct((seqs, D, width), f32),
            jax.ShapeDtypeStruct((seqs, CD, width), bf16),
            jax.ShapeDtypeStruct(triple, bf16),
            jax.ShapeDtypeStruct((seqs, HEADS // ranks, ranks, 8, width), f32),
            jax.ShapeDtypeStruct(mixed, bf16),
            jax.ShapeDtypeStruct((dp, up_rows.shape[0], late), bf16),
            jax.ShapeDtypeStruct((dp,) + down_rows.shape, bf16),
        ],
        scratch_shapes=[
            pltpu.VMEM(triple, bf16),
            pltpu.VMEM(mixed, bf16),
            dma((2,)),
            dma((2, 2, dp // 2)),
            dma((2, 2, dp // 2)),
            dma((2, seqs, ranks)),
            dma((2, seqs, ranks)),
        ],
        compiler_params=pltpu.CompilerParams(
            collective_id=collective, has_side_effects=True, vmem_limit_bytes=VMEM_BYTES
        ),
        name="word_fwd",
    )(sums, counts, words, char_in, early, g3, up_rows, down_rows)


def word_bwd_kernel(dp, ranks, *refs):
    (start_ref, pooled_ref, triple_in, lse_ref, mixed_in, cot_ref, count_ref) = refs[:7]
    (in_ref, early_ref, up_ref, down_ref, g3_ref, g4_ref) = refs[7:13]
    (output_ref, input_grad_ref, spread_ref, d_qkv, d_pool, d_g3, d_g4) = refs[13:20]
    sums = refs[20:23]
    (acts, hiddens, grad_ups, cots, lows, mixes, triples) = refs[23:30]
    (afters, mixed_ref, mixed_back, triple_ref, triple_back, dk, dv) = refs[30:37]
    grads, pair_in, plane_in = refs[37:40], refs[40:43], refs[43:46]
    mixed_sem, triple_sem, pair_sem, plane_sem = refs[46:]
    ring = Ring(dp, ranks)
    chips = ring.chips
    f32, bf16 = jnp.float32, jnp.bfloat16
    ring.meet()
    seqs, _, width = start_ref.shape
    hidden_size = up_ref.shape[1]
    part = D // ranks
    pairs, planes = {}, {}

    def put_grad(i, value):
        grads[i][...] = value.astype(bf16).reshape(grads[i].shape)
        pairs[i] = send(
            grads[i].at[:, 1 - ring.core], pair_in[i], pair_sem, (i,), ring.sibling()
        )

    def pass_on(i):
        pairs[i].wait()

        def add_pair(p, carry):
            both = grads[i][p, ring.core].astype(f32) + pair_in[i][p].astype(f32)
            pair_in[i][p] = both.astype(bf16)
            return carry

        lax.fori_loop(0, chips, add_pair, 0)
        planes[i] = [
            send(
                pair_in[i].at[ring.chip_at(k)], plane_in[i].at[k], plane_sem, (i, k), ring.plane(k)
            )
            for k in range(1, chips)
        ]

    moving = []
    gain = None
    g3, g4 = lane_copies(g3_ref, width), lane_copies(g4_ref, width)
    for s in range(seqs):
        lanes = slice(s * width, (s + 1) * width)
        mixed = mixed_in[s].reshape(D, width)
        mixes[:, lanes] = mixed
        after = start_ref[s] + dot_tn(early_ref[:, 3 * D :], mixed)
        normed, inverse = column_rms(after)
        act = (normed * g4).astype(bf16)
        acts[:, lanes] = act
        cot = cot_ref[s].astype(f32).T
        cot_low = cot.astype(bf16)
        cots[:, lanes] = cot_low
        result, grad = after, None
        for c in range(hidden_size // D):
            rows = slice(c * D, (c + 1) * D)
            hidden, slope = gelu_pair(dot_tn(up_ref[:, rows], act))
            hidden = hidden.astype(bf16)
            hiddens[rows, lanes] = hidden
            result = result + dot_tn(down_ref[rows, :], hidden)
            grad_upper = (dot_nn(down_ref[rows, :], cot_low) * slope).astype(bf16)
            grad_ups[rows, lanes] = grad_upper
            piece = dot_nn(up_ref[:, rows], grad_upper)
            grad = piece if grad is None else grad + piece
        output_ref[s] = result.T.astype(bf16)
        piece = fold_lanes(grad * normed)
        gain = piece if gain is None else gain + piece
        total = cot + column_rms_back(grad, g4, normed, inverse)
        afters[s] = total
        low = total.astype(bf16)
        lows[:, lanes] = low
        mixed_ref[s] = dot_nn(early_ref[:, 3 * D :], low).astype(bf16).reshape(ranks, part, width)
        moving.append(swap_start(ring, mixed_ref, mixed_back, s, mixed_sem))
    d_g4[...] = gain
    put_grad(0, dot_nt(hiddens[...], cots[...]))
    moved = []
    for s in range(seqs):
        wait_all(moving[s])
        word_attention_back(s, triple_in, lse_ref, mixed_back, triple_ref, dk, dv)
        moved.append(swap_start(ring, triple_ref, triple_back, s, triple_sem))
        if s == 0:
            pass_on(0)
    put_grad(1, dot_nt(acts[...], grad_ups[...]))
    put_grad(2, dot_nt(mixes[...], lows[...]))
    pass_on(1)
    pass_on(2)
    gain = None
    for s in range(seqs):
        lanes = slice(s * width, (s + 1) * width)
        wait_all(moved[s])
        for t in range(3):
            for r in range(ranks):
                triples[t * D + r * part : t * D + (r + 1) * part, lanes] = triple_back[
                    s, r, t * part : (t + 1) * part, :
                ]
        normed, inverse = column_rms(start_ref[s])
        acts[:, lanes] = (normed * g3).astype(bf16)
        grad = dot_nn(early_ref[:, : 3 * D], triples[:, lanes])
        piece = fold_lanes(grad * normed)
        gain = piece if gain is None else gain + piece
        total = afters[s] + column_rms_back(grad, g3, normed, inverse)
        input_grad_ref[s] = total.T
        low = total.astype(bf16)
        lows[:, lanes] = low
        count = count_ref[s : s + 1, :].astype(f32)
        high, rest = split_two(dot_nn(in_ref[:, 4 * CD + CFF :], low) / count)
        spread_ref[s, :CD, :] = high
        spread_ref[s, CD:, :] = rest
    d_g3[...] = gain
    d_qkv[...] = dot_nt(acts[...], triples[...]).astype(bf16)
    d_pool[...] = sum(
        dot_nt(pooled_ref[s], lows[:, s * width : (s + 1) * width]) for s in range(seqs)
    ).astype(bf16)
    for i in range(3):
        total = pair_in[i][ring.chip].astype(f32)
        for k in range(1, chips):
            planes[i][k - 1].wait()
            total = total + plane_in[i][k].astype(f32)
        sums[i][...] = total.astype(bf16)


def word_bwd(saved, cot, counts, weights, gains, collective):
    dp, ranks = lax.axis_size("dp"), lax.axis_size("head")
    start, pooled, triple, lse, mixed = saved
    char_in, early, up, down = weights
    seqs, _, width = start.shape
    hidden = up.shape[1]
    chips = dp // 2
    bf16, f32 = jnp.bfloat16, jnp.float32
    vmem = pl.BlockSpec(memory_space=pltpu.VMEM)
    rows = ((hidden // dp, D), (D // dp, hidden), (D // dp, D))
    columns = seqs * width
    dma = pltpu.SemaphoreType.DMA
    operands = (*saved, cot, counts, char_in, early, up, down, *gains)
    shapes = [
        ((seqs, width, D), bf16),
        ((seqs, width, D), f32),
        ((seqs, 2 * CD, width), bf16),
        ((D, 3 * D), bf16),
        ((CD, D), bf16),
        ((D, GROUP), f32),
        ((D, GROUP), f32),
    ] + [(r, bf16) for r in rows]
    return pl.pallas_call(
        functools.partial(word_bwd_kernel, dp, ranks),
        in_specs=[vmem] * len(operands),
        out_specs=[vmem] * len(shapes),
        out_shape=[jax.ShapeDtypeStruct(shape, kind) for shape, kind in shapes],
        scratch_shapes=[
            pltpu.VMEM((D, columns), bf16),
            pltpu.VMEM((hidden, columns), bf16),
            pltpu.VMEM((hidden, columns), bf16),
            pltpu.VMEM((D, columns), bf16),
            pltpu.VMEM((D, columns), bf16),
            pltpu.VMEM((D, columns), bf16),
            pltpu.VMEM((3 * D, columns), bf16),
            pltpu.VMEM((seqs, D, width), f32),
            pltpu.VMEM(mixed.shape, bf16),
            pltpu.VMEM(mixed.shape, bf16),
            pltpu.VMEM(triple.shape, bf16),
            pltpu.VMEM(triple.shape, bf16),
            pltpu.VMEM((ranks, D // HEADS, width), f32),
            pltpu.VMEM((ranks, D // HEADS, width), f32),
        ]
        + [pltpu.VMEM((chips, 2) + r, bf16) for r in rows]
        + [pltpu.VMEM((chips,) + r, bf16) for r in rows] * 2
        + [
            dma((2, seqs, ranks)),
            dma((2, seqs, ranks)),
            dma((2, 3)),
            dma((2, 3, chips)),
        ],
        compiler_params=pltpu.CompilerParams(
            collective_id=collective, has_side_effects=True, vmem_limit_bytes=VMEM_BYTES
        ),
        name="word_bwd",
    )(*operands)


def block_of(ref, d, h, shard):
    if len(ref.shape) == 4:
        return ref.at[d, h]
    rows, cols = shard.shape
    return ref.at[
        pl.ds(pl.multiple_of(h * rows, rows), rows), pl.ds(pl.multiple_of(d * cols, cols), cols)
    ]


def rows_of(ref, d, shard):
    if len(ref.shape) > 2:
        return ref.at[d]
    cols = shard.shape[1]
    return ref.at[:, pl.ds(pl.multiple_of(d * cols, cols), cols)]


def gather_kernel(dp, ranks, *refs):
    shards, (counts_ref, ids_ref, gains_ref) = refs[:5], refs[5:8]
    outs, (pack_ref, tiles_ref), gain_refs = refs[8:14], refs[14:16], refs[16:20]
    low = refs[20:25]
    own_sem, line_sem, plane_sem, pair_sem, copy_sem = refs[25:]
    table, char_in, down, early, word_rows, down_rows = outs
    ring = Ring(dp, ranks)
    for shard, ref in zip(shards, low):
        ref[...] = shard[...].astype(jnp.bfloat16)
    ring.meet()

    def column(ref, like):
        wide = like.shape[1]
        return ref.at[:, pl.ds(pl.multiple_of(ring.h * wide, GROUP), wide)]

    places = (
        block_of(table, ring.d, ring.h, low[0]),
        column(char_in.at[ring.d], low[1]),
        block_of(down, ring.d, ring.h, low[2]),
        column(word_rows, low[3]),
        column(down_rows, low[4]),
    )
    own, first = [], []

    def along_line(m):
        own.append(pltpu.make_async_copy(low[m], places[m], own_sem.at[m]))
        own[m].start()
        first.append(
            [send(low[m], places[m], line_sem, (m, k), ring.line(k)) for k in range(1, ranks)]
        )

    def arrived(m):
        own[m].wait()
        for copy in first[m]:
            copy.wait_recv()

    blocks = (table, char_in, down, early)
    second, sent = [], []

    def onward(m, block):
        place = rows_of(blocks[m], ring.d, low[m])
        second.append(
            [send(block, place, plane_sem, (m, k), ring.plane(k)) for k in range(1, ring.chips)]
        )
        sent.append(send(block, place, pair_sem, (m, 0), ring.sibling()))

    for m in range(3):
        along_line(m)
    for seq in range(ids_ref.shape[0]):
        pack_words(counts_ref[seq : seq + 1, :], ids_ref[seq], pack_ref, tiles_ref, seq)
    row = 0
    for ref in gain_refs:
        for at in range(0, ref.shape[0], GROUP):
            gain = jnp.broadcast_to(gains_ref[row : row + 1, :], (GROUP, GROUP))
            ref[at : at + GROUP, :] = gain.T
            row += 1
    for m in range(3):
        arrived(m)
        onward(m, rows_of(blocks[m], ring.d, low[m]))
    along_line(3)
    along_line(4)
    arrived(3)
    block = word_rows.at[:, : early.shape[2]]
    copy = pltpu.make_async_copy(block, early.at[ring.d], copy_sem)
    copy.start()
    onward(3, block)
    for m in range(4):
        for k in range(1, ring.chips):
            second[m][k - 1].wait_recv()
            place = 2 * ring.chip_at(ring.chips - k) + ring.core
            block = rows_of(blocks[m], place, low[m])
            sent.append(send(block, block, pair_sem, (m, k), ring.sibling()))
    arrived(4)
    copy.wait()
    wait_all(sent)
    for m in range(5):
        for copy in first[m]:
            copy.wait_send()
    for m in range(4):
        for copy in second[m]:
            copy.wait_send()


def gather(shards, counts, ids, gains, collective):
    dp, ranks = lax.axis_size("dp"), lax.axis_size("head")
    bf16 = jnp.bfloat16
    vmem = pl.BlockSpec(memory_space=pltpu.VMEM)
    anywhere = pl.BlockSpec(memory_space=pl.ANY)
    table, char_in, down, word_in, word_down = (s.shape for s in shards)
    dma = pltpu.SemaphoreType.DMA

    def narrow(shape):
        if shape[1] % GROUP == 0:
            return (ranks * shape[0], dp * shape[1])
        return (dp, ranks) + shape

    seqs, slots, words = ids.shape
    outs = [
        narrow(table),
        (dp, char_in[0], ranks * char_in[1]),
        narrow(down),
        (dp, word_in[0], 4 * D),
        (word_in[0], ranks * word_in[1]),
        (word_down[0], ranks * word_down[1]),
    ]
    return pl.pallas_call(
        functools.partial(gather_kernel, dp, ranks),
        in_specs=[vmem] * 8,
        out_specs=[anywhere] * 6 + [vmem, pl.BlockSpec(memory_space=pltpu.SMEM)] + [vmem] * 4,
        out_shape=[jax.ShapeDtypeStruct(s, bf16) for s in outs]
        + [
            jax.ShapeDtypeStruct((seqs, 4, tile_count(words) * (ROWS // GROUP), GROUP), jnp.int32),
            jax.ShapeDtypeStruct((seqs,), jnp.int32),
        ]
        + [jax.ShapeDtypeStruct((n, GROUP), jnp.float32) for n in (CD, CD, D, D)],
        scratch_shapes=[pltpu.VMEM(s.shape, bf16) for s in shards]
        + [
            dma((5,)),
            dma((2, 5, ranks)),
            dma((2, 4, dp // 2)),
            dma((2, 4, dp // 2)),
            dma(()),
        ],
        compiler_params=pltpu.CompilerParams(
            collective_id=collective, has_side_effects=True, vmem_limit_bytes=VMEM_BYTES
        ),
        name="gather",
    )(*shards, counts, ids, gains)


def column_cuts(widths, ranks):
    block = sum(widths) // ranks
    cuts, start = [], 0
    for width in widths:
        mine, at = [], 0
        while at < width:
            rank, inside = divmod(start + at, block)
            take = min(width - at, block - inside)
            mine.append((rank, at, at + take, inside))
            at += take
        cuts.append(mine)
        start += width
    return cuts


def reduce_kernel(dp, ranks, groups, extra, *refs):
    pieces = sum(len(g) - done for g, done in groups)
    mats = len(groups)
    parts = refs[:pieces]
    gain_refs = refs[pieces : pieces + 4]
    ready = refs[pieces + 4 : pieces + 4 + extra]
    place = pieces + 4 + extra
    outs = refs[place : place + mats]
    gain_out, square_out = refs[place + mats : place + mats + 2]
    place += mats + 2
    pair_in = refs[place : place + pieces]
    pair_sum = refs[place + pieces : place + 2 * pieces]
    plane_in = refs[place + 2 * pieces : place + 3 * pieces]
    place += 3 * pieces
    line_sum, line_in = refs[place : place + mats], refs[place + mats : place + 2 * mats]
    place += 2 * mats
    small, pair_sem, plane_sem, line_sem, small_sem = refs[place:]
    ring = Ring(dp, ranks)
    chips = ring.chips
    f32, bf16 = jnp.float32, jnp.bfloat16
    ring.meet()
    sent = []

    def share(slot, value, stage):
        others, here, count = (
            (lambda k: ring.sibling(), ring.core, 2),
            (ring.plane, ring.chip, chips),
            (ring.line, ring.h, ranks),
        )[stage]
        small[slot, stage, here] = value
        copies = []
        for k in range(1, count):
            spot = small.at[slot, stage, here]
            copies.append(send(spot, spot, small_sem, (slot, stage, k), others(k)))
        return copies

    def shared(slot, copies, stage):
        for copy in copies:
            copy.wait()
        count = (2, chips, ranks)[stage]
        total = small[slot, stage, 0]
        for k in range(1, count):
            total = total + small[slot, stage, k]
        return total

    def total_of(slot, value):
        for stage in range(3):
            value = shared(slot, share(slot, value, stage), stage)
        return value

    def line_copy(m, k):
        return pltpu.make_async_remote_copy(
            src_ref=line_sum[m].at[ring.rank_at(k)],
            dst_ref=line_in[m].at[k],
            send_sem=line_sem.at[0, m, k],
            recv_sem=line_sem.at[1, m, k],
            device_id=ring.line(k),
            device_id_type=pl.DeviceIdType.MESH,
        )

    def put_columns(m, cuts, total):
        for rank, first, last, inside in cuts:
            line_sum[m][rank, :, inside : inside + last - first] = total[:, first:last]

    def early_rank(m):
        widths, done = groups[m]
        own = sum(widths[: len(widths) - done])
        ready_from = sum(
            w for at, w in enumerate(widths) if at < len(widths) - done
        ) if done else sum(widths)
        block = sum(widths) // ranks
        return -(-max(own, ready_from) // block)

    def begin(copy, now, first):
        if first == 0:
            copy.start()
        elif first < ranks:
            pl.when(now)(copy.start)

    pairs = [
        send(parts[i].at[:, 1 - ring.core], pair_in[i], pair_sem, (i,), ring.sibling())
        for i in range(pieces)
    ]
    starts = []
    j = 0
    for m, (widths, done) in enumerate(groups):
        lines = [line_copy(m, k) for k in range(1, ranks)]
        starts.append(lines)
        cuts = column_cuts(widths, ranks)
        for at in range(len(widths) - done, len(widths)):
            put_columns(m, cuts[at], ready[j][...])
            j += 1
        for k in range(1, ranks):
            begin(lines[k - 1], early_rank(m) <= ring.rank_at(k), early_rank(m))
    rows = []
    for ref in gain_refs:
        for at in range(0, ref.shape[0], GROUP):
            rows.append(jnp.sum(ref[at : at + GROUP, :].T, axis=0, keepdims=True))
    rows.append(jnp.zeros((small.shape[3] - len(rows), GROUP), f32))
    gain = shared(0, share(0, jnp.concatenate(rows, axis=0), 0), 0)
    planes = []
    for i in range(pieces):
        pairs[i].wait()

        def add_pair(p, carry, i=i):
            both = parts[i][p, ring.core].astype(f32) + pair_in[i][p].astype(f32)
            pair_sum[i][p] = both.astype(bf16)
            return carry

        lax.fori_loop(0, chips, add_pair, 0)
        planes.append(
            [
                send(
                    pair_sum[i].at[ring.chip_at(k)],
                    plane_in[i].at[k],
                    plane_sem,
                    (i, k),
                    ring.plane(k),
                )
                for k in range(1, chips)
            ]
        )
    gain = shared(0, share(0, gain, 1), 1)
    gain_out[...] = shared(0, share(0, gain, 2), 2)[: gain_out.shape[0]]
    i = 0
    for m, (widths, done) in enumerate(groups):
        for cuts in column_cuts(widths, ranks)[: len(widths) - done]:
            total = pair_sum[i][ring.chip].astype(f32)
            for k in range(1, chips):
                planes[i][k - 1].wait()
                total = total + plane_in[i][k].astype(f32)
            put_columns(m, cuts, total.astype(bf16))
            i += 1
        first = early_rank(m)
        for k in range(1, ranks):
            if first >= ranks:
                starts[m][k - 1].start()
            elif first > 0:
                pl.when(ring.rank_at(k) < first)(starts[m][k - 1].start)
    square = jnp.zeros(square_out.shape, f32)

    def squares(value):
        value = value * value
        rows, cols = value.shape
        if cols % GROUP:
            value = jnp.concatenate([value, jnp.zeros((rows, GROUP - cols % GROUP), f32)], axis=1)
        return jnp.sum(fold_lanes(value).reshape(rows // 8, 8, GROUP), axis=0)

    for m in range(mats):
        total = line_sum[m][ring.h].astype(f32)
        for k in range(1, ranks):
            starts[m][k - 1].wait()
            total = total + line_in[m][k].astype(f32)
        outs[m][...] = total if outs[m].shape == total.shape else total.T
        square = square + squares(total)
    small_square = jnp.concatenate([square, jnp.zeros_like(square)], axis=0)
    square_out[...] = total_of(1, small_square)[:8]


def reduce_grads(groups, gains, collective):
    dp, ranks = lax.axis_size("dp"), lax.axis_size("head")
    chips = dp // 2
    bf16, f32 = jnp.bfloat16, jnp.float32
    pieces, ready, widths, shards = [], [], [], []
    for group, done in groups:
        rows = done[0].shape[0] if done else group[0].shape[0] // dp
        pieces += [p.reshape(chips, 2, rows, p.shape[1]) for p in group]
        ready += done
        widths.append((tuple(p.shape[1] for p in group + done), len(done)))
        shards.append((rows, sum(widths[-1][0]) // ranks))
    blocks = [p.shape[2:] for p in pieces]
    vmem = pl.BlockSpec(memory_space=pltpu.VMEM)
    n, mats = len(pieces), len(groups)
    gain_rows = sum(g.shape[0] for g in gains) // GROUP
    return pl.pallas_call(
        functools.partial(reduce_kernel, dp, ranks, widths, len(ready)),
        in_specs=[vmem] * (n + 4 + len(ready)),
        out_specs=[vmem] * (mats + 2),
        out_shape=[jax.ShapeDtypeStruct(s if s[1] % GROUP == 0 else s[::-1], f32) for s in shards]
        + [jax.ShapeDtypeStruct((gain_rows, GROUP), f32), jax.ShapeDtypeStruct((8, GROUP), f32)],
        scratch_shapes=[pltpu.VMEM((chips,) + b, bf16) for b in blocks] * 3
        + [pltpu.VMEM((ranks,) + s, bf16) for s in shards] * 2
        + [
            pltpu.VMEM((2, 3, max(2, chips, ranks), 16, GROUP), f32),
            pltpu.SemaphoreType.DMA((2, n)),
            pltpu.SemaphoreType.DMA((2, n, chips)),
            pltpu.SemaphoreType.DMA((2, mats, ranks)),
            pltpu.SemaphoreType.DMA((2, 2, 3, max(2, chips, ranks))),
        ],
        compiler_params=pltpu.CompilerParams(
            collective_id=collective, has_side_effects=True, vmem_limit_bytes=VMEM_BYTES
        ),
        name="reduce_grads",
    )(*pieces, *gains, *ready)


def update_kernel(count, *refs):
    weights, grads = refs[:count], refs[count : 2 * count]
    firsts, seconds = refs[2 * count : 3 * count], refs[3 * count : 4 * count]
    square_ref = refs[4 * count]
    norm_ref, outs = refs[4 * count + 1], refs[4 * count + 2 :]
    gain_grad = grads[-1][...]
    square = jnp.sum(square_ref[...]) + jnp.sum(gain_grad * gain_grad)
    norm = jnp.sqrt(jnp.full((1, GROUP), square, jnp.float32))
    norm_ref[...] = norm
    clip_factor = jnp.minimum(1.0, CLIP / norm)[:, :1]
    for i in range(count):
        gains = i == count - 1
        result = adam_step(
            weights[i][...],
            grads[i][...],
            firsts[i][...],
            seconds[i][...],
            clip_factor,
            GAIN_RATE if gains else MATRIX_RATE,
            0.0 if gains else MATRIX_DECAY,
        )
        for ref, value in zip(outs[5 * i : 5 * i + 5], result):
            ref[...] = value


def update(weights, grads, firsts, seconds, square):
    count = len(weights)
    shapes = [jax.ShapeDtypeStruct((1, GROUP), jnp.float32)]
    for w in weights:
        shapes += [jax.ShapeDtypeStruct(w.shape, jnp.float32)] * 4
        shapes.append(jax.ShapeDtypeStruct(w.shape, jnp.bfloat16))
    return pl.pallas_call(
        functools.partial(update_kernel, count),
        out_shape=shapes,
        compiler_params=pltpu.CompilerParams(vmem_limit_bytes=VMEM_BYTES),
        name="update",
    )(*weights, *grads, *firsts, *seconds, square)


def body(
    char_ids,
    char_counts,
    language,
    words_in,
    out_cotangent,
    char_table,
    char_in,
    char_down,
    word_in,
    word_down,
    norm_gains,
    old_table_first,
    old_table_second,
    old_char_in_first,
    old_char_in_second,
    old_char_down_first,
    old_char_down_second,
    old_word_in_first,
    old_word_in_second,
    old_word_down_first,
    old_word_down_second,
    old_gains_first,
    old_gains_second,
):
    narrow = (norm_gains.shape[0] // GROUP, GROUP)
    table_t, char_in_low, char_down_t, early, up_rows, down_rows, packed, tiles, *gains = gather(
        (char_table.T, char_in, char_down.T, word_in, word_down),
        char_counts,
        char_ids.transpose(0, 2, 1),
        norm_gains.reshape(narrow),
        0,
    )

    def joined(block):
        if block.ndim == 2:
            return block
        dp, ranks, cols, rows = block.shape
        return block.transpose(1, 2, 0, 3).reshape(ranks * cols, dp * rows)

    def stacked(block):
        return block.reshape(-1, block.shape[2])

    table_t = joined(table_t)
    char_in_low, early = stacked(char_in_low), stacked(early)
    char_others = (char_in_low, joined(char_down_t), gains[0], gains[1])
    sums, *kept = char_fwd(tiles, language, packed, table_t, char_others, words_in.shape[1])
    *saved, up, down = word_fwd(
        sums, char_counts, words_in, char_in_low, early, gains[2], up_rows, down_rows, 1
    )
    (
        output,
        input_grad,
        spread,
        grad_qkv,
        grad_pool,
        gain_three,
        gain_four,
        down_sum,
        up_sum,
        out_sum,
    ) = word_bwd(
        tuple(saved),
        out_cotangent,
        char_counts,
        (char_in_low, early, stacked(up), stacked(down)),
        gains[2:],
        2,
    )
    grad_table, c_qkv, c_out, c_up, c_down, gain_one, gain_two = char_bwd(
        tiles, language, packed, table_t, char_others, spread, kept
    )
    *shards, gains_sum, square = reduce_grads(
        [
            ([grad_table], []),
            ([c_qkv, c_out, c_up, grad_pool], []),
            ([c_down], []),
            ([grad_qkv], [out_sum, up_sum]),
            ([], [down_sum]),
        ],
        (gain_one, gain_two, gain_three, gain_four),
        3,
    )

    def turned(parts):
        parts = list(parts)
        parts[0], parts[2] = parts[0].T, parts[2].T
        parts[5] = parts[5].reshape(narrow)
        return parts

    norm, *updated = update(
        turned((char_table, char_in, char_down, word_in, word_down, norm_gains)),
        (*shards, gains_sum),
        turned(
            (
                old_table_first,
                old_char_in_first,
                old_char_down_first,
                old_word_in_first,
                old_word_down_first,
                old_gains_first,
            )
        ),
        turned(
            (
                old_table_second,
                old_char_in_second,
                old_char_down_second,
                old_word_in_second,
                old_word_down_second,
                old_gains_second,
            )
        ),
        square,
    )
    for place in (*range(5), *range(10, 15)):
        updated[place] = updated[place].T
    updated[-5:] = [part.reshape(norm_gains.shape) for part in updated[-5:]]
    return (output, input_grad, norm[0, 0], *updated)


def solution(mesh):
    return jax.shard_map(
        body,
        mesh=mesh,
        in_specs=(
            P("dp", "head", None),
            P("dp", "head"),
            P("dp"),
            P("dp", "head", None),
            P("dp", "head", None),
            P("dp", "head"),
            P("dp", "head"),
            P("dp", "head"),
            P("dp", "head"),
            P("dp", "head"),
            P(),
            P("dp", "head"),
            P("dp", "head"),
            P("dp", "head"),
            P("dp", "head"),
            P("dp", "head"),
            P("dp", "head"),
            P("dp", "head"),
            P("dp", "head"),
            P("dp", "head"),
            P("dp", "head"),
            P(),
            P(),
        ),
        out_specs=(
            P("dp", "head", None),
            P("dp", "head", None),
            P(),
            P("dp", "head"),
            P("dp", "head"),
            P("dp", "head"),
            P("dp", "head"),
            P("dp", "head"),
            P("dp", "head"),
            P("dp", "head"),
            P("dp", "head"),
            P("dp", "head"),
            P("dp", "head"),
            P("dp", "head"),
            P("dp", "head"),
            P("dp", "head"),
            P("dp", "head"),
            P("dp", "head"),
            P("dp", "head"),
            P("dp", "head"),
            P("dp", "head"),
            P("dp", "head"),
            P("dp", "head"),
            P("dp", "head"),
            P("dp", "head"),
            P("dp", "head"),
            P("dp", "head"),
            P("dp", "head"),
            P(),
            P(),
            P(),
            P(),
            P(),
        ),
        check_vma=False,
    )
```

```python
import functools

import jax
import jax.numpy as jnp
from jax import lax
from jax.experimental import pallas as pl
from jax.experimental.pallas import tpu as pltpu
from jax.sharding import PartitionSpec as P

D = 512
HEADS = 8
CD = 256
CHEADS = 4
CFF = 1024
CV = 256
STEP = 5


EPS = 1e-05
CLIP = 1.0
MATRIX_RATE = 0.03
GAIN_RATE = 0.25
MATRIX_DECAY = 0.1
BETA_ONE = 0.5
BETA_TWO = 0.5
ADAM_EPS = 1e-08
NEG_FILL = -1e30
SQRT_HALF = 0.7071067811865476
INV_ROOT_TWO_PI = 0.3989422804014327


ROWS = 512
SLOTS = 16
CHAINS = 1
GROUP = 128
VMEM_BYTES = 56 * 1024 * 1024


def dot_nn(left_side, right_side):
    return lax.dot_general(
        left_side, right_side, (((1,), (0,)), ((), ())), preferred_element_type=jnp.float32
    )


def dot_tn(left_side, right_side):
    return lax.dot_general(
        left_side, right_side, (((0,), (0,)), ((), ())), preferred_element_type=jnp.float32
    )


def dot_nt(left_side, right_side):
    return lax.dot_general(
        left_side, right_side, (((1,), (1,)), ((), ())), preferred_element_type=jnp.float32
    )


def gelu_pair(upper):
    phi = 0.5 + 0.5 * lax.erf(upper * SQRT_HALF)
    bell = jnp.exp(upper * upper * -0.5)
    return upper * phi, phi + upper * (bell * INV_ROOT_TWO_PI)


def iota(shape, dim):
    return lax.broadcasted_iota(jnp.int32, shape, dim)


def split_two(values):
    high = values.astype(jnp.bfloat16)
    return high, (values - high.astype(jnp.float32)).astype(jnp.bfloat16)


def pack_words(row, ids, out_ref, tiles_ref, seq):
    n = row.shape[1]
    col = jnp.broadcast_to(row.astype(jnp.float32), (8, n)).T[:, :1].astype(jnp.int32)
    sub, lane = iota((n, n), 0), iota((n, n), 1)
    ahead = (row > col) | ((row == col) & (lane < sub))
    rank_col = jnp.sum(ahead.astype(jnp.float32), axis=1, keepdims=True).astype(jnp.int32)
    ahead = (col > row) | ((col == row) & (sub < lane))
    rank_row = jnp.sum(ahead.astype(jnp.float32), axis=0, keepdims=True).astype(jnp.int32)
    clash = (rank_col < rank_row) & (col + row > SLOTS)
    alone = jnp.max(jnp.where(clash, rank_col + rank_row, 0).astype(jnp.float32))
    alone = jnp.maximum(alone.astype(jnp.int32) - n + 2, 0)
    partner = n - 1 + alone - rank_row
    second = (rank_row >= alone) & (rank_row > partner)
    bins = jnp.where(second, partner, rank_row)
    here = sub == bins
    first_map = (here & jnp.logical_not(second)).astype(jnp.float32).astype(jnp.bfloat16)
    second_map = (here & second).astype(jnp.float32).astype(jnp.bfloat16)
    pos = lax.rem(iota((GROUP, n), 0), SLOTS)
    word = iota((GROUP, n), 1) + 1
    wide = jnp.broadcast_to(row, (GROUP, n))
    in_first, in_second = pos < wide, pos >= SLOTS - wide

    def kept(mask, values):
        return jnp.where(mask, values, 0).astype(jnp.float32).astype(jnp.bfloat16)

    groups = n * SLOTS // GROUP
    spare = out_ref.shape[2] - groups
    per = GROUP // SLOTS
    own = iota((groups, per, GROUP), 1) == lax.div(iota((groups, per, GROUP), 2), SLOTS)
    back = jnp.concatenate([ids[SLOTS - 1 - j : SLOTS - j] for j in range(SLOTS)] * per, axis=0)
    ids = jnp.concatenate([ids] * per, axis=0)
    zero = jnp.zeros_like(wide)
    for k, (one, two) in enumerate(
        ((ids + 1, back + 1), (word, word), (zero, SLOTS - wide), (wide, zero + SLOTS))
    ):
        full = dot_nt(first_map, kept(in_first, one)) + dot_nt(second_map, kept(in_second, two))
        full = jnp.where(own, full.reshape(groups, per, GROUP), 0.0)
        full = jnp.sum(full, axis=1).astype(jnp.int32)
        if spare:
            full = jnp.concatenate([full, jnp.zeros((spare, GROUP), jnp.int32)], axis=0)
        out_ref[seq, k] = full
    used = alone + lax.div(n - alone + 1, 2)
    tiles_ref[seq] = lax.div(used * SLOTS + ROWS - 1, ROWS)


def lane_map(rows, size):
    spots = iota((size, GROUP), 0) + 1
    maps = [
        (spots == rows[g : g + 1]).astype(jnp.float32).astype(jnp.bfloat16)
        for g in range(rows.shape[0])
    ]
    return jnp.concatenate(maps, axis=1)


def in_step(chains):
    results = [None] * len(chains)
    waiting = list(enumerate(chains))
    running = []
    while waiting or running:
        if waiting:
            running.append(waiting.pop(0))
        for item in list(running):
            try:
                next(item[1])
            except StopIteration as stop:
                results[item[0]] = stop.value
                running.remove(item)
    return results


def lane_copies(ref, width):
    return jnp.concatenate([ref[...]] * (width // GROUP), axis=1)


def column_rms(values):
    inverse = lax.rsqrt(jnp.mean(values * values, axis=0, keepdims=True) + EPS)
    return values * inverse, inverse


def cost(flops, moved, powers):
    return pl.CostEstimate(flops=int(flops), bytes_accessed=int(moved), transcendentals=int(powers))


def tile_count(words):
    return -(-words * SLOTS // ROWS)


def tile_at(step, tiles_ref, seqs):
    seq, start, total = 0, 0, tiles_ref[0]
    for s in range(1, seqs):
        past = step >= total
        seq, start = jnp.where(past, s, seq), jnp.where(past, total, start)
        total = total + tiles_ref[s]
    return seq, step - start, total


def placed(seqs, index):
    def place(step, tiles_ref, language_ref):
        total = tile_at(step, tiles_ref, seqs)[2]
        seq, tile, _ = tile_at(jnp.minimum(step, total - 1), tiles_ref, seqs)
        return index(seq, tile, language_ref)

    return place


def own_block():
    shape = (GROUP // SLOTS, SLOTS, CHEADS * GROUP)
    return iota(shape, 0) == lax.div(lax.rem(iota(shape, 2), GROUP), SLOTS)


def to_compact(block, own):
    return jnp.sum(jnp.where(own, block.reshape(own.shape), 0.0), axis=0)


def from_compact(compact, own):
    wide = jnp.broadcast_to(compact[None], own.shape)
    return jnp.where(own, wide, 0.0).astype(jnp.bfloat16).reshape(GROUP, -1)


def stack_heads(wide):
    return jnp.concatenate([wide[:, h * GROUP : (h + 1) * GROUP] for h in range(CHEADS)], axis=0)


def spread_heads(values):
    head = values.shape[0] // CHEADS
    zero = jnp.zeros((head, GROUP), values.dtype)
    rows = []
    for h in range(CHEADS):
        parts = [zero] * CHEADS
        parts[h] = values[h * head : (h + 1) * head]
        rows.append(jnp.concatenate(parts, axis=1))
    return jnp.concatenate(rows, axis=0)


def char_fwd_kernel(seqs, tiles_ref, language_ref, *refs):
    step = pl.program_id(0)
    _, tile, total = tile_at(step, tiles_ref, seqs)

    @pl.when(step < total)
    def _():
        char_fwd_tile(tile, *refs)


def char_fwd_tile(
    step, pack_ref, table_ref, in_ref, down_ref, g1_ref, g2_ref, pooled_ref,
    keep_values, keep_probs, keep_qkv, keep_mixed, keep_first, keep_hidden, keep_slope,
):
    words = pooled_ref.shape[2]
    per = ROWS // GROUP
    head = CD // CHEADS

    @pl.when(step == 0)
    def _():
        pooled_ref[...] = jnp.zeros_like(pooled_ref)

    own = own_block()
    key_pos = iota((SLOTS, GROUP), 0)
    packs = [pack_ref[0, k, pl.ds(step * per, per), :] for k in range(4)]

    def chain(part):
        groups = per // CHAINS
        cols = slice(part * groups * GROUP, (part + 1) * groups * GROUP)
        size = groups * GROUP
        ids, spots, low_rows, high_rows = (p[part * groups : (part + 1) * groups] for p in packs)
        embedded = dot_nn(table_ref[...], lane_map(ids, CV))
        yield
        act_one = (column_rms(embedded)[0] * lane_copies(g1_ref, size)).astype(jnp.bfloat16)
        triple = dot_tn(in_ref[:, : 3 * CD], act_one).astype(jnp.bfloat16)
        keep_qkv[:, cols] = triple
        yield
        key_rows = triple[CD : 2 * CD].T
        keep_values[cols, :] = triple[2 * CD :].T
        all_probs = []
        for g in range(groups):
            valid = (key_pos >= low_rows[g : g + 1]) & (key_pos < high_rows[g : g + 1])
            valid = jnp.concatenate([valid.astype(jnp.float32)] * CHEADS, axis=1) > 0
            lanes = slice(g * GROUP, (g + 1) * GROUP)
            scores = to_compact(dot_nn(key_rows[lanes], spread_heads(triple[:CD, lanes])), own)
            scores = jnp.where(valid, scores * head**-0.5, NEG_FILL)
            powers = jnp.exp(scores - jnp.max(scores, axis=0, keepdims=True))
            powers = jnp.where(valid, powers, 0.0)
            total = jnp.sum(powers, axis=0, keepdims=True)
            probs = powers / jnp.where(total > 0, total, 1.0)
            wide = (part * groups + g) * CHEADS * GROUP
            keep_probs[:, wide : wide + CHEADS * GROUP] = probs
            all_probs.append(from_compact(probs, own))
        yield
        mixed = []
        for g in range(groups):
            lanes = slice(g * GROUP, (g + 1) * GROUP)
            values = spread_heads(triple[2 * CD :, lanes])
            mixed.append(dot_nn(values, stack_heads(all_probs[g])).astype(jnp.bfloat16))
        mixed = jnp.concatenate(mixed, axis=1)
        keep_mixed[:, cols] = mixed
        yield
        first = embedded + dot_tn(in_ref[:, 3 * CD : 4 * CD], mixed)
        keep_first[:, cols] = first
        act_two = (column_rms(first)[0] * lane_copies(g2_ref, size)).astype(jnp.bfloat16)
        second = first
        for c in range(CFF // CD):
            yield
            rows = slice(c * CD, (c + 1) * CD)
            up = in_ref[:, 4 * CD + c * CD : 4 * CD + (c + 1) * CD]
            hidden, slope = gelu_pair(dot_tn(up, act_two))
            hidden = hidden.astype(jnp.bfloat16)
            keep_hidden[rows, cols] = hidden
            keep_slope[rows, cols] = slope.astype(jnp.bfloat16)
            second = second + dot_nn(down_ref[:, rows], hidden)
        yield
        return lane_map(spots, words), split_two(second)

    ends = in_step([chain(part) for part in range(CHAINS)])
    word_map = jnp.concatenate([end[0] for end in ends], axis=1)
    high = jnp.concatenate([end[1][0] for end in ends], axis=1)
    low = jnp.concatenate([end[1][1] for end in ends], axis=1)
    halves = dot_nt(jnp.concatenate([high, low], axis=0), word_map)
    pooled_ref[0] += halves[:CD] + halves[CD:]


KEPT = (
    (3 * CD, jnp.bfloat16),
    (CD, jnp.bfloat16),
    (CD, jnp.float32),
    (CFF, jnp.bfloat16),
    (CFF, jnp.bfloat16),
)


def kept_specs(seqs, count):
    place = placed(seqs, lambda seq, tile, _: (0, seq * count + tile))
    return [
        pl.BlockSpec((ROWS, CD), lambda *at: place(*at)[::-1]),
        pl.BlockSpec((SLOTS, CHEADS * ROWS), place),
    ] + [pl.BlockSpec((depth, ROWS), place) for depth, _ in KEPT]


def kept_shapes(rows):
    return [
        jax.ShapeDtypeStruct((rows, CD), jnp.bfloat16),
        jax.ShapeDtypeStruct((SLOTS, CHEADS * rows), jnp.float32),
    ] + [jax.ShapeDtypeStruct((depth, rows), dtype) for depth, dtype in KEPT]


def whole(array):
    zeros = (0,) * array.ndim
    return pl.BlockSpec(array.shape, lambda *_: zeros)


def char_specs(seqs, pack, others):
    one = (1,) + pack.shape[1:]
    return [
        pl.BlockSpec(one, placed(seqs, lambda seq, tile, _: (seq, 0, 0, 0))),
        pl.BlockSpec((CD, CV), placed(seqs, lambda seq, tile, language: (0, language[seq]))),
    ] + [whole(a) for a in others]


def char_fwd(tiles, language, pack, table, others, words):
    seqs = pack.shape[0]
    count = tile_count(words)
    one = placed(seqs, lambda seq, tile, _: (seq, 0, 0))
    return pl.pallas_call(
        functools.partial(char_fwd_kernel, seqs),
        grid_spec=pltpu.PrefetchScalarGridSpec(
            num_scalar_prefetch=2,
            grid=(seqs * count,),
            in_specs=char_specs(seqs, pack, others),
            out_specs=[pl.BlockSpec((1, CD, words), one)] + kept_specs(seqs, count),
        ),
        out_shape=[jax.ShapeDtypeStruct((seqs, CD, words), jnp.float32)]
        + kept_shapes(seqs * count * ROWS),
        compiler_params=pltpu.CompilerParams(vmem_limit_bytes=VMEM_BYTES),
        cost_estimate=cost(3e10, 6e7, 1e7),
        name="char_fwd",
    )(tiles, language, pack, table, *others)


def fold_lanes(values):
    total = values[:, :GROUP]
    for g in range(1, values.shape[1] // GROUP):
        total = total + values[:, g * GROUP : (g + 1) * GROUP]
    return total


def column_rms_back(grad_in, gain, normed, inverse):
    scaled = grad_in * gain
    return inverse * (scaled - normed * jnp.mean(scaled * normed, axis=0, keepdims=True))


def char_bwd_kernel(seqs, tiles_ref, language_ref, *refs):
    step = pl.program_id(0)
    seq, tile, total = tile_at(step, tiles_ref, seqs)

    @pl.when(step < total)
    def _():
        char_bwd_tile(tile, step == 0, step == total - 1, language_ref[seq] * CV, *refs)


def char_bwd_tile(
    step, at_start, at_end, letter, pack_ref, table_ref, in_ref, down_ref, g1_ref, g2_ref, spread_ref,
    keep_values, keep_probs, keep_qkv, keep_mixed, keep_first, keep_hidden, keep_slope,
    *refs,
):
    results, totals = refs[:7], refs[7:]
    d_table, d_qkv, d_out, d_up, d_down, d_g1, d_g2 = totals
    words = spread_ref.shape[2]
    per = ROWS // GROUP
    head = CD // CHEADS

    @pl.when(at_start)
    def _():
        for ref in totals:
            ref[...] = jnp.zeros_like(ref)

    own = own_block()
    packs = [pack_ref[0, k, pl.ds(step * per, per), :] for k in range(2)]

    def chain(part):
        groups = per // CHAINS
        cols = slice(part * groups * GROUP, (part + 1) * groups * GROUP)
        size = groups * GROUP
        ids, spots = (p[part * groups : (part + 1) * groups] for p in packs)
        halves = dot_nn(spread_ref[0], lane_map(spots, words))
        grad_second = halves[:CD] + halves[CD:]
        grad_branch = grad_second.astype(jnp.bfloat16)
        normed_two, inverse_two = column_rms(keep_first[:, cols])
        gain_two = lane_copies(g2_ref, size)
        act_two = (normed_two * gain_two).astype(jnp.bfloat16)
        grad_uppers = []
        grad_act_two = None
        for c in range(CFF // CD):
            yield
            rows = slice(c * CD, (c + 1) * CD)
            slope = keep_slope[rows, cols].astype(jnp.float32)
            grad_upper = dot_tn(down_ref[:, rows], grad_branch) * slope
            grad_upper = grad_upper.astype(jnp.bfloat16)
            grad_uppers.append(grad_upper)
            piece = dot_nn(in_ref[:, 4 * CD + c * CD : 4 * CD + (c + 1) * CD], grad_upper)
            grad_act_two = piece if grad_act_two is None else grad_act_two + piece
        yield
        gain_sum_two = fold_lanes(grad_act_two * normed_two)
        grad_first = grad_second + column_rms_back(
            grad_act_two, gain_two, normed_two, inverse_two
        )
        grad_attn = grad_first.astype(jnp.bfloat16)
        grad_mixed = dot_nn(in_ref[:, 3 * CD : 4 * CD], grad_attn).astype(jnp.bfloat16)
        yield
        triple = keep_qkv[:, cols]
        raws, lows = [], []
        for g in range(groups):
            lanes = slice(g * GROUP, (g + 1) * GROUP)
            at = part * groups + g
            wide = slice(at * CHEADS * GROUP, (at + 1) * CHEADS * GROUP)
            probs = keep_probs[:, wide]
            values = keep_values[at * GROUP : (at + 1) * GROUP, :]
            grad_probs = to_compact(dot_nn(values, spread_heads(grad_mixed[:, lanes])), own)
            grad_scores = probs * (
                grad_probs - jnp.sum(probs * grad_probs, axis=0, keepdims=True)
            )
            raws.append(from_compact(grad_scores * head**-0.5, own))
            lows.append(from_compact(probs, own))
        yield
        columns = []
        for g in range(groups):
            lanes = slice(g * GROUP, (g + 1) * GROUP)
            grad_q = dot_nn(spread_heads(triple[CD : 2 * CD, lanes]), stack_heads(raws[g]))
            grad_k = dot_nt(spread_heads(triple[:CD, lanes]), raws[g])
            grad_v = dot_nt(spread_heads(grad_mixed[:, lanes]), lows[g])
            columns.append(jnp.concatenate([grad_q, grad_k, grad_v], axis=0).astype(jnp.bfloat16))
        grad_triple = jnp.concatenate(columns, axis=1)
        yield
        one_hot = lane_map(ids, CV)
        embedded = dot_nn(table_ref[...], one_hot)
        normed_one, inverse_one = column_rms(embedded)
        gain_one = lane_copies(g1_ref, size)
        act_one = (normed_one * gain_one).astype(jnp.bfloat16)
        grad_act_one = dot_nn(in_ref[:, : 3 * CD], grad_triple)
        yield
        gain_sum_one = fold_lanes(grad_act_one * normed_one)
        back_one = column_rms_back(grad_act_one, gain_one, normed_one, inverse_one)
        grad_embedded = (grad_first + back_one).astype(jnp.bfloat16)
        grad_upper = jnp.concatenate(grad_uppers, axis=0)
        return (
            gain_sum_one, gain_sum_two, grad_branch, act_two, grad_upper, grad_attn,
            act_one, grad_triple, one_hot, grad_embedded,
        )

    ends = in_step([chain(part) for part in range(CHAINS)])
    for end in ends:
        d_g1[...] += end[0]
        d_g2[...] += end[1]
    grad_branch, act_two, grad_upper, grad_attn, act_one, grad_triple, one_hot, grad_embedded = (
        jnp.concatenate(parts, axis=1) for parts in list(zip(*ends))[2:]
    )
    d_down[...] += dot_nt(keep_hidden[...], grad_branch)
    d_up[...] += dot_nt(act_two, grad_upper)
    d_out[...] += dot_nt(keep_mixed[...], grad_attn)
    d_qkv[...] += dot_nt(act_one, grad_triple)
    d_table[pl.ds(pl.multiple_of(letter, CV), CV), :] += dot_nt(one_hot, grad_embedded)

    @pl.when(at_end)
    def _():
        for ref, total in zip(results, totals):
            ref[...] = total[...].astype(ref.dtype)


def char_bwd(tiles, language, pack, table, others, spread, kept):
    shapes = (
        table.shape[::-1],
        (CD, 3 * CD),
        (CD, CD),
        (CD, CFF),
        (CFF, CD),
        (CD, GROUP),
        (CD, GROUP),
    )
    f32, bf16 = jnp.float32, jnp.bfloat16
    kinds = [bf16] * 5 + [f32] * 2
    seqs = pack.shape[0]
    count = tile_count(spread.shape[2])
    one = (1,) + spread.shape[1:]
    return pl.pallas_call(
        functools.partial(char_bwd_kernel, seqs),
        grid_spec=pltpu.PrefetchScalarGridSpec(
            num_scalar_prefetch=2,
            grid=(seqs * count,),
            in_specs=char_specs(seqs, pack, others)
            + [pl.BlockSpec(one, placed(seqs, lambda seq, tile, _: (seq, 0, 0)))]
            + kept_specs(seqs, count),
            out_specs=[pl.BlockSpec(s, lambda *_: (0, 0)) for s in shapes],
            scratch_shapes=[pltpu.VMEM(s, f32) for s in shapes],
        ),
        out_shape=[jax.ShapeDtypeStruct(s, kind) for s, kind in zip(shapes, kinds)],
        compiler_params=pltpu.CompilerParams(vmem_limit_bytes=VMEM_BYTES),
        cost_estimate=cost(5e10, 6e7, 1e6),
        name="char_bwd",
    )(tiles, language, pack, table, *others, spread, *kept)


def adam_step(weight, grad, first_old, second_old, clip_factor, rate, decay):
    clipped = grad * clip_factor
    first_new = BETA_ONE * first_old + (1.0 - BETA_ONE) * clipped
    second_new = BETA_TWO * second_old + (1.0 - BETA_TWO) * clipped * clipped
    first_hat = first_new / (1.0 - BETA_ONE**STEP)
    second_hat = second_new / (1.0 - BETA_TWO**STEP)
    weight_new = weight - rate * (first_hat / (jnp.sqrt(second_hat) + ADAM_EPS) + decay * weight)
    return (grad, first_new, second_new, weight_new, weight_new.astype(jnp.bfloat16))


class Ring:
    def __init__(self, dp, ranks):
        self.chips, self.ranks = dp // 2, ranks
        self.d, self.h = lax.axis_index("dp"), lax.axis_index("head")
        self.chip, self.core = lax.div(self.d, 2), lax.rem(self.d, 2)

    def sibling(self):
        return (self.d + 1 - 2 * self.core, self.h)

    def chip_at(self, k):
        if self.chips != 4:
            return lax.rem(self.chip + k, self.chips)
        return (None, self.chip + 1 - 2 * lax.rem(self.chip, 2), lax.rem(self.chip + 2, 4), 3 - self.chip)[k]

    def chip_from(self, k):
        if self.chips != 4:
            return lax.rem(self.chip + self.chips - k, self.chips)
        return self.chip_at(k)

    def plane(self, k):
        return (2 * self.chip_at(k) + self.core, self.h)

    def across(self, k):
        return (lax.rem(self.d + k, 2 * self.chips), self.h)

    def rank_at(self, k):
        return lax.rem(self.h + k, self.ranks)

    def line(self, k):
        return (self.d, self.rank_at(k))

    def meet(self, all_dp=False):
        barrier = pltpu.get_barrier_semaphore()
        if all_dp:
            peers = [self.across(k) for k in range(1, 2 * self.chips)]
        else:
            peers = [self.sibling()]
            peers += [self.plane(k) for k in range(1, self.chips)]
        peers += [self.line(k) for k in range(1, self.ranks)]
        for peer in peers:
            pl.semaphore_signal(barrier, inc=1, device_id=peer, device_id_type=pl.DeviceIdType.MESH)
        pl.semaphore_wait(barrier, len(peers))


def send(src, dst, sems, place, peer):
    copy = pltpu.make_async_remote_copy(
        src_ref=src,
        dst_ref=dst,
        send_sem=sems.at[(0,) + place],
        recv_sem=sems.at[(1,) + place],
        device_id=peer,
        device_id_type=pl.DeviceIdType.MESH,
    )
    copy.start()
    return copy


def word_scores(q, k, diagonal):
    scores = dot_tn(k, q) * (D // HEADS) ** -0.5
    if diagonal:
        scores = jnp.where(iota(scores.shape, 0) <= iota(scores.shape, 1), scores, NEG_FILL)
    return scores


def head_rows(ref, n, part, kind):
    head = D // HEADS
    return ref[n, part, kind * head : (kind + 1) * head, :]


def word_attention(n, triple_ref, mixed_ref, lse_ref):
    for i in range(triple_ref.shape[1]):
        q = head_rows(triple_ref, n, i, 0)
        scores = [word_scores(q, head_rows(triple_ref, n, j, 1), i == j) for j in range(i + 1)]
        highest = jnp.max(scores[0], axis=0, keepdims=True)
        for block in scores[1:]:
            highest = jnp.maximum(highest, jnp.max(block, axis=0, keepdims=True))
        powers = [jnp.exp(block - highest) for block in scores]
        total = jnp.sum(powers[0], axis=0, keepdims=True)
        for block in powers[1:]:
            total = total + jnp.sum(block, axis=0, keepdims=True)
        inverse = 1.0 / total
        mixed = None
        for j, block in enumerate(powers):
            part = dot_nn(head_rows(triple_ref, n, j, 2), (block * inverse).astype(jnp.bfloat16))
            mixed = part if mixed is None else mixed + part
        mixed_ref[n, i] = mixed.astype(jnp.bfloat16)
        lse_ref[n, i] = jnp.broadcast_to(highest + jnp.log(total), lse_ref.shape[2:])


def word_attention_back(n, triple_ref, lse_ref, grad_ref, out_ref, dk, dv):
    parts = triple_ref.shape[1]
    head = D // HEADS
    for i in range(parts):
        q = head_rows(triple_ref, n, i, 0)
        grad_o = grad_ref[n, i]
        lse = lse_ref[n, i][:1]
        probs, grads = [], []
        dot_sum = None
        for j in range(i + 1):
            scores = word_scores(q, head_rows(triple_ref, n, j, 1), i == j)
            probs.append(jnp.exp(scores - lse))
            grads.append(dot_tn(head_rows(triple_ref, n, j, 2), grad_o))
            part = jnp.sum(probs[-1] * grads[-1], axis=0, keepdims=True)
            dot_sum = part if dot_sum is None else dot_sum + part
        grad_q = None
        for j in range(i + 1):
            raw = (probs[j] * (grads[j] - dot_sum) * head**-0.5).astype(jnp.bfloat16)
            part = dot_nn(head_rows(triple_ref, n, j, 1), raw)
            grad_q = part if grad_q is None else grad_q + part
            part_k = dot_nt(q, raw)
            part_v = dot_nt(grad_o, probs[j].astype(jnp.bfloat16))
            if i == j:
                dk[j] = part_k
                dv[j] = part_v
            else:
                dk[j] += part_k
                dv[j] += part_v
        out_ref[n, i, :head, :] = grad_q.astype(jnp.bfloat16)
    for j in range(parts):
        out_ref[n, j, head : 2 * head, :] = dk[j].astype(jnp.bfloat16)
        out_ref[n, j, 2 * head :, :] = dv[j].astype(jnp.bfloat16)


def swap_copies(ring, src, dst, n, sems):
    return [
        pltpu.make_async_remote_copy(
            src_ref=src.at[n, ring.rank_at(k)],
            dst_ref=dst.at[n, ring.h],
            send_sem=sems.at[0, n, k],
            recv_sem=sems.at[1, n, k],
            device_id=ring.line(k),
            device_id_type=pl.DeviceIdType.MESH,
        )
        for k in range(1, ring.ranks)
    ]


def swap_start(ring, src, dst, n, sems):
    for copy in swap_copies(ring, src, dst, n, sems):
        copy.start()
    dst[n, ring.h] = src[n, ring.h]


def swap_wait(ring, src, dst, n, sems):
    wait_all(swap_copies(ring, src, dst, n, sems))


def wait_all(copies):
    for copy in copies:
        copy.wait()


def word_kernel(dp, ranks, *refs):
    (sum_ref, count_ref, words_ref, cot_ref, in_ref, early_ref, g3_ref, g4_ref) = refs[:8]
    up_rows, down_rows = refs[8:10]
    (output_ref, input_grad_ref, spread_ref, d_qkv, d_pool, d_g3, d_g4) = refs[10:17]
    sums = refs[17:20]
    (starts, pooleds, afters, lses, up_ref, down_ref) = refs[20:26]
    (acts, hiddens, grad_ups, cots, lows, mixes, triples) = refs[26:33]
    (triple_ref, triple_in, triple_back, mixed_ref, mixed_in, mixed_back) = refs[33:39]
    dk, dv = refs[39:41]
    grads, pair_in, plane_in = refs[41:44], refs[44:47], refs[47:50]
    (own_sem, late_sem, late_pair_sem) = refs[50:53]
    (triple_sem, mixed_sem, mixed_back_sem, triple_back_sem, pair_sem, plane_sem) = refs[53:]
    ring = Ring(dp, ranks)
    chips = ring.chips
    f32, bf16 = jnp.float32, jnp.bfloat16
    ring.meet()
    seqs, width, _ = words_ref.shape
    hidden_size = up_ref.shape[1]
    head = D // HEADS
    heads = HEADS // ranks
    count = seqs * heads
    g3, g4 = lane_copies(g3_ref, width), lane_copies(g4_ref, width)

    wide = early_ref.shape[1]

    def late_place(m, d):
        ref = (up_ref, down_ref)[m]
        rows = ref.shape[0] // dp
        return ref.at[pl.ds(pl.multiple_of(d * rows, rows), rows), :]

    late = (up_rows.at[:, wide:], down_rows)
    own, rounds, late_pairs = [], [], []
    for m in range(2):
        place = late_place(m, ring.d)
        own.append(pltpu.make_async_copy(late[m], place, own_sem.at[m]))
        own[-1].start()
        rounds.append(
            [send(late[m], place, late_sem, (m, k), ring.plane(k)) for k in range(1, chips)]
        )
        late_pairs.append(send(late[m], place, late_pair_sem, (m, 0), ring.sibling()))

    for s in range(seqs):
        pooled = (sum_ref[s] / count_ref[s : s + 1, :].astype(f32)).astype(bf16)
        pooleds[s] = pooled
        start = words_ref[s].astype(f32).T + dot_tn(in_ref[:, 4 * CD + CFF :], pooled)
        starts[s] = start
        act = (column_rms(start)[0] * g3).astype(bf16)
        for t in range(3):
            triple = dot_tn(early_ref[:, t * D : (t + 1) * D], act).astype(bf16)
            for r in range(ranks):
                for h in range(heads):
                    at = (r * heads + h) * head
                    triple_ref[s * heads + h, r, t * head : (t + 1) * head, :] = triple[
                        at : at + head
                    ]
        for h in range(heads):
            swap_start(ring, triple_ref, triple_in, s * heads + h, triple_sem)
    for m in range(2):
        for k in range(1, chips):
            rounds[m][k - 1].wait_recv()
            block = late_place(m, 2 * ring.chip_from(k) + ring.core)
            late_pairs.append(send(block, block, late_pair_sem, (m, k), ring.sibling()))

    def attend(n, carry):
        swap_wait(ring, triple_ref, triple_in, n, triple_sem)
        word_attention(n, triple_in, mixed_ref, lses)
        swap_start(ring, mixed_ref, mixed_in, n, mixed_sem)
        return carry

    def attend_back(n, carry):
        swap_wait(ring, mixed_ref, mixed_back, n, mixed_back_sem)
        word_attention_back(n, triple_in, lses, mixed_back, triple_ref, dk, dv)
        swap_start(ring, triple_ref, triple_back, n, triple_back_sem)
        return carry

    pairs, planes = {}, {}

    def put_grad(i, value):
        grads[i][...] = value.astype(bf16).reshape(grads[i].shape)
        pairs[i] = send(
            grads[i].at[:, 1 - ring.core], pair_in[i], pair_sem, (i,), ring.sibling()
        )

    def pass_on(i):
        pairs[i].wait()

        def add_pair(p, carry):
            both = grads[i][p, ring.core].astype(f32) + pair_in[i][p].astype(f32)
            pair_in[i][p] = both.astype(bf16)
            return carry

        lax.fori_loop(0, chips, add_pair, 0)
        planes[i] = [
            send(
                pair_in[i].at[ring.chip_at(k)], plane_in[i].at[k], plane_sem, (i, k), ring.plane(k)
            )
            for k in range(1, chips)
        ]

    lax.fori_loop(0, count - 1, attend, 0)
    gain = None
    for s in range(seqs):
        if s == 0:
            for m in range(2):
                own[m].wait()
                for copy in rounds[m]:
                    copy.wait_send()
            wait_all(late_pairs)
        if s == seqs - 1:
            attend(count - 1, 0)
        lanes = slice(s * width, (s + 1) * width)
        for h in range(heads):
            n = s * heads + h
            swap_wait(ring, mixed_ref, mixed_in, n, mixed_sem)
            for r in range(ranks):
                at = (r * heads + h) * head
                mixes[at : at + head, lanes] = mixed_in[n, r]
        after = starts[s] + dot_tn(early_ref[:, 3 * D :], mixes[:, lanes])
        normed, inverse = column_rms(after)
        act = (normed * g4).astype(bf16)
        acts[:, lanes] = act
        cot = cot_ref[s].astype(f32).T
        cot_low = cot.astype(bf16)
        cots[:, lanes] = cot_low
        result, grad = after, None
        for c in range(hidden_size // D):
            rows = slice(c * D, (c + 1) * D)
            hidden, slope = gelu_pair(dot_tn(up_ref[:, rows], act))
            hidden = hidden.astype(bf16)
            hiddens[rows, lanes] = hidden
            result = result + dot_tn(down_ref[rows, :], hidden)
            grad_upper = (dot_nn(down_ref[rows, :], cot_low) * slope).astype(bf16)
            grad_ups[rows, lanes] = grad_upper
            piece = dot_nn(up_ref[:, rows], grad_upper)
            grad = piece if grad is None else grad + piece
        piece = fold_lanes(grad * normed)
        gain = piece if gain is None else gain + piece
        total = cot + column_rms_back(grad, g4, normed, inverse)
        afters[s] = total
        low = total.astype(bf16)
        lows[:, lanes] = low
        mixed = dot_nn(early_ref[:, 3 * D :], low).astype(bf16)
        for h in range(heads):
            n = s * heads + h
            for r in range(ranks):
                at = (r * heads + h) * head
                mixed_ref[n, r] = mixed[at : at + head]
            swap_start(ring, mixed_ref, mixed_back, n, mixed_back_sem)
        output_ref[s] = result.T.astype(bf16)
    d_g4[...] = gain
    attend_back(0, 0)
    put_grad(0, dot_nt(hiddens[...], cots[...]))
    lax.fori_loop(1, heads, attend_back, 0)
    pass_on(0)
    lax.fori_loop(heads, count, attend_back, 0)
    put_grad(1, dot_nt(acts[...], grad_ups[...]))
    put_grad(2, dot_nt(mixes[...], lows[...]))
    pass_on(1)
    pass_on(2)
    gain = None
    for s in range(seqs):
        lanes = slice(s * width, (s + 1) * width)
        for h in range(heads):
            n = s * heads + h
            swap_wait(ring, triple_ref, triple_back, n, triple_back_sem)
            for t in range(3):
                for r in range(ranks):
                    at = t * D + (r * heads + h) * head
                    triples[at : at + head, lanes] = head_rows(triple_back, n, r, t)
        normed, inverse = column_rms(starts[s])
        acts[:, lanes] = (normed * g3).astype(bf16)
        grad = dot_nn(early_ref[:, : 3 * D], triples[:, lanes])
        piece = fold_lanes(grad * normed)
        gain = piece if gain is None else gain + piece
        total = afters[s] + column_rms_back(grad, g3, normed, inverse)
        input_grad_ref[s] = total.T
        low = total.astype(bf16)
        lows[:, lanes] = low
        high, rest = split_two(
            dot_nn(in_ref[:, 4 * CD + CFF :], low) / count_ref[s : s + 1, :].astype(f32)
        )
        spread_ref[s, :CD, :] = high
        spread_ref[s, CD:, :] = rest
    d_g3[...] = gain
    d_qkv[...] = dot_nt(acts[...], triples[...]).astype(bf16)
    d_pool[...] = sum(
        dot_nt(pooleds[s], lows[:, s * width : (s + 1) * width]) for s in range(seqs)
    ).astype(bf16)
    for i in range(3):
        total = pair_in[i][ring.chip].astype(f32)
        for k in range(1, chips):
            planes[i][k - 1].wait()
            total = total + plane_in[i][k].astype(f32)
        sums[i][...] = total.astype(bf16)


def word_layer(sums, counts, words, cot, char_in, early, gains, up_rows, down_rows, collective):
    dp, ranks = lax.axis_size("dp"), lax.axis_size("head")
    seqs, width, _ = words.shape
    hidden = up_rows.shape[1] - early.shape[1]
    chips = dp // 2
    bf16, f32 = jnp.bfloat16, jnp.float32
    vmem = pl.BlockSpec(memory_space=pltpu.VMEM)
    anywhere = pl.BlockSpec(memory_space=pl.ANY)
    rows = ((hidden // dp, D), (D // dp, hidden), (D // dp, D))
    columns = seqs * width
    count, head = seqs * HEADS // ranks, D // HEADS
    triple, mixed = (count, ranks, 3 * head, width), (count, ranks, head, width)
    dma = pltpu.SemaphoreType.DMA
    shapes = [
        ((seqs, width, D), bf16),
        ((seqs, width, D), f32),
        ((seqs, 2 * CD, width), bf16),
        ((D, 3 * D), bf16),
        ((CD, D), bf16),
        ((D, GROUP), f32),
        ((D, GROUP), f32),
    ] + [(r, bf16) for r in rows]
    held = [
        ((seqs, D, width), f32),
        ((seqs, CD, width), bf16),
        ((seqs, D, width), f32),
        ((count, ranks, 8, width), f32),
        ((D, hidden), bf16),
        ((hidden, D), bf16),
        ((D, columns), bf16),
        ((hidden, columns), bf16),
        ((hidden, columns), bf16),
        ((D, columns), bf16),
        ((D, columns), bf16),
        ((D, columns), bf16),
        ((3 * D, columns), bf16),
    ]
    held += [(triple, bf16)] * 3 + [(mixed, bf16)] * 3 + [((ranks, head, width), f32)] * 2
    held += [((chips, 2) + r, bf16) for r in rows] + [((chips,) + r, bf16) for r in rows] * 2
    return pl.pallas_call(
        functools.partial(word_kernel, dp, ranks),
        in_specs=[vmem] * 8 + [anywhere] * 2,
        out_specs=[vmem] * len(shapes),
        out_shape=[jax.ShapeDtypeStruct(shape, kind) for shape, kind in shapes],
        scratch_shapes=[pltpu.VMEM(shape, kind) for shape, kind in held]
        + [dma((2,)), dma((2, 2, chips)), dma((2, 2, chips))]
        + [dma((2, count, ranks))] * 4
        + [dma((2, 3)), dma((2, 3, chips))],
        compiler_params=pltpu.CompilerParams(
            collective_id=collective, has_side_effects=True, vmem_limit_bytes=VMEM_BYTES
        ),
        name="word_layer",
    )(sums, counts, words, cot, char_in, early, *gains, up_rows, down_rows)


def block_of(ref, d, h, shard):
    if len(ref.shape) == 4:
        return ref.at[d, h]
    rows, cols = shard.shape
    return ref.at[
        pl.ds(pl.multiple_of(h * rows, rows), rows), pl.ds(pl.multiple_of(d * cols, cols), cols)
    ]


def rows_of(ref, d, shard):
    if len(ref.shape) > 2:
        return ref.at[d]
    cols = shard.shape[1]
    return ref.at[:, pl.ds(pl.multiple_of(d * cols, cols), cols)]


def gather_kernel(dp, ranks, *refs):
    shards, (counts_ref, ids_ref, gains_ref) = refs[:5], refs[5:8]
    outs, (pack_ref, tiles_ref), gain_refs = refs[8:14], refs[14:16], refs[16:20]
    low = refs[20:25]
    own_sem, line_sem, plane_sem, pair_sem, copy_sem = refs[25:]
    table, char_in, down, early, word_rows, down_rows = outs
    ring = Ring(dp, ranks)
    for shard, ref in zip(shards, low):
        ref[...] = shard[...].astype(jnp.bfloat16)
    ring.meet()

    def column(ref, like):
        wide = like.shape[1]
        return ref.at[:, pl.ds(pl.multiple_of(ring.h * wide, GROUP), wide)]

    places = (
        block_of(table, ring.d, ring.h, low[0]),
        column(char_in.at[ring.d], low[1]),
        block_of(down, ring.d, ring.h, low[2]),
        column(word_rows, low[3]),
        column(down_rows, low[4]),
    )
    own, first = [], []

    def along_line(m):
        own.append(pltpu.make_async_copy(low[m], places[m], own_sem.at[m]))
        own[m].start()
        first.append(
            [send(low[m], places[m], line_sem, (m, k), ring.line(k)) for k in range(1, ranks)]
        )

    def arrived(m):
        own[m].wait()
        for copy in first[m]:
            copy.wait_recv()

    blocks = (table, char_in, down, early)
    second, sent = [], []

    def onward(m, block):
        place = rows_of(blocks[m], ring.d, low[m])
        second.append(
            [send(block, place, plane_sem, (m, k), ring.plane(k)) for k in range(1, ring.chips)]
        )
        sent.append(send(block, place, pair_sem, (m, 0), ring.sibling()))

    for m in range(3):
        along_line(m)
    for seq in range(ids_ref.shape[0]):
        pack_words(counts_ref[seq : seq + 1, :], ids_ref[seq], pack_ref, tiles_ref, seq)
    row = 0
    for ref in gain_refs:
        for at in range(0, ref.shape[0], GROUP):
            gain = jnp.broadcast_to(gains_ref[row : row + 1, :], (GROUP, GROUP))
            ref[at : at + GROUP, :] = gain.T
            row += 1
    for m in range(3):
        arrived(m)
        onward(m, rows_of(blocks[m], ring.d, low[m]))
    along_line(3)
    along_line(4)
    arrived(3)
    block = word_rows.at[:, : early.shape[2]]
    copy = pltpu.make_async_copy(block, early.at[ring.d], copy_sem)
    copy.start()
    onward(3, block)
    for m in range(4):
        for k in range(1, ring.chips):
            second[m][k - 1].wait_recv()
            place = 2 * ring.chip_from(k) + ring.core
            block = rows_of(blocks[m], place, low[m])
            sent.append(send(block, block, pair_sem, (m, k), ring.sibling()))
    arrived(4)
    copy.wait()
    wait_all(sent)
    for m in range(5):
        for copy in first[m]:
            copy.wait_send()
    for m in range(4):
        for copy in second[m]:
            copy.wait_send()


def gather(shards, counts, ids, gains, collective):
    dp, ranks = lax.axis_size("dp"), lax.axis_size("head")
    bf16 = jnp.bfloat16
    vmem = pl.BlockSpec(memory_space=pltpu.VMEM)
    anywhere = pl.BlockSpec(memory_space=pl.ANY)
    table, char_in, down, word_in, word_down = (s.shape for s in shards)
    dma = pltpu.SemaphoreType.DMA

    def narrow(shape):
        if shape[1] % GROUP == 0:
            return (ranks * shape[0], dp * shape[1])
        return (dp, ranks) + shape

    seqs, slots, words = ids.shape
    outs = [
        narrow(table),
        (dp, char_in[0], ranks * char_in[1]),
        narrow(down),
        (dp, word_in[0], 4 * D),
        (word_in[0], ranks * word_in[1]),
        (word_down[0], ranks * word_down[1]),
    ]
    return pl.pallas_call(
        functools.partial(gather_kernel, dp, ranks),
        in_specs=[vmem] * 8,
        out_specs=[anywhere] * 6 + [vmem, pl.BlockSpec(memory_space=pltpu.SMEM)] + [vmem] * 4,
        out_shape=[jax.ShapeDtypeStruct(s, bf16) for s in outs]
        + [
            jax.ShapeDtypeStruct((seqs, 4, tile_count(words) * (ROWS // GROUP), GROUP), jnp.int32),
            jax.ShapeDtypeStruct((seqs,), jnp.int32),
        ]
        + [jax.ShapeDtypeStruct((n, GROUP), jnp.float32) for n in (CD, CD, D, D)],
        scratch_shapes=[pltpu.VMEM(s.shape, bf16) for s in shards]
        + [
            dma((5,)),
            dma((2, 5, ranks)),
            dma((2, 4, dp // 2)),
            dma((2, 4, dp // 2)),
            dma(()),
        ],
        compiler_params=pltpu.CompilerParams(
            collective_id=collective, has_side_effects=True, vmem_limit_bytes=VMEM_BYTES
        ),
        name="gather",
    )(*shards, counts, ids, gains)


def column_cuts(widths, ranks):
    block = sum(widths) // ranks
    cuts, start = [], 0
    for width in widths:
        mine, at = [], 0
        while at < width:
            rank, inside = divmod(start + at, block)
            take = min(width - at, block - inside)
            mine.append((rank, at, at + take, inside))
            at += take
        cuts.append(mine)
        start += width
    return cuts


def reduce_kernel(dp, ranks, groups, extra, *refs):
    pieces = sum(len(g) - done for g, done in groups)
    mats = len(groups)
    parts = refs[:pieces]
    gain_refs = refs[pieces : pieces + 4]
    ready = refs[pieces + 4 : pieces + 4 + extra]
    place = pieces + 4 + extra
    outs = refs[place : place + mats]
    gain_out, square_out = refs[place + mats : place + mats + 2]
    place += mats + 2
    pair_in = refs[place : place + pieces]
    pair_sum = refs[place + pieces : place + 2 * pieces]
    plane_in = refs[place + 2 * pieces : place + 3 * pieces]
    place += 3 * pieces
    line_sum, line_in = refs[place : place + mats], refs[place + mats : place + 2 * mats]
    place += 2 * mats
    small, pair_sem, plane_sem, line_sem, small_sem = refs[place:]
    ring = Ring(dp, ranks)
    chips = ring.chips
    f32, bf16 = jnp.float32, jnp.bfloat16
    ring.meet(all_dp=True)

    def share(slot, value, stage):
        peer, here, count = ((ring.across, ring.d, dp), (ring.line, ring.h, ranks))[stage]
        small[slot, stage, here] = value
        spot = small.at[slot, stage, here]
        return [send(spot, spot, small_sem, (slot, stage, k), peer(k)) for k in range(1, count)]

    def shared(slot, copies, stage):
        wait_all(copies)
        total = small[slot, stage, 0]
        for k in range(1, (dp, ranks)[stage]):
            total = total + small[slot, stage, k]
        return total

    def line_copy(m, k):
        return pltpu.make_async_remote_copy(
            src_ref=line_sum[m].at[ring.rank_at(k)],
            dst_ref=line_in[m].at[k],
            send_sem=line_sem.at[0, m, k],
            recv_sem=line_sem.at[1, m, k],
            device_id=ring.line(k),
            device_id_type=pl.DeviceIdType.MESH,
        )

    def put_columns(m, cuts, total):
        for rank, first, last, inside in cuts:
            line_sum[m][rank, :, inside : inside + last - first] = total[:, first:last]

    def early_rank(m):
        widths, done = groups[m]
        own = sum(widths[: len(widths) - done])
        ready_from = sum(
            w for at, w in enumerate(widths) if at < len(widths) - done
        ) if done else sum(widths)
        block = sum(widths) // ranks
        return -(-max(own, ready_from) // block)

    def begin(copy, now, first):
        if first == 0:
            copy.start()
        elif first < ranks:
            pl.when(now)(copy.start)

    pairs = [
        send(parts[i].at[:, 1 - ring.core], pair_in[i], pair_sem, (i,), ring.sibling())
        for i in range(pieces)
    ]
    starts = []
    j = 0
    for m, (widths, done) in enumerate(groups):
        lines = [line_copy(m, k) for k in range(1, ranks)]
        starts.append(lines)
        cuts = column_cuts(widths, ranks)
        for at in range(len(widths) - done, len(widths)):
            put_columns(m, cuts[at], ready[j][...])
            j += 1
        for k in range(1, ranks):
            begin(lines[k - 1], early_rank(m) <= ring.rank_at(k), early_rank(m))
    rows = []
    for ref in gain_refs:
        for at in range(0, ref.shape[0], GROUP):
            rows.append(jnp.sum(ref[at : at + GROUP, :].T, axis=0, keepdims=True))
    rows.append(jnp.zeros((small.shape[3] - len(rows), GROUP), f32))
    gain_copies = share(0, jnp.concatenate(rows, axis=0), 0)
    planes = []
    for i in range(pieces):
        pairs[i].wait()

        def add_pair(p, carry, i=i):
            both = parts[i][p, ring.core].astype(f32) + pair_in[i][p].astype(f32)
            pair_sum[i][p] = both.astype(bf16)
            return carry

        lax.fori_loop(0, chips, add_pair, 0)
        planes.append(
            [
                send(
                    pair_sum[i].at[ring.chip_at(k)],
                    plane_in[i].at[k],
                    plane_sem,
                    (i, k),
                    ring.plane(k),
                )
                for k in range(1, chips)
            ]
        )
    gain_copies = share(0, shared(0, gain_copies, 0), 1)
    i = 0
    for m, (widths, done) in enumerate(groups):
        for cuts in column_cuts(widths, ranks)[: len(widths) - done]:
            total = pair_sum[i][ring.chip].astype(f32)
            for k in range(1, chips):
                planes[i][k - 1].wait()
                total = total + plane_in[i][k].astype(f32)
            put_columns(m, cuts, total.astype(bf16))
            i += 1
        first = early_rank(m)
        for k in range(1, ranks):
            if first >= ranks:
                starts[m][k - 1].start()
            elif first > 0:
                pl.when(ring.rank_at(k) < first)(starts[m][k - 1].start)
    square = jnp.zeros(square_out.shape, f32)

    def squares(value):
        value = value * value
        rows, cols = value.shape
        if cols % GROUP:
            value = jnp.concatenate([value, jnp.zeros((rows, GROUP - cols % GROUP), f32)], axis=1)
        return jnp.sum(fold_lanes(value).reshape(rows // 8, 8, GROUP), axis=0)

    for m in range(mats):
        total = line_sum[m][ring.h].astype(f32)
        for k in range(1, ranks):
            starts[m][k - 1].wait()
            total = total + line_in[m][k].astype(f32)
        outs[m][...] = total if outs[m].shape == total.shape else total.T
        square = square + squares(total)
    small_square = jnp.concatenate([square, jnp.zeros_like(square)], axis=0)
    square_copies = share(1, small_square, 0)
    gain_out[...] = shared(0, gain_copies, 1)[: gain_out.shape[0]]
    square_copies = share(1, shared(1, square_copies, 0), 1)
    square_out[...] = shared(1, square_copies, 1)[:8]


def reduce_grads(groups, gains, collective):
    dp, ranks = lax.axis_size("dp"), lax.axis_size("head")
    chips = dp // 2
    bf16, f32 = jnp.bfloat16, jnp.float32
    pieces, ready, widths, shards = [], [], [], []
    for group, done in groups:
        rows = done[0].shape[0] if done else group[0].shape[0] // dp
        pieces += [p.reshape(chips, 2, rows, p.shape[1]) for p in group]
        ready += done
        widths.append((tuple(p.shape[1] for p in group + done), len(done)))
        shards.append((rows, sum(widths[-1][0]) // ranks))
    blocks = [p.shape[2:] for p in pieces]
    vmem = pl.BlockSpec(memory_space=pltpu.VMEM)
    n, mats = len(pieces), len(groups)
    gain_rows = sum(g.shape[0] for g in gains) // GROUP
    return pl.pallas_call(
        functools.partial(reduce_kernel, dp, ranks, widths, len(ready)),
        in_specs=[vmem] * (n + 4 + len(ready)),
        out_specs=[vmem] * (mats + 2),
        out_shape=[jax.ShapeDtypeStruct(s if s[1] % GROUP == 0 else s[::-1], f32) for s in shards]
        + [jax.ShapeDtypeStruct((gain_rows, GROUP), f32), jax.ShapeDtypeStruct((8, GROUP), f32)],
        scratch_shapes=[pltpu.VMEM((chips,) + b, bf16) for b in blocks] * 3
        + [pltpu.VMEM((ranks,) + s, bf16) for s in shards] * 2
        + [
            pltpu.VMEM((2, 2, max(dp, ranks), 16, GROUP), f32),
            pltpu.SemaphoreType.DMA((2, n)),
            pltpu.SemaphoreType.DMA((2, n, chips)),
            pltpu.SemaphoreType.DMA((2, mats, ranks)),
            pltpu.SemaphoreType.DMA((2, 2, 2, max(dp, ranks))),
        ],
        compiler_params=pltpu.CompilerParams(
            collective_id=collective, has_side_effects=True, vmem_limit_bytes=VMEM_BYTES
        ),
        name="reduce_grads",
    )(*pieces, *gains, *ready)


def update_kernel(count, *refs):
    weights, grads = refs[:count], refs[count : 2 * count]
    firsts, seconds = refs[2 * count : 3 * count], refs[3 * count : 4 * count]
    square_ref = refs[4 * count]
    norm_ref, outs = refs[4 * count + 1], refs[4 * count + 2 :]
    gain_grad = grads[-1][...]
    square = jnp.sum(square_ref[...]) + jnp.sum(gain_grad * gain_grad)
    norm = jnp.sqrt(jnp.full((1, GROUP), square, jnp.float32))
    norm_ref[...] = norm
    clip_factor = jnp.minimum(1.0, CLIP / norm)[:, :1]
    for i in range(count):
        gains = i == count - 1
        result = adam_step(
            weights[i][...],
            grads[i][...],
            firsts[i][...],
            seconds[i][...],
            clip_factor,
            GAIN_RATE if gains else MATRIX_RATE,
            0.0 if gains else MATRIX_DECAY,
        )
        for ref, value in zip(outs[5 * i : 5 * i + 5], result):
            ref[...] = value


def update(weights, grads, firsts, seconds, square):
    count = len(weights)
    shapes = [jax.ShapeDtypeStruct((1, GROUP), jnp.float32)]
    for w in weights:
        shapes += [jax.ShapeDtypeStruct(w.shape, jnp.float32)] * 4
        shapes.append(jax.ShapeDtypeStruct(w.shape, jnp.bfloat16))
    return pl.pallas_call(
        functools.partial(update_kernel, count),
        out_shape=shapes,
        compiler_params=pltpu.CompilerParams(vmem_limit_bytes=VMEM_BYTES),
        name="update",
    )(*weights, *grads, *firsts, *seconds, square)


def body(
    char_ids,
    char_counts,
    language,
    words_in,
    out_cotangent,
    char_table,
    char_in,
    char_down,
    word_in,
    word_down,
    norm_gains,
    old_table_first,
    old_table_second,
    old_char_in_first,
    old_char_in_second,
    old_char_down_first,
    old_char_down_second,
    old_word_in_first,
    old_word_in_second,
    old_word_down_first,
    old_word_down_second,
    old_gains_first,
    old_gains_second,
):
    narrow = (norm_gains.shape[0] // GROUP, GROUP)
    table_t, char_in_low, char_down_t, early, up_rows, down_rows, packed, tiles, *gains = gather(
        (char_table.T, char_in, char_down.T, word_in, word_down),
        char_counts,
        char_ids.transpose(0, 2, 1),
        norm_gains.reshape(narrow),
        0,
    )

    def joined(block):
        if block.ndim == 2:
            return block
        dp, ranks, cols, rows = block.shape
        return block.transpose(1, 2, 0, 3).reshape(ranks * cols, dp * rows)

    def stacked(block):
        return block.reshape(-1, block.shape[2])

    table_t = joined(table_t)
    char_in_low, early = stacked(char_in_low), stacked(early)
    char_others = (char_in_low, joined(char_down_t), gains[0], gains[1])
    sums, *kept = char_fwd(tiles, language, packed, table_t, char_others, words_in.shape[1])
    (
        output,
        input_grad,
        spread,
        grad_qkv,
        grad_pool,
        gain_three,
        gain_four,
        down_sum,
        up_sum,
        out_sum,
    ) = word_layer(
        sums,
        char_counts,
        words_in,
        out_cotangent,
        char_in_low,
        early,
        gains[2:],
        up_rows,
        down_rows,
        1,
    )
    grad_table, c_qkv, c_out, c_up, c_down, gain_one, gain_two = char_bwd(
        tiles, language, packed, table_t, char_others, spread, kept
    )
    blocks = lax.all_to_all(
        grad_qkv.reshape(lax.axis_size("dp"), -1, grad_qkv.shape[1]), "dp", 0, 0, tiled=True
    )
    qkv_sum = jnp.sum(blocks.astype(jnp.float32), axis=0).astype(jnp.bfloat16)
    *shards, gains_sum, square = reduce_grads(
        [
            ([grad_table], []),
            ([c_qkv, c_out, c_up, grad_pool], []),
            ([c_down], []),
            ([], [qkv_sum, out_sum, up_sum]),
            ([], [down_sum]),
        ],
        (gain_one, gain_two, gain_three, gain_four),
        2,
    )

    def turned(parts):
        parts = list(parts)
        parts[0], parts[2] = parts[0].T, parts[2].T
        parts[5] = parts[5].reshape(narrow)
        return parts

    norm, *updated = update(
        turned((char_table, char_in, char_down, word_in, word_down, norm_gains)),
        (*shards, gains_sum),
        turned(
            (
                old_table_first,
                old_char_in_first,
                old_char_down_first,
                old_word_in_first,
                old_word_down_first,
                old_gains_first,
            )
        ),
        turned(
            (
                old_table_second,
                old_char_in_second,
                old_char_down_second,
                old_word_in_second,
                old_word_down_second,
                old_gains_second,
            )
        ),
        square,
    )
    for place in (*range(5), *range(10, 15)):
        updated[place] = updated[place].T
    updated[-5:] = [part.reshape(norm_gains.shape) for part in updated[-5:]]
    return (output, input_grad, norm[0, 0], *updated)


def solution(mesh):
    return jax.shard_map(
        body,
        mesh=mesh,
        in_specs=(
            P("dp", "head", None),
            P("dp", "head"),
            P("dp"),
            P("dp", "head", None),
            P("dp", "head", None),
            P("dp", "head"),
            P("dp", "head"),
            P("dp", "head"),
            P("dp", "head"),
            P("dp", "head"),
            P(),
            P("dp", "head"),
            P("dp", "head"),
            P("dp", "head"),
            P("dp", "head"),
            P("dp", "head"),
            P("dp", "head"),
            P("dp", "head"),
            P("dp", "head"),
            P("dp", "head"),
            P("dp", "head"),
            P(),
            P(),
        ),
        out_specs=(
            P("dp", "head", None),
            P("dp", "head", None),
            P(),
            P("dp", "head"),
            P("dp", "head"),
            P("dp", "head"),
            P("dp", "head"),
            P("dp", "head"),
            P("dp", "head"),
            P("dp", "head"),
            P("dp", "head"),
            P("dp", "head"),
            P("dp", "head"),
            P("dp", "head"),
            P("dp", "head"),
            P("dp", "head"),
            P("dp", "head"),
            P("dp", "head"),
            P("dp", "head"),
            P("dp", "head"),
            P("dp", "head"),
            P("dp", "head"),
            P("dp", "head"),
            P("dp", "head"),
            P("dp", "head"),
            P("dp", "head"),
            P("dp", "head"),
            P("dp", "head"),
            P(),
            P(),
            P(),
            P(),
            P(),
        ),
        check_vma=False,
    )
```

```python
import functools

import jax
import jax.numpy as jnp
from jax import lax
from jax.experimental import pallas as pl
from jax.experimental.pallas import tpu as pltpu
from jax.sharding import PartitionSpec as P

D = 512
HEADS = 8
CD = 256
CHEADS = 4
CFF = 1024
CV = 256
STEP = 5


EPS = 1e-05
CLIP = 1.0
MATRIX_RATE = 0.03
GAIN_RATE = 0.25
MATRIX_DECAY = 0.1
BETA_ONE = 0.5
BETA_TWO = 0.5
ADAM_EPS = 1e-08
NEG_FILL = -1e30
SQRT_HALF = 0.7071067811865476
INV_ROOT_TWO_PI = 0.3989422804014327


ROWS = 512
SLOTS = 16
FWD_CHUNK = 512
BWD_CHUNK = 1024
WORD_CHUNK = 512
CHAINS = 1
GROUP = 128
VMEM_BYTES = 56 * 1024 * 1024


def dot_nn(left_side, right_side):
    return lax.dot_general(
        left_side, right_side, (((1,), (0,)), ((), ())), preferred_element_type=jnp.float32
    )


def dot_tn(left_side, right_side):
    return lax.dot_general(
        left_side, right_side, (((0,), (0,)), ((), ())), preferred_element_type=jnp.float32
    )


def dot_nt(left_side, right_side):
    return lax.dot_general(
        left_side, right_side, (((1,), (1,)), ((), ())), preferred_element_type=jnp.float32
    )


def gelu_pair(upper):
    phi = 0.5 + 0.5 * lax.erf(upper * SQRT_HALF)
    bell = jnp.exp(upper * upper * -0.5)
    return upper * phi, phi + upper * (bell * INV_ROOT_TWO_PI)


def iota(shape, dim):
    return lax.broadcasted_iota(jnp.int32, shape, dim)


def split_two(values):
    high = values.astype(jnp.bfloat16)
    return high, (values - high.astype(jnp.float32)).astype(jnp.bfloat16)


def pack_words(row, ids, out_ref, tiles_ref, seq):
    n = row.shape[1]
    col = jnp.broadcast_to(row.astype(jnp.float32), (8, n)).T[:, :1].astype(jnp.int32)
    sub, lane = iota((n, n), 0), iota((n, n), 1)
    ahead = (row > col) | ((row == col) & (lane < sub))
    rank_col = jnp.sum(ahead.astype(jnp.float32), axis=1, keepdims=True).astype(jnp.int32)
    ahead = (col > row) | ((col == row) & (sub < lane))
    rank_row = jnp.sum(ahead.astype(jnp.float32), axis=0, keepdims=True).astype(jnp.int32)
    clash = (rank_col < rank_row) & (col + row > SLOTS)
    alone = jnp.max(jnp.where(clash, rank_col + rank_row, 0).astype(jnp.float32))
    alone = jnp.maximum(alone.astype(jnp.int32) - n + 2, 0)
    partner = n - 1 + alone - rank_row
    second = (rank_row >= alone) & (rank_row > partner)
    bins = jnp.where(second, partner, rank_row)
    here = sub == bins
    first_map = (here & jnp.logical_not(second)).astype(jnp.float32).astype(jnp.bfloat16)
    second_map = (here & second).astype(jnp.float32).astype(jnp.bfloat16)
    pos = lax.rem(iota((GROUP, n), 0), SLOTS)
    word = iota((GROUP, n), 1) + 1
    wide = jnp.broadcast_to(row, (GROUP, n))
    in_first, in_second = pos < wide, pos >= SLOTS - wide

    def kept(mask, values):
        return jnp.where(mask, values, 0).astype(jnp.float32).astype(jnp.bfloat16)

    groups = n * SLOTS // GROUP
    spare = out_ref.shape[2] - groups
    per = GROUP // SLOTS
    own = iota((groups, per, GROUP), 1) == lax.div(iota((groups, per, GROUP), 2), SLOTS)
    back = jnp.concatenate([ids[SLOTS - 1 - j : SLOTS - j] for j in range(SLOTS)] * per, axis=0)
    ids = jnp.concatenate([ids] * per, axis=0)
    zero = jnp.zeros_like(wide)
    for k, (one, two) in enumerate(
        ((ids + 1, back + 1), (word, word), (zero, SLOTS - wide), (wide, zero + SLOTS))
    ):
        full = dot_nt(first_map, kept(in_first, one)) + dot_nt(second_map, kept(in_second, two))
        full = jnp.where(own, full.reshape(groups, per, GROUP), 0.0)
        full = jnp.sum(full, axis=1).astype(jnp.int32)
        if spare:
            full = jnp.concatenate([full, jnp.zeros((spare, GROUP), jnp.int32)], axis=0)
        out_ref[seq, k] = full
    used = alone + lax.div(n - alone + 1, 2)
    tiles_ref[seq] = lax.div(used * SLOTS + ROWS - 1, ROWS)


def lane_map(rows, size):
    spots = iota((size, GROUP), 0) + 1
    maps = [
        (spots == rows[g : g + 1]).astype(jnp.float32).astype(jnp.bfloat16)
        for g in range(rows.shape[0])
    ]
    return jnp.concatenate(maps, axis=1)


def in_step(chains):
    results = [None] * len(chains)
    waiting = list(enumerate(chains))
    running = []
    while waiting or running:
        if waiting:
            running.append(waiting.pop(0))
        for item in list(running):
            try:
                next(item[1])
            except StopIteration as stop:
                results[item[0]] = stop.value
                running.remove(item)
    return results


def lane_copies(ref, width):
    return jnp.concatenate([ref[...]] * (width // GROUP), axis=1)


def column_rms(values):
    inverse = lax.rsqrt(jnp.mean(values * values, axis=0, keepdims=True) + EPS)
    return values * inverse, inverse


def cost(flops, moved, powers):
    return pl.CostEstimate(flops=int(flops), bytes_accessed=int(moved), transcendentals=int(powers))


def tile_count(words):
    return -(-words * SLOTS // ROWS)


def tile_at(step, tiles_ref, seqs):
    seq, start, total = 0, 0, tiles_ref[0]
    for s in range(1, seqs):
        past = step >= total
        seq, start = jnp.where(past, s, seq), jnp.where(past, total, start)
        total = total + tiles_ref[s]
    return seq, step - start, total


def placed(seqs, index):
    def place(step, tiles_ref, language_ref):
        total = tile_at(step, tiles_ref, seqs)[2]
        seq, tile, _ = tile_at(jnp.minimum(step, total - 1), tiles_ref, seqs)
        return index(seq, tile, language_ref)

    return place


def own_block():
    shape = (GROUP // SLOTS, SLOTS, CHEADS * GROUP)
    return iota(shape, 0) == lax.div(lax.rem(iota(shape, 2), GROUP), SLOTS)


def to_compact(block, own):
    return jnp.sum(jnp.where(own, block.reshape(own.shape), 0.0), axis=0)


def from_compact(compact, own):
    wide = jnp.broadcast_to(compact[None], own.shape)
    return jnp.where(own, wide, 0.0).astype(jnp.bfloat16).reshape(GROUP, -1)


def stack_heads(wide):
    return jnp.concatenate([wide[:, h * GROUP : (h + 1) * GROUP] for h in range(CHEADS)], axis=0)


def spread_heads(values):
    head = values.shape[0] // CHEADS
    zero = jnp.zeros((head, GROUP), values.dtype)
    rows = []
    for h in range(CHEADS):
        parts = [zero] * CHEADS
        parts[h] = values[h * head : (h + 1) * head]
        rows.append(jnp.concatenate(parts, axis=1))
    return jnp.concatenate(rows, axis=0)


def char_fwd_kernel(seqs, tiles_ref, language_ref, *refs):
    step = pl.program_id(0)
    _, tile, total = tile_at(step, tiles_ref, seqs)

    @pl.when(step < total)
    def _():
        char_fwd_tile(tile, *refs)


def char_fwd_tile(
    step, pack_ref, table_ref, in_ref, down_ref, g1_ref, g2_ref, pooled_ref,
    keep_values, keep_probs, keep_qkv, keep_mixed, keep_first, keep_hidden, keep_slope,
):
    words = pooled_ref.shape[2]
    per = ROWS // GROUP
    head = CD // CHEADS

    @pl.when(step == 0)
    def _():
        pooled_ref[...] = jnp.zeros_like(pooled_ref)

    own = own_block()
    key_pos = iota((SLOTS, GROUP), 0)
    packs = [pack_ref[0, k, pl.ds(step * per, per), :] for k in range(4)]

    def chain(part):
        groups = per // CHAINS
        cols = slice(part * groups * GROUP, (part + 1) * groups * GROUP)
        size = groups * GROUP
        ids, spots, low_rows, high_rows = (p[part * groups : (part + 1) * groups] for p in packs)
        embedded = dot_nn(table_ref[...], lane_map(ids, CV))
        yield
        act_one = (column_rms(embedded)[0] * lane_copies(g1_ref, size)).astype(jnp.bfloat16)
        triple = dot_tn(in_ref[:, : 3 * CD], act_one).astype(jnp.bfloat16)
        keep_qkv[:, cols] = triple
        yield
        key_rows = triple[CD : 2 * CD].T
        keep_values[cols, :] = triple[2 * CD :].T
        all_probs = []
        for g in range(groups):
            valid = (key_pos >= low_rows[g : g + 1]) & (key_pos < high_rows[g : g + 1])
            valid = jnp.concatenate([valid.astype(jnp.float32)] * CHEADS, axis=1) > 0
            lanes = slice(g * GROUP, (g + 1) * GROUP)
            scores = to_compact(dot_nn(key_rows[lanes], spread_heads(triple[:CD, lanes])), own)
            scores = jnp.where(valid, scores * head**-0.5, NEG_FILL)
            powers = jnp.exp(scores - jnp.max(scores, axis=0, keepdims=True))
            powers = jnp.where(valid, powers, 0.0)
            total = jnp.sum(powers, axis=0, keepdims=True)
            probs = powers / jnp.where(total > 0, total, 1.0)
            wide = (part * groups + g) * CHEADS * GROUP
            keep_probs[:, wide : wide + CHEADS * GROUP] = probs
            all_probs.append(from_compact(probs, own))
        yield
        mixed = []
        for g in range(groups):
            lanes = slice(g * GROUP, (g + 1) * GROUP)
            values = spread_heads(triple[2 * CD :, lanes])
            mixed.append(dot_nn(values, stack_heads(all_probs[g])).astype(jnp.bfloat16))
        mixed = jnp.concatenate(mixed, axis=1)
        keep_mixed[:, cols] = mixed
        yield
        first = embedded + dot_tn(in_ref[:, 3 * CD : 4 * CD], mixed)
        keep_first[:, cols] = first
        act_two = (column_rms(first)[0] * lane_copies(g2_ref, size)).astype(jnp.bfloat16)
        second = first
        for c in range(CFF // FWD_CHUNK):
            yield
            rows = slice(c * FWD_CHUNK, (c + 1) * FWD_CHUNK)
            up = in_ref[:, 4 * CD + c * FWD_CHUNK : 4 * CD + (c + 1) * FWD_CHUNK]
            hidden, slope = gelu_pair(dot_tn(up, act_two))
            hidden = hidden.astype(jnp.bfloat16)
            keep_hidden[rows, cols] = hidden
            keep_slope[rows, cols] = slope.astype(jnp.bfloat16)
            second = second + dot_nn(down_ref[:, rows], hidden)
        yield
        return lane_map(spots, words), split_two(second)

    ends = in_step([chain(part) for part in range(CHAINS)])
    word_map = jnp.concatenate([end[0] for end in ends], axis=1)
    high = jnp.concatenate([end[1][0] for end in ends], axis=1)
    low = jnp.concatenate([end[1][1] for end in ends], axis=1)
    halves = dot_nt(jnp.concatenate([high, low], axis=0), word_map)
    pooled_ref[0] += halves[:CD] + halves[CD:]


KEPT = (
    (3 * CD, jnp.bfloat16),
    (CD, jnp.bfloat16),
    (CD, jnp.float32),
    (CFF, jnp.bfloat16),
    (CFF, jnp.bfloat16),
)


def kept_specs(seqs, count):
    place = placed(seqs, lambda seq, tile, _: (0, seq * count + tile))
    return [
        pl.BlockSpec((ROWS, CD), lambda *at: place(*at)[::-1]),
        pl.BlockSpec((SLOTS, CHEADS * ROWS), place),
    ] + [pl.BlockSpec((depth, ROWS), place) for depth, _ in KEPT]


def kept_shapes(rows):
    return [
        jax.ShapeDtypeStruct((rows, CD), jnp.bfloat16),
        jax.ShapeDtypeStruct((SLOTS, CHEADS * rows), jnp.float32),
    ] + [jax.ShapeDtypeStruct((depth, rows), dtype) for depth, dtype in KEPT]


def whole(array):
    zeros = (0,) * array.ndim
    return pl.BlockSpec(array.shape, lambda *_: zeros)


def char_specs(seqs, pack, others):
    one = (1,) + pack.shape[1:]
    return [
        pl.BlockSpec(one, placed(seqs, lambda seq, tile, _: (seq, 0, 0, 0))),
        pl.BlockSpec((CD, CV), placed(seqs, lambda seq, tile, language: (0, language[seq]))),
    ] + [whole(a) for a in others]


def char_fwd(tiles, language, pack, table, others, words):
    seqs = pack.shape[0]
    count = tile_count(words)
    one = placed(seqs, lambda seq, tile, _: (seq, 0, 0))
    return pl.pallas_call(
        functools.partial(char_fwd_kernel, seqs),
        grid_spec=pltpu.PrefetchScalarGridSpec(
            num_scalar_prefetch=2,
            grid=(seqs * count,),
            in_specs=char_specs(seqs, pack, others),
            out_specs=[pl.BlockSpec((1, CD, words), one)] + kept_specs(seqs, count),
        ),
        out_shape=[jax.ShapeDtypeStruct((seqs, CD, words), jnp.float32)]
        + kept_shapes(seqs * count * ROWS),
        compiler_params=pltpu.CompilerParams(vmem_limit_bytes=VMEM_BYTES),
        cost_estimate=cost(3e10, 6e7, 1e7),
        name="char_fwd",
    )(tiles, language, pack, table, *others)


def fold_lanes(values):
    total = values[:, :GROUP]
    for g in range(1, values.shape[1] // GROUP):
        total = total + values[:, g * GROUP : (g + 1) * GROUP]
    return total


def column_rms_back(grad_in, gain, normed, inverse):
    scaled = grad_in * gain
    return inverse * (scaled - normed * jnp.mean(scaled * normed, axis=0, keepdims=True))


def char_bwd_kernel(seqs, tiles_ref, language_ref, *refs):
    step = pl.program_id(0)
    seq, tile, total = tile_at(step, tiles_ref, seqs)

    @pl.when(step < total)
    def _():
        char_bwd_tile(tile, step == 0, step == total - 1, language_ref[seq] * CV, *refs)


def char_bwd_tile(
    step, at_start, at_end, letter, pack_ref, table_ref, in_ref, down_ref, g1_ref, g2_ref, spread_ref,
    keep_values, keep_probs, keep_qkv, keep_mixed, keep_first, keep_hidden, keep_slope,
    *refs,
):
    results, totals = refs[:7], refs[7:]
    d_table, d_qkv, d_out, d_up, d_down, d_g1, d_g2 = totals
    words = spread_ref.shape[2]
    per = ROWS // GROUP
    head = CD // CHEADS

    @pl.when(at_start)
    def _():
        for ref in totals:
            ref[...] = jnp.zeros_like(ref)

    own = own_block()
    packs = [pack_ref[0, k, pl.ds(step * per, per), :] for k in range(2)]

    def chain(part):
        groups = per // CHAINS
        cols = slice(part * groups * GROUP, (part + 1) * groups * GROUP)
        size = groups * GROUP
        ids, spots = (p[part * groups : (part + 1) * groups] for p in packs)
        halves = dot_nn(spread_ref[0], lane_map(spots, words))
        grad_second = halves[:CD] + halves[CD:]
        grad_branch = grad_second.astype(jnp.bfloat16)
        normed_two, inverse_two = column_rms(keep_first[:, cols])
        gain_two = lane_copies(g2_ref, size)
        act_two = (normed_two * gain_two).astype(jnp.bfloat16)
        grad_uppers = []
        grad_act_two = None
        for c in range(CFF // BWD_CHUNK):
            yield
            rows = slice(c * BWD_CHUNK, (c + 1) * BWD_CHUNK)
            slope = keep_slope[rows, cols].astype(jnp.float32)
            grad_upper = dot_tn(down_ref[:, rows], grad_branch) * slope
            grad_upper = grad_upper.astype(jnp.bfloat16)
            grad_uppers.append(grad_upper)
            piece = dot_nn(in_ref[:, 4 * CD + c * BWD_CHUNK : 4 * CD + (c + 1) * BWD_CHUNK], grad_upper)
            grad_act_two = piece if grad_act_two is None else grad_act_two + piece
        yield
        gain_sum_two = fold_lanes(grad_act_two * normed_two)
        grad_first = grad_second + column_rms_back(
            grad_act_two, gain_two, normed_two, inverse_two
        )
        grad_attn = grad_first.astype(jnp.bfloat16)
        grad_mixed = dot_nn(in_ref[:, 3 * CD : 4 * CD], grad_attn).astype(jnp.bfloat16)
        yield
        triple = keep_qkv[:, cols]
        raws, lows = [], []
        for g in range(groups):
            lanes = slice(g * GROUP, (g + 1) * GROUP)
            at = part * groups + g
            wide = slice(at * CHEADS * GROUP, (at + 1) * CHEADS * GROUP)
            probs = keep_probs[:, wide]
            values = keep_values[at * GROUP : (at + 1) * GROUP, :]
            grad_probs = to_compact(dot_nn(values, spread_heads(grad_mixed[:, lanes])), own)
            grad_scores = probs * (
                grad_probs - jnp.sum(probs * grad_probs, axis=0, keepdims=True)
            )
            raws.append(from_compact(grad_scores * head**-0.5, own))
            lows.append(from_compact(probs, own))
        yield
        columns = []
        for g in range(groups):
            lanes = slice(g * GROUP, (g + 1) * GROUP)
            grad_q = dot_nn(spread_heads(triple[CD : 2 * CD, lanes]), stack_heads(raws[g]))
            grad_k = dot_nt(spread_heads(triple[:CD, lanes]), raws[g])
            grad_v = dot_nt(spread_heads(grad_mixed[:, lanes]), lows[g])
            columns.append(jnp.concatenate([grad_q, grad_k, grad_v], axis=0).astype(jnp.bfloat16))
        grad_triple = jnp.concatenate(columns, axis=1)
        yield
        one_hot = lane_map(ids, CV)
        embedded = dot_nn(table_ref[...], one_hot)
        normed_one, inverse_one = column_rms(embedded)
        gain_one = lane_copies(g1_ref, size)
        act_one = (normed_one * gain_one).astype(jnp.bfloat16)
        grad_act_one = dot_nn(in_ref[:, : 3 * CD], grad_triple)
        yield
        gain_sum_one = fold_lanes(grad_act_one * normed_one)
        back_one = column_rms_back(grad_act_one, gain_one, normed_one, inverse_one)
        grad_embedded = (grad_first + back_one).astype(jnp.bfloat16)
        grad_upper = jnp.concatenate(grad_uppers, axis=0)
        return (
            gain_sum_one, gain_sum_two, grad_branch, act_two, grad_upper, grad_attn,
            act_one, grad_triple, one_hot, grad_embedded,
        )

    ends = in_step([chain(part) for part in range(CHAINS)])
    for end in ends:
        d_g1[...] += end[0]
        d_g2[...] += end[1]
    grad_branch, act_two, grad_upper, grad_attn, act_one, grad_triple, one_hot, grad_embedded = (
        jnp.concatenate(parts, axis=1) for parts in list(zip(*ends))[2:]
    )
    d_down[...] += dot_nt(keep_hidden[...], grad_branch)
    d_up[...] += dot_nt(act_two, grad_upper)
    d_out[...] += dot_nt(keep_mixed[...], grad_attn)
    d_qkv[...] += dot_nt(act_one, grad_triple)
    d_table[pl.ds(pl.multiple_of(letter, CV), CV), :] += dot_nt(one_hot, grad_embedded)

    @pl.when(at_end)
    def _():
        for ref, total in zip(results, totals):
            ref[...] = total[...].astype(ref.dtype)


def char_bwd(tiles, language, pack, table, others, spread, kept):
    shapes = (
        table.shape[::-1],
        (CD, 3 * CD),
        (CD, CD),
        (CD, CFF),
        (CFF, CD),
        (CD, GROUP),
        (CD, GROUP),
    )
    f32, bf16 = jnp.float32, jnp.bfloat16
    kinds = [bf16] * 5 + [f32] * 2
    seqs = pack.shape[0]
    count = tile_count(spread.shape[2])
    one = (1,) + spread.shape[1:]
    return pl.pallas_call(
        functools.partial(char_bwd_kernel, seqs),
        grid_spec=pltpu.PrefetchScalarGridSpec(
            num_scalar_prefetch=2,
            grid=(seqs * count,),
            in_specs=char_specs(seqs, pack, others)
            + [pl.BlockSpec(one, placed(seqs, lambda seq, tile, _: (seq, 0, 0)))]
            + kept_specs(seqs, count),
            out_specs=[pl.BlockSpec(s, lambda *_: (0, 0)) for s in shapes],
            scratch_shapes=[pltpu.VMEM(s, f32) for s in shapes],
        ),
        out_shape=[jax.ShapeDtypeStruct(s, kind) for s, kind in zip(shapes, kinds)],
        compiler_params=pltpu.CompilerParams(vmem_limit_bytes=VMEM_BYTES),
        cost_estimate=cost(5e10, 6e7, 1e6),
        name="char_bwd",
    )(tiles, language, pack, table, *others, spread, *kept)


def adam_step(weight, grad, first_old, second_old, clip_factor, rate, decay):
    clipped = grad * clip_factor
    first_new = BETA_ONE * first_old + (1.0 - BETA_ONE) * clipped
    second_new = BETA_TWO * second_old + (1.0 - BETA_TWO) * clipped * clipped
    first_hat = first_new / (1.0 - BETA_ONE**STEP)
    second_hat = second_new / (1.0 - BETA_TWO**STEP)
    weight_new = weight - rate * (first_hat / (jnp.sqrt(second_hat) + ADAM_EPS) + decay * weight)
    return (grad, first_new, second_new, weight_new, weight_new.astype(jnp.bfloat16))


class Ring:
    def __init__(self, dp, ranks):
        self.chips, self.ranks = dp // 2, ranks
        self.d, self.h = lax.axis_index("dp"), lax.axis_index("head")
        self.chip, self.core = lax.div(self.d, 2), lax.rem(self.d, 2)

    def sibling(self):
        return (self.d + 1 - 2 * self.core, self.h)

    def chip_at(self, k):
        if self.chips != 4:
            return lax.rem(self.chip + k, self.chips)
        return (None, self.chip + 1 - 2 * lax.rem(self.chip, 2), lax.rem(self.chip + 2, 4), 3 - self.chip)[k]

    def chip_from(self, k):
        if self.chips != 4:
            return lax.rem(self.chip + self.chips - k, self.chips)
        return self.chip_at(k)

    def plane(self, k):
        return (2 * self.chip_at(k) + self.core, self.h)

    def across(self, k):
        return (lax.rem(self.d + k, 2 * self.chips), self.h)

    def rank_at(self, k):
        return lax.rem(self.h + k, self.ranks)

    def line(self, k):
        return (self.d, self.rank_at(k))

    def greet(self, all_dp=False):
        barrier = pltpu.get_barrier_semaphore()
        if all_dp:
            peers = [self.across(k) for k in range(1, 2 * self.chips)]
        else:
            peers = [self.sibling()]
            peers += [self.plane(k) for k in range(1, self.chips)]
        peers += [self.line(k) for k in range(1, self.ranks)]
        self.partners = len(peers)
        for peer in peers:
            pl.semaphore_signal(barrier, inc=1, device_id=peer, device_id_type=pl.DeviceIdType.MESH)

    def meet(self):
        pl.semaphore_wait(pltpu.get_barrier_semaphore(), self.partners)


def send(src, dst, sems, place, peer):
    copy = pltpu.make_async_remote_copy(
        src_ref=src,
        dst_ref=dst,
        send_sem=sems.at[(0,) + place],
        recv_sem=sems.at[(1,) + place],
        device_id=peer,
        device_id_type=pl.DeviceIdType.MESH,
    )
    copy.start()
    return copy


def word_scores(q, k, diagonal):
    scores = dot_tn(k, q) * (D // HEADS) ** -0.5
    if diagonal:
        scores = jnp.where(iota(scores.shape, 0) <= iota(scores.shape, 1), scores, NEG_FILL)
    return scores


def head_rows(ref, n, part, kind):
    head = D // HEADS
    return ref[n, part, kind * head : (kind + 1) * head, :]


def word_attention(n, triple_ref, mixed_ref, lse_ref):
    for i in range(triple_ref.shape[1]):
        q = head_rows(triple_ref, n, i, 0)
        scores = [word_scores(q, head_rows(triple_ref, n, j, 1), i == j) for j in range(i + 1)]
        highest = jnp.max(scores[0], axis=0, keepdims=True)
        for block in scores[1:]:
            highest = jnp.maximum(highest, jnp.max(block, axis=0, keepdims=True))
        powers = [jnp.exp(block - highest) for block in scores]
        total = jnp.sum(powers[0], axis=0, keepdims=True)
        for block in powers[1:]:
            total = total + jnp.sum(block, axis=0, keepdims=True)
        inverse = 1.0 / total
        mixed = None
        for j, block in enumerate(powers):
            part = dot_nn(head_rows(triple_ref, n, j, 2), (block * inverse).astype(jnp.bfloat16))
            mixed = part if mixed is None else mixed + part
        mixed_ref[n, i] = mixed.astype(jnp.bfloat16)
        lse_ref[n, i] = jnp.broadcast_to(highest + jnp.log(total), lse_ref.shape[2:])


def word_attention_back(n, triple_ref, lse_ref, grad_ref, out_ref, dk, dv):
    parts = triple_ref.shape[1]
    head = D // HEADS
    for i in range(parts):
        q = head_rows(triple_ref, n, i, 0)
        grad_o = grad_ref[n, i]
        lse = lse_ref[n, i][:1]
        probs, grads = [], []
        dot_sum = None
        for j in range(i + 1):
            scores = word_scores(q, head_rows(triple_ref, n, j, 1), i == j)
            probs.append(jnp.exp(scores - lse))
            grads.append(dot_tn(head_rows(triple_ref, n, j, 2), grad_o))
            part = jnp.sum(probs[-1] * grads[-1], axis=0, keepdims=True)
            dot_sum = part if dot_sum is None else dot_sum + part
        grad_q = None
        for j in range(i + 1):
            raw = (probs[j] * (grads[j] - dot_sum) * head**-0.5).astype(jnp.bfloat16)
            part = dot_nn(head_rows(triple_ref, n, j, 1), raw)
            grad_q = part if grad_q is None else grad_q + part
            part_k = dot_nt(q, raw)
            part_v = dot_nt(grad_o, probs[j].astype(jnp.bfloat16))
            if i == j:
                dk[j] = part_k
                dv[j] = part_v
            else:
                dk[j] += part_k
                dv[j] += part_v
        out_ref[n, i, :head, :] = grad_q.astype(jnp.bfloat16)
    for j in range(parts):
        out_ref[n, j, head : 2 * head, :] = dk[j].astype(jnp.bfloat16)
        out_ref[n, j, 2 * head :, :] = dv[j].astype(jnp.bfloat16)


def swap_copies(ring, src, dst, n, sems):
    return [
        pltpu.make_async_remote_copy(
            src_ref=src.at[n, ring.rank_at(k)],
            dst_ref=dst.at[n, ring.h],
            send_sem=sems.at[0, n, k],
            recv_sem=sems.at[1, n, k],
            device_id=ring.line(k),
            device_id_type=pl.DeviceIdType.MESH,
        )
        for k in range(1, ring.ranks)
    ]


def swap_start(ring, src, dst, n, sems):
    for copy in swap_copies(ring, src, dst, n, sems):
        copy.start()
    dst[n, ring.h] = src[n, ring.h]


def swap_wait(ring, src, dst, n, sems):
    wait_all(swap_copies(ring, src, dst, n, sems))


def wait_all(copies):
    for copy in copies:
        copy.wait()


def word_kernel(dp, ranks, *refs):
    (sum_ref, count_ref, words_ref, cot_ref, in_ref, early_ref, g3_ref, g4_ref) = refs[:8]
    up_rows, down_rows = refs[8:10]
    (output_ref, input_grad_ref, spread_ref, d_qkv, d_pool, d_g3, d_g4) = refs[10:17]
    sums = refs[17:20]
    (starts, pooleds, afters, lses, up_ref, down_ref) = refs[20:26]
    (acts, hiddens, grad_ups, cots, lows, mixes, triples) = refs[26:33]
    (triple_ref, triple_in, triple_back, mixed_ref, mixed_in, mixed_back) = refs[33:39]
    dk, dv = refs[39:41]
    grads, pair_in, plane_in = refs[41:44], refs[44:47], refs[47:50]
    (own_sem, late_sem, late_pair_sem) = refs[50:53]
    (triple_sem, mixed_sem, mixed_back_sem, triple_back_sem, pair_sem, plane_sem) = refs[53:]
    ring = Ring(dp, ranks)
    chips = ring.chips
    f32, bf16 = jnp.float32, jnp.bfloat16
    ring.greet()
    seqs, width, _ = words_ref.shape
    hidden_size = up_ref.shape[1]
    head = D // HEADS
    heads = HEADS // ranks
    count = seqs * heads
    g3, g4 = lane_copies(g3_ref, width), lane_copies(g4_ref, width)

    def begin(s):
        pooled = (sum_ref[s] / count_ref[s : s + 1, :].astype(f32)).astype(bf16)
        pooleds[s] = pooled
        start = words_ref[s].astype(f32).T + dot_tn(in_ref[:, 4 * CD + CFF :], pooled)
        starts[s] = start
        act = (column_rms(start)[0] * g3).astype(bf16)
        for t in range(3):
            triple = dot_tn(early_ref[:, t * D : (t + 1) * D], act).astype(bf16)
            for r in range(ranks):
                for h in range(heads):
                    at = (r * heads + h) * head
                    triple_ref[s * heads + h, r, t * head : (t + 1) * head, :] = triple[
                        at : at + head
                    ]

    def begin_sends(s):
        for h in range(heads):
            swap_start(ring, triple_ref, triple_in, s * heads + h, triple_sem)

    begin(0)
    ring.meet()
    begin_sends(0)

    wide = early_ref.shape[1]

    def late_place(m, d):
        ref = (up_ref, down_ref)[m]
        rows = ref.shape[0] // dp
        return ref.at[pl.ds(pl.multiple_of(d * rows, rows), rows), :]

    late = (up_rows.at[:, wide:], down_rows)
    own, rounds, late_pairs = [], [], []
    for m in range(2):
        place = late_place(m, ring.d)
        own.append(pltpu.make_async_copy(late[m], place, own_sem.at[m]))
        own[-1].start()
        rounds.append(
            [send(late[m], place, late_sem, (m, k), ring.plane(k)) for k in range(1, chips)]
        )
        late_pairs.append(send(late[m], place, late_pair_sem, (m, 0), ring.sibling()))

    for s in range(1, seqs):
        begin(s)
        begin_sends(s)
    for m in range(2):
        for k in range(1, chips):
            rounds[m][k - 1].wait_recv()
            block = late_place(m, 2 * ring.chip_from(k) + ring.core)
            late_pairs.append(send(block, block, late_pair_sem, (m, k), ring.sibling()))

    def attend(n, carry):
        swap_wait(ring, triple_ref, triple_in, n, triple_sem)
        word_attention(n, triple_in, mixed_ref, lses)
        swap_start(ring, mixed_ref, mixed_in, n, mixed_sem)
        return carry

    def attend_back(n, carry):
        swap_wait(ring, mixed_ref, mixed_back, n, mixed_back_sem)
        word_attention_back(n, triple_in, lses, mixed_back, triple_ref, dk, dv)
        swap_start(ring, triple_ref, triple_back, n, triple_back_sem)
        return carry

    pairs, planes = {}, {}

    def put_grad(i, value):
        grads[i][...] = value.astype(bf16).reshape(grads[i].shape)
        pairs[i] = send(
            grads[i].at[:, 1 - ring.core], pair_in[i], pair_sem, (i,), ring.sibling()
        )

    def pass_on(i):
        pairs[i].wait()

        def add_pair(p, carry):
            both = grads[i][p, ring.core].astype(f32) + pair_in[i][p].astype(f32)
            pair_in[i][p] = both.astype(bf16)
            return carry

        lax.fori_loop(0, chips, add_pair, 0)
        planes[i] = [
            send(
                pair_in[i].at[ring.chip_at(k)], plane_in[i].at[k], plane_sem, (i, k), ring.plane(k)
            )
            for k in range(1, chips)
        ]

    lax.fori_loop(0, count - 1, attend, 0)
    gain = None
    for s in range(seqs):
        if s == 0:
            for m in range(2):
                own[m].wait()
                for copy in rounds[m]:
                    copy.wait_send()
            wait_all(late_pairs)
        if s == seqs - 1:
            attend(count - 1, 0)
        lanes = slice(s * width, (s + 1) * width)
        for h in range(heads):
            n = s * heads + h
            swap_wait(ring, mixed_ref, mixed_in, n, mixed_sem)
            for r in range(ranks):
                at = (r * heads + h) * head
                mixes[at : at + head, lanes] = mixed_in[n, r]
        after = starts[s] + dot_tn(early_ref[:, 3 * D :], mixes[:, lanes])
        normed, inverse = column_rms(after)
        act = (normed * g4).astype(bf16)
        acts[:, lanes] = act
        cot = cot_ref[s].astype(f32).T
        cot_low = cot.astype(bf16)
        cots[:, lanes] = cot_low
        result, grad = after, None
        for c in range(hidden_size // WORD_CHUNK):
            rows = slice(c * WORD_CHUNK, (c + 1) * WORD_CHUNK)
            hidden, slope = gelu_pair(dot_tn(up_ref[:, rows], act))
            hidden = hidden.astype(bf16)
            hiddens[rows, lanes] = hidden
            result = result + dot_tn(down_ref[rows, :], hidden)
            grad_upper = (dot_nn(down_ref[rows, :], cot_low) * slope).astype(bf16)
            grad_ups[rows, lanes] = grad_upper
            piece = dot_nn(up_ref[:, rows], grad_upper)
            grad = piece if grad is None else grad + piece
        piece = fold_lanes(grad * normed)
        gain = piece if gain is None else gain + piece
        total = cot + column_rms_back(grad, g4, normed, inverse)
        afters[s] = total
        low = total.astype(bf16)
        lows[:, lanes] = low
        mixed = dot_nn(early_ref[:, 3 * D :], low).astype(bf16)
        for h in range(heads):
            n = s * heads + h
            for r in range(ranks):
                at = (r * heads + h) * head
                mixed_ref[n, r] = mixed[at : at + head]
            swap_start(ring, mixed_ref, mixed_back, n, mixed_back_sem)
        output_ref[s] = result.T.astype(bf16)
    d_g4[...] = gain
    attend_back(0, 0)
    put_grad(0, dot_nt(hiddens[...], cots[...]))
    lax.fori_loop(1, heads, attend_back, 0)
    pass_on(0)
    lax.fori_loop(heads, count, attend_back, 0)
    put_grad(1, dot_nt(acts[...], grad_ups[...]))
    put_grad(2, dot_nt(mixes[...], lows[...]))
    pass_on(1)
    pass_on(2)
    gain = None
    for s in range(seqs):
        lanes = slice(s * width, (s + 1) * width)
        for h in range(heads):
            n = s * heads + h
            swap_wait(ring, triple_ref, triple_back, n, triple_back_sem)
            for t in range(3):
                for r in range(ranks):
                    at = t * D + (r * heads + h) * head
                    triples[at : at + head, lanes] = head_rows(triple_back, n, r, t)
        normed, inverse = column_rms(starts[s])
        acts[:, lanes] = (normed * g3).astype(bf16)
        grad = dot_nn(early_ref[:, : 3 * D], triples[:, lanes])
        piece = fold_lanes(grad * normed)
        gain = piece if gain is None else gain + piece
        total = afters[s] + column_rms_back(grad, g3, normed, inverse)
        input_grad_ref[s] = total.T
        low = total.astype(bf16)
        lows[:, lanes] = low
        high, rest = split_two(
            dot_nn(in_ref[:, 4 * CD + CFF :], low) / count_ref[s : s + 1, :].astype(f32)
        )
        spread_ref[s, :CD, :] = high
        spread_ref[s, CD:, :] = rest
    d_g3[...] = gain
    d_qkv[...] = dot_nt(acts[...], triples[...]).astype(bf16)
    d_pool[...] = sum(
        dot_nt(pooleds[s], lows[:, s * width : (s + 1) * width]) for s in range(seqs)
    ).astype(bf16)
    for i in range(3):
        total = pair_in[i][ring.chip].astype(f32)
        for k in range(1, chips):
            planes[i][k - 1].wait()
            total = total + plane_in[i][k].astype(f32)
        sums[i][...] = total.astype(bf16)


def word_layer(sums, counts, words, cot, char_in, early, gains, up_rows, down_rows, collective):
    dp, ranks = lax.axis_size("dp"), lax.axis_size("head")
    seqs, width, _ = words.shape
    hidden = up_rows.shape[1] - early.shape[1]
    chips = dp // 2
    bf16, f32 = jnp.bfloat16, jnp.float32
    vmem = pl.BlockSpec(memory_space=pltpu.VMEM)
    anywhere = pl.BlockSpec(memory_space=pl.ANY)
    rows = ((hidden // dp, D), (D // dp, hidden), (D // dp, D))
    columns = seqs * width
    count, head = seqs * HEADS // ranks, D // HEADS
    triple, mixed = (count, ranks, 3 * head, width), (count, ranks, head, width)
    dma = pltpu.SemaphoreType.DMA
    shapes = [
        ((seqs, width, D), bf16),
        ((seqs, width, D), f32),
        ((seqs, 2 * CD, width), bf16),
        ((D, 3 * D), bf16),
        ((CD, D), bf16),
        ((D, GROUP), f32),
        ((D, GROUP), f32),
    ] + [(r, bf16) for r in rows]
    held = [
        ((seqs, D, width), f32),
        ((seqs, CD, width), bf16),
        ((seqs, D, width), f32),
        ((count, ranks, 8, width), f32),
        ((D, hidden), bf16),
        ((hidden, D), bf16),
        ((D, columns), bf16),
        ((hidden, columns), bf16),
        ((hidden, columns), bf16),
        ((D, columns), bf16),
        ((D, columns), bf16),
        ((D, columns), bf16),
        ((3 * D, columns), bf16),
    ]
    held += [(triple, bf16)] * 3 + [(mixed, bf16)] * 3 + [((ranks, head, width), f32)] * 2
    held += [((chips, 2) + r, bf16) for r in rows] + [((chips,) + r, bf16) for r in rows] * 2
    return pl.pallas_call(
        functools.partial(word_kernel, dp, ranks),
        in_specs=[vmem] * 8 + [anywhere] * 2,
        out_specs=[vmem] * len(shapes),
        out_shape=[jax.ShapeDtypeStruct(shape, kind) for shape, kind in shapes],
        scratch_shapes=[pltpu.VMEM(shape, kind) for shape, kind in held]
        + [dma((2,)), dma((2, 2, chips)), dma((2, 2, chips))]
        + [dma((2, count, ranks))] * 4
        + [dma((2, 3)), dma((2, 3, chips))],
        compiler_params=pltpu.CompilerParams(
            collective_id=collective, has_side_effects=True, vmem_limit_bytes=VMEM_BYTES
        ),
        name="word_layer",
    )(sums, counts, words, cot, char_in, early, *gains, up_rows, down_rows)


def block_of(ref, d, h, shard):
    if len(ref.shape) == 4:
        return ref.at[d, h]
    rows, cols = shard.shape
    return ref.at[
        pl.ds(pl.multiple_of(h * rows, rows), rows), pl.ds(pl.multiple_of(d * cols, cols), cols)
    ]


def rows_of(ref, d, shard):
    if len(ref.shape) > 2:
        return ref.at[d]
    cols = shard.shape[1]
    return ref.at[:, pl.ds(pl.multiple_of(d * cols, cols), cols)]


def gather_kernel(dp, ranks, *refs):
    shards, (counts_ref, ids_ref, gains_ref) = refs[:5], refs[5:8]
    outs, (pack_ref, tiles_ref), gain_refs = refs[8:14], refs[14:16], refs[16:20]
    low = refs[20:25]
    own_sem, line_sem, plane_sem, pair_sem, copy_sem = refs[25:]
    table, char_in, down, early, word_rows, down_rows = outs
    ring = Ring(dp, ranks)
    ring.greet()
    for shard, ref in zip(shards, low):
        ref[...] = shard[...].astype(jnp.bfloat16)
    ring.meet()

    def column(ref, like):
        wide = like.shape[1]
        return ref.at[:, pl.ds(pl.multiple_of(ring.h * wide, GROUP), wide)]

    places = (
        block_of(table, ring.d, ring.h, low[0]),
        column(char_in.at[ring.d], low[1]),
        block_of(down, ring.d, ring.h, low[2]),
        column(word_rows, low[3]),
        column(down_rows, low[4]),
    )
    own, first = [], []

    def along_line(m):
        own.append(pltpu.make_async_copy(low[m], places[m], own_sem.at[m]))
        own[m].start()
        first.append(
            [send(low[m], places[m], line_sem, (m, k), ring.line(k)) for k in range(1, ranks)]
        )

    def arrived(m):
        own[m].wait()
        for copy in first[m]:
            copy.wait_recv()

    blocks = (table, char_in, down)
    second, sent = [], []

    def onward(m, block):
        place = rows_of(blocks[m], ring.d, low[m])
        second.append(
            [send(block, place, plane_sem, (m, k), ring.plane(k)) for k in range(1, ring.chips)]
        )
        sent.append(send(block, place, pair_sem, (m, 0), ring.sibling()))

    for m in range(3):
        along_line(m)
    for seq in range(ids_ref.shape[0]):
        pack_words(counts_ref[seq : seq + 1, :], ids_ref[seq], pack_ref, tiles_ref, seq)
    row = 0
    for ref in gain_refs:
        for at in range(0, ref.shape[0], GROUP):
            gain = jnp.broadcast_to(gains_ref[row : row + 1, :], (GROUP, GROUP))
            ref[at : at + GROUP, :] = gain.T
            row += 1
    for m in range(3):
        arrived(m)
        onward(m, rows_of(blocks[m], ring.d, low[m]))
    along_line(3)
    along_line(4)
    arrived(3)
    copies = []
    for d in range(dp):
        block = word_rows.at[:, : early.shape[2]]
        copies.append(pltpu.make_async_copy(block, early.at[d], copy_sem.at[d]))
        copies[d].start()
    for m in range(3):
        for k in range(1, ring.chips):
            second[m][k - 1].wait_recv()
            place = 2 * ring.chip_from(k) + ring.core
            block = rows_of(blocks[m], place, low[m])
            sent.append(send(block, block, pair_sem, (m, k), ring.sibling()))
    arrived(4)
    wait_all(sent)
    wait_all(copies)
    for m in range(5):
        for copy in first[m]:
            copy.wait_send()
    for m in range(3):
        for copy in second[m]:
            copy.wait_send()


def gather(shards, counts, ids, gains, collective):
    dp, ranks = lax.axis_size("dp"), lax.axis_size("head")
    bf16 = jnp.bfloat16
    vmem = pl.BlockSpec(memory_space=pltpu.VMEM)
    anywhere = pl.BlockSpec(memory_space=pl.ANY)
    table, char_in, down, word_in, word_down = (s.shape for s in shards)
    dma = pltpu.SemaphoreType.DMA

    def narrow(shape):
        if shape[1] % GROUP == 0:
            return (ranks * shape[0], dp * shape[1])
        return (dp, ranks) + shape

    seqs, slots, words = ids.shape
    outs = [
        narrow(table),
        (dp, char_in[0], ranks * char_in[1]),
        narrow(down),
        (dp, word_in[0], 4 * D),
        (word_in[0], ranks * word_in[1]),
        (word_down[0], ranks * word_down[1]),
    ]
    return pl.pallas_call(
        functools.partial(gather_kernel, dp, ranks),
        in_specs=[vmem] * 8,
        out_specs=[anywhere] * 4 + [vmem, anywhere] + [vmem, pl.BlockSpec(memory_space=pltpu.SMEM)] + [vmem] * 4,
        out_shape=[jax.ShapeDtypeStruct(s, bf16) for s in outs]
        + [
            jax.ShapeDtypeStruct((seqs, 4, tile_count(words) * (ROWS // GROUP), GROUP), jnp.int32),
            jax.ShapeDtypeStruct((seqs,), jnp.int32),
        ]
        + [jax.ShapeDtypeStruct((n, GROUP), jnp.float32) for n in (CD, CD, D, D)],
        scratch_shapes=[pltpu.VMEM(s.shape, bf16) for s in shards]
        + [
            dma((5,)),
            dma((2, 5, ranks)),
            dma((2, 4, dp // 2)),
            dma((2, 4, dp // 2)),
            dma((dp,)),
        ],
        compiler_params=pltpu.CompilerParams(
            collective_id=collective, has_side_effects=True, vmem_limit_bytes=VMEM_BYTES
        ),
        name="gather",
    )(*shards, counts, ids, gains)


def column_cuts(widths, ranks):
    block = sum(widths) // ranks
    cuts, start = [], 0
    for width in widths:
        mine, at = [], 0
        while at < width:
            rank, inside = divmod(start + at, block)
            take = min(width - at, block - inside)
            mine.append((rank, at, at + take, inside))
            at += take
        cuts.append(mine)
        start += width
    return cuts


def reduce_kernel(dp, ranks, groups, extra, *refs):
    pieces = sum(len(g) - done for g, done in groups)
    mats = len(groups)
    parts = refs[:pieces]
    gain_refs = refs[pieces : pieces + 4]
    ready = refs[pieces + 4 : pieces + 4 + extra]
    place = pieces + 4 + extra
    outs = refs[place : place + mats]
    gain_out, square_out = refs[place + mats : place + mats + 2]
    place += mats + 2
    pair_in = refs[place : place + pieces]
    pair_sum = refs[place + pieces : place + 2 * pieces]
    plane_in = refs[place + 2 * pieces : place + 3 * pieces]
    place += 3 * pieces
    line_sum, line_in = refs[place : place + mats], refs[place + mats : place + 2 * mats]
    place += 2 * mats
    small, pair_sem, plane_sem, line_sem, small_sem = refs[place:]
    ring = Ring(dp, ranks)
    chips = ring.chips
    f32, bf16 = jnp.float32, jnp.bfloat16
    ring.greet(all_dp=True)

    def share(slot, value, stage):
        peer, here, count = ((ring.across, ring.d, dp), (ring.line, ring.h, ranks))[stage]
        small[slot, stage, here] = value
        spot = small.at[slot, stage, here]
        return [send(spot, spot, small_sem, (slot, stage, k), peer(k)) for k in range(1, count)]

    def shared(slot, copies, stage):
        wait_all(copies)
        total = small[slot, stage, 0]
        for k in range(1, (dp, ranks)[stage]):
            total = total + small[slot, stage, k]
        return total

    def line_copy(m, k):
        return pltpu.make_async_remote_copy(
            src_ref=line_sum[m].at[ring.rank_at(k)],
            dst_ref=line_in[m].at[k],
            send_sem=line_sem.at[0, m, k],
            recv_sem=line_sem.at[1, m, k],
            device_id=ring.line(k),
            device_id_type=pl.DeviceIdType.MESH,
        )

    def put_columns(m, cuts, total):
        for rank, first, last, inside in cuts:
            line_sum[m][rank, :, inside : inside + last - first] = total[:, first:last]

    def early_rank(m):
        widths, done = groups[m]
        own = sum(widths[: len(widths) - done])
        ready_from = sum(
            w for at, w in enumerate(widths) if at < len(widths) - done
        ) if done else sum(widths)
        block = sum(widths) // ranks
        return -(-max(own, ready_from) // block)

    def begin(copy, now, first):
        if first == 0:
            copy.start()
        elif first < ranks:
            pl.when(now)(copy.start)

    starts = []
    j = 0
    for m, (widths, done) in enumerate(groups):
        lines = [line_copy(m, k) for k in range(1, ranks)]
        starts.append(lines)
        cuts = column_cuts(widths, ranks)
        for at in range(len(widths) - done, len(widths)):
            put_columns(m, cuts[at], ready[j][...])
            j += 1
    rows = []
    for ref in gain_refs:
        for at in range(0, ref.shape[0], GROUP):
            rows.append(jnp.sum(ref[at : at + GROUP, :].T, axis=0, keepdims=True))
    rows.append(jnp.zeros((small.shape[3] - len(rows), GROUP), f32))
    ring.meet()
    pairs = [
        send(parts[i].at[:, 1 - ring.core], pair_in[i], pair_sem, (i,), ring.sibling())
        for i in range(pieces)
    ]
    for m in range(mats):
        for k in range(1, ranks):
            begin(starts[m][k - 1], early_rank(m) <= ring.rank_at(k), early_rank(m))
    gain_copies = share(0, jnp.concatenate(rows, axis=0), 0)
    planes = []
    for i in range(pieces):
        pairs[i].wait()

        def add_pair(p, carry, i=i):
            both = parts[i][p, ring.core].astype(f32) + pair_in[i][p].astype(f32)
            pair_sum[i][p] = both.astype(bf16)
            return carry

        lax.fori_loop(0, chips, add_pair, 0)
        planes.append(
            [
                send(
                    pair_sum[i].at[ring.chip_at(k)],
                    plane_in[i].at[k],
                    plane_sem,
                    (i, k),
                    ring.plane(k),
                )
                for k in range(1, chips)
            ]
        )
    gain_copies = share(0, shared(0, gain_copies, 0), 1)
    i = 0
    for m, (widths, done) in enumerate(groups):
        for cuts in column_cuts(widths, ranks)[: len(widths) - done]:
            total = pair_sum[i][ring.chip].astype(f32)
            for k in range(1, chips):
                planes[i][k - 1].wait()
                total = total + plane_in[i][k].astype(f32)
            put_columns(m, cuts, total.astype(bf16))
            i += 1
        first = early_rank(m)
        for k in range(1, ranks):
            if first >= ranks:
                starts[m][k - 1].start()
            elif first > 0:
                pl.when(ring.rank_at(k) < first)(starts[m][k - 1].start)
    square = jnp.zeros(square_out.shape, f32)

    def squares(value):
        value = value * value
        rows, cols = value.shape
        if cols % GROUP:
            value = jnp.concatenate([value, jnp.zeros((rows, GROUP - cols % GROUP), f32)], axis=1)
        return jnp.sum(fold_lanes(value).reshape(rows // 8, 8, GROUP), axis=0)

    for m in range(mats):
        total = line_sum[m][ring.h].astype(f32)
        for k in range(1, ranks):
            starts[m][k - 1].wait()
            total = total + line_in[m][k].astype(f32)
        outs[m][...] = total if outs[m].shape == total.shape else total.T
        square = square + squares(total)
    small_square = jnp.concatenate([square, jnp.zeros_like(square)], axis=0)
    square_copies = share(1, small_square, 0)
    gain_out[...] = shared(0, gain_copies, 1)[: gain_out.shape[0]]
    square_copies = share(1, shared(1, square_copies, 0), 1)
    square_out[...] = shared(1, square_copies, 1)[:8]


def reduce_grads(groups, gains, collective):
    dp, ranks = lax.axis_size("dp"), lax.axis_size("head")
    chips = dp // 2
    bf16, f32 = jnp.bfloat16, jnp.float32
    pieces, ready, widths, shards = [], [], [], []
    for group, done in groups:
        rows = done[0].shape[0] if done else group[0].shape[0] // dp
        pieces += [p.reshape(chips, 2, rows, p.shape[1]) for p in group]
        ready += done
        widths.append((tuple(p.shape[1] for p in group + done), len(done)))
        shards.append((rows, sum(widths[-1][0]) // ranks))
    blocks = [p.shape[2:] for p in pieces]
    vmem = pl.BlockSpec(memory_space=pltpu.VMEM)
    n, mats = len(pieces), len(groups)
    gain_rows = sum(g.shape[0] for g in gains) // GROUP
    return pl.pallas_call(
        functools.partial(reduce_kernel, dp, ranks, widths, len(ready)),
        in_specs=[vmem] * (n + 4 + len(ready)),
        out_specs=[vmem] * (mats + 2),
        out_shape=[jax.ShapeDtypeStruct(s if s[1] % GROUP == 0 else s[::-1], f32) for s in shards]
        + [jax.ShapeDtypeStruct((gain_rows, GROUP), f32), jax.ShapeDtypeStruct((8, GROUP), f32)],
        scratch_shapes=[pltpu.VMEM((chips,) + b, bf16) for b in blocks] * 3
        + [pltpu.VMEM((ranks,) + s, bf16) for s in shards] * 2
        + [
            pltpu.VMEM((2, 2, max(dp, ranks), 16, GROUP), f32),
            pltpu.SemaphoreType.DMA((2, n)),
            pltpu.SemaphoreType.DMA((2, n, chips)),
            pltpu.SemaphoreType.DMA((2, mats, ranks)),
            pltpu.SemaphoreType.DMA((2, 2, 2, max(dp, ranks))),
        ],
        compiler_params=pltpu.CompilerParams(
            collective_id=collective, has_side_effects=True, vmem_limit_bytes=VMEM_BYTES
        ),
        name="reduce_grads",
    )(*pieces, *gains, *ready)


def update_kernel(count, *refs):
    weights, grads = refs[:count], refs[count : 2 * count]
    firsts, seconds = refs[2 * count : 3 * count], refs[3 * count : 4 * count]
    square_ref = refs[4 * count]
    norm_ref, outs = refs[4 * count + 1], refs[4 * count + 2 :]
    gain_grad = grads[-1][...]
    square = jnp.sum(square_ref[...]) + jnp.sum(gain_grad * gain_grad)
    norm = jnp.sqrt(jnp.full((1, GROUP), square, jnp.float32))
    norm_ref[...] = norm
    clip_factor = jnp.minimum(1.0, CLIP / norm)[:, :1]
    for i in range(count):
        gains = i == count - 1
        result = adam_step(
            weights[i][...],
            grads[i][...],
            firsts[i][...],
            seconds[i][...],
            clip_factor,
            GAIN_RATE if gains else MATRIX_RATE,
            0.0 if gains else MATRIX_DECAY,
        )
        for ref, value in zip(outs[5 * i : 5 * i + 5], result):
            ref[...] = value


def update(weights, grads, firsts, seconds, square):
    count = len(weights)
    shapes = [jax.ShapeDtypeStruct((1, GROUP), jnp.float32)]
    for w in weights:
        shapes += [jax.ShapeDtypeStruct(w.shape, jnp.float32)] * 4
        shapes.append(jax.ShapeDtypeStruct(w.shape, jnp.bfloat16))
    return pl.pallas_call(
        functools.partial(update_kernel, count),
        out_shape=shapes,
        compiler_params=pltpu.CompilerParams(vmem_limit_bytes=VMEM_BYTES),
        name="update",
    )(*weights, *grads, *firsts, *seconds, square)


def body(
    char_ids,
    char_counts,
    language,
    words_in,
    out_cotangent,
    char_table,
    char_in,
    char_down,
    word_in,
    word_down,
    norm_gains,
    old_table_first,
    old_table_second,
    old_char_in_first,
    old_char_in_second,
    old_char_down_first,
    old_char_down_second,
    old_word_in_first,
    old_word_in_second,
    old_word_down_first,
    old_word_down_second,
    old_gains_first,
    old_gains_second,
):
    narrow = (norm_gains.shape[0] // GROUP, GROUP)
    table_t, char_in_low, char_down_t, early, up_rows, down_rows, packed, tiles, *gains = gather(
        (char_table.T, char_in, char_down.T, word_in, word_down),
        char_counts,
        char_ids.transpose(0, 2, 1),
        norm_gains.reshape(narrow),
        0,
    )

    def joined(block):
        if block.ndim == 2:
            return block
        dp, ranks, cols, rows = block.shape
        return block.transpose(1, 2, 0, 3).reshape(ranks * cols, dp * rows)

    def stacked(block):
        return block.reshape(-1, block.shape[2])

    table_t = joined(table_t)
    char_in_low = stacked(char_in_low)
    early = stacked(lax.all_to_all(early, "dp", 0, 0, tiled=True))
    char_others = (char_in_low, joined(char_down_t), gains[0], gains[1])
    sums, *kept = char_fwd(tiles, language, packed, table_t, char_others, words_in.shape[1])
    (
        output,
        input_grad,
        spread,
        grad_qkv,
        grad_pool,
        gain_three,
        gain_four,
        down_sum,
        up_sum,
        out_sum,
    ) = word_layer(
        sums,
        char_counts,
        words_in,
        out_cotangent,
        char_in_low,
        early,
        gains[2:],
        up_rows,
        down_rows,
        1,
    )
    grad_table, c_qkv, c_out, c_up, c_down, gain_one, gain_two = char_bwd(
        tiles, language, packed, table_t, char_others, spread, kept
    )
    blocks = lax.all_to_all(
        grad_qkv.reshape(lax.axis_size("dp"), -1, grad_qkv.shape[1]), "dp", 0, 0, tiled=True
    )
    qkv_sum = jnp.sum(blocks.astype(jnp.float32), axis=0).astype(jnp.bfloat16)
    *shards, gains_sum, square = reduce_grads(
        [
            ([grad_table], []),
            ([c_qkv, c_out, c_up, grad_pool], []),
            ([c_down], []),
            ([], [qkv_sum, out_sum, up_sum]),
            ([], [down_sum]),
        ],
        (gain_one, gain_two, gain_three, gain_four),
        2,
    )

    def turned(parts):
        parts = list(parts)
        parts[0], parts[2] = parts[0].T, parts[2].T
        parts[5] = parts[5].reshape(narrow)
        return parts

    norm, *updated = update(
        turned((char_table, char_in, char_down, word_in, word_down, norm_gains)),
        (*shards, gains_sum),
        turned(
            (
                old_table_first,
                old_char_in_first,
                old_char_down_first,
                old_word_in_first,
                old_word_down_first,
                old_gains_first,
            )
        ),
        turned(
            (
                old_table_second,
                old_char_in_second,
                old_char_down_second,
                old_word_in_second,
                old_word_down_second,
                old_gains_second,
            )
        ),
        square,
    )
    for place in (*range(5), *range(10, 15)):
        updated[place] = updated[place].T
    updated[-5:] = [part.reshape(norm_gains.shape) for part in updated[-5:]]
    return (output, input_grad, norm[0, 0], *updated)


def solution(mesh):
    return jax.shard_map(
        body,
        mesh=mesh,
        in_specs=(
            P("dp", "head", None),
            P("dp", "head"),
            P("dp"),
            P("dp", "head", None),
            P("dp", "head", None),
            P("dp", "head"),
            P("dp", "head"),
            P("dp", "head"),
            P("dp", "head"),
            P("dp", "head"),
            P(),
            P("dp", "head"),
            P("dp", "head"),
            P("dp", "head"),
            P("dp", "head"),
            P("dp", "head"),
            P("dp", "head"),
            P("dp", "head"),
            P("dp", "head"),
            P("dp", "head"),
            P("dp", "head"),
            P(),
            P(),
        ),
        out_specs=(
            P("dp", "head", None),
            P("dp", "head", None),
            P(),
            P("dp", "head"),
            P("dp", "head"),
            P("dp", "head"),
            P("dp", "head"),
            P("dp", "head"),
            P("dp", "head"),
            P("dp", "head"),
            P("dp", "head"),
            P("dp", "head"),
            P("dp", "head"),
            P("dp", "head"),
            P("dp", "head"),
            P("dp", "head"),
            P("dp", "head"),
            P("dp", "head"),
            P("dp", "head"),
            P("dp", "head"),
            P("dp", "head"),
            P("dp", "head"),
            P("dp", "head"),
            P("dp", "head"),
            P("dp", "head"),
            P("dp", "head"),
            P("dp", "head"),
            P("dp", "head"),
            P(),
            P(),
            P(),
            P(),
            P(),
        ),
        check_vma=False,
    )
```

```python
import functools

import jax
import jax.numpy as jnp
from jax import lax
from jax.experimental import pallas as pl
from jax.experimental.pallas import tpu as pltpu
from jax.sharding import PartitionSpec as P

D = 512
HEADS = 8
CD = 256
CHEADS = 4
CFF = 1024
CV = 256
STEP = 5


EPS = 1e-05
CLIP = 1.0
MATRIX_RATE = 0.03
GAIN_RATE = 0.25
MATRIX_DECAY = 0.1
BETA_ONE = 0.5
BETA_TWO = 0.5
ADAM_EPS = 1e-08
NEG_FILL = -1e30
SQRT_HALF = 0.7071067811865476
INV_ROOT_TWO_PI = 0.3989422804014327


ROWS = 512
SLOTS = 16
FWD_CHUNK = 512
BWD_CHUNK = 1024
WORD_CHUNK = 512
CHAINS = 1
GROUP = 128
VMEM_BYTES = 56 * 1024 * 1024


def dot_nn(left_side, right_side):
    return lax.dot_general(
        left_side, right_side, (((1,), (0,)), ((), ())), preferred_element_type=jnp.float32
    )


def dot_tn(left_side, right_side):
    return lax.dot_general(
        left_side, right_side, (((0,), (0,)), ((), ())), preferred_element_type=jnp.float32
    )


def dot_nt(left_side, right_side):
    return lax.dot_general(
        left_side, right_side, (((1,), (1,)), ((), ())), preferred_element_type=jnp.float32
    )


def gelu_pair(upper):
    phi = 0.5 + 0.5 * lax.erf(upper * SQRT_HALF)
    bell = jnp.exp(upper * upper * -0.5)
    return upper * phi, phi + upper * (bell * INV_ROOT_TWO_PI)


def iota(shape, dim):
    return lax.broadcasted_iota(jnp.int32, shape, dim)


def split_two(values):
    high = values.astype(jnp.bfloat16)
    return high, (values - high.astype(jnp.float32)).astype(jnp.bfloat16)


def pack_words(row, ids, out_ref, tiles_ref, seq):
    n = row.shape[1]
    col = jnp.broadcast_to(row.astype(jnp.float32), (8, n)).T[:, :1].astype(jnp.int32)
    sub, lane = iota((n, n), 0), iota((n, n), 1)
    ahead = (row > col) | ((row == col) & (lane < sub))
    rank_col = jnp.sum(ahead.astype(jnp.float32), axis=1, keepdims=True).astype(jnp.int32)
    ahead = (col > row) | ((col == row) & (sub < lane))
    rank_row = jnp.sum(ahead.astype(jnp.float32), axis=0, keepdims=True).astype(jnp.int32)
    clash = (rank_col < rank_row) & (col + row > SLOTS)
    alone = jnp.max(jnp.where(clash, rank_col + rank_row, 0).astype(jnp.float32))
    alone = jnp.maximum(alone.astype(jnp.int32) - n + 2, 0)
    partner = n - 1 + alone - rank_row
    second = (rank_row >= alone) & (rank_row > partner)
    bins = jnp.where(second, partner, rank_row)
    here = sub == bins
    first_map = (here & jnp.logical_not(second)).astype(jnp.float32).astype(jnp.bfloat16)
    second_map = (here & second).astype(jnp.float32).astype(jnp.bfloat16)
    pos = lax.rem(iota((GROUP, n), 0), SLOTS)
    word = iota((GROUP, n), 1) + 1
    wide = jnp.broadcast_to(row, (GROUP, n))
    in_first, in_second = pos < wide, pos >= SLOTS - wide

    def kept(mask, values):
        return jnp.where(mask, values, 0).astype(jnp.float32).astype(jnp.bfloat16)

    groups = n * SLOTS // GROUP
    spare = out_ref.shape[2] - groups
    per = GROUP // SLOTS
    own = iota((groups, per, GROUP), 1) == lax.div(iota((groups, per, GROUP), 2), SLOTS)
    back = jnp.concatenate([ids[SLOTS - 1 - j : SLOTS - j] for j in range(SLOTS)] * per, axis=0)
    ids = jnp.concatenate([ids] * per, axis=0)
    zero = jnp.zeros_like(wide)
    for k, (one, two) in enumerate(
        ((ids + 1, back + 1), (word, word), (zero, SLOTS - wide), (wide, zero + SLOTS))
    ):
        full = dot_nt(first_map, kept(in_first, one)) + dot_nt(second_map, kept(in_second, two))
        full = jnp.where(own, full.reshape(groups, per, GROUP), 0.0)
        full = jnp.sum(full, axis=1).astype(jnp.int32)
        if spare:
            full = jnp.concatenate([full, jnp.zeros((spare, GROUP), jnp.int32)], axis=0)
        out_ref[seq, k] = full
    used = alone + lax.div(n - alone + 1, 2)
    tiles_ref[seq] = lax.div(used * SLOTS + ROWS - 1, ROWS)


def lane_map(rows, size):
    spots = iota((size, GROUP), 0) + 1
    maps = [
        (spots == rows[g : g + 1]).astype(jnp.float32).astype(jnp.bfloat16)
        for g in range(rows.shape[0])
    ]
    return jnp.concatenate(maps, axis=1)


def in_step(chains):
    results = [None] * len(chains)
    waiting = list(enumerate(chains))
    running = []
    while waiting or running:
        if waiting:
            running.append(waiting.pop(0))
        for item in list(running):
            try:
                next(item[1])
            except StopIteration as stop:
                results[item[0]] = stop.value
                running.remove(item)
    return results


def lane_copies(ref, width):
    return jnp.concatenate([ref[...]] * (width // GROUP), axis=1)


def column_rms(values):
    inverse = lax.rsqrt(jnp.mean(values * values, axis=0, keepdims=True) + EPS)
    return values * inverse, inverse


def cost(flops, moved, powers):
    return pl.CostEstimate(flops=int(flops), bytes_accessed=int(moved), transcendentals=int(powers))


def tile_count(words):
    return -(-words * SLOTS // ROWS)


def tile_at(step, tiles_ref, seqs):
    seq, start, total = 0, 0, tiles_ref[0]
    for s in range(1, seqs):
        past = step >= total
        seq, start = jnp.where(past, s, seq), jnp.where(past, total, start)
        total = total + tiles_ref[s]
    return seq, step - start, total


def placed(seqs, index):
    def place(step, tiles_ref, language_ref):
        total = tile_at(step, tiles_ref, seqs)[2]
        seq, tile, _ = tile_at(jnp.minimum(step, total - 1), tiles_ref, seqs)
        return index(seq, tile, language_ref)

    return place


def own_block():
    shape = (GROUP // SLOTS, SLOTS, CHEADS * GROUP)
    return iota(shape, 0) == lax.div(lax.rem(iota(shape, 2), GROUP), SLOTS)


def to_compact(block, own):
    return jnp.sum(jnp.where(own, block.reshape(own.shape), 0.0), axis=0)


def from_compact(compact, own):
    wide = jnp.broadcast_to(compact[None], own.shape)
    return jnp.where(own, wide, 0.0).astype(jnp.bfloat16).reshape(GROUP, -1)


def stack_heads(wide):
    return jnp.concatenate([wide[:, h * GROUP : (h + 1) * GROUP] for h in range(CHEADS)], axis=0)


def spread_heads(values):
    head = values.shape[0] // CHEADS
    zero = jnp.zeros((head, GROUP), values.dtype)
    rows = []
    for h in range(CHEADS):
        parts = [zero] * CHEADS
        parts[h] = values[h * head : (h + 1) * head]
        rows.append(jnp.concatenate(parts, axis=1))
    return jnp.concatenate(rows, axis=0)


def char_fwd_kernel(seqs, tiles_ref, language_ref, *refs):
    step = pl.program_id(0)
    _, tile, total = tile_at(step, tiles_ref, seqs)

    @pl.when(step < total)
    def _():
        char_fwd_tile(tile, *refs)


def char_fwd_tile(
    step, pack_ref, table_ref, in_ref, down_ref, g1_ref, g2_ref, pooled_ref,
    keep_values, keep_probs, keep_qkv, keep_mixed, keep_first, keep_hidden, keep_slope,
):
    words = pooled_ref.shape[2]
    per = ROWS // GROUP
    head = CD // CHEADS

    @pl.when(step == 0)
    def _():
        pooled_ref[...] = jnp.zeros_like(pooled_ref)

    own = own_block()
    key_pos = iota((SLOTS, GROUP), 0)
    packs = [pack_ref[0, k, pl.ds(step * per, per), :] for k in range(4)]

    def chain(part):
        groups = per // CHAINS
        cols = slice(part * groups * GROUP, (part + 1) * groups * GROUP)
        size = groups * GROUP
        ids, spots, low_rows, high_rows = (p[part * groups : (part + 1) * groups] for p in packs)
        embedded = dot_nn(table_ref[...], lane_map(ids, CV))
        yield
        act_one = (column_rms(embedded)[0] * lane_copies(g1_ref, size)).astype(jnp.bfloat16)
        triple = dot_tn(in_ref[:, : 3 * CD], act_one).astype(jnp.bfloat16)
        keep_qkv[:, cols] = triple
        yield
        key_rows = triple[CD : 2 * CD].T
        keep_values[cols, :] = triple[2 * CD :].T
        all_probs = []
        for g in range(groups):
            valid = (key_pos >= low_rows[g : g + 1]) & (key_pos < high_rows[g : g + 1])
            valid = jnp.concatenate([valid.astype(jnp.float32)] * CHEADS, axis=1) > 0
            lanes = slice(g * GROUP, (g + 1) * GROUP)
            scores = to_compact(dot_nn(key_rows[lanes], spread_heads(triple[:CD, lanes])), own)
            scores = jnp.where(valid, scores * head**-0.5, NEG_FILL)
            powers = jnp.exp(scores - jnp.max(scores, axis=0, keepdims=True))
            powers = jnp.where(valid, powers, 0.0)
            total = jnp.sum(powers, axis=0, keepdims=True)
            probs = powers / jnp.where(total > 0, total, 1.0)
            wide = (part * groups + g) * CHEADS * GROUP
            keep_probs[:, wide : wide + CHEADS * GROUP] = probs
            all_probs.append(from_compact(probs, own))
        yield
        mixed = []
        for g in range(groups):
            lanes = slice(g * GROUP, (g + 1) * GROUP)
            values = spread_heads(triple[2 * CD :, lanes])
            mixed.append(dot_nn(values, stack_heads(all_probs[g])).astype(jnp.bfloat16))
        mixed = jnp.concatenate(mixed, axis=1)
        keep_mixed[:, cols] = mixed
        yield
        first = embedded + dot_tn(in_ref[:, 3 * CD : 4 * CD], mixed)
        keep_first[:, cols] = first
        act_two = (column_rms(first)[0] * lane_copies(g2_ref, size)).astype(jnp.bfloat16)
        second = first
        for c in range(CFF // FWD_CHUNK):
            yield
            rows = slice(c * FWD_CHUNK, (c + 1) * FWD_CHUNK)
            up = in_ref[:, 4 * CD + c * FWD_CHUNK : 4 * CD + (c + 1) * FWD_CHUNK]
            hidden, slope = gelu_pair(dot_tn(up, act_two))
            hidden = hidden.astype(jnp.bfloat16)
            keep_hidden[rows, cols] = hidden
            keep_slope[rows, cols] = slope.astype(jnp.bfloat16)
            second = second + dot_nn(down_ref[:, rows], hidden)
        yield
        return lane_map(spots, words), split_two(second)

    ends = in_step([chain(part) for part in range(CHAINS)])
    word_map = jnp.concatenate([end[0] for end in ends], axis=1)
    high = jnp.concatenate([end[1][0] for end in ends], axis=1)
    low = jnp.concatenate([end[1][1] for end in ends], axis=1)
    halves = dot_nt(jnp.concatenate([high, low], axis=0), word_map)
    pooled_ref[0] += halves[:CD] + halves[CD:]


KEPT = (
    (3 * CD, jnp.bfloat16),
    (CD, jnp.bfloat16),
    (CD, jnp.float32),
    (CFF, jnp.bfloat16),
    (CFF, jnp.bfloat16),
)


def kept_specs(seqs, count):
    place = placed(seqs, lambda seq, tile, _: (0, seq * count + tile))
    return [
        pl.BlockSpec((ROWS, CD), lambda *at: place(*at)[::-1]),
        pl.BlockSpec((SLOTS, CHEADS * ROWS), place),
    ] + [pl.BlockSpec((depth, ROWS), place) for depth, _ in KEPT]


def kept_shapes(rows):
    return [
        jax.ShapeDtypeStruct((rows, CD), jnp.bfloat16),
        jax.ShapeDtypeStruct((SLOTS, CHEADS * rows), jnp.float32),
    ] + [jax.ShapeDtypeStruct((depth, rows), dtype) for depth, dtype in KEPT]


def whole(array):
    zeros = (0,) * array.ndim
    return pl.BlockSpec(array.shape, lambda *_: zeros)


def char_specs(seqs, pack, others):
    one = (1,) + pack.shape[1:]
    return [
        pl.BlockSpec(one, placed(seqs, lambda seq, tile, _: (seq, 0, 0, 0))),
        pl.BlockSpec((CD, CV), placed(seqs, lambda seq, tile, language: (0, language[seq]))),
    ] + [whole(a) for a in others]


def char_fwd(tiles, language, pack, table, others, words):
    seqs = pack.shape[0]
    count = tile_count(words)
    one = placed(seqs, lambda seq, tile, _: (seq, 0, 0))
    return pl.pallas_call(
        functools.partial(char_fwd_kernel, seqs),
        grid_spec=pltpu.PrefetchScalarGridSpec(
            num_scalar_prefetch=2,
            grid=(seqs * count,),
            in_specs=char_specs(seqs, pack, others),
            out_specs=[pl.BlockSpec((1, CD, words), one)] + kept_specs(seqs, count),
        ),
        out_shape=[jax.ShapeDtypeStruct((seqs, CD, words), jnp.float32)]
        + kept_shapes(seqs * count * ROWS),
        compiler_params=pltpu.CompilerParams(vmem_limit_bytes=VMEM_BYTES),
        cost_estimate=cost(3e10, 6e7, 1e7),
        name="char_fwd",
    )(tiles, language, pack, table, *others)


def fold_lanes(values):
    total = values[:, :GROUP]
    for g in range(1, values.shape[1] // GROUP):
        total = total + values[:, g * GROUP : (g + 1) * GROUP]
    return total


def column_rms_back(grad_in, gain, normed, inverse):
    scaled = grad_in * gain
    return inverse * (scaled - normed * jnp.mean(scaled * normed, axis=0, keepdims=True))


def char_bwd_kernel(seqs, tiles_ref, language_ref, *refs):
    step = pl.program_id(0)
    seq, tile, total = tile_at(step, tiles_ref, seqs)

    @pl.when(step < total)
    def _():
        char_bwd_tile(tile, step == 0, step == total - 1, language_ref[seq] * CV, *refs)


def char_bwd_tile(
    step, at_start, at_end, letter, pack_ref, table_ref, in_ref, down_ref, g1_ref, g2_ref, spread_ref,
    keep_values, keep_probs, keep_qkv, keep_mixed, keep_first, keep_hidden, keep_slope,
    *refs,
):
    results, totals = refs[:7], refs[7:]
    d_table, d_qkv, d_out, d_up, d_down, d_g1, d_g2 = totals
    words = spread_ref.shape[2]
    per = ROWS // GROUP
    head = CD // CHEADS

    @pl.when(at_start)
    def _():
        for ref in totals:
            ref[...] = jnp.zeros_like(ref)

    own = own_block()
    packs = [pack_ref[0, k, pl.ds(step * per, per), :] for k in range(2)]

    def chain(part):
        groups = per // CHAINS
        cols = slice(part * groups * GROUP, (part + 1) * groups * GROUP)
        size = groups * GROUP
        ids, spots = (p[part * groups : (part + 1) * groups] for p in packs)
        halves = dot_nn(spread_ref[0], lane_map(spots, words))
        grad_second = halves[:CD] + halves[CD:]
        grad_branch = grad_second.astype(jnp.bfloat16)
        normed_two, inverse_two = column_rms(keep_first[:, cols])
        gain_two = lane_copies(g2_ref, size)
        act_two = (normed_two * gain_two).astype(jnp.bfloat16)
        grad_uppers = []
        grad_act_two = None
        for c in range(CFF // BWD_CHUNK):
            yield
            rows = slice(c * BWD_CHUNK, (c + 1) * BWD_CHUNK)
            slope = keep_slope[rows, cols].astype(jnp.float32)
            grad_upper = dot_tn(down_ref[:, rows], grad_branch) * slope
            grad_upper = grad_upper.astype(jnp.bfloat16)
            grad_uppers.append(grad_upper)
            piece = dot_nn(in_ref[:, 4 * CD + c * BWD_CHUNK : 4 * CD + (c + 1) * BWD_CHUNK], grad_upper)
            grad_act_two = piece if grad_act_two is None else grad_act_two + piece
        yield
        gain_sum_two = fold_lanes(grad_act_two * normed_two)
        grad_first = grad_second + column_rms_back(
            grad_act_two, gain_two, normed_two, inverse_two
        )
        grad_attn = grad_first.astype(jnp.bfloat16)
        grad_mixed = dot_nn(in_ref[:, 3 * CD : 4 * CD], grad_attn).astype(jnp.bfloat16)
        yield
        triple = keep_qkv[:, cols]
        raws, lows = [], []
        for g in range(groups):
            lanes = slice(g * GROUP, (g + 1) * GROUP)
            at = part * groups + g
            wide = slice(at * CHEADS * GROUP, (at + 1) * CHEADS * GROUP)
            probs = keep_probs[:, wide]
            values = keep_values[at * GROUP : (at + 1) * GROUP, :]
            grad_probs = to_compact(dot_nn(values, spread_heads(grad_mixed[:, lanes])), own)
            grad_scores = probs * (
                grad_probs - jnp.sum(probs * grad_probs, axis=0, keepdims=True)
            )
            raws.append(from_compact(grad_scores * head**-0.5, own))
            lows.append(from_compact(probs, own))
        yield
        columns = []
        for g in range(groups):
            lanes = slice(g * GROUP, (g + 1) * GROUP)
            grad_q = dot_nn(spread_heads(triple[CD : 2 * CD, lanes]), stack_heads(raws[g]))
            grad_k = dot_nt(spread_heads(triple[:CD, lanes]), raws[g])
            grad_v = dot_nt(spread_heads(grad_mixed[:, lanes]), lows[g])
            columns.append(jnp.concatenate([grad_q, grad_k, grad_v], axis=0).astype(jnp.bfloat16))
        grad_triple = jnp.concatenate(columns, axis=1)
        yield
        one_hot = lane_map(ids, CV)
        embedded = dot_nn(table_ref[...], one_hot)
        normed_one, inverse_one = column_rms(embedded)
        gain_one = lane_copies(g1_ref, size)
        act_one = (normed_one * gain_one).astype(jnp.bfloat16)
        grad_act_one = dot_nn(in_ref[:, : 3 * CD], grad_triple)
        yield
        gain_sum_one = fold_lanes(grad_act_one * normed_one)
        back_one = column_rms_back(grad_act_one, gain_one, normed_one, inverse_one)
        grad_embedded = (grad_first + back_one).astype(jnp.bfloat16)
        grad_upper = jnp.concatenate(grad_uppers, axis=0)
        return (
            gain_sum_one, gain_sum_two, grad_branch, act_two, grad_upper, grad_attn,
            act_one, grad_triple, one_hot, grad_embedded,
        )

    ends = in_step([chain(part) for part in range(CHAINS)])
    for end in ends:
        d_g1[...] += end[0]
        d_g2[...] += end[1]
    grad_branch, act_two, grad_upper, grad_attn, act_one, grad_triple, one_hot, grad_embedded = (
        jnp.concatenate(parts, axis=1) for parts in list(zip(*ends))[2:]
    )
    d_down[...] += dot_nt(keep_hidden[...], grad_branch)
    d_up[...] += dot_nt(act_two, grad_upper)
    d_out[...] += dot_nt(keep_mixed[...], grad_attn)
    d_qkv[...] += dot_nt(act_one, grad_triple)
    d_table[pl.ds(pl.multiple_of(letter, CV), CV), :] += dot_nt(one_hot, grad_embedded)

    @pl.when(at_end)
    def _():
        for ref, total in zip(results, totals):
            ref[...] = total[...].astype(ref.dtype)


def char_bwd(tiles, language, pack, table, others, spread, kept):
    shapes = (
        table.shape[::-1],
        (CD, 3 * CD),
        (CD, CD),
        (CD, CFF),
        (CFF, CD),
        (CD, GROUP),
        (CD, GROUP),
    )
    f32, bf16 = jnp.float32, jnp.bfloat16
    kinds = [bf16] * 5 + [f32] * 2
    seqs = pack.shape[0]
    count = tile_count(spread.shape[2])
    one = (1,) + spread.shape[1:]
    return pl.pallas_call(
        functools.partial(char_bwd_kernel, seqs),
        grid_spec=pltpu.PrefetchScalarGridSpec(
            num_scalar_prefetch=2,
            grid=(seqs * count,),
            in_specs=char_specs(seqs, pack, others)
            + [pl.BlockSpec(one, placed(seqs, lambda seq, tile, _: (seq, 0, 0)))]
            + kept_specs(seqs, count),
            out_specs=[pl.BlockSpec(s, lambda *_: (0, 0)) for s in shapes],
            scratch_shapes=[pltpu.VMEM(s, f32) for s in shapes],
        ),
        out_shape=[jax.ShapeDtypeStruct(s, kind) for s, kind in zip(shapes, kinds)],
        compiler_params=pltpu.CompilerParams(vmem_limit_bytes=VMEM_BYTES),
        cost_estimate=cost(5e10, 6e7, 1e6),
        name="char_bwd",
    )(tiles, language, pack, table, *others, spread, *kept)


def adam_step(weight, grad, first_old, second_old, clip_factor, rate, decay):
    clipped = grad * clip_factor
    first_new = BETA_ONE * first_old + (1.0 - BETA_ONE) * clipped
    second_new = BETA_TWO * second_old + (1.0 - BETA_TWO) * clipped * clipped
    first_hat = first_new / (1.0 - BETA_ONE**STEP)
    second_hat = second_new / (1.0 - BETA_TWO**STEP)
    weight_new = weight - rate * (first_hat / (jnp.sqrt(second_hat) + ADAM_EPS) + decay * weight)
    return (grad, first_new, second_new, weight_new, weight_new.astype(jnp.bfloat16))


class Ring:
    def __init__(self, dp, ranks):
        self.chips, self.ranks = dp // 2, ranks
        self.d, self.h = lax.axis_index("dp"), lax.axis_index("head")
        self.chip, self.core = lax.div(self.d, 2), lax.rem(self.d, 2)

    def sibling(self):
        return (self.d + 1 - 2 * self.core, self.h)

    def chip_at(self, k):
        if self.chips != 4:
            return lax.rem(self.chip + k, self.chips)
        return (None, self.chip + 1 - 2 * lax.rem(self.chip, 2), lax.rem(self.chip + 2, 4), 3 - self.chip)[k]

    def chip_from(self, k):
        if self.chips != 4:
            return lax.rem(self.chip + self.chips - k, self.chips)
        return self.chip_at(k)

    def plane(self, k):
        return (2 * self.chip_at(k) + self.core, self.h)

    def across(self, k):
        return (lax.rem(self.d + k, 2 * self.chips), self.h)

    def rank_at(self, k):
        return lax.rem(self.h + k, self.ranks)

    def line(self, k):
        return (self.d, self.rank_at(k))

    def greet(self, all_dp=False):
        barrier = pltpu.get_barrier_semaphore()
        if all_dp:
            peers = [self.across(k) for k in range(1, 2 * self.chips)]
        else:
            peers = [self.sibling()]
            peers += [self.plane(k) for k in range(1, self.chips)]
        peers += [self.line(k) for k in range(1, self.ranks)]
        self.partners = len(peers)
        for peer in peers:
            pl.semaphore_signal(barrier, inc=1, device_id=peer, device_id_type=pl.DeviceIdType.MESH)

    def meet(self):
        pl.semaphore_wait(pltpu.get_barrier_semaphore(), self.partners)


def send(src, dst, sems, place, peer):
    copy = pltpu.make_async_remote_copy(
        src_ref=src,
        dst_ref=dst,
        send_sem=sems.at[(0,) + place],
        recv_sem=sems.at[(1,) + place],
        device_id=peer,
        device_id_type=pl.DeviceIdType.MESH,
    )
    copy.start()
    return copy


def word_scores(q, k, diagonal):
    scores = dot_tn(k, q) * (D // HEADS) ** -0.5
    if diagonal:
        scores = jnp.where(iota(scores.shape, 0) <= iota(scores.shape, 1), scores, NEG_FILL)
    return scores


def head_rows(ref, n, part, kind):
    head = D // HEADS
    return ref[n, part, kind * head : (kind + 1) * head, :]


def word_attention(n, triple_ref, mixed_ref, lse_ref):
    for i in range(triple_ref.shape[1]):
        q = head_rows(triple_ref, n, i, 0)
        scores = [word_scores(q, head_rows(triple_ref, n, j, 1), i == j) for j in range(i + 1)]
        highest = jnp.max(scores[0], axis=0, keepdims=True)
        for block in scores[1:]:
            highest = jnp.maximum(highest, jnp.max(block, axis=0, keepdims=True))
        powers = [jnp.exp(block - highest) for block in scores]
        total = jnp.sum(powers[0], axis=0, keepdims=True)
        for block in powers[1:]:
            total = total + jnp.sum(block, axis=0, keepdims=True)
        inverse = 1.0 / total
        mixed = None
        for j, block in enumerate(powers):
            part = dot_nn(head_rows(triple_ref, n, j, 2), (block * inverse).astype(jnp.bfloat16))
            mixed = part if mixed is None else mixed + part
        mixed_ref[n, i] = mixed.astype(jnp.bfloat16)
        lse_ref[n, i] = jnp.broadcast_to(highest + jnp.log(total), lse_ref.shape[2:])


def word_attention_back(n, triple_ref, lse_ref, grad_ref, out_ref, dk, dv):
    parts = triple_ref.shape[1]
    head = D // HEADS
    for i in range(parts):
        q = head_rows(triple_ref, n, i, 0)
        grad_o = grad_ref[n, i]
        lse = lse_ref[n, i][:1]
        probs, grads = [], []
        dot_sum = None
        for j in range(i + 1):
            scores = word_scores(q, head_rows(triple_ref, n, j, 1), i == j)
            probs.append(jnp.exp(scores - lse))
            grads.append(dot_tn(head_rows(triple_ref, n, j, 2), grad_o))
            part = jnp.sum(probs[-1] * grads[-1], axis=0, keepdims=True)
            dot_sum = part if dot_sum is None else dot_sum + part
        grad_q = None
        for j in range(i + 1):
            raw = (probs[j] * (grads[j] - dot_sum) * head**-0.5).astype(jnp.bfloat16)
            part = dot_nn(head_rows(triple_ref, n, j, 1), raw)
            grad_q = part if grad_q is None else grad_q + part
            part_k = dot_nt(q, raw)
            part_v = dot_nt(grad_o, probs[j].astype(jnp.bfloat16))
            if i == j:
                dk[j] = part_k
                dv[j] = part_v
            else:
                dk[j] += part_k
                dv[j] += part_v
        out_ref[n, i, :head, :] = grad_q.astype(jnp.bfloat16)
    for j in range(parts):
        out_ref[n, j, head : 2 * head, :] = dk[j].astype(jnp.bfloat16)
        out_ref[n, j, 2 * head :, :] = dv[j].astype(jnp.bfloat16)


def swap_copies(ring, src, dst, n, sems):
    return [
        pltpu.make_async_remote_copy(
            src_ref=src.at[n, ring.rank_at(k)],
            dst_ref=dst.at[n, ring.h],
            send_sem=sems.at[0, n, k],
            recv_sem=sems.at[1, n, k],
            device_id=ring.line(k),
            device_id_type=pl.DeviceIdType.MESH,
        )
        for k in range(1, ring.ranks)
    ]


def swap_start(ring, src, dst, n, sems):
    for copy in swap_copies(ring, src, dst, n, sems):
        copy.start()
    dst[n, ring.h] = src[n, ring.h]


def swap_wait(ring, src, dst, n, sems):
    wait_all(swap_copies(ring, src, dst, n, sems))


def wait_all(copies):
    for copy in copies:
        copy.wait()


def word_kernel(dp, ranks, *refs):
    (sum_ref, count_ref, words_ref, cot_ref, in_ref, early_ref, g3_ref, g4_ref) = refs[:8]
    up_rows, down_rows = refs[8:10]
    (output_ref, input_grad_ref, spread_ref, d_qkv, d_pool, d_g3, d_g4) = refs[10:17]
    sums = refs[17:20]
    (starts, pooleds, afters, lses, up_ref, down_ref) = refs[20:26]
    (acts, hiddens, grad_ups, cots, lows, mixes, triples) = refs[26:33]
    (triple_ref, triple_in, triple_back, mixed_ref, mixed_in, mixed_back) = refs[33:39]
    dk, dv = refs[39:41]
    grads, pair_in, plane_in = refs[41:44], refs[44:47], refs[47:50]
    (own_sem, late_sem, late_pair_sem) = refs[50:53]
    (triple_sem, mixed_sem, mixed_back_sem, triple_back_sem, pair_sem, plane_sem) = refs[53:]
    ring = Ring(dp, ranks)
    chips = ring.chips
    f32, bf16 = jnp.float32, jnp.bfloat16
    ring.greet()
    seqs, width, _ = words_ref.shape
    hidden_size = up_ref.shape[1]
    head = D // HEADS
    heads = HEADS // ranks
    count = seqs * heads
    g3, g4 = lane_copies(g3_ref, width), lane_copies(g4_ref, width)

    def begin(s):
        pooled = (sum_ref[s] / count_ref[s : s + 1, :].astype(f32)).astype(bf16)
        pooleds[s] = pooled
        start = words_ref[s].astype(f32).T + dot_tn(in_ref[:, 4 * CD + CFF :], pooled)
        starts[s] = start
        act = (column_rms(start)[0] * g3).astype(bf16)
        for t in range(3):
            triple = dot_tn(early_ref[:, t * D : (t + 1) * D], act).astype(bf16)
            for r in range(ranks):
                for h in range(heads):
                    at = (r * heads + h) * head
                    triple_ref[s * heads + h, r, t * head : (t + 1) * head, :] = triple[
                        at : at + head
                    ]

    def begin_sends(s):
        for h in range(heads):
            swap_start(ring, triple_ref, triple_in, s * heads + h, triple_sem)

    begin(0)
    ring.meet()
    begin_sends(0)

    wide = early_ref.shape[1]

    def late_place(m, d):
        ref = (up_ref, down_ref)[m]
        rows = ref.shape[0] // dp
        return ref.at[pl.ds(pl.multiple_of(d * rows, rows), rows), :]

    late = (up_rows.at[:, wide:], down_rows)
    own, rounds, late_pairs = [], [], []
    for m in range(2):
        place = late_place(m, ring.d)
        own.append(pltpu.make_async_copy(late[m], place, own_sem.at[m]))
        own[-1].start()
        rounds.append(
            [send(late[m], place, late_sem, (m, k), ring.plane(k)) for k in range(1, chips)]
        )
        late_pairs.append(send(late[m], place, late_pair_sem, (m, 0), ring.sibling()))

    for s in range(1, seqs):
        begin(s)
        begin_sends(s)
    for m in range(2):
        for k in range(1, chips):
            rounds[m][k - 1].wait_recv()
            block = late_place(m, 2 * ring.chip_from(k) + ring.core)
            late_pairs.append(send(block, block, late_pair_sem, (m, k), ring.sibling()))

    def attend(n, carry):
        swap_wait(ring, triple_ref, triple_in, n, triple_sem)
        word_attention(n, triple_in, mixed_ref, lses)
        swap_start(ring, mixed_ref, mixed_in, n, mixed_sem)
        return carry

    def attend_back(n, carry):
        swap_wait(ring, mixed_ref, mixed_back, n, mixed_back_sem)
        word_attention_back(n, triple_in, lses, mixed_back, triple_ref, dk, dv)
        swap_start(ring, triple_ref, triple_back, n, triple_back_sem)
        return carry

    pairs, planes = {}, {}

    def put_grad(i, value):
        grads[i][...] = value.astype(bf16).reshape(grads[i].shape)
        pairs[i] = send(
            grads[i].at[:, 1 - ring.core], pair_in[i], pair_sem, (i,), ring.sibling()
        )

    def pass_on(i):
        pairs[i].wait()

        def add_pair(p, carry):
            both = grads[i][p, ring.core].astype(f32) + pair_in[i][p].astype(f32)
            pair_in[i][p] = both.astype(bf16)
            return carry

        lax.fori_loop(0, chips, add_pair, 0)
        planes[i] = [
            send(
                pair_in[i].at[ring.chip_at(k)], plane_in[i].at[k], plane_sem, (i, k), ring.plane(k)
            )
            for k in range(1, chips)
        ]

    lax.fori_loop(0, count - 1, attend, 0)
    gain = None
    for s in range(seqs):
        if s == 0:
            for m in range(2):
                own[m].wait()
                for copy in rounds[m]:
                    copy.wait_send()
            wait_all(late_pairs)
        if s == seqs - 1:
            attend(count - 1, 0)
        lanes = slice(s * width, (s + 1) * width)
        for h in range(heads):
            n = s * heads + h
            swap_wait(ring, mixed_ref, mixed_in, n, mixed_sem)
            for r in range(ranks):
                at = (r * heads + h) * head
                mixes[at : at + head, lanes] = mixed_in[n, r]
        after = starts[s] + dot_tn(early_ref[:, 3 * D :], mixes[:, lanes])
        normed, inverse = column_rms(after)
        act = (normed * g4).astype(bf16)
        acts[:, lanes] = act
        cot = cot_ref[s].astype(f32).T
        cot_low = cot.astype(bf16)
        cots[:, lanes] = cot_low
        result, grad = after, None
        for c in range(hidden_size // WORD_CHUNK):
            rows = slice(c * WORD_CHUNK, (c + 1) * WORD_CHUNK)
            hidden, slope = gelu_pair(dot_tn(up_ref[:, rows], act))
            hidden = hidden.astype(bf16)
            hiddens[rows, lanes] = hidden
            result = result + dot_tn(down_ref[rows, :], hidden)
            grad_upper = (dot_nn(down_ref[rows, :], cot_low) * slope).astype(bf16)
            grad_ups[rows, lanes] = grad_upper
            piece = dot_nn(up_ref[:, rows], grad_upper)
            grad = piece if grad is None else grad + piece
        piece = fold_lanes(grad * normed)
        gain = piece if gain is None else gain + piece
        total = cot + column_rms_back(grad, g4, normed, inverse)
        afters[s] = total
        low = total.astype(bf16)
        lows[:, lanes] = low
        mixed = dot_nn(early_ref[:, 3 * D :], low).astype(bf16)
        for h in range(heads):
            n = s * heads + h
            for r in range(ranks):
                at = (r * heads + h) * head
                mixed_ref[n, r] = mixed[at : at + head]
            swap_start(ring, mixed_ref, mixed_back, n, mixed_back_sem)
        output_ref[s] = result.T.astype(bf16)
    d_g4[...] = gain
    attend_back(0, 0)
    put_grad(0, dot_nt(hiddens[...], cots[...]))
    lax.fori_loop(1, heads, attend_back, 0)
    pass_on(0)
    lax.fori_loop(heads, count, attend_back, 0)
    put_grad(1, dot_nt(acts[...], grad_ups[...]))
    put_grad(2, dot_nt(mixes[...], lows[...]))
    pass_on(1)
    pass_on(2)
    gain = None
    for s in range(seqs):
        lanes = slice(s * width, (s + 1) * width)
        for h in range(heads):
            n = s * heads + h
            swap_wait(ring, triple_ref, triple_back, n, triple_back_sem)
            for t in range(3):
                for r in range(ranks):
                    at = t * D + (r * heads + h) * head
                    triples[at : at + head, lanes] = head_rows(triple_back, n, r, t)
        normed, inverse = column_rms(starts[s])
        acts[:, lanes] = (normed * g3).astype(bf16)
        grad = dot_nn(early_ref[:, : 3 * D], triples[:, lanes])
        piece = fold_lanes(grad * normed)
        gain = piece if gain is None else gain + piece
        total = afters[s] + column_rms_back(grad, g3, normed, inverse)
        input_grad_ref[s] = total.T
        low = total.astype(bf16)
        lows[:, lanes] = low
        high, rest = split_two(
            dot_nn(in_ref[:, 4 * CD + CFF :], low) / count_ref[s : s + 1, :].astype(f32)
        )
        spread_ref[s, :CD, :] = high
        spread_ref[s, CD:, :] = rest
    d_g3[...] = gain
    d_qkv[...] = dot_nt(acts[...], triples[...]).astype(bf16)
    d_pool[...] = sum(
        dot_nt(pooleds[s], lows[:, s * width : (s + 1) * width]) for s in range(seqs)
    ).astype(bf16)
    for i in range(3):
        total = pair_in[i][ring.chip].astype(f32)
        for k in range(1, chips):
            planes[i][k - 1].wait()
            total = total + plane_in[i][k].astype(f32)
        sums[i][...] = total.astype(bf16)


def word_layer(sums, counts, words, cot, char_in, early, gains, up_rows, down_rows, collective):
    dp, ranks = lax.axis_size("dp"), lax.axis_size("head")
    seqs, width, _ = words.shape
    hidden = up_rows.shape[1] - early.shape[1]
    chips = dp // 2
    bf16, f32 = jnp.bfloat16, jnp.float32
    vmem = pl.BlockSpec(memory_space=pltpu.VMEM)
    anywhere = pl.BlockSpec(memory_space=pl.ANY)
    rows = ((hidden // dp, D), (D // dp, hidden), (D // dp, D))
    columns = seqs * width
    count, head = seqs * HEADS // ranks, D // HEADS
    triple, mixed = (count, ranks, 3 * head, width), (count, ranks, head, width)
    dma = pltpu.SemaphoreType.DMA
    shapes = [
        ((seqs, width, D), bf16),
        ((seqs, width, D), f32),
        ((seqs, 2 * CD, width), bf16),
        ((D, 3 * D), bf16),
        ((CD, D), bf16),
        ((D, GROUP), f32),
        ((D, GROUP), f32),
    ] + [(r, bf16) for r in rows]
    held = [
        ((seqs, D, width), f32),
        ((seqs, CD, width), bf16),
        ((seqs, D, width), f32),
        ((count, ranks, 8, width), f32),
        ((D, hidden), bf16),
        ((hidden, D), bf16),
        ((D, columns), bf16),
        ((hidden, columns), bf16),
        ((hidden, columns), bf16),
        ((D, columns), bf16),
        ((D, columns), bf16),
        ((D, columns), bf16),
        ((3 * D, columns), bf16),
    ]
    held += [(triple, bf16)] * 3 + [(mixed, bf16)] * 3 + [((ranks, head, width), f32)] * 2
    held += [((chips, 2) + r, bf16) for r in rows] + [((chips,) + r, bf16) for r in rows] * 2
    return pl.pallas_call(
        functools.partial(word_kernel, dp, ranks),
        in_specs=[vmem] * 8 + [anywhere] * 2,
        out_specs=[vmem] * len(shapes),
        out_shape=[jax.ShapeDtypeStruct(shape, kind) for shape, kind in shapes],
        scratch_shapes=[pltpu.VMEM(shape, kind) for shape, kind in held]
        + [dma((2,)), dma((2, 2, chips)), dma((2, 2, chips))]
        + [dma((2, count, ranks))] * 4
        + [dma((2, 3)), dma((2, 3, chips))],
        compiler_params=pltpu.CompilerParams(
            collective_id=collective, has_side_effects=True, vmem_limit_bytes=VMEM_BYTES
        ),
        name="word_layer",
    )(sums, counts, words, cot, char_in, early, *gains, up_rows, down_rows)


def block_of(ref, d, h, shard):
    if len(ref.shape) == 4:
        return ref.at[d, h]
    rows, cols = shard.shape
    return ref.at[
        pl.ds(pl.multiple_of(h * rows, rows), rows), pl.ds(pl.multiple_of(d * cols, cols), cols)
    ]


def rows_of(ref, d, shard):
    if len(ref.shape) > 2:
        return ref.at[d]
    cols = shard.shape[1]
    return ref.at[:, pl.ds(pl.multiple_of(d * cols, cols), cols)]


def gather_kernel(dp, ranks, *refs):
    shards, (counts_ref, ids_ref, gains_ref) = refs[:5], refs[5:8]
    outs, (pack_ref, tiles_ref), gain_refs = refs[8:14], refs[14:16], refs[16:20]
    low = refs[20:25]
    own_sem, line_sem, relay_sem, plane_sem, pair_sem, copy_sem = refs[25:]
    table, char_in, down, early, word_rows, down_rows = outs
    ring = Ring(dp, ranks)
    ring.greet()
    for shard, ref in zip(shards, low):
        ref[...] = shard[...].astype(jnp.bfloat16)
    ring.meet()

    def shard_place(m, h):
        if m in (0, 2):
            return block_of((table, down)[m // 2], ring.d, h, low[m])
        wide = low[m].shape[1]
        ref = (None, char_in.at[ring.d], None, word_rows, down_rows)[m]
        return ref.at[:, pl.ds(pl.multiple_of(h * wide, GROUP), wide)]

    four = ranks == 4
    between = lax.rem(ring.h + 1, ranks) >= 2
    own, first = [], []

    def direct(k, act):
        if four and k != 2:
            pl.when(ring.h != (0 if k == 3 else 3))(act)
        else:
            act()

    def along_line(m):
        mine = shard_place(m, ring.h)
        own.append(pltpu.make_async_copy(low[m], mine, own_sem.at[m]))
        own[m].start()
        copies = [
            pltpu.make_async_remote_copy(
                src_ref=low[m],
                dst_ref=mine,
                send_sem=line_sem.at[0, m, k],
                recv_sem=line_sem.at[1, m, k],
                device_id=ring.line(k),
                device_id_type=pl.DeviceIdType.MESH,
            )
            for k in range(1, ranks)
        ]
        for k, copy in enumerate(copies, 1):
            direct(k, copy.start)
        first.append(copies)

    def relayed(m, act):
        if four:

            @pl.when(between)
            def _():
                block = shard_place(m, lax.rem(ring.h + 2, ranks))
                act(
                    pltpu.make_async_remote_copy(
                        src_ref=block,
                        dst_ref=block,
                        send_sem=relay_sem.at[m],
                        recv_sem=line_sem.at[1, m, 2 * ring.h - 1],
                        device_id=(ring.d, 3 * (ring.h - 1)),
                        device_id_type=pl.DeviceIdType.MESH,
                    )
                )

    def relay(m):
        first[m][1].wait_recv()
        relayed(m, lambda copy: copy.start())

    def arrived(m):
        own[m].wait()
        for k in range(1, ranks):
            if k != 2:
                first[m][k - 1].wait_recv()

    blocks = (table, char_in, down)
    second, sent = [], []

    def onward(m, block):
        place = rows_of(blocks[m], ring.d, low[m])
        second.append(
            [send(block, place, plane_sem, (m, k), ring.plane(k)) for k in range(1, ring.chips)]
        )
        sent.append(send(block, place, pair_sem, (m, 0), ring.sibling()))

    for m in range(3):
        along_line(m)
    for m in range(3):
        relay(m)
    for m in range(3):
        arrived(m)
        onward(m, rows_of(blocks[m], ring.d, low[m]))
    along_line(3)
    along_line(4)
    for seq in range(ids_ref.shape[0]):
        pack_words(counts_ref[seq : seq + 1, :], ids_ref[seq], pack_ref, tiles_ref, seq)
    row = 0
    for ref in gain_refs:
        for at in range(0, ref.shape[0], GROUP):
            gain = jnp.broadcast_to(gains_ref[row : row + 1, :], (GROUP, GROUP))
            ref[at : at + GROUP, :] = gain.T
            row += 1
    relay(3)
    for m in range(3):
        for k in range(1, ring.chips):
            second[m][k - 1].wait_recv()
            place = 2 * ring.chip_from(k) + ring.core
            block = rows_of(blocks[m], place, low[m])
            sent.append(send(block, block, pair_sem, (m, k), ring.sibling()))
    relay(4)
    arrived(3)
    copies = []
    for d in range(dp):
        block = word_rows.at[:, : early.shape[2]]
        copies.append(pltpu.make_async_copy(block, early.at[d], copy_sem.at[d]))
        copies[d].start()
    arrived(4)
    wait_all(sent)
    wait_all(copies)
    for m in range(5):
        for k, copy in enumerate(first[m], 1):
            direct(k, copy.wait_send)
        relayed(m, lambda copy: copy.wait_send())
    for m in range(3):
        for copy in second[m]:
            copy.wait_send()


def gather(shards, counts, ids, gains, collective):
    dp, ranks = lax.axis_size("dp"), lax.axis_size("head")
    bf16 = jnp.bfloat16
    vmem = pl.BlockSpec(memory_space=pltpu.VMEM)
    anywhere = pl.BlockSpec(memory_space=pl.ANY)
    table, char_in, down, word_in, word_down = (s.shape for s in shards)
    dma = pltpu.SemaphoreType.DMA

    def narrow(shape):
        if shape[1] % GROUP == 0:
            return (ranks * shape[0], dp * shape[1])
        return (dp, ranks) + shape

    seqs, slots, words = ids.shape
    outs = [
        narrow(table),
        (dp, char_in[0], ranks * char_in[1]),
        narrow(down),
        (dp, word_in[0], 4 * D),
        (word_in[0], ranks * word_in[1]),
        (word_down[0], ranks * word_down[1]),
    ]
    return pl.pallas_call(
        functools.partial(gather_kernel, dp, ranks),
        in_specs=[vmem] * 8,
        out_specs=[anywhere] * 4 + [vmem, anywhere] + [vmem, pl.BlockSpec(memory_space=pltpu.SMEM)] + [vmem] * 4,
        out_shape=[jax.ShapeDtypeStruct(s, bf16) for s in outs]
        + [
            jax.ShapeDtypeStruct((seqs, 4, tile_count(words) * (ROWS // GROUP), GROUP), jnp.int32),
            jax.ShapeDtypeStruct((seqs,), jnp.int32),
        ]
        + [jax.ShapeDtypeStruct((n, GROUP), jnp.float32) for n in (CD, CD, D, D)],
        scratch_shapes=[pltpu.VMEM(s.shape, bf16) for s in shards]
        + [
            dma((5,)),
            dma((2, 5, ranks)),
            dma((5,)),
            dma((2, 4, dp // 2)),
            dma((2, 4, dp // 2)),
            dma((dp,)),
        ],
        compiler_params=pltpu.CompilerParams(
            collective_id=collective, has_side_effects=True, vmem_limit_bytes=VMEM_BYTES
        ),
        name="gather",
    )(*shards, counts, ids, gains)


def column_cuts(widths, ranks):
    block = sum(widths) // ranks
    cuts, start = [], 0
    for width in widths:
        mine, at = [], 0
        while at < width:
            rank, inside = divmod(start + at, block)
            take = min(width - at, block - inside)
            mine.append((rank, at, at + take, inside))
            at += take
        cuts.append(mine)
        start += width
    return cuts


def reduce_kernel(dp, ranks, groups, extra, *refs):
    pieces = sum(len(g) - done for g, done in groups)
    mats = len(groups)
    parts = refs[:pieces]
    gain_refs = refs[pieces : pieces + 4]
    ready = refs[pieces + 4 : pieces + 4 + extra]
    place = pieces + 4 + extra
    outs = refs[place : place + mats]
    gain_out, square_out = refs[place + mats : place + mats + 2]
    place += mats + 2
    pair_in = refs[place : place + pieces]
    pair_sum = refs[place + pieces : place + 2 * pieces]
    plane_in = refs[place + 2 * pieces : place + 3 * pieces]
    place += 3 * pieces
    line_sum, line_in = refs[place : place + mats], refs[place + mats : place + 2 * mats]
    place += 2 * mats
    small, pair_sem, plane_sem, line_sem, small_sem = refs[place:]
    ring = Ring(dp, ranks)
    chips = ring.chips
    f32, bf16 = jnp.float32, jnp.bfloat16
    ring.greet(all_dp=True)

    def share(slot, value, stage):
        peer, here, count = ((ring.across, ring.d, dp), (ring.line, ring.h, ranks))[stage]
        small[slot, stage, here] = value
        spot = small.at[slot, stage, here]
        return [send(spot, spot, small_sem, (slot, stage, k), peer(k)) for k in range(1, count)]

    def shared(slot, copies, stage):
        wait_all(copies)
        total = small[slot, stage, 0]
        for k in range(1, (dp, ranks)[stage]):
            total = total + small[slot, stage, k]
        return total

    def line_copy(m, k):
        return pltpu.make_async_remote_copy(
            src_ref=line_sum[m].at[ring.rank_at(k)],
            dst_ref=line_in[m].at[k],
            send_sem=line_sem.at[0, m, k],
            recv_sem=line_sem.at[1, m, k],
            device_id=ring.line(k),
            device_id_type=pl.DeviceIdType.MESH,
        )

    def put_columns(m, cuts, total):
        for rank, first, last, inside in cuts:
            line_sum[m][rank, :, inside : inside + last - first] = total[:, first:last]

    def early_rank(m):
        widths, done = groups[m]
        own = sum(widths[: len(widths) - done])
        ready_from = sum(
            w for at, w in enumerate(widths) if at < len(widths) - done
        ) if done else sum(widths)
        block = sum(widths) // ranks
        return -(-max(own, ready_from) // block)

    def begin(copy, now, first):
        if first == 0:
            copy.start()
        elif first < ranks:
            pl.when(now)(copy.start)

    starts = []
    j = 0
    for m, (widths, done) in enumerate(groups):
        lines = [line_copy(m, k) for k in range(1, ranks)]
        starts.append(lines)
        cuts = column_cuts(widths, ranks)
        for at in range(len(widths) - done, len(widths)):
            put_columns(m, cuts[at], ready[j][...])
            j += 1
    rows = []
    for ref in gain_refs:
        for at in range(0, ref.shape[0], GROUP):
            rows.append(jnp.sum(ref[at : at + GROUP, :].T, axis=0, keepdims=True))
    rows.append(jnp.zeros((small.shape[3] - len(rows), GROUP), f32))
    ring.meet()
    pairs = [
        send(parts[i].at[:, 1 - ring.core], pair_in[i], pair_sem, (i,), ring.sibling())
        for i in range(pieces)
    ]
    for m in range(mats):
        for k in range(1, ranks):
            begin(starts[m][k - 1], early_rank(m) <= ring.rank_at(k), early_rank(m))
    gain_copies = share(0, jnp.concatenate(rows, axis=0), 0)
    planes = []
    for i in range(pieces):
        pairs[i].wait()

        def add_pair(p, carry, i=i):
            both = parts[i][p, ring.core].astype(f32) + pair_in[i][p].astype(f32)
            pair_sum[i][p] = both.astype(bf16)
            return carry

        lax.fori_loop(0, chips, add_pair, 0)
        planes.append(
            [
                send(
                    pair_sum[i].at[ring.chip_at(k)],
                    plane_in[i].at[k],
                    plane_sem,
                    (i, k),
                    ring.plane(k),
                )
                for k in range(1, chips)
            ]
        )
    gain_copies = share(0, shared(0, gain_copies, 0), 1)
    i = 0
    for m, (widths, done) in enumerate(groups):
        for cuts in column_cuts(widths, ranks)[: len(widths) - done]:
            total = pair_sum[i][ring.chip].astype(f32)
            for k in range(1, chips):
                planes[i][k - 1].wait()
                total = total + plane_in[i][k].astype(f32)
            put_columns(m, cuts, total.astype(bf16))
            i += 1
        first = early_rank(m)
        for k in range(1, ranks):
            if first >= ranks:
                starts[m][k - 1].start()
            elif first > 0:
                pl.when(ring.rank_at(k) < first)(starts[m][k - 1].start)
    square = jnp.zeros(square_out.shape, f32)

    def squares(value):
        value = value * value
        rows, cols = value.shape
        if cols % GROUP:
            value = jnp.concatenate([value, jnp.zeros((rows, GROUP - cols % GROUP), f32)], axis=1)
        return jnp.sum(fold_lanes(value).reshape(rows // 8, 8, GROUP), axis=0)

    for m in range(mats):
        total = line_sum[m][ring.h].astype(f32)
        for k in range(1, ranks):
            starts[m][k - 1].wait()
            total = total + line_in[m][k].astype(f32)
        outs[m][...] = total if outs[m].shape == total.shape else total.T
        square = square + squares(total)
    small_square = jnp.concatenate([square, jnp.zeros_like(square)], axis=0)
    square_copies = share(1, small_square, 0)
    gain_out[...] = shared(0, gain_copies, 1)[: gain_out.shape[0]]
    square_copies = share(1, shared(1, square_copies, 0), 1)
    square_out[...] = shared(1, square_copies, 1)[:8]


def reduce_grads(groups, gains, collective):
    dp, ranks = lax.axis_size("dp"), lax.axis_size("head")
    chips = dp // 2
    bf16, f32 = jnp.bfloat16, jnp.float32
    pieces, ready, widths, shards = [], [], [], []
    for group, done in groups:
        rows = done[0].shape[0] if done else group[0].shape[0] // dp
        pieces += [p.reshape(chips, 2, rows, p.shape[1]) for p in group]
        ready += done
        widths.append((tuple(p.shape[1] for p in group + done), len(done)))
        shards.append((rows, sum(widths[-1][0]) // ranks))
    blocks = [p.shape[2:] for p in pieces]
    vmem = pl.BlockSpec(memory_space=pltpu.VMEM)
    n, mats = len(pieces), len(groups)
    gain_rows = sum(g.shape[0] for g in gains) // GROUP
    return pl.pallas_call(
        functools.partial(reduce_kernel, dp, ranks, widths, len(ready)),
        in_specs=[vmem] * (n + 4 + len(ready)),
        out_specs=[vmem] * (mats + 2),
        out_shape=[jax.ShapeDtypeStruct(s if s[1] % GROUP == 0 else s[::-1], f32) for s in shards]
        + [jax.ShapeDtypeStruct((gain_rows, GROUP), f32), jax.ShapeDtypeStruct((8, GROUP), f32)],
        scratch_shapes=[pltpu.VMEM((chips,) + b, bf16) for b in blocks] * 3
        + [pltpu.VMEM((ranks,) + s, bf16) for s in shards] * 2
        + [
            pltpu.VMEM((2, 2, max(dp, ranks), 16, GROUP), f32),
            pltpu.SemaphoreType.DMA((2, n)),
            pltpu.SemaphoreType.DMA((2, n, chips)),
            pltpu.SemaphoreType.DMA((2, mats, ranks)),
            pltpu.SemaphoreType.DMA((2, 2, 2, max(dp, ranks))),
        ],
        compiler_params=pltpu.CompilerParams(
            collective_id=collective, has_side_effects=True, vmem_limit_bytes=VMEM_BYTES
        ),
        name="reduce_grads",
    )(*pieces, *gains, *ready)


def update_kernel(count, *refs):
    weights, grads = refs[:count], refs[count : 2 * count]
    firsts, seconds = refs[2 * count : 3 * count], refs[3 * count : 4 * count]
    square_ref = refs[4 * count]
    norm_ref, outs = refs[4 * count + 1], refs[4 * count + 2 :]
    gain_grad = grads[-1][...]
    square = jnp.sum(square_ref[...]) + jnp.sum(gain_grad * gain_grad)
    norm = jnp.sqrt(jnp.full((1, GROUP), square, jnp.float32))
    norm_ref[...] = norm
    clip_factor = jnp.minimum(1.0, CLIP / norm)[:, :1]
    for i in range(count):
        gains = i == count - 1
        result = adam_step(
            weights[i][...],
            grads[i][...],
            firsts[i][...],
            seconds[i][...],
            clip_factor,
            GAIN_RATE if gains else MATRIX_RATE,
            0.0 if gains else MATRIX_DECAY,
        )
        for ref, value in zip(outs[5 * i : 5 * i + 5], result):
            ref[...] = value


def update(weights, grads, firsts, seconds, square):
    count = len(weights)
    shapes = [jax.ShapeDtypeStruct((1, GROUP), jnp.float32)]
    for w in weights:
        shapes += [jax.ShapeDtypeStruct(w.shape, jnp.float32)] * 4
        shapes.append(jax.ShapeDtypeStruct(w.shape, jnp.bfloat16))
    return pl.pallas_call(
        functools.partial(update_kernel, count),
        out_shape=shapes,
        compiler_params=pltpu.CompilerParams(vmem_limit_bytes=VMEM_BYTES),
        name="update",
    )(*weights, *grads, *firsts, *seconds, square)


def body(
    char_ids,
    char_counts,
    language,
    words_in,
    out_cotangent,
    char_table,
    char_in,
    char_down,
    word_in,
    word_down,
    norm_gains,
    old_table_first,
    old_table_second,
    old_char_in_first,
    old_char_in_second,
    old_char_down_first,
    old_char_down_second,
    old_word_in_first,
    old_word_in_second,
    old_word_down_first,
    old_word_down_second,
    old_gains_first,
    old_gains_second,
):
    narrow = (norm_gains.shape[0] // GROUP, GROUP)
    table_t, char_in_low, char_down_t, early, up_rows, down_rows, packed, tiles, *gains = gather(
        (char_table.T, char_in, char_down.T, word_in, word_down),
        char_counts,
        char_ids.transpose(0, 2, 1),
        norm_gains.reshape(narrow),
        0,
    )

    def joined(block):
        if block.ndim == 2:
            return block
        dp, ranks, cols, rows = block.shape
        return block.transpose(1, 2, 0, 3).reshape(ranks * cols, dp * rows)

    def stacked(block):
        return block.reshape(-1, block.shape[2])

    table_t = joined(table_t)
    char_in_low = stacked(char_in_low)
    early = stacked(lax.all_to_all(early, "dp", 0, 0, tiled=True))
    char_others = (char_in_low, joined(char_down_t), gains[0], gains[1])
    sums, *kept = char_fwd(tiles, language, packed, table_t, char_others, words_in.shape[1])
    (
        output,
        input_grad,
        spread,
        grad_qkv,
        grad_pool,
        gain_three,
        gain_four,
        down_sum,
        up_sum,
        out_sum,
    ) = word_layer(
        sums,
        char_counts,
        words_in,
        out_cotangent,
        char_in_low,
        early,
        gains[2:],
        up_rows,
        down_rows,
        1,
    )
    grad_table, c_qkv, c_out, c_up, c_down, gain_one, gain_two = char_bwd(
        tiles, language, packed, table_t, char_others, spread, kept
    )
    blocks = lax.all_to_all(
        grad_qkv.reshape(lax.axis_size("dp"), -1, grad_qkv.shape[1]), "dp", 0, 0, tiled=True
    )
    qkv_sum = jnp.sum(blocks.astype(jnp.float32), axis=0).astype(jnp.bfloat16)
    *shards, gains_sum, square = reduce_grads(
        [
            ([grad_table], []),
            ([c_qkv, c_out, c_up, grad_pool], []),
            ([c_down], []),
            ([], [qkv_sum, out_sum, up_sum]),
            ([], [down_sum]),
        ],
        (gain_one, gain_two, gain_three, gain_four),
        2,
    )

    def turned(parts):
        parts = list(parts)
        parts[0], parts[2] = parts[0].T, parts[2].T
        parts[5] = parts[5].reshape(narrow)
        return parts

    norm, *updated = update(
        turned((char_table, char_in, char_down, word_in, word_down, norm_gains)),
        (*shards, gains_sum),
        turned(
            (
                old_table_first,
                old_char_in_first,
                old_char_down_first,
                old_word_in_first,
                old_word_down_first,
                old_gains_first,
            )
        ),
        turned(
            (
                old_table_second,
                old_char_in_second,
                old_char_down_second,
                old_word_in_second,
                old_word_down_second,
                old_gains_second,
            )
        ),
        square,
    )
    for place in (*range(5), *range(10, 15)):
        updated[place] = updated[place].T
    updated[-5:] = [part.reshape(norm_gains.shape) for part in updated[-5:]]
    return (output, input_grad, norm[0, 0], *updated)


def solution(mesh):
    return jax.shard_map(
        body,
        mesh=mesh,
        in_specs=(
            P("dp", "head", None),
            P("dp", "head"),
            P("dp"),
            P("dp", "head", None),
            P("dp", "head", None),
            P("dp", "head"),
            P("dp", "head"),
            P("dp", "head"),
            P("dp", "head"),
            P("dp", "head"),
            P(),
            P("dp", "head"),
            P("dp", "head"),
            P("dp", "head"),
            P("dp", "head"),
            P("dp", "head"),
            P("dp", "head"),
            P("dp", "head"),
            P("dp", "head"),
            P("dp", "head"),
            P("dp", "head"),
            P(),
            P(),
        ),
        out_specs=(
            P("dp", "head", None),
            P("dp", "head", None),
            P(),
            P("dp", "head"),
            P("dp", "head"),
            P("dp", "head"),
            P("dp", "head"),
            P("dp", "head"),
            P("dp", "head"),
            P("dp", "head"),
            P("dp", "head"),
            P("dp", "head"),
            P("dp", "head"),
            P("dp", "head"),
            P("dp", "head"),
            P("dp", "head"),
            P("dp", "head"),
            P("dp", "head"),
            P("dp", "head"),
            P("dp", "head"),
            P("dp", "head"),
            P("dp", "head"),
            P("dp", "head"),
            P("dp", "head"),
            P("dp", "head"),
            P("dp", "head"),
            P("dp", "head"),
            P("dp", "head"),
            P(),
            P(),
            P(),
            P(),
            P(),
        ),
        check_vma=False,
    )
```

```python
import functools

import jax
import jax.numpy as jnp
from jax import lax
from jax.experimental import pallas as pl
from jax.experimental.pallas import tpu as pltpu
from jax.sharding import PartitionSpec as P

D = 512
HEADS = 8
CD = 256
CHEADS = 4
CFF = 1024
CV = 256
STEP = 5


EPS = 1e-05
CLIP = 1.0
MATRIX_RATE = 0.03
GAIN_RATE = 0.25
MATRIX_DECAY = 0.1
BETA_ONE = 0.5
BETA_TWO = 0.5
ADAM_EPS = 1e-08
NEG_FILL = -1e30
SQRT_HALF = 0.7071067811865476
INV_ROOT_TWO_PI = 0.3989422804014327


ROWS = 512
SLOTS = 16
FWD_CHUNK = 512
BWD_CHUNK = 1024
WORD_CHUNK = 512
CHAINS = 1
GROUP = 128
VMEM_BYTES = 56 * 1024 * 1024


def dot_nn(left_side, right_side):
    return lax.dot_general(
        left_side, right_side, (((1,), (0,)), ((), ())), preferred_element_type=jnp.float32
    )


def dot_tn(left_side, right_side):
    return lax.dot_general(
        left_side, right_side, (((0,), (0,)), ((), ())), preferred_element_type=jnp.float32
    )


def dot_nt(left_side, right_side):
    return lax.dot_general(
        left_side, right_side, (((1,), (1,)), ((), ())), preferred_element_type=jnp.float32
    )


def gelu_pair(upper):
    phi = 0.5 + 0.5 * lax.erf(upper * SQRT_HALF)
    bell = jnp.exp(upper * upper * -0.5)
    return upper * phi, phi + upper * (bell * INV_ROOT_TWO_PI)


def iota(shape, dim):
    return lax.broadcasted_iota(jnp.int32, shape, dim)


def split_two(values):
    high = values.astype(jnp.bfloat16)
    return high, (values - high.astype(jnp.float32)).astype(jnp.bfloat16)


def pack_words(row, ids, out_ref, tiles_ref, seq):
    n = row.shape[1]
    col = jnp.broadcast_to(row.astype(jnp.float32), (8, n)).T[:, :1].astype(jnp.int32)
    sub, lane = iota((n, n), 0), iota((n, n), 1)
    ahead = (row > col) | ((row == col) & (lane < sub))
    rank_col = jnp.sum(ahead.astype(jnp.float32), axis=1, keepdims=True).astype(jnp.int32)
    ahead = (col > row) | ((col == row) & (sub < lane))
    rank_row = jnp.sum(ahead.astype(jnp.float32), axis=0, keepdims=True).astype(jnp.int32)
    clash = (rank_col < rank_row) & (col + row > SLOTS)
    alone = jnp.max(jnp.where(clash, rank_col + rank_row, 0).astype(jnp.float32))
    alone = jnp.maximum(alone.astype(jnp.int32) - n + 2, 0)
    partner = n - 1 + alone - rank_row
    second = (rank_row >= alone) & (rank_row > partner)
    bins = jnp.where(second, partner, rank_row)
    here = sub == bins
    first_map = (here & jnp.logical_not(second)).astype(jnp.float32).astype(jnp.bfloat16)
    second_map = (here & second).astype(jnp.float32).astype(jnp.bfloat16)
    pos = lax.rem(iota((GROUP, n), 0), SLOTS)
    word = iota((GROUP, n), 1) + 1
    wide = jnp.broadcast_to(row, (GROUP, n))
    in_first, in_second = pos < wide, pos >= SLOTS - wide

    def kept(mask, values):
        return jnp.where(mask, values, 0).astype(jnp.float32).astype(jnp.bfloat16)

    groups = n * SLOTS // GROUP
    spare = out_ref.shape[2] - groups
    per = GROUP // SLOTS
    own = iota((groups, per, GROUP), 1) == lax.div(iota((groups, per, GROUP), 2), SLOTS)
    back = jnp.concatenate([ids[SLOTS - 1 - j : SLOTS - j] for j in range(SLOTS)] * per, axis=0)
    ids = jnp.concatenate([ids] * per, axis=0)
    zero = jnp.zeros_like(wide)
    for k, (one, two) in enumerate(
        ((ids + 1, back + 1), (word, word), (zero, SLOTS - wide), (wide, zero + SLOTS))
    ):
        full = dot_nt(first_map, kept(in_first, one)) + dot_nt(second_map, kept(in_second, two))
        full = jnp.where(own, full.reshape(groups, per, GROUP), 0.0)
        full = jnp.sum(full, axis=1).astype(jnp.int32)
        if spare:
            full = jnp.concatenate([full, jnp.zeros((spare, GROUP), jnp.int32)], axis=0)
        out_ref[seq, k] = full
    used = alone + lax.div(n - alone + 1, 2)
    tiles_ref[seq] = lax.div(used * SLOTS + ROWS - 1, ROWS)


def lane_map(rows, size):
    spots = iota((size, GROUP), 0) + 1
    maps = [
        (spots == rows[g : g + 1]).astype(jnp.float32).astype(jnp.bfloat16)
        for g in range(rows.shape[0])
    ]
    return jnp.concatenate(maps, axis=1)


def in_step(chains):
    results = [None] * len(chains)
    waiting = list(enumerate(chains))
    running = []
    while waiting or running:
        if waiting:
            running.append(waiting.pop(0))
        for item in list(running):
            try:
                next(item[1])
            except StopIteration as stop:
                results[item[0]] = stop.value
                running.remove(item)
    return results


def lane_copies(ref, width):
    return jnp.concatenate([ref[...]] * (width // GROUP), axis=1)


def column_rms(values):
    inverse = lax.rsqrt(jnp.mean(values * values, axis=0, keepdims=True) + EPS)
    return values * inverse, inverse


def cost(flops, moved, powers):
    return pl.CostEstimate(flops=int(flops), bytes_accessed=int(moved), transcendentals=int(powers))


def tile_count(words):
    return -(-words * SLOTS // ROWS)


def tile_at(step, tiles_ref, seqs):
    seq, start, total = 0, 0, tiles_ref[0]
    for s in range(1, seqs):
        past = step >= total
        seq, start = jnp.where(past, s, seq), jnp.where(past, total, start)
        total = total + tiles_ref[s]
    return seq, step - start, total


def placed(seqs, index):
    def place(step, tiles_ref, language_ref):
        total = tile_at(step, tiles_ref, seqs)[2]
        seq, tile, _ = tile_at(jnp.minimum(step, total - 1), tiles_ref, seqs)
        return index(seq, tile, language_ref)

    return place


def own_block():
    shape = (GROUP // SLOTS, SLOTS, CHEADS * GROUP)
    return iota(shape, 0) == lax.div(lax.rem(iota(shape, 2), GROUP), SLOTS)


def to_compact(block, own):
    return jnp.sum(jnp.where(own, block.reshape(own.shape), 0.0), axis=0)


def from_compact(compact, own):
    wide = jnp.broadcast_to(compact[None], own.shape)
    return jnp.where(own, wide, 0.0).astype(jnp.bfloat16).reshape(GROUP, -1)


def stack_heads(wide):
    return jnp.concatenate([wide[:, h * GROUP : (h + 1) * GROUP] for h in range(CHEADS)], axis=0)


def spread_heads(values):
    head = values.shape[0] // CHEADS
    zero = jnp.zeros((head, GROUP), values.dtype)
    rows = []
    for h in range(CHEADS):
        parts = [zero] * CHEADS
        parts[h] = values[h * head : (h + 1) * head]
        rows.append(jnp.concatenate(parts, axis=1))
    return jnp.concatenate(rows, axis=0)


def char_fwd_kernel(seqs, tiles_ref, language_ref, *refs):
    step = pl.program_id(0)
    _, tile, total = tile_at(step, tiles_ref, seqs)

    @pl.when(step < total)
    def _():
        char_fwd_tile(tile, *refs)


def char_fwd_tile(
    step, pack_ref, table_ref, in_ref, down_ref, g1_ref, g2_ref, pooled_ref,
    keep_values, keep_probs, keep_qkv, keep_mixed, keep_first, keep_hidden, keep_slope,
):
    words = pooled_ref.shape[2]
    per = ROWS // GROUP
    head = CD // CHEADS

    @pl.when(step == 0)
    def _():
        pooled_ref[...] = jnp.zeros_like(pooled_ref)

    own = own_block()
    key_pos = iota((SLOTS, GROUP), 0)
    packs = [pack_ref[0, k, pl.ds(step * per, per), :] for k in range(4)]

    def chain(part):
        groups = per // CHAINS
        cols = slice(part * groups * GROUP, (part + 1) * groups * GROUP)
        size = groups * GROUP
        ids, spots, low_rows, high_rows = (p[part * groups : (part + 1) * groups] for p in packs)
        embedded = dot_nn(table_ref[...], lane_map(ids, CV))
        yield
        act_one = (column_rms(embedded)[0] * lane_copies(g1_ref, size)).astype(jnp.bfloat16)
        triple = dot_tn(in_ref[:, : 3 * CD], act_one).astype(jnp.bfloat16)
        keep_qkv[:, cols] = triple
        yield
        key_rows = triple[CD : 2 * CD].T
        keep_values[cols, :] = triple[2 * CD :].T
        all_probs = []
        for g in range(groups):
            valid = (key_pos >= low_rows[g : g + 1]) & (key_pos < high_rows[g : g + 1])
            valid = jnp.concatenate([valid.astype(jnp.float32)] * CHEADS, axis=1) > 0
            lanes = slice(g * GROUP, (g + 1) * GROUP)
            scores = to_compact(dot_nn(key_rows[lanes], spread_heads(triple[:CD, lanes])), own)
            scores = jnp.where(valid, scores * head**-0.5, NEG_FILL)
            powers = jnp.exp(scores - jnp.max(scores, axis=0, keepdims=True))
            powers = jnp.where(valid, powers, 0.0)
            total = jnp.sum(powers, axis=0, keepdims=True)
            probs = powers / jnp.where(total > 0, total, 1.0)
            wide = (part * groups + g) * CHEADS * GROUP
            keep_probs[:, wide : wide + CHEADS * GROUP] = probs
            all_probs.append(from_compact(probs, own))
        yield
        mixed = []
        for g in range(groups):
            lanes = slice(g * GROUP, (g + 1) * GROUP)
            values = spread_heads(triple[2 * CD :, lanes])
            mixed.append(dot_nn(values, stack_heads(all_probs[g])).astype(jnp.bfloat16))
        mixed = jnp.concatenate(mixed, axis=1)
        keep_mixed[:, cols] = mixed
        yield
        first = embedded + dot_tn(in_ref[:, 3 * CD : 4 * CD], mixed)
        keep_first[:, cols] = first
        act_two = (column_rms(first)[0] * lane_copies(g2_ref, size)).astype(jnp.bfloat16)
        second = first
        for c in range(CFF // FWD_CHUNK):
            yield
            rows = slice(c * FWD_CHUNK, (c + 1) * FWD_CHUNK)
            up = in_ref[:, 4 * CD + c * FWD_CHUNK : 4 * CD + (c + 1) * FWD_CHUNK]
            hidden, slope = gelu_pair(dot_tn(up, act_two))
            hidden = hidden.astype(jnp.bfloat16)
            keep_hidden[rows, cols] = hidden
            keep_slope[rows, cols] = slope.astype(jnp.bfloat16)
            second = second + dot_nn(down_ref[:, rows], hidden)
        yield
        return lane_map(spots, words), split_two(second)

    ends = in_step([chain(part) for part in range(CHAINS)])
    word_map = jnp.concatenate([end[0] for end in ends], axis=1)
    high = jnp.concatenate([end[1][0] for end in ends], axis=1)
    low = jnp.concatenate([end[1][1] for end in ends], axis=1)
    halves = dot_nt(jnp.concatenate([high, low], axis=0), word_map)
    pooled_ref[0] += halves[:CD] + halves[CD:]


KEPT = (
    (3 * CD, jnp.bfloat16),
    (CD, jnp.bfloat16),
    (CD, jnp.float32),
    (CFF, jnp.bfloat16),
    (CFF, jnp.bfloat16),
)


def kept_specs(seqs, count):
    place = placed(seqs, lambda seq, tile, _: (0, seq * count + tile))
    return [
        pl.BlockSpec((ROWS, CD), lambda *at: place(*at)[::-1]),
        pl.BlockSpec((SLOTS, CHEADS * ROWS), place),
    ] + [pl.BlockSpec((depth, ROWS), place) for depth, _ in KEPT]


def kept_shapes(rows):
    return [
        jax.ShapeDtypeStruct((rows, CD), jnp.bfloat16),
        jax.ShapeDtypeStruct((SLOTS, CHEADS * rows), jnp.float32),
    ] + [jax.ShapeDtypeStruct((depth, rows), dtype) for depth, dtype in KEPT]


def whole(array):
    zeros = (0,) * array.ndim
    return pl.BlockSpec(array.shape, lambda *_: zeros)


def char_specs(seqs, pack, others):
    one = (1,) + pack.shape[1:]
    return [
        pl.BlockSpec(one, placed(seqs, lambda seq, tile, _: (seq, 0, 0, 0))),
        pl.BlockSpec((CD, CV), placed(seqs, lambda seq, tile, language: (0, language[seq]))),
    ] + [whole(a) for a in others]


def char_fwd(tiles, language, pack, table, others, words):
    seqs = pack.shape[0]
    count = tile_count(words)
    one = placed(seqs, lambda seq, tile, _: (seq, 0, 0))
    return pl.pallas_call(
        functools.partial(char_fwd_kernel, seqs),
        grid_spec=pltpu.PrefetchScalarGridSpec(
            num_scalar_prefetch=2,
            grid=(seqs * count,),
            in_specs=char_specs(seqs, pack, others),
            out_specs=[pl.BlockSpec((1, CD, words), one)] + kept_specs(seqs, count),
        ),
        out_shape=[jax.ShapeDtypeStruct((seqs, CD, words), jnp.float32)]
        + kept_shapes(seqs * count * ROWS),
        compiler_params=pltpu.CompilerParams(vmem_limit_bytes=VMEM_BYTES),
        cost_estimate=cost(3e10, 6e7, 1e7),
        name="char_fwd",
    )(tiles, language, pack, table, *others)


def fold_lanes(values):
    total = values[:, :GROUP]
    for g in range(1, values.shape[1] // GROUP):
        total = total + values[:, g * GROUP : (g + 1) * GROUP]
    return total


def column_rms_back(grad_in, gain, normed, inverse):
    scaled = grad_in * gain
    return inverse * (scaled - normed * jnp.mean(scaled * normed, axis=0, keepdims=True))


def char_bwd_kernel(seqs, tiles_ref, language_ref, *refs):
    step = pl.program_id(0)
    seq, tile, total = tile_at(step, tiles_ref, seqs)

    @pl.when(step < total)
    def _():
        char_bwd_tile(tile, step == 0, step == total - 1, language_ref[seq] * CV, *refs)


def char_bwd_tile(
    step, at_start, at_end, letter, pack_ref, table_ref, in_ref, down_ref, g1_ref, g2_ref, spread_ref,
    keep_values, keep_probs, keep_qkv, keep_mixed, keep_first, keep_hidden, keep_slope,
    *refs,
):
    results, totals = refs[:5], refs[5:]
    d_table, d_in, d_down, d_g1, d_g2 = totals
    words = spread_ref.shape[2]
    per = ROWS // GROUP
    head = CD // CHEADS

    @pl.when(at_start)
    def _():
        for ref in totals:
            ref[...] = jnp.zeros_like(ref)

    own = own_block()
    packs = [pack_ref[0, k, pl.ds(step * per, per), :] for k in range(2)]

    def chain(part):
        groups = per // CHAINS
        cols = slice(part * groups * GROUP, (part + 1) * groups * GROUP)
        size = groups * GROUP
        ids, spots = (p[part * groups : (part + 1) * groups] for p in packs)
        halves = dot_nn(spread_ref[0], lane_map(spots, words))
        grad_second = halves[:CD] + halves[CD:]
        grad_branch = grad_second.astype(jnp.bfloat16)
        normed_two, inverse_two = column_rms(keep_first[:, cols])
        gain_two = lane_copies(g2_ref, size)
        act_two = (normed_two * gain_two).astype(jnp.bfloat16)
        grad_uppers = []
        grad_act_two = None
        for c in range(CFF // BWD_CHUNK):
            yield
            rows = slice(c * BWD_CHUNK, (c + 1) * BWD_CHUNK)
            slope = keep_slope[rows, cols].astype(jnp.float32)
            grad_upper = dot_tn(down_ref[:, rows], grad_branch) * slope
            grad_upper = grad_upper.astype(jnp.bfloat16)
            grad_uppers.append(grad_upper)
            piece = dot_nn(in_ref[:, 4 * CD + c * BWD_CHUNK : 4 * CD + (c + 1) * BWD_CHUNK], grad_upper)
            grad_act_two = piece if grad_act_two is None else grad_act_two + piece
        yield
        gain_sum_two = fold_lanes(grad_act_two * normed_two)
        grad_first = grad_second + column_rms_back(
            grad_act_two, gain_two, normed_two, inverse_two
        )
        grad_attn = grad_first.astype(jnp.bfloat16)
        grad_mixed = dot_nn(in_ref[:, 3 * CD : 4 * CD], grad_attn).astype(jnp.bfloat16)
        yield
        triple = keep_qkv[:, cols]
        raws, lows = [], []
        for g in range(groups):
            lanes = slice(g * GROUP, (g + 1) * GROUP)
            at = part * groups + g
            wide = slice(at * CHEADS * GROUP, (at + 1) * CHEADS * GROUP)
            probs = keep_probs[:, wide]
            values = keep_values[at * GROUP : (at + 1) * GROUP, :]
            grad_probs = to_compact(dot_nn(values, spread_heads(grad_mixed[:, lanes])), own)
            grad_scores = probs * (
                grad_probs - jnp.sum(probs * grad_probs, axis=0, keepdims=True)
            )
            raws.append(from_compact(grad_scores * head**-0.5, own))
            lows.append(from_compact(probs, own))
        yield
        columns = []
        for g in range(groups):
            lanes = slice(g * GROUP, (g + 1) * GROUP)
            grad_q = dot_nn(spread_heads(triple[CD : 2 * CD, lanes]), stack_heads(raws[g]))
            grad_k = dot_nt(spread_heads(triple[:CD, lanes]), raws[g])
            grad_v = dot_nt(spread_heads(grad_mixed[:, lanes]), lows[g])
            columns.append(jnp.concatenate([grad_q, grad_k, grad_v], axis=0).astype(jnp.bfloat16))
        grad_triple = jnp.concatenate(columns, axis=1)
        yield
        one_hot = lane_map(ids, CV)
        embedded = dot_nn(table_ref[...], one_hot)
        normed_one, inverse_one = column_rms(embedded)
        gain_one = lane_copies(g1_ref, size)
        act_one = (normed_one * gain_one).astype(jnp.bfloat16)
        grad_act_one = dot_nn(in_ref[:, : 3 * CD], grad_triple)
        yield
        gain_sum_one = fold_lanes(grad_act_one * normed_one)
        back_one = column_rms_back(grad_act_one, gain_one, normed_one, inverse_one)
        grad_embedded = (grad_first + back_one).astype(jnp.bfloat16)
        grad_upper = jnp.concatenate(grad_uppers, axis=0)
        return (
            gain_sum_one, gain_sum_two, grad_branch, act_two, grad_upper, grad_attn,
            act_one, grad_triple, one_hot, grad_embedded,
        )

    ends = in_step([chain(part) for part in range(CHAINS)])
    for end in ends:
        d_g1[...] += end[0]
        d_g2[...] += end[1]
    grad_branch, act_two, grad_upper, grad_attn, act_one, grad_triple, one_hot, grad_embedded = (
        jnp.concatenate(parts, axis=1) for parts in list(zip(*ends))[2:]
    )
    d_down[...] += dot_nt(keep_hidden[...], grad_branch)
    d_in[:, 4 * CD :] += dot_nt(act_two, grad_upper)
    d_in[:, 3 * CD : 4 * CD] += dot_nt(keep_mixed[...], grad_attn)
    d_in[:, : 3 * CD] += dot_nt(act_one, grad_triple)
    d_table[pl.ds(pl.multiple_of(letter, CV), CV), :] += dot_nt(one_hot, grad_embedded)

    @pl.when(at_end)
    def _():
        for ref, total in zip(results, totals):
            ref[...] = total[...].astype(ref.dtype)


def char_bwd(tiles, language, pack, table, others, spread, kept):
    shapes = (
        table.shape[::-1],
        (CD, 4 * CD + CFF),
        (CFF, CD),
        (CD, GROUP),
        (CD, GROUP),
    )
    f32, bf16 = jnp.float32, jnp.bfloat16
    kinds = [bf16] * 3 + [f32] * 2
    seqs = pack.shape[0]
    count = tile_count(spread.shape[2])
    one = (1,) + spread.shape[1:]
    return pl.pallas_call(
        functools.partial(char_bwd_kernel, seqs),
        grid_spec=pltpu.PrefetchScalarGridSpec(
            num_scalar_prefetch=2,
            grid=(seqs * count,),
            in_specs=char_specs(seqs, pack, others)
            + [pl.BlockSpec(one, placed(seqs, lambda seq, tile, _: (seq, 0, 0)))]
            + kept_specs(seqs, count),
            out_specs=[pl.BlockSpec(s, lambda *_: (0, 0)) for s in shapes],
            scratch_shapes=[pltpu.VMEM(s, f32) for s in shapes],
        ),
        out_shape=[jax.ShapeDtypeStruct(s, kind) for s, kind in zip(shapes, kinds)],
        compiler_params=pltpu.CompilerParams(vmem_limit_bytes=VMEM_BYTES),
        cost_estimate=cost(5e10, 6e7, 1e6),
        name="char_bwd",
    )(tiles, language, pack, table, *others, spread, *kept)


def adam_step(weight, grad, first_old, second_old, clip_factor, rate, decay):
    clipped = grad * clip_factor
    first_new = BETA_ONE * first_old + (1.0 - BETA_ONE) * clipped
    second_new = BETA_TWO * second_old + (1.0 - BETA_TWO) * clipped * clipped
    first_hat = first_new / (1.0 - BETA_ONE**STEP)
    second_hat = second_new / (1.0 - BETA_TWO**STEP)
    weight_new = weight - rate * (first_hat / (jnp.sqrt(second_hat) + ADAM_EPS) + decay * weight)
    return (grad, first_new, second_new, weight_new, weight_new.astype(jnp.bfloat16))


class Ring:
    def __init__(self, dp, ranks):
        self.chips, self.ranks = dp // 2, ranks
        self.d, self.h = lax.axis_index("dp"), lax.axis_index("head")
        self.chip, self.core = lax.div(self.d, 2), lax.rem(self.d, 2)

    def sibling(self):
        return (self.d + 1 - 2 * self.core, self.h)

    def chip_at(self, k):
        if self.chips != 4:
            return lax.rem(self.chip + k, self.chips)
        return (None, self.chip + 1 - 2 * lax.rem(self.chip, 2), lax.rem(self.chip + 2, 4), 3 - self.chip)[k]

    def chip_from(self, k):
        if self.chips != 4:
            return lax.rem(self.chip + self.chips - k, self.chips)
        return self.chip_at(k)

    def plane(self, k):
        return (2 * self.chip_at(k) + self.core, self.h)

    def across(self, k):
        return (lax.rem(self.d + k, 2 * self.chips), self.h)

    def rank_at(self, k):
        return lax.rem(self.h + k, self.ranks)

    def line(self, k):
        return (self.d, self.rank_at(k))

    def greet(self, all_dp=False):
        barrier = pltpu.get_barrier_semaphore()
        if all_dp:
            peers = [self.across(k) for k in range(1, 2 * self.chips)]
        else:
            peers = [self.sibling()]
            peers += [self.plane(k) for k in range(1, self.chips)]
        peers += [self.line(k) for k in range(1, self.ranks)]
        self.partners = len(peers)
        for peer in peers:
            pl.semaphore_signal(barrier, inc=1, device_id=peer, device_id_type=pl.DeviceIdType.MESH)

    def meet(self):
        pl.semaphore_wait(pltpu.get_barrier_semaphore(), self.partners)


def send(src, dst, sems, place, peer):
    copy = pltpu.make_async_remote_copy(
        src_ref=src,
        dst_ref=dst,
        send_sem=sems.at[(0,) + place],
        recv_sem=sems.at[(1,) + place],
        device_id=peer,
        device_id_type=pl.DeviceIdType.MESH,
    )
    copy.start()
    return copy


def word_scores(q, k, diagonal):
    scores = dot_tn(k, q) * (D // HEADS) ** -0.5
    if diagonal:
        scores = jnp.where(iota(scores.shape, 0) <= iota(scores.shape, 1), scores, NEG_FILL)
    return scores


def head_rows(ref, n, part, kind):
    head = D // HEADS
    return ref[n, part, kind * head : (kind + 1) * head, :]


def word_attention(n, triple_ref, mixed_ref, lse_ref):
    for i in range(triple_ref.shape[1]):
        q = head_rows(triple_ref, n, i, 0)
        scores = [word_scores(q, head_rows(triple_ref, n, j, 1), i == j) for j in range(i + 1)]
        highest = jnp.max(scores[0], axis=0, keepdims=True)
        for block in scores[1:]:
            highest = jnp.maximum(highest, jnp.max(block, axis=0, keepdims=True))
        powers = [jnp.exp(block - highest) for block in scores]
        total = jnp.sum(powers[0], axis=0, keepdims=True)
        for block in powers[1:]:
            total = total + jnp.sum(block, axis=0, keepdims=True)
        inverse = 1.0 / total
        mixed = None
        for j, block in enumerate(powers):
            part = dot_nn(head_rows(triple_ref, n, j, 2), (block * inverse).astype(jnp.bfloat16))
            mixed = part if mixed is None else mixed + part
        mixed_ref[n, i] = mixed.astype(jnp.bfloat16)
        lse_ref[n, i] = jnp.broadcast_to(highest + jnp.log(total), lse_ref.shape[2:])


def word_attention_back(n, triple_ref, lse_ref, grad_ref, out_ref, dk, dv):
    parts = triple_ref.shape[1]
    head = D // HEADS
    for i in range(parts):
        q = head_rows(triple_ref, n, i, 0)
        grad_o = grad_ref[n, i]
        lse = lse_ref[n, i][:1]
        probs, grads = [], []
        dot_sum = None
        for j in range(i + 1):
            scores = word_scores(q, head_rows(triple_ref, n, j, 1), i == j)
            probs.append(jnp.exp(scores - lse))
            grads.append(dot_tn(head_rows(triple_ref, n, j, 2), grad_o))
            part = jnp.sum(probs[-1] * grads[-1], axis=0, keepdims=True)
            dot_sum = part if dot_sum is None else dot_sum + part
        grad_q = None
        for j in range(i + 1):
            raw = (probs[j] * (grads[j] - dot_sum) * head**-0.5).astype(jnp.bfloat16)
            part = dot_nn(head_rows(triple_ref, n, j, 1), raw)
            grad_q = part if grad_q is None else grad_q + part
            part_k = dot_nt(q, raw)
            part_v = dot_nt(grad_o, probs[j].astype(jnp.bfloat16))
            if i == j:
                dk[j] = part_k
                dv[j] = part_v
            else:
                dk[j] += part_k
                dv[j] += part_v
        out_ref[n, i, :head, :] = grad_q.astype(jnp.bfloat16)
    for j in range(parts):
        out_ref[n, j, head : 2 * head, :] = dk[j].astype(jnp.bfloat16)
        out_ref[n, j, 2 * head :, :] = dv[j].astype(jnp.bfloat16)


def swap_copies(ring, src, dst, n, sems):
    return [
        pltpu.make_async_remote_copy(
            src_ref=src.at[n, ring.rank_at(k)],
            dst_ref=dst.at[n, ring.h],
            send_sem=sems.at[0, n, k],
            recv_sem=sems.at[1, n, k],
            device_id=ring.line(k),
            device_id_type=pl.DeviceIdType.MESH,
        )
        for k in range(1, ring.ranks)
    ]


def swap_start(ring, src, dst, n, sems):
    for copy in swap_copies(ring, src, dst, n, sems):
        copy.start()
    dst[n, ring.h] = src[n, ring.h]


def swap_wait(ring, src, dst, n, sems):
    wait_all(swap_copies(ring, src, dst, n, sems))


def wait_all(copies):
    for copy in copies:
        copy.wait()


def word_kernel(dp, ranks, *refs):
    (sum_ref, count_ref, words_ref, cot_ref, in_ref, early_ref, g3_ref, g4_ref) = refs[:8]
    up_rows, down_rows = refs[8:10]
    (output_ref, input_grad_ref, spread_ref, d_qkv, d_pool, d_g3, d_g4) = refs[10:17]
    sums = refs[17:20]
    (starts, pooleds, afters, lses, up_ref, down_ref) = refs[20:26]
    (acts, hiddens, grad_ups, cots, lows, mixes, triples) = refs[26:33]
    (triple_ref, triple_in, triple_back, mixed_ref, mixed_in, mixed_back) = refs[33:39]
    dk, dv = refs[39:41]
    grads, pair_in, plane_in = refs[41:44], refs[44:47], refs[47:50]
    (own_sem, late_sem, late_pair_sem) = refs[50:53]
    (triple_sem, mixed_sem, mixed_back_sem, triple_back_sem, pair_sem, plane_sem) = refs[53:]
    ring = Ring(dp, ranks)
    chips = ring.chips
    f32, bf16 = jnp.float32, jnp.bfloat16
    ring.greet()
    seqs, width, _ = words_ref.shape
    hidden_size = up_ref.shape[1]
    head = D // HEADS
    heads = HEADS // ranks
    count = seqs * heads
    g3, g4 = lane_copies(g3_ref, width), lane_copies(g4_ref, width)

    def begin(s):
        pooled = (sum_ref[s] / count_ref[s : s + 1, :].astype(f32)).astype(bf16)
        pooleds[s] = pooled
        start = words_ref[s].astype(f32).T + dot_tn(in_ref[:, 4 * CD + CFF :], pooled)
        starts[s] = start
        act = (column_rms(start)[0] * g3).astype(bf16)
        for t in range(3):
            triple = dot_tn(early_ref[:, t * D : (t + 1) * D], act).astype(bf16)
            for r in range(ranks):
                for h in range(heads):
                    at = (r * heads + h) * head
                    triple_ref[s * heads + h, r, t * head : (t + 1) * head, :] = triple[
                        at : at + head
                    ]

    def begin_sends(s):
        for h in range(heads):
            swap_start(ring, triple_ref, triple_in, s * heads + h, triple_sem)

    begin(0)
    ring.meet()
    begin_sends(0)

    wide = early_ref.shape[1]

    def late_place(m, d):
        ref = (up_ref, down_ref)[m]
        rows = ref.shape[0] // dp
        return ref.at[pl.ds(pl.multiple_of(d * rows, rows), rows), :]

    late = (up_rows.at[:, wide:], down_rows)
    own, rounds, late_pairs = [], [], []
    for m in range(2):
        place = late_place(m, ring.d)
        own.append(pltpu.make_async_copy(late[m], place, own_sem.at[m]))
        own[-1].start()
        rounds.append(
            [send(late[m], place, late_sem, (m, k), ring.plane(k)) for k in range(1, chips)]
        )
        late_pairs.append(send(late[m], place, late_pair_sem, (m, 0), ring.sibling()))

    for s in range(1, seqs):
        begin(s)
        begin_sends(s)
    for m in range(2):
        for k in range(1, chips):
            rounds[m][k - 1].wait_recv()
            block = late_place(m, 2 * ring.chip_from(k) + ring.core)
            late_pairs.append(send(block, block, late_pair_sem, (m, k), ring.sibling()))

    def attend(n, carry):
        swap_wait(ring, triple_ref, triple_in, n, triple_sem)
        word_attention(n, triple_in, mixed_ref, lses)
        swap_start(ring, mixed_ref, mixed_in, n, mixed_sem)
        return carry

    def attend_back(n, carry):
        swap_wait(ring, mixed_ref, mixed_back, n, mixed_back_sem)
        word_attention_back(n, triple_in, lses, mixed_back, triple_ref, dk, dv)
        swap_start(ring, triple_ref, triple_back, n, triple_back_sem)
        return carry

    pairs, planes = {}, {}

    def put_grad(i, value):
        grads[i][...] = value.astype(bf16).reshape(grads[i].shape)
        pairs[i] = send(
            grads[i].at[:, 1 - ring.core], pair_in[i], pair_sem, (i,), ring.sibling()
        )

    def pass_on(i):
        pairs[i].wait()

        def add_pair(p, carry):
            both = grads[i][p, ring.core].astype(f32) + pair_in[i][p].astype(f32)
            pair_in[i][p] = both.astype(bf16)
            return carry

        lax.fori_loop(0, chips, add_pair, 0)
        planes[i] = [
            send(
                pair_in[i].at[ring.chip_at(k)], plane_in[i].at[k], plane_sem, (i, k), ring.plane(k)
            )
            for k in range(1, chips)
        ]

    lax.fori_loop(0, count - 1, attend, 0)
    gain = None
    for s in range(seqs):
        if s == 0:
            for m in range(2):
                own[m].wait()
                for copy in rounds[m]:
                    copy.wait_send()
            wait_all(late_pairs)
        if s == seqs - 1:
            attend(count - 1, 0)
        lanes = slice(s * width, (s + 1) * width)
        for h in range(heads):
            n = s * heads + h
            swap_wait(ring, mixed_ref, mixed_in, n, mixed_sem)
            for r in range(ranks):
                at = (r * heads + h) * head
                mixes[at : at + head, lanes] = mixed_in[n, r]
        after = starts[s] + dot_tn(early_ref[:, 3 * D :], mixes[:, lanes])
        normed, inverse = column_rms(after)
        act = (normed * g4).astype(bf16)
        acts[:, lanes] = act
        cot = cot_ref[s].astype(f32).T
        cot_low = cot.astype(bf16)
        cots[:, lanes] = cot_low
        result, grad = after, None
        for c in range(hidden_size // WORD_CHUNK):
            rows = slice(c * WORD_CHUNK, (c + 1) * WORD_CHUNK)
            hidden, slope = gelu_pair(dot_tn(up_ref[:, rows], act))
            hidden = hidden.astype(bf16)
            hiddens[rows, lanes] = hidden
            result = result + dot_tn(down_ref[rows, :], hidden)
            grad_upper = (dot_nn(down_ref[rows, :], cot_low) * slope).astype(bf16)
            grad_ups[rows, lanes] = grad_upper
            piece = dot_nn(up_ref[:, rows], grad_upper)
            grad = piece if grad is None else grad + piece
        piece = fold_lanes(grad * normed)
        gain = piece if gain is None else gain + piece
        total = cot + column_rms_back(grad, g4, normed, inverse)
        afters[s] = total
        low = total.astype(bf16)
        lows[:, lanes] = low
        mixed = dot_nn(early_ref[:, 3 * D :], low).astype(bf16)
        for h in range(heads):
            n = s * heads + h
            for r in range(ranks):
                at = (r * heads + h) * head
                mixed_ref[n, r] = mixed[at : at + head]
            swap_start(ring, mixed_ref, mixed_back, n, mixed_back_sem)
        output_ref[s] = result.T.astype(bf16)
    d_g4[...] = gain
    attend_back(0, 0)
    put_grad(0, dot_nt(hiddens[...], cots[...]))
    lax.fori_loop(1, heads, attend_back, 0)
    pass_on(0)
    lax.fori_loop(heads, count, attend_back, 0)
    put_grad(1, dot_nt(acts[...], grad_ups[...]))
    put_grad(2, dot_nt(mixes[...], lows[...]))
    pass_on(1)
    pass_on(2)
    gain = None
    for s in range(seqs):
        lanes = slice(s * width, (s + 1) * width)
        for h in range(heads):
            n = s * heads + h
            swap_wait(ring, triple_ref, triple_back, n, triple_back_sem)
            for t in range(3):
                for r in range(ranks):
                    at = t * D + (r * heads + h) * head
                    triples[at : at + head, lanes] = head_rows(triple_back, n, r, t)
        normed, inverse = column_rms(starts[s])
        acts[:, lanes] = (normed * g3).astype(bf16)
        grad = dot_nn(early_ref[:, : 3 * D], triples[:, lanes])
        piece = fold_lanes(grad * normed)
        gain = piece if gain is None else gain + piece
        total = afters[s] + column_rms_back(grad, g3, normed, inverse)
        input_grad_ref[s] = total.T
        low = total.astype(bf16)
        lows[:, lanes] = low
        high, rest = split_two(
            dot_nn(in_ref[:, 4 * CD + CFF :], low) / count_ref[s : s + 1, :].astype(f32)
        )
        spread_ref[s, :CD, :] = high
        spread_ref[s, CD:, :] = rest
    d_g3[...] = gain
    d_qkv[...] = dot_nt(acts[...], triples[...]).astype(bf16)
    d_pool[...] = sum(
        dot_nt(pooleds[s], lows[:, s * width : (s + 1) * width]) for s in range(seqs)
    ).astype(bf16)
    for i in range(3):
        total = pair_in[i][ring.chip].astype(f32)
        for k in range(1, chips):
            planes[i][k - 1].wait()
            total = total + plane_in[i][k].astype(f32)
        sums[i][...] = total.astype(bf16)


def word_layer(sums, counts, words, cot, char_in, early, gains, up_rows, down_rows, collective):
    dp, ranks = lax.axis_size("dp"), lax.axis_size("head")
    seqs, width, _ = words.shape
    hidden = up_rows.shape[1] - early.shape[1]
    chips = dp // 2
    bf16, f32 = jnp.bfloat16, jnp.float32
    vmem = pl.BlockSpec(memory_space=pltpu.VMEM)
    anywhere = pl.BlockSpec(memory_space=pl.ANY)
    rows = ((hidden // dp, D), (D // dp, hidden), (D // dp, D))
    columns = seqs * width
    count, head = seqs * HEADS // ranks, D // HEADS
    triple, mixed = (count, ranks, 3 * head, width), (count, ranks, head, width)
    dma = pltpu.SemaphoreType.DMA
    shapes = [
        ((seqs, width, D), bf16),
        ((seqs, width, D), f32),
        ((seqs, 2 * CD, width), bf16),
        ((D, 3 * D), bf16),
        ((CD, D), bf16),
        ((D, GROUP), f32),
        ((D, GROUP), f32),
    ] + [(r, bf16) for r in rows]
    held = [
        ((seqs, D, width), f32),
        ((seqs, CD, width), bf16),
        ((seqs, D, width), f32),
        ((count, ranks, 8, width), f32),
        ((D, hidden), bf16),
        ((hidden, D), bf16),
        ((D, columns), bf16),
        ((hidden, columns), bf16),
        ((hidden, columns), bf16),
        ((D, columns), bf16),
        ((D, columns), bf16),
        ((D, columns), bf16),
        ((3 * D, columns), bf16),
    ]
    held += [(triple, bf16)] * 3 + [(mixed, bf16)] * 3 + [((ranks, head, width), f32)] * 2
    held += [((chips, 2) + r, bf16) for r in rows] + [((chips,) + r, bf16) for r in rows] * 2
    return pl.pallas_call(
        functools.partial(word_kernel, dp, ranks),
        in_specs=[vmem] * 8 + [anywhere] * 2,
        out_specs=[vmem] * len(shapes),
        out_shape=[jax.ShapeDtypeStruct(shape, kind) for shape, kind in shapes],
        scratch_shapes=[pltpu.VMEM(shape, kind) for shape, kind in held]
        + [dma((2,)), dma((2, 2, chips)), dma((2, 2, chips))]
        + [dma((2, count, ranks))] * 4
        + [dma((2, 3)), dma((2, 3, chips))],
        compiler_params=pltpu.CompilerParams(
            collective_id=collective, has_side_effects=True, vmem_limit_bytes=VMEM_BYTES
        ),
        name="word_layer",
    )(sums, counts, words, cot, char_in, early, *gains, up_rows, down_rows)


def block_of(ref, d, h, shard):
    if len(ref.shape) == 4:
        return ref.at[d, h]
    rows, cols = shard.shape
    return ref.at[
        pl.ds(pl.multiple_of(h * rows, rows), rows), pl.ds(pl.multiple_of(d * cols, cols), cols)
    ]


def rows_of(ref, d, shard):
    if len(ref.shape) > 2:
        return ref.at[d]
    cols = shard.shape[1]
    return ref.at[:, pl.ds(pl.multiple_of(d * cols, cols), cols)]


def gather_kernel(dp, ranks, *refs):
    shards, (counts_ref, ids_ref, gains_ref) = refs[:5], refs[5:8]
    outs, (pack_ref, tiles_ref), gain_refs = refs[8:14], refs[14:16], refs[16:20]
    low = refs[20:25]
    own_sem, line_sem, relay_sem, plane_sem, pair_sem, copy_sem = refs[25:]
    table, char_in, down, early, word_rows, down_rows = outs
    ring = Ring(dp, ranks)
    ring.greet()
    for shard, ref in zip(shards, low):
        ref[...] = shard[...].astype(jnp.bfloat16)
    ring.meet()

    def shard_place(m, h):
        if m in (0, 2):
            return block_of((table, down)[m // 2], ring.d, h, low[m])
        wide = low[m].shape[1]
        ref = (None, char_in.at[ring.d], None, word_rows, down_rows)[m]
        return ref.at[:, pl.ds(pl.multiple_of(h * wide, GROUP), wide)]

    four = ranks == 4
    between = lax.rem(ring.h + 1, ranks) >= 2
    own, first = [], []

    def direct(k, act):
        if four and k != 2:
            pl.when(ring.h != (0 if k == 3 else 3))(act)
        else:
            act()

    def along_line(m):
        mine = shard_place(m, ring.h)
        own.append(pltpu.make_async_copy(low[m], mine, own_sem.at[m]))
        own[m].start()
        copies = [
            pltpu.make_async_remote_copy(
                src_ref=low[m],
                dst_ref=mine,
                send_sem=line_sem.at[0, m, k],
                recv_sem=line_sem.at[1, m, k],
                device_id=ring.line(k),
                device_id_type=pl.DeviceIdType.MESH,
            )
            for k in range(1, ranks)
        ]
        for k, copy in enumerate(copies, 1):
            direct(k, copy.start)
        first.append(copies)

    def relayed(m, act):
        if four:

            @pl.when(between)
            def _():
                block = shard_place(m, lax.rem(ring.h + 2, ranks))
                act(
                    pltpu.make_async_remote_copy(
                        src_ref=block,
                        dst_ref=block,
                        send_sem=relay_sem.at[m],
                        recv_sem=line_sem.at[1, m, 2 * ring.h - 1],
                        device_id=(ring.d, 3 * (ring.h - 1)),
                        device_id_type=pl.DeviceIdType.MESH,
                    )
                )

    def relay(m):
        first[m][1].wait_recv()
        relayed(m, lambda copy: copy.start())

    def arrived(m):
        own[m].wait()
        for k in range(1, ranks):
            if k != 2:
                first[m][k - 1].wait_recv()

    blocks = (table, char_in, down)
    second, sent = [], []

    def onward(m, block):
        place = rows_of(blocks[m], ring.d, low[m])
        second.append(
            [send(block, place, plane_sem, (m, k), ring.plane(k)) for k in range(1, ring.chips)]
        )
        sent.append(send(block, place, pair_sem, (m, 0), ring.sibling()))

    for m in range(3):
        along_line(m)
    for m in range(3):
        relay(m)
    for m in range(3):
        arrived(m)
        onward(m, rows_of(blocks[m], ring.d, low[m]))
    along_line(3)
    along_line(4)
    for seq in range(ids_ref.shape[0]):
        pack_words(counts_ref[seq : seq + 1, :], ids_ref[seq], pack_ref, tiles_ref, seq)
    row = 0
    for ref in gain_refs:
        for at in range(0, ref.shape[0], GROUP):
            gain = jnp.broadcast_to(gains_ref[row : row + 1, :], (GROUP, GROUP))
            ref[at : at + GROUP, :] = gain.T
            row += 1
    relay(3)
    for m in range(3):
        for k in range(1, ring.chips):
            second[m][k - 1].wait_recv()
            place = 2 * ring.chip_from(k) + ring.core
            block = rows_of(blocks[m], place, low[m])
            sent.append(send(block, block, pair_sem, (m, k), ring.sibling()))
    relay(4)
    arrived(3)
    copies = []
    for d in range(dp):
        block = word_rows.at[:, : early.shape[2]]
        copies.append(pltpu.make_async_copy(block, early.at[d], copy_sem.at[d]))
        copies[d].start()
    arrived(4)
    wait_all(sent)
    wait_all(copies)
    for m in range(5):
        for k, copy in enumerate(first[m], 1):
            direct(k, copy.wait_send)
        relayed(m, lambda copy: copy.wait_send())
    for m in range(3):
        for copy in second[m]:
            copy.wait_send()


def gather(shards, counts, ids, gains, collective):
    dp, ranks = lax.axis_size("dp"), lax.axis_size("head")
    bf16 = jnp.bfloat16
    vmem = pl.BlockSpec(memory_space=pltpu.VMEM)
    anywhere = pl.BlockSpec(memory_space=pl.ANY)
    table, char_in, down, word_in, word_down = (s.shape for s in shards)
    dma = pltpu.SemaphoreType.DMA

    def narrow(shape):
        if shape[1] % GROUP == 0:
            return (ranks * shape[0], dp * shape[1])
        return (dp, ranks) + shape

    seqs, slots, words = ids.shape
    outs = [
        narrow(table),
        (dp, char_in[0], ranks * char_in[1]),
        narrow(down),
        (dp, word_in[0], 4 * D),
        (word_in[0], ranks * word_in[1]),
        (word_down[0], ranks * word_down[1]),
    ]
    return pl.pallas_call(
        functools.partial(gather_kernel, dp, ranks),
        in_specs=[vmem] * 8,
        out_specs=[anywhere] * 4 + [vmem, anywhere] + [vmem, pl.BlockSpec(memory_space=pltpu.SMEM)] + [vmem] * 4,
        out_shape=[jax.ShapeDtypeStruct(s, bf16) for s in outs]
        + [
            jax.ShapeDtypeStruct((seqs, 4, tile_count(words) * (ROWS // GROUP), GROUP), jnp.int32),
            jax.ShapeDtypeStruct((seqs,), jnp.int32),
        ]
        + [jax.ShapeDtypeStruct((n, GROUP), jnp.float32) for n in (CD, CD, D, D)],
        scratch_shapes=[pltpu.VMEM(s.shape, bf16) for s in shards]
        + [
            dma((5,)),
            dma((2, 5, ranks)),
            dma((5,)),
            dma((2, 4, dp // 2)),
            dma((2, 4, dp // 2)),
            dma((dp,)),
        ],
        compiler_params=pltpu.CompilerParams(
            collective_id=collective, has_side_effects=True, vmem_limit_bytes=VMEM_BYTES
        ),
        name="gather",
    )(*shards, counts, ids, gains)


def column_cuts(widths, ranks):
    block = sum(widths) // ranks
    cuts, start = [], 0
    for width in widths:
        mine, at = [], 0
        while at < width:
            rank, inside = divmod(start + at, block)
            take = min(width - at, block - inside)
            mine.append((rank, at, at + take, inside))
            at += take
        cuts.append(mine)
        start += width
    return cuts


def reduce_kernel(dp, ranks, groups, extra, *refs):
    pieces = sum(len(g) - done for g, done in groups)
    mats = len(groups)
    parts = refs[:pieces]
    gain_refs = refs[pieces : pieces + 4]
    ready = refs[pieces + 4 : pieces + 4 + extra]
    place = pieces + 4 + extra
    outs = refs[place : place + mats]
    gain_out, square_out = refs[place + mats : place + mats + 2]
    place += mats + 2
    pair_in = refs[place : place + pieces]
    pair_sum = refs[place + pieces : place + 2 * pieces]
    plane_in = refs[place + 2 * pieces : place + 3 * pieces]
    place += 3 * pieces
    line_sum, line_in = refs[place : place + mats], refs[place + mats : place + 2 * mats]
    place += 2 * mats
    small, pair_sem, plane_sem, line_sem, small_sem = refs[place:]
    ring = Ring(dp, ranks)
    chips = ring.chips
    f32, bf16 = jnp.float32, jnp.bfloat16
    ring.greet(all_dp=True)

    def share(slot, value, stage):
        peer, here, count = ((ring.across, ring.d, dp), (ring.line, ring.h, ranks))[stage]
        small[slot, stage, here] = value
        spot = small.at[slot, stage, here]
        return [send(spot, spot, small_sem, (slot, stage, k), peer(k)) for k in range(1, count)]

    def shared(slot, copies, stage):
        wait_all(copies)
        total = small[slot, stage, 0]
        for k in range(1, (dp, ranks)[stage]):
            total = total + small[slot, stage, k]
        return total

    def line_copy(m, k):
        return pltpu.make_async_remote_copy(
            src_ref=line_sum[m].at[ring.rank_at(k)],
            dst_ref=line_in[m].at[k],
            send_sem=line_sem.at[0, m, k],
            recv_sem=line_sem.at[1, m, k],
            device_id=ring.line(k),
            device_id_type=pl.DeviceIdType.MESH,
        )

    def put_columns(m, cuts, total):
        for rank, first, last, inside in cuts:
            line_sum[m][rank, :, inside : inside + last - first] = total[:, first:last]

    def early_rank(m):
        widths, done = groups[m]
        own = sum(widths[: len(widths) - done])
        ready_from = sum(
            w for at, w in enumerate(widths) if at < len(widths) - done
        ) if done else sum(widths)
        block = sum(widths) // ranks
        return -(-max(own, ready_from) // block)

    def begin(copy, now, first):
        if first == 0:
            copy.start()
        elif first < ranks:
            pl.when(now)(copy.start)

    starts = []
    j = 0
    for m, (widths, done) in enumerate(groups):
        lines = [line_copy(m, k) for k in range(1, ranks)]
        starts.append(lines)
        cuts = column_cuts(widths, ranks)
        for at in range(len(widths) - done, len(widths)):
            put_columns(m, cuts[at], ready[j][...])
            j += 1
    rows = []
    for ref in gain_refs:
        for at in range(0, ref.shape[0], GROUP):
            rows.append(jnp.sum(ref[at : at + GROUP, :].T, axis=0, keepdims=True))
    rows.append(jnp.zeros((small.shape[3] - len(rows), GROUP), f32))
    ring.meet()
    pairs = [
        send(parts[i].at[:, 1 - ring.core], pair_in[i], pair_sem, (i,), ring.sibling())
        for i in range(pieces)
    ]
    for m in range(mats):
        for k in range(1, ranks):
            begin(starts[m][k - 1], early_rank(m) <= ring.rank_at(k), early_rank(m))
    gain_copies = share(0, jnp.concatenate(rows, axis=0), 0)
    planes = []
    for i in range(pieces):
        pairs[i].wait()

        def add_pair(p, carry, i=i):
            both = parts[i][p, ring.core].astype(f32) + pair_in[i][p].astype(f32)
            pair_sum[i][p] = both.astype(bf16)
            return carry

        lax.fori_loop(0, chips, add_pair, 0)
        planes.append(
            [
                send(
                    pair_sum[i].at[ring.chip_at(k)],
                    plane_in[i].at[k],
                    plane_sem,
                    (i, k),
                    ring.plane(k),
                )
                for k in range(1, chips)
            ]
        )
    gain_copies = share(0, shared(0, gain_copies, 0), 1)
    i = 0
    for m, (widths, done) in enumerate(groups):
        for cuts in column_cuts(widths, ranks)[: len(widths) - done]:
            total = pair_sum[i][ring.chip].astype(f32)
            for k in range(1, chips):
                planes[i][k - 1].wait()
                total = total + plane_in[i][k].astype(f32)
            put_columns(m, cuts, total.astype(bf16))
            i += 1
        first = early_rank(m)
        for k in range(1, ranks):
            if first >= ranks:
                starts[m][k - 1].start()
            elif first > 0:
                pl.when(ring.rank_at(k) < first)(starts[m][k - 1].start)
    square = jnp.zeros(square_out.shape, f32)

    def squares(value):
        value = value * value
        rows, cols = value.shape
        if cols % GROUP:
            value = jnp.concatenate([value, jnp.zeros((rows, GROUP - cols % GROUP), f32)], axis=1)
        return jnp.sum(fold_lanes(value).reshape(rows // 8, 8, GROUP), axis=0)

    for m in range(mats):
        total = line_sum[m][ring.h].astype(f32)
        for k in range(1, ranks):
            starts[m][k - 1].wait()
            total = total + line_in[m][k].astype(f32)
        outs[m][...] = total if outs[m].shape == total.shape else total.T
        square = square + squares(total)
    small_square = jnp.concatenate([square, jnp.zeros_like(square)], axis=0)
    square_copies = share(1, small_square, 0)
    gain_out[...] = shared(0, gain_copies, 1)[: gain_out.shape[0]]
    square_copies = share(1, shared(1, square_copies, 0), 1)
    square_out[...] = shared(1, square_copies, 1)[:8]


def reduce_grads(groups, gains, collective):
    dp, ranks = lax.axis_size("dp"), lax.axis_size("head")
    chips = dp // 2
    bf16, f32 = jnp.bfloat16, jnp.float32
    pieces, ready, widths, shards = [], [], [], []
    for group, done in groups:
        rows = done[0].shape[0] if done else group[0].shape[0] // dp
        pieces += [p.reshape(chips, 2, rows, p.shape[1]) for p in group]
        ready += done
        widths.append((tuple(p.shape[1] for p in group + done), len(done)))
        shards.append((rows, sum(widths[-1][0]) // ranks))
    blocks = [p.shape[2:] for p in pieces]
    vmem = pl.BlockSpec(memory_space=pltpu.VMEM)
    n, mats = len(pieces), len(groups)
    gain_rows = sum(g.shape[0] for g in gains) // GROUP
    return pl.pallas_call(
        functools.partial(reduce_kernel, dp, ranks, widths, len(ready)),
        in_specs=[vmem] * (n + 4 + len(ready)),
        out_specs=[vmem] * (mats + 2),
        out_shape=[jax.ShapeDtypeStruct(s if s[1] % GROUP == 0 else s[::-1], f32) for s in shards]
        + [jax.ShapeDtypeStruct((gain_rows, GROUP), f32), jax.ShapeDtypeStruct((8, GROUP), f32)],
        scratch_shapes=[pltpu.VMEM((chips,) + b, bf16) for b in blocks] * 3
        + [pltpu.VMEM((ranks,) + s, bf16) for s in shards] * 2
        + [
            pltpu.VMEM((2, 2, max(dp, ranks), 16, GROUP), f32),
            pltpu.SemaphoreType.DMA((2, n)),
            pltpu.SemaphoreType.DMA((2, n, chips)),
            pltpu.SemaphoreType.DMA((2, mats, ranks)),
            pltpu.SemaphoreType.DMA((2, 2, 2, max(dp, ranks))),
        ],
        compiler_params=pltpu.CompilerParams(
            collective_id=collective, has_side_effects=True, vmem_limit_bytes=VMEM_BYTES
        ),
        name="reduce_grads",
    )(*pieces, *gains, *ready)


def update_kernel(count, *refs):
    weights, grads = refs[:count], refs[count : 2 * count]
    firsts, seconds = refs[2 * count : 3 * count], refs[3 * count : 4 * count]
    square_ref = refs[4 * count]
    norm_ref, outs = refs[4 * count + 1], refs[4 * count + 2 :]
    gain_grad = grads[-1][...]
    square = jnp.sum(square_ref[...]) + jnp.sum(gain_grad * gain_grad)
    norm = jnp.sqrt(jnp.full((1, GROUP), square, jnp.float32))
    norm_ref[...] = norm
    clip_factor = jnp.minimum(1.0, CLIP / norm)[:, :1]
    for i in range(count):
        gains = i == count - 1
        result = adam_step(
            weights[i][...],
            grads[i][...],
            firsts[i][...],
            seconds[i][...],
            clip_factor,
            GAIN_RATE if gains else MATRIX_RATE,
            0.0 if gains else MATRIX_DECAY,
        )
        for ref, value in zip(outs[5 * i : 5 * i + 5], result):
            ref[...] = value


def update(weights, grads, firsts, seconds, square):
    count = len(weights)
    shapes = [jax.ShapeDtypeStruct((1, GROUP), jnp.float32)]
    for w in weights:
        shapes += [jax.ShapeDtypeStruct(w.shape, jnp.float32)] * 4
        shapes.append(jax.ShapeDtypeStruct(w.shape, jnp.bfloat16))
    return pl.pallas_call(
        functools.partial(update_kernel, count),
        out_shape=shapes,
        compiler_params=pltpu.CompilerParams(vmem_limit_bytes=VMEM_BYTES),
        name="update",
    )(*weights, *grads, *firsts, *seconds, square)


def body(
    char_ids,
    char_counts,
    language,
    words_in,
    out_cotangent,
    char_table,
    char_in,
    char_down,
    word_in,
    word_down,
    norm_gains,
    old_table_first,
    old_table_second,
    old_char_in_first,
    old_char_in_second,
    old_char_down_first,
    old_char_down_second,
    old_word_in_first,
    old_word_in_second,
    old_word_down_first,
    old_word_down_second,
    old_gains_first,
    old_gains_second,
):
    narrow = (norm_gains.shape[0] // GROUP, GROUP)
    table_t, char_in_low, char_down_t, early, up_rows, down_rows, packed, tiles, *gains = gather(
        (char_table.T, char_in, char_down.T, word_in, word_down),
        char_counts,
        char_ids.transpose(0, 2, 1),
        norm_gains.reshape(narrow),
        0,
    )

    def joined(block):
        if block.ndim == 2:
            return block
        dp, ranks, cols, rows = block.shape
        return block.transpose(1, 2, 0, 3).reshape(ranks * cols, dp * rows)

    def stacked(block):
        return block.reshape(-1, block.shape[2])

    table_t = joined(table_t)
    char_in_low = stacked(char_in_low)
    early = stacked(lax.all_to_all(early, "dp", 0, 0, tiled=True))
    char_others = (char_in_low, joined(char_down_t), gains[0], gains[1])
    sums, *kept = char_fwd(tiles, language, packed, table_t, char_others, words_in.shape[1])
    (
        output,
        input_grad,
        spread,
        grad_qkv,
        grad_pool,
        gain_three,
        gain_four,
        down_sum,
        up_sum,
        out_sum,
    ) = word_layer(
        sums,
        char_counts,
        words_in,
        out_cotangent,
        char_in_low,
        early,
        gains[2:],
        up_rows,
        down_rows,
        1,
    )
    grad_table, grad_in, grad_down, gain_one, gain_two = char_bwd(
        tiles, language, packed, table_t, char_others, spread, kept
    )
    blocks = lax.all_to_all(
        grad_qkv.reshape(lax.axis_size("dp"), -1, grad_qkv.shape[1]), "dp", 0, 0, tiled=True
    )
    qkv_sum = jnp.sum(blocks.astype(jnp.float32), axis=0).astype(jnp.bfloat16)
    *shards, gains_sum, square = reduce_grads(
        [
            ([grad_table], []),
            ([grad_in, grad_pool], []),
            ([grad_down], []),
            ([], [qkv_sum, out_sum, up_sum]),
            ([], [down_sum]),
        ],
        (gain_one, gain_two, gain_three, gain_four),
        2,
    )

    def turned(parts):
        parts = list(parts)
        parts[0], parts[2] = parts[0].T, parts[2].T
        parts[5] = parts[5].reshape(narrow)
        return parts

    norm, *updated = update(
        turned((char_table, char_in, char_down, word_in, word_down, norm_gains)),
        (*shards, gains_sum),
        turned(
            (
                old_table_first,
                old_char_in_first,
                old_char_down_first,
                old_word_in_first,
                old_word_down_first,
                old_gains_first,
            )
        ),
        turned(
            (
                old_table_second,
                old_char_in_second,
                old_char_down_second,
                old_word_in_second,
                old_word_down_second,
                old_gains_second,
            )
        ),
        square,
    )
    for place in (*range(5), *range(10, 15)):
        updated[place] = updated[place].T
    updated[-5:] = [part.reshape(norm_gains.shape) for part in updated[-5:]]
    return (output, input_grad, norm[0, 0], *updated)


def solution(mesh):
    return jax.shard_map(
        body,
        mesh=mesh,
        in_specs=(
            P("dp", "head", None),
            P("dp", "head"),
            P("dp"),
            P("dp", "head", None),
            P("dp", "head", None),
            P("dp", "head"),
            P("dp", "head"),
            P("dp", "head"),
            P("dp", "head"),
            P("dp", "head"),
            P(),
            P("dp", "head"),
            P("dp", "head"),
            P("dp", "head"),
            P("dp", "head"),
            P("dp", "head"),
            P("dp", "head"),
            P("dp", "head"),
            P("dp", "head"),
            P("dp", "head"),
            P("dp", "head"),
            P(),
            P(),
        ),
        out_specs=(
            P("dp", "head", None),
            P("dp", "head", None),
            P(),
            P("dp", "head"),
            P("dp", "head"),
            P("dp", "head"),
            P("dp", "head"),
            P("dp", "head"),
            P("dp", "head"),
            P("dp", "head"),
            P("dp", "head"),
            P("dp", "head"),
            P("dp", "head"),
            P("dp", "head"),
            P("dp", "head"),
            P("dp", "head"),
            P("dp", "head"),
            P("dp", "head"),
            P("dp", "head"),
            P("dp", "head"),
            P("dp", "head"),
            P("dp", "head"),
            P("dp", "head"),
            P("dp", "head"),
            P("dp", "head"),
            P("dp", "head"),
            P("dp", "head"),
            P("dp", "head"),
            P(),
            P(),
            P(),
            P(),
            P(),
        ),
        check_vma=False,
    )
```

```python
import functools

import jax
import jax.numpy as jnp
from jax import lax
from jax.experimental import pallas as pl
from jax.experimental.pallas import tpu as pltpu
from jax.sharding import PartitionSpec as P

D = 512
HEADS = 8
CD = 256
CHEADS = 4
CFF = 1024
CV = 256
STEP = 5


EPS = 1e-05
CLIP = 1.0
MATRIX_RATE = 0.03
GAIN_RATE = 0.25
MATRIX_DECAY = 0.1
BETA_ONE = 0.5
BETA_TWO = 0.5
ADAM_EPS = 1e-08
NEG_FILL = -1e30
SQRT_HALF = 0.7071067811865476
INV_ROOT_TWO_PI = 0.3989422804014327


ROWS = 512
SLOTS = 16
FWD_CHUNK = 512
BWD_CHUNK = 1024
WORD_CHUNK = 512
CHAINS = 1
GROUP = 128
VMEM_BYTES = 56 * 1024 * 1024


def dot_nn(left_side, right_side):
    return lax.dot_general(
        left_side, right_side, (((1,), (0,)), ((), ())), preferred_element_type=jnp.float32
    )


def dot_tn(left_side, right_side):
    return lax.dot_general(
        left_side, right_side, (((0,), (0,)), ((), ())), preferred_element_type=jnp.float32
    )


def dot_nt(left_side, right_side):
    return lax.dot_general(
        left_side, right_side, (((1,), (1,)), ((), ())), preferred_element_type=jnp.float32
    )


def gelu_pair(upper):
    phi = 0.5 + 0.5 * lax.erf(upper * SQRT_HALF)
    bell = jnp.exp(upper * upper * -0.5)
    return upper * phi, phi + upper * (bell * INV_ROOT_TWO_PI)


def iota(shape, dim):
    return lax.broadcasted_iota(jnp.int32, shape, dim)


def split_two(values):
    high = values.astype(jnp.bfloat16)
    return high, (values - high.astype(jnp.float32)).astype(jnp.bfloat16)


def pack_words(row, ids, out_ref, tiles_ref, seq):
    n = row.shape[1]
    col = jnp.broadcast_to(row.astype(jnp.float32), (8, n)).T[:, :1].astype(jnp.int32)
    sub, lane = iota((n, n), 0), iota((n, n), 1)
    ahead = (row > col) | ((row == col) & (lane < sub))
    rank_col = jnp.sum(ahead.astype(jnp.float32), axis=1, keepdims=True).astype(jnp.int32)
    ahead = (col > row) | ((col == row) & (sub < lane))
    rank_row = jnp.sum(ahead.astype(jnp.float32), axis=0, keepdims=True).astype(jnp.int32)
    clash = (rank_col < rank_row) & (col + row > SLOTS)
    alone = jnp.max(jnp.where(clash, rank_col + rank_row, 0).astype(jnp.float32))
    alone = jnp.maximum(alone.astype(jnp.int32) - n + 2, 0)
    partner = n - 1 + alone - rank_row
    second = (rank_row >= alone) & (rank_row > partner)
    bins = jnp.where(second, partner, rank_row)
    here = sub == bins
    first_map = (here & jnp.logical_not(second)).astype(jnp.float32).astype(jnp.bfloat16)
    second_map = (here & second).astype(jnp.float32).astype(jnp.bfloat16)
    pos = lax.rem(iota((GROUP, n), 0), SLOTS)
    word = iota((GROUP, n), 1) + 1
    wide = jnp.broadcast_to(row, (GROUP, n))
    in_first, in_second = pos < wide, pos >= SLOTS - wide

    def kept(mask, values):
        return jnp.where(mask, values, 0).astype(jnp.float32).astype(jnp.bfloat16)

    groups = n * SLOTS // GROUP
    spare = out_ref.shape[2] - groups
    per = GROUP // SLOTS
    own = iota((groups, per, GROUP), 1) == lax.div(iota((groups, per, GROUP), 2), SLOTS)
    back = jnp.concatenate([ids[SLOTS - 1 - j : SLOTS - j] for j in range(SLOTS)] * per, axis=0)
    ids = jnp.concatenate([ids] * per, axis=0)
    zero = jnp.zeros_like(wide)
    for k, (one, two) in enumerate(
        ((ids + 1, back + 1), (word, word), (zero, SLOTS - wide), (wide, zero + SLOTS))
    ):
        full = dot_nt(first_map, kept(in_first, one)) + dot_nt(second_map, kept(in_second, two))
        full = jnp.where(own, full.reshape(groups, per, GROUP), 0.0)
        full = jnp.sum(full, axis=1).astype(jnp.int32)
        if spare:
            full = jnp.concatenate([full, jnp.zeros((spare, GROUP), jnp.int32)], axis=0)
        out_ref[seq, k] = full
    used = alone + lax.div(n - alone + 1, 2)
    tiles_ref[seq] = lax.div(used * SLOTS + ROWS - 1, ROWS)


def lane_map(rows, size):
    spots = iota((size, GROUP), 0) + 1
    maps = [
        (spots == rows[g : g + 1]).astype(jnp.float32).astype(jnp.bfloat16)
        for g in range(rows.shape[0])
    ]
    return jnp.concatenate(maps, axis=1)


def in_step(chains):
    results = [None] * len(chains)
    waiting = list(enumerate(chains))
    running = []
    while waiting or running:
        if waiting:
            running.append(waiting.pop(0))
        for item in list(running):
            try:
                next(item[1])
            except StopIteration as stop:
                results[item[0]] = stop.value
                running.remove(item)
    return results


def lane_copies(ref, width):
    return jnp.concatenate([ref[...]] * (width // GROUP), axis=1)


def column_rms(values):
    inverse = lax.rsqrt(jnp.mean(values * values, axis=0, keepdims=True) + EPS)
    return values * inverse, inverse


def cost(flops, moved, powers):
    return pl.CostEstimate(flops=int(flops), bytes_accessed=int(moved), transcendentals=int(powers))


def tile_count(words):
    return -(-words * SLOTS // ROWS)


def tile_at(step, tiles_ref, seqs):
    seq, start, total = 0, 0, tiles_ref[0]
    for s in range(1, seqs):
        past = step >= total
        seq, start = jnp.where(past, s, seq), jnp.where(past, total, start)
        total = total + tiles_ref[s]
    return seq, step - start, total


def placed(seqs, index):
    def place(step, tiles_ref, language_ref):
        total = tile_at(step, tiles_ref, seqs)[2]
        seq, tile, _ = tile_at(jnp.minimum(step, total - 1), tiles_ref, seqs)
        return index(seq, tile, language_ref)

    return place


def own_block():
    shape = (GROUP // SLOTS, SLOTS, CHEADS * GROUP)
    return iota(shape, 0) == lax.div(lax.rem(iota(shape, 2), GROUP), SLOTS)


def to_compact(block, own):
    return jnp.sum(jnp.where(own, block.reshape(own.shape), 0.0), axis=0)


def from_compact(compact, own):
    wide = jnp.broadcast_to(compact[None], own.shape)
    return jnp.where(own, wide, 0.0).astype(jnp.bfloat16).reshape(GROUP, -1)


def stack_heads(wide):
    return jnp.concatenate([wide[:, h * GROUP : (h + 1) * GROUP] for h in range(CHEADS)], axis=0)


def spread_heads(values):
    head = values.shape[0] // CHEADS
    zero = jnp.zeros((head, GROUP), values.dtype)
    rows = []
    for h in range(CHEADS):
        parts = [zero] * CHEADS
        parts[h] = values[h * head : (h + 1) * head]
        rows.append(jnp.concatenate(parts, axis=1))
    return jnp.concatenate(rows, axis=0)


def char_fwd_kernel(seqs, tiles_ref, language_ref, *refs):
    step = pl.program_id(0)
    _, tile, total = tile_at(step, tiles_ref, seqs)

    @pl.when(step < total)
    def _():
        char_fwd_tile(tile, *refs)


def char_fwd_tile(
    step, pack_ref, table_ref, in_ref, down_ref, g1_ref, g2_ref, pooled_ref,
    keep_values, keep_probs, keep_qkv, keep_mixed, keep_first, keep_hidden, keep_slope,
):
    words = pooled_ref.shape[2]
    per = ROWS // GROUP
    head = CD // CHEADS

    @pl.when(step == 0)
    def _():
        pooled_ref[...] = jnp.zeros_like(pooled_ref)

    own = own_block()
    key_pos = iota((SLOTS, GROUP), 0)
    packs = [pack_ref[0, k, pl.ds(step * per, per), :] for k in range(4)]

    def chain(part):
        groups = per // CHAINS
        cols = slice(part * groups * GROUP, (part + 1) * groups * GROUP)
        size = groups * GROUP
        ids, spots, low_rows, high_rows = (p[part * groups : (part + 1) * groups] for p in packs)
        embedded = dot_nn(table_ref[...], lane_map(ids, CV))
        yield
        act_one = (column_rms(embedded)[0] * lane_copies(g1_ref, size)).astype(jnp.bfloat16)
        triple = dot_tn(in_ref[:, : 3 * CD], act_one).astype(jnp.bfloat16)
        keep_qkv[:, cols] = triple
        yield
        key_rows = triple[CD : 2 * CD].T
        keep_values[cols, :] = triple[2 * CD :].T
        all_probs = []
        for g in range(groups):
            valid = (key_pos >= low_rows[g : g + 1]) & (key_pos < high_rows[g : g + 1])
            valid = jnp.concatenate([valid.astype(jnp.float32)] * CHEADS, axis=1) > 0
            lanes = slice(g * GROUP, (g + 1) * GROUP)
            scores = to_compact(dot_nn(key_rows[lanes], spread_heads(triple[:CD, lanes])), own)
            scores = jnp.where(valid, scores * head**-0.5, NEG_FILL)
            powers = jnp.exp(scores - jnp.max(scores, axis=0, keepdims=True))
            powers = jnp.where(valid, powers, 0.0)
            total = jnp.sum(powers, axis=0, keepdims=True)
            probs = powers / jnp.where(total > 0, total, 1.0)
            wide = (part * groups + g) * CHEADS * GROUP
            keep_probs[:, wide : wide + CHEADS * GROUP] = probs
            all_probs.append(from_compact(probs, own))
        yield
        mixed = []
        for g in range(groups):
            lanes = slice(g * GROUP, (g + 1) * GROUP)
            values = spread_heads(triple[2 * CD :, lanes])
            mixed.append(dot_nn(values, stack_heads(all_probs[g])).astype(jnp.bfloat16))
        mixed = jnp.concatenate(mixed, axis=1)
        keep_mixed[:, cols] = mixed
        yield
        first = embedded + dot_tn(in_ref[:, 3 * CD : 4 * CD], mixed)
        keep_first[:, cols] = first
        act_two = (column_rms(first)[0] * lane_copies(g2_ref, size)).astype(jnp.bfloat16)
        second = first
        for c in range(CFF // FWD_CHUNK):
            yield
            rows = slice(c * FWD_CHUNK, (c + 1) * FWD_CHUNK)
            up = in_ref[:, 4 * CD + c * FWD_CHUNK : 4 * CD + (c + 1) * FWD_CHUNK]
            hidden, slope = gelu_pair(dot_tn(up, act_two))
            hidden = hidden.astype(jnp.bfloat16)
            keep_hidden[rows, cols] = hidden
            keep_slope[rows, cols] = slope.astype(jnp.bfloat16)
            second = second + dot_nn(down_ref[:, rows], hidden)
        yield
        return lane_map(spots, words), split_two(second)

    ends = in_step([chain(part) for part in range(CHAINS)])
    word_map = jnp.concatenate([end[0] for end in ends], axis=1)
    high = jnp.concatenate([end[1][0] for end in ends], axis=1)
    low = jnp.concatenate([end[1][1] for end in ends], axis=1)
    halves = dot_nt(jnp.concatenate([high, low], axis=0), word_map)
    pooled_ref[0] += halves[:CD] + halves[CD:]


KEPT = (
    (3 * CD, jnp.bfloat16),
    (CD, jnp.bfloat16),
    (CD, jnp.float32),
    (CFF, jnp.bfloat16),
    (CFF, jnp.bfloat16),
)


def kept_specs(seqs, count):
    place = placed(seqs, lambda seq, tile, _: (0, seq * count + tile))
    return [
        pl.BlockSpec((ROWS, CD), lambda *at: place(*at)[::-1]),
        pl.BlockSpec((SLOTS, CHEADS * ROWS), place),
    ] + [pl.BlockSpec((depth, ROWS), place) for depth, _ in KEPT]


def kept_shapes(rows):
    return [
        jax.ShapeDtypeStruct((rows, CD), jnp.bfloat16),
        jax.ShapeDtypeStruct((SLOTS, CHEADS * rows), jnp.float32),
    ] + [jax.ShapeDtypeStruct((depth, rows), dtype) for depth, dtype in KEPT]


def whole(array):
    zeros = (0,) * array.ndim
    return pl.BlockSpec(array.shape, lambda *_: zeros)


def char_specs(seqs, pack, others):
    one = (1,) + pack.shape[1:]
    return [
        pl.BlockSpec(one, placed(seqs, lambda seq, tile, _: (seq, 0, 0, 0))),
        pl.BlockSpec((CD, CV), placed(seqs, lambda seq, tile, language: (0, language[seq]))),
    ] + [whole(a) for a in others]


def char_fwd(tiles, language, pack, table, others, words):
    seqs = pack.shape[0]
    count = tile_count(words)
    one = placed(seqs, lambda seq, tile, _: (seq, 0, 0))
    return pl.pallas_call(
        functools.partial(char_fwd_kernel, seqs),
        grid_spec=pltpu.PrefetchScalarGridSpec(
            num_scalar_prefetch=2,
            grid=(seqs * count,),
            in_specs=char_specs(seqs, pack, others),
            out_specs=[pl.BlockSpec((1, CD, words), one)] + kept_specs(seqs, count),
        ),
        out_shape=[jax.ShapeDtypeStruct((seqs, CD, words), jnp.float32)]
        + kept_shapes(seqs * count * ROWS),
        compiler_params=pltpu.CompilerParams(vmem_limit_bytes=VMEM_BYTES),
        cost_estimate=cost(3e10, 6e7, 1e7),
        name="char_fwd",
    )(tiles, language, pack, table, *others)


def fold_lanes(values):
    total = values[:, :GROUP]
    for g in range(1, values.shape[1] // GROUP):
        total = total + values[:, g * GROUP : (g + 1) * GROUP]
    return total


def column_rms_back(grad_in, gain, normed, inverse):
    scaled = grad_in * gain
    return inverse * (scaled - normed * jnp.mean(scaled * normed, axis=0, keepdims=True))


def char_bwd_kernel(seqs, tiles_ref, language_ref, *refs):
    step = pl.program_id(0)
    seq, tile, total = tile_at(step, tiles_ref, seqs)

    @pl.when(step < total)
    def _():
        char_bwd_tile(tile, step == 0, step == total - 1, language_ref[seq] * CV, *refs)


def char_bwd_tile(
    step, at_start, at_end, letter, pack_ref, table_ref, in_ref, down_ref, g1_ref, g2_ref, spread_ref,
    keep_values, keep_probs, keep_qkv, keep_mixed, keep_first, keep_hidden, keep_slope,
    *refs,
):
    results, totals = refs[:5], refs[5:]
    d_table, d_in, d_down, d_g1, d_g2 = totals
    words = spread_ref.shape[2]
    per = ROWS // GROUP
    head = CD // CHEADS

    @pl.when(at_start)
    def _():
        for ref in totals:
            ref[...] = jnp.zeros_like(ref)

    own = own_block()
    packs = [pack_ref[0, k, pl.ds(step * per, per), :] for k in range(2)]

    def chain(part):
        groups = per // CHAINS
        cols = slice(part * groups * GROUP, (part + 1) * groups * GROUP)
        size = groups * GROUP
        ids, spots = (p[part * groups : (part + 1) * groups] for p in packs)
        halves = dot_nn(spread_ref[0], lane_map(spots, words))
        grad_second = halves[:CD] + halves[CD:]
        grad_branch = grad_second.astype(jnp.bfloat16)
        normed_two, inverse_two = column_rms(keep_first[:, cols])
        gain_two = lane_copies(g2_ref, size)
        act_two = (normed_two * gain_two).astype(jnp.bfloat16)
        grad_uppers = []
        grad_act_two = None
        for c in range(CFF // BWD_CHUNK):
            yield
            rows = slice(c * BWD_CHUNK, (c + 1) * BWD_CHUNK)
            slope = keep_slope[rows, cols].astype(jnp.float32)
            grad_upper = dot_tn(down_ref[:, rows], grad_branch) * slope
            grad_upper = grad_upper.astype(jnp.bfloat16)
            grad_uppers.append(grad_upper)
            piece = dot_nn(in_ref[:, 4 * CD + c * BWD_CHUNK : 4 * CD + (c + 1) * BWD_CHUNK], grad_upper)
            grad_act_two = piece if grad_act_two is None else grad_act_two + piece
        yield
        gain_sum_two = fold_lanes(grad_act_two * normed_two)
        grad_first = grad_second + column_rms_back(
            grad_act_two, gain_two, normed_two, inverse_two
        )
        grad_attn = grad_first.astype(jnp.bfloat16)
        grad_mixed = dot_nn(in_ref[:, 3 * CD : 4 * CD], grad_attn).astype(jnp.bfloat16)
        yield
        triple = keep_qkv[:, cols]
        raws, lows = [], []
        for g in range(groups):
            lanes = slice(g * GROUP, (g + 1) * GROUP)
            at = part * groups + g
            wide = slice(at * CHEADS * GROUP, (at + 1) * CHEADS * GROUP)
            probs = keep_probs[:, wide]
            values = keep_values[at * GROUP : (at + 1) * GROUP, :]
            grad_probs = to_compact(dot_nn(values, spread_heads(grad_mixed[:, lanes])), own)
            grad_scores = probs * (
                grad_probs - jnp.sum(probs * grad_probs, axis=0, keepdims=True)
            )
            raws.append(from_compact(grad_scores * head**-0.5, own))
            lows.append(from_compact(probs, own))
        yield
        columns = []
        for g in range(groups):
            lanes = slice(g * GROUP, (g + 1) * GROUP)
            grad_q = dot_nn(spread_heads(triple[CD : 2 * CD, lanes]), stack_heads(raws[g]))
            grad_k = dot_nt(spread_heads(triple[:CD, lanes]), raws[g])
            grad_v = dot_nt(spread_heads(grad_mixed[:, lanes]), lows[g])
            columns.append(jnp.concatenate([grad_q, grad_k, grad_v], axis=0).astype(jnp.bfloat16))
        grad_triple = jnp.concatenate(columns, axis=1)
        yield
        one_hot = lane_map(ids, CV)
        embedded = dot_nn(table_ref[...], one_hot)
        normed_one, inverse_one = column_rms(embedded)
        gain_one = lane_copies(g1_ref, size)
        act_one = (normed_one * gain_one).astype(jnp.bfloat16)
        grad_act_one = dot_nn(in_ref[:, : 3 * CD], grad_triple)
        yield
        gain_sum_one = fold_lanes(grad_act_one * normed_one)
        back_one = column_rms_back(grad_act_one, gain_one, normed_one, inverse_one)
        grad_embedded = (grad_first + back_one).astype(jnp.bfloat16)
        grad_upper = jnp.concatenate(grad_uppers, axis=0)
        return (
            gain_sum_one, gain_sum_two, grad_branch, act_two, grad_upper, grad_attn,
            act_one, grad_triple, one_hot, grad_embedded,
        )

    ends = in_step([chain(part) for part in range(CHAINS)])
    for end in ends:
        d_g1[...] += end[0]
        d_g2[...] += end[1]
    grad_branch, act_two, grad_upper, grad_attn, act_one, grad_triple, one_hot, grad_embedded = (
        jnp.concatenate(parts, axis=1) for parts in list(zip(*ends))[2:]
    )
    d_down[...] += dot_nt(keep_hidden[...], grad_branch)
    d_in[:, 4 * CD :] += dot_nt(act_two, grad_upper)
    d_in[:, 3 * CD : 4 * CD] += dot_nt(keep_mixed[...], grad_attn)
    d_in[:, : 3 * CD] += dot_nt(act_one, grad_triple)
    d_table[pl.ds(pl.multiple_of(letter, CV), CV), :] += dot_nt(one_hot, grad_embedded)

    @pl.when(at_end)
    def _():
        for ref, total in zip(results, totals):
            ref[...] = total[...].astype(ref.dtype)


def char_bwd(tiles, language, pack, table, others, spread, kept):
    shapes = (
        table.shape[::-1],
        (CD, 4 * CD + CFF),
        (CFF, CD),
        (CD, GROUP),
        (CD, GROUP),
    )
    f32, bf16 = jnp.float32, jnp.bfloat16
    kinds = [bf16] * 3 + [f32] * 2
    seqs = pack.shape[0]
    count = tile_count(spread.shape[2])
    one = (1,) + spread.shape[1:]
    return pl.pallas_call(
        functools.partial(char_bwd_kernel, seqs),
        grid_spec=pltpu.PrefetchScalarGridSpec(
            num_scalar_prefetch=2,
            grid=(seqs * count,),
            in_specs=char_specs(seqs, pack, others)
            + [pl.BlockSpec(one, placed(seqs, lambda seq, tile, _: (seq, 0, 0)))]
            + kept_specs(seqs, count),
            out_specs=[pl.BlockSpec(s, lambda *_: (0, 0)) for s in shapes],
            scratch_shapes=[pltpu.VMEM(s, f32) for s in shapes],
        ),
        out_shape=[jax.ShapeDtypeStruct(s, kind) for s, kind in zip(shapes, kinds)],
        compiler_params=pltpu.CompilerParams(vmem_limit_bytes=VMEM_BYTES),
        cost_estimate=cost(5e10, 6e7, 1e6),
        name="char_bwd",
    )(tiles, language, pack, table, *others, spread, *kept)


def adam_step(weight, grad, first_old, second_old, clip_factor, rate, decay):
    clipped = grad * clip_factor
    first_new = BETA_ONE * first_old + (1.0 - BETA_ONE) * clipped
    second_new = BETA_TWO * second_old + (1.0 - BETA_TWO) * clipped * clipped
    first_hat = first_new / (1.0 - BETA_ONE**STEP)
    second_hat = second_new / (1.0 - BETA_TWO**STEP)
    weight_new = weight - rate * (first_hat / (jnp.sqrt(second_hat) + ADAM_EPS) + decay * weight)
    return (grad, first_new, second_new, weight_new, weight_new.astype(jnp.bfloat16))


class Ring:
    def __init__(self, dp, ranks):
        self.chips, self.ranks = dp // 2, ranks
        self.d, self.h = lax.axis_index("dp"), lax.axis_index("head")
        self.chip, self.core = lax.div(self.d, 2), lax.rem(self.d, 2)

    def sibling(self):
        return (self.d + 1 - 2 * self.core, self.h)

    def chip_at(self, k):
        if self.chips != 4:
            return lax.rem(self.chip + k, self.chips)
        return (None, self.chip + 1 - 2 * lax.rem(self.chip, 2), lax.rem(self.chip + 2, 4), 3 - self.chip)[k]

    def chip_from(self, k):
        if self.chips != 4:
            return lax.rem(self.chip + self.chips - k, self.chips)
        return self.chip_at(k)

    def plane(self, k):
        return (2 * self.chip_at(k) + self.core, self.h)

    def across(self, k):
        return (lax.rem(self.d + k, 2 * self.chips), self.h)

    def rank_at(self, k):
        return lax.rem(self.h + k, self.ranks)

    def line(self, k):
        return (self.d, self.rank_at(k))

    def greet(self, all_dp=False):
        barrier = pltpu.get_barrier_semaphore()
        if all_dp:
            peers = [self.across(k) for k in range(1, 2 * self.chips)]
        else:
            peers = [self.sibling()]
            peers += [self.plane(k) for k in range(1, self.chips)]
        peers += [self.line(k) for k in range(1, self.ranks)]
        self.partners = len(peers)
        for peer in peers:
            pl.semaphore_signal(barrier, inc=1, device_id=peer, device_id_type=pl.DeviceIdType.MESH)

    def meet(self):
        pl.semaphore_wait(pltpu.get_barrier_semaphore(), self.partners)


def send(src, dst, sems, place, peer):
    copy = pltpu.make_async_remote_copy(
        src_ref=src,
        dst_ref=dst,
        send_sem=sems.at[(0,) + place],
        recv_sem=sems.at[(1,) + place],
        device_id=peer,
        device_id_type=pl.DeviceIdType.MESH,
    )
    copy.start()
    return copy


def word_scores(q, k, diagonal):
    scores = dot_tn(k, q) * (D // HEADS) ** -0.5
    if diagonal:
        scores = jnp.where(iota(scores.shape, 0) <= iota(scores.shape, 1), scores, NEG_FILL)
    return scores


def head_rows(ref, n, part, kind):
    head = D // HEADS
    return ref[n, part, kind * head : (kind + 1) * head, :]


def word_attention(n, triple_ref, mixed_ref, lse_ref):
    for i in range(triple_ref.shape[1]):
        q = head_rows(triple_ref, n, i, 0)
        scores = [word_scores(q, head_rows(triple_ref, n, j, 1), i == j) for j in range(i + 1)]
        highest = jnp.max(scores[0], axis=0, keepdims=True)
        for block in scores[1:]:
            highest = jnp.maximum(highest, jnp.max(block, axis=0, keepdims=True))
        powers = [jnp.exp(block - highest) for block in scores]
        total = jnp.sum(powers[0], axis=0, keepdims=True)
        for block in powers[1:]:
            total = total + jnp.sum(block, axis=0, keepdims=True)
        inverse = 1.0 / total
        mixed = None
        for j, block in enumerate(powers):
            part = dot_nn(head_rows(triple_ref, n, j, 2), (block * inverse).astype(jnp.bfloat16))
            mixed = part if mixed is None else mixed + part
        mixed_ref[n, i] = mixed.astype(jnp.bfloat16)
        lse_ref[n, i] = jnp.broadcast_to(highest + jnp.log(total), lse_ref.shape[2:])


def word_attention_back(n, triple_ref, lse_ref, grad_ref, out_ref, dk, dv):
    parts = triple_ref.shape[1]
    head = D // HEADS
    for i in range(parts):
        q = head_rows(triple_ref, n, i, 0)
        grad_o = grad_ref[n, i]
        lse = lse_ref[n, i][:1]
        probs, grads = [], []
        dot_sum = None
        for j in range(i + 1):
            scores = word_scores(q, head_rows(triple_ref, n, j, 1), i == j)
            probs.append(jnp.exp(scores - lse))
            grads.append(dot_tn(head_rows(triple_ref, n, j, 2), grad_o))
            part = jnp.sum(probs[-1] * grads[-1], axis=0, keepdims=True)
            dot_sum = part if dot_sum is None else dot_sum + part
        grad_q = None
        for j in range(i + 1):
            raw = (probs[j] * (grads[j] - dot_sum) * head**-0.5).astype(jnp.bfloat16)
            part = dot_nn(head_rows(triple_ref, n, j, 1), raw)
            grad_q = part if grad_q is None else grad_q + part
            part_k = dot_nt(q, raw)
            part_v = dot_nt(grad_o, probs[j].astype(jnp.bfloat16))
            if i == j:
                dk[j] = part_k
                dv[j] = part_v
            else:
                dk[j] += part_k
                dv[j] += part_v
        out_ref[n, i, :head, :] = grad_q.astype(jnp.bfloat16)
    for j in range(parts):
        out_ref[n, j, head : 2 * head, :] = dk[j].astype(jnp.bfloat16)
        out_ref[n, j, 2 * head :, :] = dv[j].astype(jnp.bfloat16)


def swap_copies(ring, src, dst, n, sems):
    return [
        pltpu.make_async_remote_copy(
            src_ref=src.at[n, ring.rank_at(k)],
            dst_ref=dst.at[n, ring.h],
            send_sem=sems.at[0, n, k],
            recv_sem=sems.at[1, n, k],
            device_id=ring.line(k),
            device_id_type=pl.DeviceIdType.MESH,
        )
        for k in range(1, ring.ranks)
    ]


def swap_start(ring, src, dst, n, sems):
    for copy in swap_copies(ring, src, dst, n, sems):
        copy.start()
    dst[n, ring.h] = src[n, ring.h]


def swap_wait(ring, src, dst, n, sems):
    wait_all(swap_copies(ring, src, dst, n, sems))


def wait_all(copies):
    for copy in copies:
        copy.wait()


def word_kernel(dp, ranks, *refs):
    (sum_ref, count_ref, words_ref, cot_ref, in_ref, early_ref, g3_ref, g4_ref) = refs[:8]
    up_rows, down_rows = refs[8:10]
    (output_ref, input_grad_ref, spread_ref, d_qkv, d_pool, d_g3, d_g4) = refs[10:17]
    sums = refs[17:20]
    (starts, pooleds, afters, lses, up_ref, down_ref) = refs[20:26]
    (acts, hiddens, grad_ups, cots, lows, mixes, triples) = refs[26:33]
    (triple_ref, triple_in, triple_back, mixed_ref, mixed_in, mixed_back) = refs[33:39]
    dk, dv = refs[39:41]
    grads, pair_in, plane_in = refs[41:44], refs[44:47], refs[47:50]
    (own_sem, late_sem, late_pair_sem) = refs[50:53]
    (triple_sem, mixed_sem, mixed_back_sem, triple_back_sem, pair_sem, plane_sem) = refs[53:]
    ring = Ring(dp, ranks)
    chips = ring.chips
    f32, bf16 = jnp.float32, jnp.bfloat16
    ring.greet()
    seqs, width, _ = words_ref.shape
    hidden_size = up_ref.shape[1]
    head = D // HEADS
    heads = HEADS // ranks
    count = seqs * heads
    g3, g4 = lane_copies(g3_ref, width), lane_copies(g4_ref, width)

    def begin(s):
        pooled = (sum_ref[s] / count_ref[s : s + 1, :].astype(f32)).astype(bf16)
        pooleds[s] = pooled
        start = words_ref[s].astype(f32).T + dot_tn(in_ref[:, 4 * CD + CFF :], pooled)
        starts[s] = start
        act = (column_rms(start)[0] * g3).astype(bf16)
        for t in range(3):
            triple = dot_tn(early_ref[:, t * D : (t + 1) * D], act).astype(bf16)
            for r in range(ranks):
                for h in range(heads):
                    at = (r * heads + h) * head
                    triple_ref[s * heads + h, r, t * head : (t + 1) * head, :] = triple[
                        at : at + head
                    ]

    def begin_sends(s):
        for h in range(heads):
            swap_start(ring, triple_ref, triple_in, s * heads + h, triple_sem)

    begin(0)
    ring.meet()
    begin_sends(0)

    wide = early_ref.shape[1]

    def late_place(m, d):
        ref = (up_ref, down_ref)[m]
        rows = ref.shape[0] // dp
        return ref.at[pl.ds(pl.multiple_of(d * rows, rows), rows), :]

    late = (up_rows.at[:, wide:], down_rows)
    own, rounds, late_pairs = [], [], []
    for m in range(2):
        place = late_place(m, ring.d)
        own.append(pltpu.make_async_copy(late[m], place, own_sem.at[m]))
        own[-1].start()
        rounds.append(
            [send(late[m], place, late_sem, (m, k), ring.plane(k)) for k in range(1, chips)]
        )
        late_pairs.append(send(late[m], place, late_pair_sem, (m, 0), ring.sibling()))

    for s in range(1, seqs):
        begin(s)
        begin_sends(s)
    for m in range(2):
        for k in range(1, chips):
            rounds[m][k - 1].wait_recv()
            block = late_place(m, 2 * ring.chip_from(k) + ring.core)
            late_pairs.append(send(block, block, late_pair_sem, (m, k), ring.sibling()))

    def attend(n, carry):
        swap_wait(ring, triple_ref, triple_in, n, triple_sem)
        word_attention(n, triple_in, mixed_ref, lses)
        swap_start(ring, mixed_ref, mixed_in, n, mixed_sem)
        return carry

    def attend_back(n, carry):
        swap_wait(ring, mixed_ref, mixed_back, n, mixed_back_sem)
        word_attention_back(n, triple_in, lses, mixed_back, triple_ref, dk, dv)
        swap_start(ring, triple_ref, triple_back, n, triple_back_sem)
        return carry

    pairs, planes = {}, {}

    def put_grad(i, value):
        grads[i][...] = value.astype(bf16).reshape(grads[i].shape)
        pairs[i] = send(
            grads[i].at[:, 1 - ring.core], pair_in[i], pair_sem, (i,), ring.sibling()
        )

    def pass_on(i):
        pairs[i].wait()

        def add_pair(p, carry):
            both = grads[i][p, ring.core].astype(f32) + pair_in[i][p].astype(f32)
            pair_in[i][p] = both.astype(bf16)
            return carry

        lax.fori_loop(0, chips, add_pair, 0)
        planes[i] = [
            send(
                pair_in[i].at[ring.chip_at(k)], plane_in[i].at[k], plane_sem, (i, k), ring.plane(k)
            )
            for k in range(1, chips)
        ]

    lax.fori_loop(0, count - 1, attend, 0)
    gain = None
    for s in range(seqs):
        if s == 0:
            for m in range(2):
                own[m].wait()
                for copy in rounds[m]:
                    copy.wait_send()
            wait_all(late_pairs)
        if s == seqs - 1:
            attend(count - 1, 0)
        lanes = slice(s * width, (s + 1) * width)
        for h in range(heads):
            n = s * heads + h
            swap_wait(ring, mixed_ref, mixed_in, n, mixed_sem)
            for r in range(ranks):
                at = (r * heads + h) * head
                mixes[at : at + head, lanes] = mixed_in[n, r]
        after = starts[s] + dot_tn(early_ref[:, 3 * D :], mixes[:, lanes])
        normed, inverse = column_rms(after)
        act = (normed * g4).astype(bf16)
        acts[:, lanes] = act
        cot = cot_ref[s].astype(f32).T
        cot_low = cot.astype(bf16)
        cots[:, lanes] = cot_low
        result, grad = after, None
        for c in range(hidden_size // WORD_CHUNK):
            rows = slice(c * WORD_CHUNK, (c + 1) * WORD_CHUNK)
            hidden, slope = gelu_pair(dot_tn(up_ref[:, rows], act))
            hidden = hidden.astype(bf16)
            hiddens[rows, lanes] = hidden
            result = result + dot_tn(down_ref[rows, :], hidden)
            grad_upper = (dot_nn(down_ref[rows, :], cot_low) * slope).astype(bf16)
            grad_ups[rows, lanes] = grad_upper
            piece = dot_nn(up_ref[:, rows], grad_upper)
            grad = piece if grad is None else grad + piece
        piece = fold_lanes(grad * normed)
        gain = piece if gain is None else gain + piece
        total = cot + column_rms_back(grad, g4, normed, inverse)
        afters[s] = total
        low = total.astype(bf16)
        lows[:, lanes] = low
        mixed = dot_nn(early_ref[:, 3 * D :], low).astype(bf16)
        for h in range(heads):
            n = s * heads + h
            for r in range(ranks):
                at = (r * heads + h) * head
                mixed_ref[n, r] = mixed[at : at + head]
            swap_start(ring, mixed_ref, mixed_back, n, mixed_back_sem)
        output_ref[s] = result.T.astype(bf16)
    d_g4[...] = gain
    attend_back(0, 0)
    put_grad(0, dot_nt(hiddens[...], cots[...]))
    lax.fori_loop(1, heads, attend_back, 0)
    pass_on(0)
    lax.fori_loop(heads, count, attend_back, 0)
    put_grad(1, dot_nt(acts[...], grad_ups[...]))
    put_grad(2, dot_nt(mixes[...], lows[...]))
    pass_on(1)
    pass_on(2)
    gain = None
    for s in range(seqs):
        lanes = slice(s * width, (s + 1) * width)
        for h in range(heads):
            n = s * heads + h
            swap_wait(ring, triple_ref, triple_back, n, triple_back_sem)
            for t in range(3):
                for r in range(ranks):
                    at = t * D + (r * heads + h) * head
                    triples[at : at + head, lanes] = head_rows(triple_back, n, r, t)
        normed, inverse = column_rms(starts[s])
        acts[:, lanes] = (normed * g3).astype(bf16)
        grad = dot_nn(early_ref[:, : 3 * D], triples[:, lanes])
        piece = fold_lanes(grad * normed)
        gain = piece if gain is None else gain + piece
        total = afters[s] + column_rms_back(grad, g3, normed, inverse)
        input_grad_ref[s] = total.T
        low = total.astype(bf16)
        lows[:, lanes] = low
        high, rest = split_two(
            dot_nn(in_ref[:, 4 * CD + CFF :], low) / count_ref[s : s + 1, :].astype(f32)
        )
        spread_ref[s, :CD, :] = high
        spread_ref[s, CD:, :] = rest
    d_g3[...] = gain
    d_qkv[...] = dot_nt(acts[...], triples[...]).astype(bf16)
    d_pool[...] = sum(
        dot_nt(pooleds[s], lows[:, s * width : (s + 1) * width]) for s in range(seqs)
    ).astype(bf16)
    for i in range(3):
        total = pair_in[i][ring.chip].astype(f32)
        for k in range(1, chips):
            planes[i][k - 1].wait()
            total = total + plane_in[i][k].astype(f32)
        sums[i][...] = total.astype(bf16)


def word_layer(sums, counts, words, cot, char_in, early, gains, up_rows, down_rows, collective):
    dp, ranks = lax.axis_size("dp"), lax.axis_size("head")
    seqs, width, _ = words.shape
    hidden = up_rows.shape[1] - early.shape[1]
    chips = dp // 2
    bf16, f32 = jnp.bfloat16, jnp.float32
    vmem = pl.BlockSpec(memory_space=pltpu.VMEM)
    anywhere = pl.BlockSpec(memory_space=pl.ANY)
    rows = ((hidden // dp, D), (D // dp, hidden), (D // dp, D))
    columns = seqs * width
    count, head = seqs * HEADS // ranks, D // HEADS
    triple, mixed = (count, ranks, 3 * head, width), (count, ranks, head, width)
    dma = pltpu.SemaphoreType.DMA
    shapes = [
        ((seqs, width, D), bf16),
        ((seqs, width, D), f32),
        ((seqs, 2 * CD, width), bf16),
        ((D, 3 * D), bf16),
        ((CD, D), bf16),
        ((D, GROUP), f32),
        ((D, GROUP), f32),
    ] + [(r, bf16) for r in rows]
    held = [
        ((seqs, D, width), f32),
        ((seqs, CD, width), bf16),
        ((seqs, D, width), f32),
        ((count, ranks, 8, width), f32),
        ((D, hidden), bf16),
        ((hidden, D), bf16),
        ((D, columns), bf16),
        ((hidden, columns), bf16),
        ((hidden, columns), bf16),
        ((D, columns), bf16),
        ((D, columns), bf16),
        ((D, columns), bf16),
        ((3 * D, columns), bf16),
    ]
    held += [(triple, bf16)] * 3 + [(mixed, bf16)] * 3 + [((ranks, head, width), f32)] * 2
    held += [((chips, 2) + r, bf16) for r in rows] + [((chips,) + r, bf16) for r in rows] * 2
    return pl.pallas_call(
        functools.partial(word_kernel, dp, ranks),
        in_specs=[vmem] * 8 + [anywhere] * 2,
        out_specs=[vmem] * len(shapes),
        out_shape=[jax.ShapeDtypeStruct(shape, kind) for shape, kind in shapes],
        scratch_shapes=[pltpu.VMEM(shape, kind) for shape, kind in held]
        + [dma((2,)), dma((2, 2, chips)), dma((2, 2, chips))]
        + [dma((2, count, ranks))] * 4
        + [dma((2, 3)), dma((2, 3, chips))],
        compiler_params=pltpu.CompilerParams(
            collective_id=collective, has_side_effects=True, vmem_limit_bytes=VMEM_BYTES
        ),
        name="word_layer",
    )(sums, counts, words, cot, char_in, early, *gains, up_rows, down_rows)


def block_of(ref, d, h, shard):
    if len(ref.shape) == 4:
        return ref.at[d, h]
    rows, cols = shard.shape
    return ref.at[
        pl.ds(pl.multiple_of(h * rows, rows), rows), pl.ds(pl.multiple_of(d * cols, cols), cols)
    ]


def rows_of(ref, d, shard):
    if len(ref.shape) > 2:
        return ref.at[d]
    cols = shard.shape[1]
    return ref.at[:, pl.ds(pl.multiple_of(d * cols, cols), cols)]


def gather_kernel(dp, ranks, *refs):
    shards, (counts_ref, ids_ref, gains_ref) = refs[:5], refs[5:8]
    outs, (pack_ref, tiles_ref), gain_refs = refs[8:14], refs[14:16], refs[16:20]
    low = refs[20:25]
    own_sem, line_sem, relay_sem, plane_sem, pair_sem, copy_sem = refs[25:]
    table, char_in, down, early, word_rows, down_rows = outs
    ring = Ring(dp, ranks)
    ring.greet()
    for shard, ref in zip(shards, low):
        ref[...] = shard[...].astype(jnp.bfloat16)
    ring.meet()

    def shard_place(m, h):
        if m in (0, 2):
            return block_of((table, down)[m // 2], ring.d, h, low[m])
        wide = low[m].shape[1]
        ref = (None, char_in.at[ring.d], None, word_rows, down_rows)[m]
        return ref.at[:, pl.ds(pl.multiple_of(h * wide, GROUP), wide)]

    four = ranks == 4
    between = lax.rem(ring.h + 1, ranks) >= 2
    own, first = [], []

    def direct(k, act):
        if four and k != 2:
            pl.when(ring.h != (0 if k == 3 else 3))(act)
        else:
            act()

    def along_line(m):
        mine = shard_place(m, ring.h)
        own.append(pltpu.make_async_copy(low[m], mine, own_sem.at[m]))
        own[m].start()
        copies = [
            pltpu.make_async_remote_copy(
                src_ref=low[m],
                dst_ref=mine,
                send_sem=line_sem.at[0, m, k],
                recv_sem=line_sem.at[1, m, k],
                device_id=ring.line(k),
                device_id_type=pl.DeviceIdType.MESH,
            )
            for k in range(1, ranks)
        ]
        for k, copy in enumerate(copies, 1):
            direct(k, copy.start)
        first.append(copies)

    def relayed(m, act):
        if four:

            @pl.when(between)
            def _():
                block = shard_place(m, lax.rem(ring.h + 2, ranks))
                act(
                    pltpu.make_async_remote_copy(
                        src_ref=block,
                        dst_ref=block,
                        send_sem=relay_sem.at[m],
                        recv_sem=line_sem.at[1, m, 2 * ring.h - 1],
                        device_id=(ring.d, 3 * (ring.h - 1)),
                        device_id_type=pl.DeviceIdType.MESH,
                    )
                )

    def relay(m):
        first[m][1].wait_recv()
        relayed(m, lambda copy: copy.start())

    def arrived(m):
        own[m].wait()
        for k in range(1, ranks):
            if k != 2:
                first[m][k - 1].wait_recv()

    blocks = (table, char_in, down)
    second, sent = [], []

    def onward(m, block):
        place = rows_of(blocks[m], ring.d, low[m])
        second.append(
            [send(block, place, plane_sem, (m, k), ring.plane(k)) for k in range(1, ring.chips)]
        )
        sent.append(send(block, place, pair_sem, (m, 0), ring.sibling()))

    for m in range(3):
        along_line(m)
    for m in range(3):
        relay(m)
    for m in range(3):
        arrived(m)
        onward(m, rows_of(blocks[m], ring.d, low[m]))
    along_line(3)
    along_line(4)
    for seq in range(ids_ref.shape[0]):
        pack_words(counts_ref[seq : seq + 1, :], ids_ref[seq], pack_ref, tiles_ref, seq)
    row = 0
    for ref in gain_refs:
        for at in range(0, ref.shape[0], GROUP):
            gain = jnp.broadcast_to(gains_ref[row : row + 1, :], (GROUP, GROUP))
            ref[at : at + GROUP, :] = gain.T
            row += 1
    relay(3)
    for m in range(3):
        for k in range(1, ring.chips):
            second[m][k - 1].wait_recv()
            place = 2 * ring.chip_from(k) + ring.core
            block = rows_of(blocks[m], place, low[m])
            sent.append(send(block, block, pair_sem, (m, k), ring.sibling()))
    relay(4)
    arrived(3)
    copies = []
    for d in range(dp):
        block = word_rows.at[:, : early.shape[2]]
        copies.append(pltpu.make_async_copy(block, early.at[d], copy_sem.at[d]))
        copies[d].start()
    arrived(4)
    wait_all(sent)
    wait_all(copies)
    for m in range(5):
        for k, copy in enumerate(first[m], 1):
            direct(k, copy.wait_send)
        relayed(m, lambda copy: copy.wait_send())
    for m in range(3):
        for copy in second[m]:
            copy.wait_send()


def gather(shards, counts, ids, gains, collective):
    dp, ranks = lax.axis_size("dp"), lax.axis_size("head")
    bf16 = jnp.bfloat16
    vmem = pl.BlockSpec(memory_space=pltpu.VMEM)
    anywhere = pl.BlockSpec(memory_space=pl.ANY)
    table, char_in, down, word_in, word_down = (s.shape for s in shards)
    dma = pltpu.SemaphoreType.DMA

    def narrow(shape):
        if shape[1] % GROUP == 0:
            return (ranks * shape[0], dp * shape[1])
        return (dp, ranks) + shape

    seqs, slots, words = ids.shape
    outs = [
        narrow(table),
        (dp, char_in[0], ranks * char_in[1]),
        narrow(down),
        (dp, word_in[0], 4 * D),
        (word_in[0], ranks * word_in[1]),
        (word_down[0], ranks * word_down[1]),
    ]
    return pl.pallas_call(
        functools.partial(gather_kernel, dp, ranks),
        in_specs=[vmem] * 8,
        out_specs=[anywhere] * 4 + [vmem, anywhere] + [vmem, pl.BlockSpec(memory_space=pltpu.SMEM)] + [vmem] * 4,
        out_shape=[jax.ShapeDtypeStruct(s, bf16) for s in outs]
        + [
            jax.ShapeDtypeStruct((seqs, 4, tile_count(words) * (ROWS // GROUP), GROUP), jnp.int32),
            jax.ShapeDtypeStruct((seqs,), jnp.int32),
        ]
        + [jax.ShapeDtypeStruct((n, GROUP), jnp.float32) for n in (CD, CD, D, D)],
        scratch_shapes=[pltpu.VMEM(s.shape, bf16) for s in shards]
        + [
            dma((5,)),
            dma((2, 5, ranks)),
            dma((5,)),
            dma((2, 4, dp // 2)),
            dma((2, 4, dp // 2)),
            dma((dp,)),
        ],
        compiler_params=pltpu.CompilerParams(
            collective_id=collective, has_side_effects=True, vmem_limit_bytes=VMEM_BYTES
        ),
        name="gather",
    )(*shards, counts, ids, gains)


def column_cuts(widths, ranks):
    block = sum(widths) // ranks
    cuts, start = [], 0
    for width in widths:
        mine, at = [], 0
        while at < width:
            rank, inside = divmod(start + at, block)
            take = min(width - at, block - inside)
            mine.append((rank, at, at + take, inside))
            at += take
        cuts.append(mine)
        start += width
    return cuts


def reduce_kernel(dp, ranks, groups, extra, *refs):
    pieces = sum(len(g) - done for g, done in groups)
    mats = len(groups)
    parts = refs[:pieces]
    gain_refs = refs[pieces : pieces + 4]
    ready = refs[pieces + 4 : pieces + 4 + extra]
    place = pieces + 4 + extra
    outs = refs[place : place + mats]
    gain_out, square_out = refs[place + mats : place + mats + 2]
    place += mats + 2
    pair_in = refs[place : place + pieces]
    pair_sum = refs[place + pieces : place + 2 * pieces]
    plane_in = refs[place + 2 * pieces : place + 3 * pieces]
    place += 3 * pieces
    line_sum, line_in = refs[place : place + mats], refs[place + mats : place + 2 * mats]
    place += 2 * mats
    small, pair_sem, plane_sem, line_sem, small_sem = refs[place:]
    ring = Ring(dp, ranks)
    chips = ring.chips
    f32, bf16 = jnp.float32, jnp.bfloat16
    ring.greet(all_dp=True)

    def share(slot, value, stage):
        peer, here, count = ((ring.across, ring.d, dp), (ring.line, ring.h, ranks))[stage]
        small[slot, stage, here] = value
        spot = small.at[slot, stage, here]
        return [send(spot, spot, small_sem, (slot, stage, k), peer(k)) for k in range(1, count)]

    def shared(slot, copies, stage):
        wait_all(copies)
        total = small[slot, stage, 0]
        for k in range(1, (dp, ranks)[stage]):
            total = total + small[slot, stage, k]
        return total

    def line_copy(m, k):
        return pltpu.make_async_remote_copy(
            src_ref=line_sum[m].at[ring.rank_at(k)],
            dst_ref=line_in[m].at[k],
            send_sem=line_sem.at[0, m, k],
            recv_sem=line_sem.at[1, m, k],
            device_id=ring.line(k),
            device_id_type=pl.DeviceIdType.MESH,
        )

    def row_block(ref):
        if len(ref.shape) == 2:
            return ref[...]
        total = ref[0].astype(f32)
        for k in range(1, ref.shape[0]):
            total = total + ref[k].astype(f32)
        return total.astype(bf16)

    def put_columns(m, cuts, total):
        for rank, first, last, inside in cuts:
            line_sum[m][rank, :, inside : inside + last - first] = total[:, first:last]

    def early_rank(m):
        widths, done = groups[m]
        own = sum(widths[: len(widths) - done])
        ready_from = sum(
            w for at, w in enumerate(widths) if at < len(widths) - done
        ) if done else sum(widths)
        block = sum(widths) // ranks
        return -(-max(own, ready_from) // block)

    def begin(copy, now, first):
        if first == 0:
            copy.start()
        elif first < ranks:
            pl.when(now)(copy.start)

    starts = []
    j = 0
    for m, (widths, done) in enumerate(groups):
        lines = [line_copy(m, k) for k in range(1, ranks)]
        starts.append(lines)
        cuts = column_cuts(widths, ranks)
        for at in range(len(widths) - done, len(widths)):
            put_columns(m, cuts[at], row_block(ready[j]))
            j += 1
    rows = []
    for ref in gain_refs:
        for at in range(0, ref.shape[0], GROUP):
            rows.append(jnp.sum(ref[at : at + GROUP, :].T, axis=0, keepdims=True))
    rows.append(jnp.zeros((small.shape[3] - len(rows), GROUP), f32))
    ring.meet()
    pairs = [
        send(parts[i].at[:, 1 - ring.core], pair_in[i], pair_sem, (i,), ring.sibling())
        for i in range(pieces)
    ]
    for m in range(mats):
        for k in range(1, ranks):
            begin(starts[m][k - 1], early_rank(m) <= ring.rank_at(k), early_rank(m))
    gain_copies = share(0, jnp.concatenate(rows, axis=0), 0)
    planes = []
    for i in range(pieces):
        pairs[i].wait()

        def add_pair(p, carry, i=i):
            both = parts[i][p, ring.core].astype(f32) + pair_in[i][p].astype(f32)
            pair_sum[i][p] = both.astype(bf16)
            return carry

        lax.fori_loop(0, chips, add_pair, 0)
        planes.append(
            [
                send(
                    pair_sum[i].at[ring.chip_at(k)],
                    plane_in[i].at[k],
                    plane_sem,
                    (i, k),
                    ring.plane(k),
                )
                for k in range(1, chips)
            ]
        )
    gain_copies = share(0, shared(0, gain_copies, 0), 1)
    i = 0
    for m, (widths, done) in enumerate(groups):
        for cuts in column_cuts(widths, ranks)[: len(widths) - done]:
            total = pair_sum[i][ring.chip].astype(f32)
            for k in range(1, chips):
                planes[i][k - 1].wait()
                total = total + plane_in[i][k].astype(f32)
            put_columns(m, cuts, total.astype(bf16))
            i += 1
        first = early_rank(m)
        for k in range(1, ranks):
            if first >= ranks:
                starts[m][k - 1].start()
            elif first > 0:
                pl.when(ring.rank_at(k) < first)(starts[m][k - 1].start)
    square = jnp.zeros(square_out.shape, f32)

    def squares(value):
        value = value * value
        rows, cols = value.shape
        if cols % GROUP:
            value = jnp.concatenate([value, jnp.zeros((rows, GROUP - cols % GROUP), f32)], axis=1)
        return jnp.sum(fold_lanes(value).reshape(rows // 8, 8, GROUP), axis=0)

    for m in range(mats):
        total = line_sum[m][ring.h].astype(f32)
        for k in range(1, ranks):
            starts[m][k - 1].wait()
            total = total + line_in[m][k].astype(f32)
        outs[m][...] = total if outs[m].shape == total.shape else total.T
        square = square + squares(total)
    small_square = jnp.concatenate([square, jnp.zeros_like(square)], axis=0)
    square_copies = share(1, small_square, 0)
    gain_out[...] = shared(0, gain_copies, 1)[: gain_out.shape[0]]
    square_copies = share(1, shared(1, square_copies, 0), 1)
    square_out[...] = shared(1, square_copies, 1)[:8]


def reduce_grads(groups, gains, collective):
    dp, ranks = lax.axis_size("dp"), lax.axis_size("head")
    chips = dp // 2
    bf16, f32 = jnp.bfloat16, jnp.float32
    pieces, ready, widths, shards = [], [], [], []
    for group, done in groups:
        rows = done[0].shape[-2] if done else group[0].shape[0] // dp
        pieces += [p.reshape(chips, 2, rows, p.shape[1]) for p in group]
        ready += done
        widths.append((tuple(p.shape[-1] for p in group + done), len(done)))
        shards.append((rows, sum(widths[-1][0]) // ranks))
    blocks = [p.shape[2:] for p in pieces]
    vmem = pl.BlockSpec(memory_space=pltpu.VMEM)
    n, mats = len(pieces), len(groups)
    gain_rows = sum(g.shape[0] for g in gains) // GROUP
    return pl.pallas_call(
        functools.partial(reduce_kernel, dp, ranks, widths, len(ready)),
        in_specs=[vmem] * (n + 4 + len(ready)),
        out_specs=[vmem] * (mats + 2),
        out_shape=[jax.ShapeDtypeStruct(s if s[1] % GROUP == 0 else s[::-1], f32) for s in shards]
        + [jax.ShapeDtypeStruct((gain_rows, GROUP), f32), jax.ShapeDtypeStruct((8, GROUP), f32)],
        scratch_shapes=[pltpu.VMEM((chips,) + b, bf16) for b in blocks] * 3
        + [pltpu.VMEM((ranks,) + s, bf16) for s in shards] * 2
        + [
            pltpu.VMEM((2, 2, max(dp, ranks), 16, GROUP), f32),
            pltpu.SemaphoreType.DMA((2, n)),
            pltpu.SemaphoreType.DMA((2, n, chips)),
            pltpu.SemaphoreType.DMA((2, mats, ranks)),
            pltpu.SemaphoreType.DMA((2, 2, 2, max(dp, ranks))),
        ],
        compiler_params=pltpu.CompilerParams(
            collective_id=collective, has_side_effects=True, vmem_limit_bytes=VMEM_BYTES
        ),
        name="reduce_grads",
    )(*pieces, *gains, *ready)


def update_kernel(count, *refs):
    weights, grads = refs[:count], refs[count : 2 * count]
    firsts, seconds = refs[2 * count : 3 * count], refs[3 * count : 4 * count]
    square_ref = refs[4 * count]
    norm_ref, outs = refs[4 * count + 1], refs[4 * count + 2 :]
    gain_grad = grads[-1][...]
    square = jnp.sum(square_ref[...]) + jnp.sum(gain_grad * gain_grad)
    norm = jnp.sqrt(jnp.full((1, GROUP), square, jnp.float32))
    norm_ref[...] = norm
    clip_factor = jnp.minimum(1.0, CLIP / norm)[:, :1]
    for i in range(count):
        gains = i == count - 1
        result = adam_step(
            weights[i][...],
            grads[i][...],
            firsts[i][...],
            seconds[i][...],
            clip_factor,
            GAIN_RATE if gains else MATRIX_RATE,
            0.0 if gains else MATRIX_DECAY,
        )
        for ref, value in zip(outs[5 * i : 5 * i + 5], result):
            ref[...] = value


def update(weights, grads, firsts, seconds, square):
    count = len(weights)
    shapes = [jax.ShapeDtypeStruct((1, GROUP), jnp.float32)]
    for w in weights:
        shapes += [jax.ShapeDtypeStruct(w.shape, jnp.float32)] * 4
        shapes.append(jax.ShapeDtypeStruct(w.shape, jnp.bfloat16))
    return pl.pallas_call(
        functools.partial(update_kernel, count),
        out_shape=shapes,
        compiler_params=pltpu.CompilerParams(vmem_limit_bytes=VMEM_BYTES),
        name="update",
    )(*weights, *grads, *firsts, *seconds, square)


def body(
    char_ids,
    char_counts,
    language,
    words_in,
    out_cotangent,
    char_table,
    char_in,
    char_down,
    word_in,
    word_down,
    norm_gains,
    old_table_first,
    old_table_second,
    old_char_in_first,
    old_char_in_second,
    old_char_down_first,
    old_char_down_second,
    old_word_in_first,
    old_word_in_second,
    old_word_down_first,
    old_word_down_second,
    old_gains_first,
    old_gains_second,
):
    narrow = (norm_gains.shape[0] // GROUP, GROUP)
    table_t, char_in_low, char_down_t, early, up_rows, down_rows, packed, tiles, *gains = gather(
        (char_table.T, char_in, char_down.T, word_in, word_down),
        char_counts,
        char_ids.transpose(0, 2, 1),
        norm_gains.reshape(narrow),
        0,
    )

    def joined(block):
        if block.ndim == 2:
            return block
        dp, ranks, cols, rows = block.shape
        return block.transpose(1, 2, 0, 3).reshape(ranks * cols, dp * rows)

    def stacked(block):
        return block.reshape(-1, block.shape[2])

    table_t = joined(table_t)
    char_in_low = stacked(char_in_low)
    early = stacked(lax.all_to_all(early, "dp", 0, 0, tiled=True))
    char_others = (char_in_low, joined(char_down_t), gains[0], gains[1])
    sums, *kept = char_fwd(tiles, language, packed, table_t, char_others, words_in.shape[1])
    (
        output,
        input_grad,
        spread,
        grad_qkv,
        grad_pool,
        gain_three,
        gain_four,
        down_sum,
        up_sum,
        out_sum,
    ) = word_layer(
        sums,
        char_counts,
        words_in,
        out_cotangent,
        char_in_low,
        early,
        gains[2:],
        up_rows,
        down_rows,
        1,
    )
    grad_table, grad_in, grad_down, gain_one, gain_two = char_bwd(
        tiles, language, packed, table_t, char_others, spread, kept
    )
    qkv_blocks = lax.all_to_all(
        grad_qkv.reshape(lax.axis_size("dp"), -1, grad_qkv.shape[1]), "dp", 0, 0, tiled=True
    )
    *shards, gains_sum, square = reduce_grads(
        [
            ([grad_table], []),
            ([grad_in, grad_pool], []),
            ([grad_down], []),
            ([], [qkv_blocks, out_sum, up_sum]),
            ([], [down_sum]),
        ],
        (gain_one, gain_two, gain_three, gain_four),
        2,
    )

    def turned(parts):
        parts = list(parts)
        parts[0], parts[2] = parts[0].T, parts[2].T
        parts[5] = parts[5].reshape(narrow)
        return parts

    norm, *updated = update(
        turned((char_table, char_in, char_down, word_in, word_down, norm_gains)),
        (*shards, gains_sum),
        turned(
            (
                old_table_first,
                old_char_in_first,
                old_char_down_first,
                old_word_in_first,
                old_word_down_first,
                old_gains_first,
            )
        ),
        turned(
            (
                old_table_second,
                old_char_in_second,
                old_char_down_second,
                old_word_in_second,
                old_word_down_second,
                old_gains_second,
            )
        ),
        square,
    )
    for place in (*range(5), *range(10, 15)):
        updated[place] = updated[place].T
    updated[-5:] = [part.reshape(norm_gains.shape) for part in updated[-5:]]
    return (output, input_grad, norm[0, 0], *updated)


def solution(mesh):
    return jax.shard_map(
        body,
        mesh=mesh,
        in_specs=(
            P("dp", "head", None),
            P("dp", "head"),
            P("dp"),
            P("dp", "head", None),
            P("dp", "head", None),
            P("dp", "head"),
            P("dp", "head"),
            P("dp", "head"),
            P("dp", "head"),
            P("dp", "head"),
            P(),
            P("dp", "head"),
            P("dp", "head"),
            P("dp", "head"),
            P("dp", "head"),
            P("dp", "head"),
            P("dp", "head"),
            P("dp", "head"),
            P("dp", "head"),
            P("dp", "head"),
            P("dp", "head"),
            P(),
            P(),
        ),
        out_specs=(
            P("dp", "head", None),
            P("dp", "head", None),
            P(),
            P("dp", "head"),
            P("dp", "head"),
            P("dp", "head"),
            P("dp", "head"),
            P("dp", "head"),
            P("dp", "head"),
            P("dp", "head"),
            P("dp", "head"),
            P("dp", "head"),
            P("dp", "head"),
            P("dp", "head"),
            P("dp", "head"),
            P("dp", "head"),
            P("dp", "head"),
            P("dp", "head"),
            P("dp", "head"),
            P("dp", "head"),
            P("dp", "head"),
            P("dp", "head"),
            P("dp", "head"),
            P("dp", "head"),
            P("dp", "head"),
            P("dp", "head"),
            P("dp", "head"),
            P("dp", "head"),
            P(),
            P(),
            P(),
            P(),
            P(),
        ),
        check_vma=False,
    )
```
